32 devices in a mesh: rep: 2 (over x), shard: 16 (over z, y, core).
Axes of the slice: x: 2, y: 2, z: 4, core: 2. Of those that a mesh axis runs over, the one named last changes fastest.
Arguments:
- inputs: bfloat16 [4096, 1024], P(('rep', 'shard')), may hold values from -6 to 6
- ff_in: bfloat16 [1, 2, 1024, 4096], P(None, None, 'shard'), may hold values from -0.1875 to 0.1875
- ff_out: bfloat16 [1, 2, 4096, 1024], P(None, None, 'shard'), may hold values from -0.09375 to 0.09375
- ff_bias: bfloat16 [1, 2, 4096], P(None, None, 'shard'), may hold values from -3 to 3
- attn_in: bfloat16 [1, 1024, 3072], P(None, 'shard'), may hold values from -0.1875 to 0.1875
- attn_out: bfloat16 [1, 1024, 1024], P(None, 'shard'), may hold values from -1.5 to 1.5
- conv_in: bfloat16 [1, 1024, 2048], P(None, 'shard'), may hold values from -0.1875 to 0.1875
- conv_out: bfloat16 [1, 1024, 1024], P(None, 'shard'), may hold values from -0.1875 to 0.1875
- depthwise: bfloat16 [1, 31, 1024], P(None, None, 'shard'), may hold values from -1 to 1
- distance: bfloat16 [1, 73, 64], replicated, may hold values from -4 to 4
- vectors: bfloat16 [1, 16, 1024], P(None, None, 'shard'), may hold values from -0.91 to 1.61, as said below
- attn_bias: bfloat16 [1, 1024], P(None, 'shard'), may hold values from -0.8984375 to 0.8984375
- cotangent: bfloat16 [4096, 1024], P(('rep', 'shard')), may hold values from -6 to 6
Outputs:
- output: bfloat16 [4096, 1024], P(('rep', 'shard'))
- grad_input: float32 [4096, 1024], P(('rep', 'shard'))
- grad_ff_in: float32 [1, 2, 1024, 4096], P(None, None, 'shard')
- grad_ff_out: float32 [1, 2, 4096, 1024], P(None, None, 'shard')
- grad_ff_bias: float32 [1, 2, 4096], P(None, None, 'shard')
- grad_attn_in: float32 [1, 1024, 3072], P(None, 'shard')
- grad_attn_out: float32 [1, 1024, 1024], P(None, 'shard')
- grad_conv_in: float32 [1, 1024, 2048], P(None, 'shard')
- grad_conv_out: float32 [1, 1024, 1024], P(None, 'shard')
- grad_depthwise: float32 [1, 31, 1024], P(None, None, 'shard')
- grad_distance: float32 [1, 73, 64], replicated
- grad_vectors: float32 [1, 16, 1024], P(None, None, 'shard')
- grad_attn_bias: float32 [1, 1024], P(None, 'shard')
The draws below stay inside these ranges and needn't reach their ends.
Inputs may be any that keep to these rules, and one draw needn't show every extreme that they name: `vectors`: in each layer rows 0, 3, 7, 9, 11 and 14 are gains near one and the other rows are biases.
All inputs are finite; a program needn't handle non-finite values.
Results may differ from the reference program's by a relative error of at most 0.015.
Values may be sent and summed in bfloat16 or wider, within the bound.
No kernel may reach another device: no remote copies, remote signals or barrier semaphores. Data moves between devices by JAX's collectives and lax.ppermute only.
A program may use at most 256 MiB of HBM per device.

```python
import jax
import jax.numpy as jnp
from jax import lax

D = 1024
HEADS = 16
HEAD = 64
FF = 4096
KW = 31
LEFT = 64
RIGHT = 8
NREL = 73
NVEC = 16
LAYERS = 1
LENGTH = 1024
TOKENS = 4096


def draw_vectors(key, part):
    key = jax.random.fold_in(key, 11)
    row_ids = jnp.arange(NVEC)
    gain_rows = (row_ids == 0) | (row_ids == 3) | (row_ids == 7) | (row_ids == 9) | (row_ids == 11) | (row_ids == 14)
    base = jnp.clip(jax.random.normal(key, (LAYERS, NVEC, D), jnp.float32), -3.0, 3.0)
    values = jnp.where(gain_rows[None, :, None], 1.0 + 0.2 * base, 0.3 * base)
    return values.astype(jnp.bfloat16)


def spiked(array, own_key, source, target, blocks, factor):
    def block_of(dim):
        return (jnp.arange(array.shape[dim]) // (array.shape[dim] // blocks)).reshape((-1,) + (1,) * (array.ndim - 1 - dim))

    one_side = jax.random.permutation(own_key, blocks)[block_of(target)]
    far = (block_of(target) + blocks // 2) % blocks
    return jnp.where((block_of(source) == one_side) | (block_of(source) == far), factor * array, array)


def level_of(key, extent, pieces, least, largest):
    factor_of = 1.0
    for dim, blocks in pieces:
        draws = jax.random.uniform(jax.random.fold_in(jax.random.fold_in(key, 6), dim), (blocks,), jnp.float32, least / len(pieces), largest / len(pieces))
        factor_of = factor_of * jnp.repeat(jnp.exp(draws), extent[dim] // blocks).reshape((-1,) + (1,) * (len(extent) - 1 - dim))
    return factor_of


def bell_draw(rng, dims, deviation, bound, split=(), kind=jnp.bfloat16):
    array = deviation * jax.random.normal(rng, dims, jnp.float32)
    if split:
        array = array * level_of(rng, dims, split, -0.22, 0.18)
    return jnp.clip(array, -bound, bound).astype(kind)


def gaussian_with(stream_key, extent, deviation, bound, split, heavy, held_as=jnp.bfloat16):
    entries = deviation * jax.random.normal(stream_key, extent, jnp.float32)
    if split:
        entries = entries * level_of(stream_key, extent, split, -0.22, 0.18)
    return jnp.clip(spiked(entries, jax.random.fold_in(stream_key, 3), *heavy), -bound, bound).astype(held_as)


def setup_inputs(seed: int = 0) -> dict:
    keys = jax.random.split(jax.random.key(seed), 14)
    return {
        "inputs": bell_draw(keys[0], (TOKENS, D), 1.0, 6.0, ((0, 32),)),
        "ff_in": bell_draw(keys[1], (LAYERS, 2, D, FF), D ** -0.5, 0.1875, ((2, 16),)),
        "ff_out": bell_draw(keys[2], (LAYERS, 2, FF, D), FF ** -0.5, 0.09375, ((2, 16),)),
        "ff_bias": bell_draw(keys[3], (LAYERS, 2, FF), 0.5, 3.0, ((2, 16),)),
        "attn_in": bell_draw(keys[4], (LAYERS, D, 3 * D), D ** -0.5, 0.1875, ((1, 16),)),
        "attn_out": bell_draw(keys[5], (LAYERS, D, D), (D // 64) ** -0.5, 1.5, ((1, 16),)),
        "conv_in": bell_draw(keys[6], (LAYERS, D, 2 * D), D ** -0.5, 0.1875, ((1, 16),)),
        "conv_out": bell_draw(keys[7], (LAYERS, D, D), D ** -0.5, 0.1875, ((1, 16),)),
        "depthwise": bell_draw(keys[8], (LAYERS, KW, D), KW ** -0.5, 1.0, ((2, 16),)),
        "distance": bell_draw(keys[9], (LAYERS, NREL, HEAD), 1.0, 4.0),
        "vectors": draw_vectors(jax.random.fold_in(keys[13], 71), 0),
        "attn_bias": bell_draw(keys[11], (LAYERS, D), 0.3, 0.8984375, ((1, 16),)),
        "cotangent": gaussian_with(keys[12], (TOKENS, D), 1.0, 6.0, ((0, 32),), (0, 1, 32, 2.75)),
    }


EPSILON = 1e-05
HIGHEST = lax.Precision.HIGHEST

@jax.custom_vjp
def low(v):
    return lax.optimization_barrier(v.astype(jnp.bfloat16)).astype(jnp.float32)

@jax.custom_vjp
def low_back(v):
    return v

def low_keep(v):
    return (low(v), None)

def low_pass(kept, grad):
    return (grad,)

def back_keep(v):
    return (v, None)

def back_low(kept, grad):
    return (low(grad),)
low.defvjp(low_keep, low_pass)
low_back.defvjp(back_keep, back_low)

def product(left_side, right_side):
    return jnp.dot(left_side, right_side, precision=HIGHEST)

def normalize(values, gain_row, shift_row):
    center = values - lax.optimization_barrier(jnp.mean(values, axis=-1, keepdims=True))
    spread = lax.optimization_barrier(jnp.mean(center * center, axis=-1, keepdims=True))
    return center * lax.rsqrt(spread + EPSILON) * gain_row + shift_row

def feed(current, weight_in, bias_in, weight_out, bias_out, gain_row, shift_row):
    hidden = low(normalize(current, gain_row, shift_row))
    upper = low_back(product(hidden, weight_in) + bias_in)
    active = low(jax.nn.silu(upper))
    return low_back(product(active, weight_out) + bias_out)

def attend(current, weight_mix, weight_out, out_bias, distance, vector):
    length = current.shape[0]
    hidden = low(normalize(current, vector[3], vector[4]))
    mixed_rows = product(hidden, weight_mix)
    queries = low(low_back(mixed_rows[:, :D] + vector[5]))
    key_rows = low(low_back(mixed_rows[:, D:2 * D]))
    values = low(low_back(mixed_rows[:, 2 * D:] + vector[6]))
    queries = queries.reshape(length, HEADS, HEAD).transpose(1, 0, 2)
    key_rows = key_rows.reshape(length, HEADS, HEAD).transpose(1, 0, 2)
    values = values.reshape(length, HEADS, HEAD).transpose(1, 0, 2)
    direct = jnp.einsum('hqe,hke->hqk', queries, key_rows, precision=HIGHEST)
    bucket_table = jnp.einsum('hqe,re->hqr', queries, distance, precision=HIGHEST)
    position = jnp.arange(length).astype(jnp.int32)
    bucket = (jnp.clip(position[None, :] - position[:, None], -LEFT, RIGHT) + LEFT).astype(jnp.int32)
    relative = jnp.take_along_axis(bucket_table, jnp.broadcast_to(bucket[None], (HEADS, length, length)), axis=2)
    scores = low_back((direct + relative) * HEAD ** (-0.5))
    weights_low = low(jax.nn.softmax(scores, axis=-1))
    context = jnp.einsum('hqk,hke->hqe', weights_low, values, precision=HIGHEST)
    context = low(low_back(context.transpose(1, 0, 2).reshape(length, D)))
    return low_back(product(context, weight_out) + out_bias)

def convolve(current, weight_in, depth, weight_out, vector):
    length = current.shape[0]
    hidden = low(normalize(current, vector[7], vector[8]))
    doubled = low_back(product(hidden, weight_in))
    glued = low(low_back(doubled[:, :D] * jax.nn.sigmoid(doubled[:, D:])))
    padded = jnp.concatenate([jnp.zeros((KW - 1, D), jnp.float32), glued], axis=0)
    summed = padded[0:length] * depth[0]
    for tap_id in range(1, KW):
        summed = summed + padded[tap_id:tap_id + length] * depth[tap_id]
    rest = low(jax.nn.silu(normalize(summed, vector[9], vector[10])))
    return low_back(product(rest, weight_out))

def layer_step(current, ff_in, ff_out, ff_bias, attn_in, attn_out, conv_in, conv_out, depth, distance, vector, out_bias):
    current = current + 0.5 * feed(current, ff_in[0], ff_bias[0], ff_out[0], vector[2], vector[0], vector[1])
    current = current + attend(current, attn_in, attn_out, out_bias, distance, vector)
    current = current + convolve(current, conv_in, depth, conv_out, vector)
    current = current + 0.5 * feed(current, ff_in[1], ff_bias[1], ff_out[1], vector[13], vector[11], vector[12])
    return normalize(current, vector[14], vector[15])

def stack_layers(current, weights):
    for layer_id in range(LAYERS):
        current = layer_step(current, *[item[layer_id] for item in weights])
    return current

def reference(inputs, ff_in, ff_out, ff_bias, attn_in, attn_out, conv_in, conv_out, depthwise, distance, vectors, attn_bias, cotangent):
    weights = tuple((item.astype(jnp.float32) for item in (ff_in, ff_out, ff_bias, attn_in, attn_out, conv_in, conv_out, depthwise, distance, vectors, attn_bias)))
    seq_count = inputs.shape[0] // LENGTH
    sequences = inputs.astype(jnp.float32).reshape(seq_count, LENGTH, D)
    cotangents = cotangent.astype(jnp.float32).reshape(seq_count, LENGTH, D)

    def one_sequence(totals, pair):
        result, pullback = jax.vjp(stack_layers, pair[0], weights)
        grad_in, grad_weights = pullback(pair[1])
        return (tuple((total + piece for total, piece in zip(totals, grad_weights))), (result, grad_in))
    start = tuple((jnp.zeros(item.shape, jnp.float32) for item in weights))
    totals, (results, grads) = lax.scan(one_sequence, start, (sequences, cotangents))
    output = results.reshape(-1, D).astype(jnp.bfloat16)
    grad_input = grads.reshape(-1, D)
    return (output, grad_input, totals[0], totals[1], totals[2], totals[3], totals[4], totals[5], totals[6], totals[7], totals[8], totals[9], totals[10])
```

```python
import functools

import jax
import jax.numpy as jnp
from jax import lax
from jax.experimental import pallas as pl
from jax.experimental.pallas import tpu as pltpu
from jax.sharding import PartitionSpec as P

LEFT = 64
RIGHT = 8
SPAN = 8
QUAD = 4
EPSILON = 1e-05
BF = jnp.bfloat16
F32 = jnp.float32
MIB = 1 << 20


def dot_nn(left, right):
    return jnp.dot(left, right, preferred_element_type=F32)


def dot_nt(left, right):
    return lax.dot_general(left, right, (((1,), (1,)), ((), ())), preferred_element_type=F32)


def dot_tn(left, right):
    return lax.dot_general(left, right, (((0,), (0,)), ((), ())), preferred_element_type=F32)


def column_sum(values):
    return jnp.sum(values.astype(F32), axis=0, keepdims=True)


def standard(values):
    center = values - jnp.mean(values, axis=-1, keepdims=True)
    scale = lax.rsqrt(jnp.mean(center * center, axis=-1, keepdims=True) + EPSILON)
    return center * scale, scale


def norm_back(values, gain, grad):
    unit, scale = standard(values)
    inner = grad * gain
    first = jnp.mean(inner, axis=-1, keepdims=True)
    second = jnp.mean(inner * unit, axis=-1, keepdims=True)
    return scale * (inner - first - unit * second), column_sum(grad * unit), column_sum(grad)


def logistic(values):
    return 1.0 / (1.0 + jnp.exp(-values))


def silu_slope(values):
    gate = logistic(values)
    return gate * (1.0 + values * (1.0 - gate))


def vmem(count):
    return [pl.BlockSpec(memory_space=pltpu.VMEM)] * count


def shape_of(rows, columns, dtype):
    return jax.ShapeDtypeStruct((rows, columns), dtype)


def kernel_call(body, name, outs, operands, scalars=0, scratch=(), flops=0):
    moved = sum(item.size * item.dtype.itemsize for item in (*operands[scalars:], *outs))
    return pl.pallas_call(
        body,
        in_specs=[pl.BlockSpec(memory_space=pltpu.SMEM)] * scalars
        + vmem(len(operands) - scalars),
        out_specs=vmem(len(outs)),
        out_shape=list(outs),
        scratch_shapes=list(scratch),
        compiler_params=pltpu.CompilerParams(vmem_limit_bytes=48 * MIB),
        cost_estimate=pl.CostEstimate(flops=flops, bytes_accessed=moved, transcendentals=0),
        name=name,
    )(*operands)


def fused(body, name, outs, *operands, flops=0):
    def kernel(*refs):
        results = body(*[ref[...] for ref in refs[: len(operands)]])
        for ref, value in zip(refs[len(operands) :], results):
            ref[...] = value.astype(ref.dtype)

    return kernel_call(kernel, name, outs, operands, flops=flops)


def flipped(value, mask):
    total = lax.axis_size("rep") * lax.axis_size("shard")
    return lax.ppermute(value, ("rep", "shard"), [(i, i ^ mask) for i in range(total)])


def ordered(pieces, position, name):
    rows, columns = pieces[0].shape

    def kernel(spot, *refs):
        for step, ref in enumerate(refs[:-1]):
            target = pl.multiple_of((spot[0] ^ step) * rows, rows)
            refs[-1][pl.ds(target, rows), :] = ref[...]

    out = shape_of(rows * len(pieces), columns, pieces[0].dtype)
    return kernel_call(kernel, name, [out], (position, *pieces), scalars=1)[0]


def group_gather(value, masks):
    first, second, core = masks
    half = value.shape[0] // 2
    via_first = flipped(value, first)
    via_second = flipped(value, second)
    cross = jnp.concatenate(
        [flipped(via_first[:half], second), flipped(via_second[half:], first)], axis=0
    )
    near = [value, via_first, via_second, cross]
    return near, [flipped(item, core) for item in near]


def group_reduce(kept, sent, masks):
    first, second, core = masks
    rows = kept.shape[0] // 4
    half = rows // 2
    swapped = flipped(sent, core)

    def corner(kept_part, swapped_part):
        total = kept_part[...] + swapped_part[...].astype(F32)
        return total[:half], total[half:]

    low, high = fused(
        corner,
        "reduce_corner",
        [shape_of(half, kept.shape[1], BF)] * 2,
        kept[3 * rows :],
        swapped[3 * rows :],
    )
    low, high = flipped(low, first), flipped(high, second)

    def sides(kept_part, swapped_part, low_part, high_part):
        total = kept_part + swapped_part.astype(F32)
        via_first, via_second = total[rows : 2 * rows], total[2 * rows :]
        via_first = jnp.concatenate(
            [via_first[:half], via_first[half:] + high_part.astype(F32)], axis=0
        )
        via_second = jnp.concatenate(
            [via_second[:half] + low_part.astype(F32), via_second[half:]], axis=0
        )
        return total[:rows], via_first, via_second

    own, via_first, via_second = fused(
        sides,
        "reduce_sides",
        [shape_of(rows, kept.shape[1], dtype) for dtype in (F32, BF, BF)],
        kept[: 3 * rows],
        swapped[: 3 * rows],
        low,
        high,
    )
    return own, flipped(via_first, first), flipped(via_second, second)


def joined(parts):
    return parts[0] + parts[1].astype(F32) + parts[2].astype(F32)


def feed_half(pieces, weight_in, bias, weight_out, norm_rows, out_dtype):
    rows = sum(item.shape[0] for item in pieces)
    width, inner = weight_in.shape
    count = len(pieces)

    def body(*values):
        hidden = jnp.concatenate(values[:count], axis=0)
        w_in, b_in, w_out, gain, shift = values[count:]
        if norm_rows is not None:
            unit, unused_scale = standard(hidden.astype(F32))
            hidden = (unit * gain + shift).astype(BF)
        upper = dot_nn(hidden, w_in) + b_in
        active = (upper * logistic(upper)).astype(BF)
        return hidden, upper, active, dot_nn(active, w_out)

    gain, shift = (bias[:, :8], bias[:, :8]) if norm_rows is None else norm_rows
    return fused(
        body,
        "feed_forward",
        [
            shape_of(rows, width, BF),
            shape_of(rows, inner, F32),
            shape_of(rows, inner, BF),
            shape_of(rows, width, out_dtype),
        ],
        *pieces,
        weight_in,
        bias,
        weight_out,
        gain,
        shift,
        flops=4 * rows * width * inner,
    )


def feed(blocks, weight_in, bias, weight_out, norm_rows, masks):
    near, far = blocks
    saved_far = feed_half(far, weight_in, bias, weight_out, norm_rows, BF)
    saved_near = feed_half(near, weight_in, bias, weight_out, norm_rows, F32)
    parts = group_reduce(saved_near[3], saved_far[3], masks)
    return parts, (saved_near[:3], saved_far[:3])


def feed_back_half(pieces, saved, weight_in, weight_out, out_dtype):
    upper = saved[1]
    rows, inner = upper.shape
    width = weight_in.shape[0]
    count = len(pieces)

    def body(*values):
        branch = jnp.concatenate(values[:count], axis=0)
        before, w_in, w_out = values[count:]
        slope = (dot_nt(branch, w_out) * silu_slope(before)).astype(BF)
        return branch, slope, column_sum(slope), dot_nt(slope, w_in)

    return fused(
        body,
        "feed_backward",
        [
            shape_of(rows, width, BF),
            shape_of(rows, inner, BF),
            shape_of(1, inner, F32),
            shape_of(rows, width, out_dtype),
        ],
        *pieces,
        upper,
        weight_in,
        weight_out,
        flops=4 * rows * width * inner,
    )


def token_product(left, right, position, places, name):
    rows, columns = left[0].shape[1], right[0].shape[1]
    extent = rows // places

    def kernel(spot, left_near, left_far, right_near, right_far, *refs):
        total = refs[-1]
        total[...] = dot_tn(left_near[...], right_near[...])
        total[...] += dot_tn(left_far[...], right_far[...])
        for step, ref in enumerate(refs[:-1]):
            source = pl.multiple_of((spot[0] ^ step) * extent, extent)
            ref[...] = total[pl.ds(source, extent), :].astype(ref.dtype)

    outs = [shape_of(extent, columns, F32)] + [shape_of(extent, columns, BF)] * (places - 1)
    return kernel_call(
        kernel,
        name,
        outs,
        (position, *left, *right),
        scalars=1,
        scratch=[pltpu.VMEM((rows, columns), F32)],
        flops=4 * left[0].shape[0] * rows * columns,
    )


def feed_back(blocks, saved, weight_in, weight_out, masks, plane, planes):
    saved_near, saved_far = saved
    far = feed_back_half(blocks[1], saved_far, weight_in, weight_out, BF)
    near = feed_back_half(blocks[0], saved_near, weight_in, weight_out, F32)
    parts = group_reduce(near[3], far[3], masks)
    grad_out = token_product(
        (saved_near[2], saved_far[2]), (near[0], far[0]), plane, planes, "feed_out_weight"
    )
    grad_in = token_product(
        (saved_near[0], saved_far[0]), (near[1], far[1]), plane, planes, "feed_in_weight"
    )
    return parts, grad_in, grad_out, near[2] + far[2]


def feed_weights(weight_in, weight_out, place):
    rows, hidden = weight_in.shape
    half = weight_out.shape[0] // 2
    columns = weight_in.reshape(rows, place.planes, QUAD, 2, half)
    columns = lax.dynamic_index_in_dim(columns, place.rep, 3, keepdims=False)
    columns = columns.transpose(2, 0, 1, 3).reshape(QUAD, rows, place.planes * half)

    def for_member(step):
        return lax.dynamic_index_in_dim(columns, place.quad ^ step, 0, keepdims=False)

    pieces = [for_member(0)] + [flipped(for_member(step), step) for step in range(1, QUAD)]
    piece_in = ordered(pieces, place.quad_spot, "order_columns")
    piece_out = lax.dynamic_slice_in_dim(weight_out, place.rep * half, half, 0)
    steps = range(1, place.planes)
    pieces_in = [piece_in] + [flipped(piece_in, QUAD * step) for step in steps]
    pieces_out = [piece_out] + [flipped(piece_out, QUAD * step) for step in steps]
    return (
        ordered(pieces_in, place.plane_spot, "order_feed_in"),
        ordered(pieces_out, place.plane_spot, "order_feed_out"),
    )


def plane_sum(pieces, name):
    arrived = [flipped(item, QUAD * step) for step, item in enumerate(pieces) if step]

    def body(*values):
        return (sum((item.astype(F32) for item in values[1:]), values[0]),)

    return fused(body, name, [shape_of(*pieces[0].shape, BF)], pieces[0], *arrived)[0]


def feed_weight_grads(grad_in, grad_out, place):
    low_out = plane_sum(grad_out, "sum_feed_out")
    other = flipped(low_out, place.shards)
    is_first = place.rep == 0
    total_out = jnp.concatenate(
        [jnp.where(is_first, low_out, other), jnp.where(is_first, other, low_out)], axis=0
    ).astype(F32)

    low_in = plane_sum(grad_in, "sum_feed_in")
    rows = low_in.shape[0] // QUAD
    blocks = low_in.reshape(QUAD, rows, low_in.shape[1])

    def for_member(step):
        return lax.dynamic_index_in_dim(blocks, place.quad ^ step, 0, keepdims=False)

    pieces = [for_member(0)] + [flipped(for_member(step), step) for step in range(1, QUAD)]
    mine = ordered(pieces, place.quad_spot, "order_grad_in")
    theirs = flipped(mine, place.shards)
    both = jnp.stack([jnp.where(is_first, mine, theirs), jnp.where(is_first, theirs, mine)])
    both = both.reshape(2, QUAD, rows, place.planes, -1).transpose(2, 3, 1, 0, 4)
    return both.reshape(rows, -1).astype(F32), total_out


def score_block(query, keys, table, bias, place, rows, length):
    scores = dot_nt(query, keys)
    spread = dot_nt(query, table)
    band = pltpu.roll(spread, 0, axis=1, stride=1, stride_axis=0)
    column = lax.broadcasted_iota(jnp.int32, (rows, length + 2 * rows), 1)
    bias[...] = jnp.where(column < place, spread[:, :1], spread[:, -1:])
    bias[:, pl.ds(place, 3 * rows)] = band[:, rows:]
    return scores + bias[:, rows : rows + length]


def place_rows(source, columns, target, position, rows):
    for step in range(SPAN):
        spot = pl.ds(pl.multiple_of((position ^ step) * rows, rows), rows)
        target[spot, :] = source[step * rows : (step + 1) * rows, columns]


def split_rows(value, kept, sent, rows):
    for index, step in enumerate((0, 4, 2, 6)):
        target = slice(index * rows, (index + 1) * rows)
        kept[target, :] = value[step * rows : (step + 1) * rows]
        sent[target, :] = value[(step + 1) * rows : (step + 2) * rows].astype(BF)


def join_pieces(refs, target, rows):
    for step, ref in enumerate(refs):
        target[step * rows : (step + 1) * rows, :] = ref[...]


def attend_kernel(*refs):
    spot, pieces, rest = refs[0], refs[1 : 1 + SPAN], refs[1 + SPAN :]
    (weight_in, bias_in, weight_out, table, hidden, mixed, context, peaks, kept, sent) = rest[:10]
    keys, values, bias = rest[10:]
    length, width = context.shape
    rows = length // SPAN
    head = table.shape[1] // 2
    position = spot[0]
    join_pieces(pieces, hidden, rows)
    mixed[...] = (dot_nn(hidden[...], weight_in[...]) + bias_in[...]).astype(BF)
    place_rows(mixed, slice(width, 2 * width), keys, position, rows)
    place_rows(mixed, slice(2 * width, 3 * width), values, position, rows)
    lane = lax.broadcasted_iota(jnp.int32, (rows, width), 1)

    def block(index, carry):
        place = pl.multiple_of(index * rows, rows)
        own = pl.ds(pl.multiple_of((position ^ index) * rows, rows), rows)
        query = mixed[own, :width] * jnp.asarray(head**-0.5, BF)
        results, logs = [], []
        for which in range(2):
            mine = lane // head == which
            part = jnp.where(mine, query, jnp.zeros_like(query))
            scores = score_block(part, keys[...], table[...], bias, place, rows, length)
            top = jnp.max(scores, axis=1, keepdims=True)
            powers = jnp.exp(scores - top)
            total = jnp.sum(powers, axis=1, keepdims=True)
            weights = (powers * (1.0 / total)).astype(BF)
            results.append(dot_nn(weights, values[...]))
            logs.append(top + jnp.log(total))
        context[own, :] = jnp.where(lane < head, results[0], results[1]).astype(BF)
        peaks[own, :] = jnp.where(lane < head, logs[0], logs[1])
        return carry

    lax.fori_loop(0, SPAN, block, 0)
    split_rows(dot_nn(context[...], weight_out[...]), kept, sent, rows)


def attend_back_kernel(*refs):
    spot, pieces, rest = refs[0], refs[1 : 1 + SPAN], refs[1 + SPAN :]
    (mixed, table, peaks, weight_in, weight_out) = rest[:5]
    (branch, grad_mixed, grad_table, far, kept, sent) = rest[5:11]
    keys, values, bias, grad_context, grad_keys, grad_values, slopes = rest[11:]
    length, width = grad_context.shape
    rows = length // SPAN
    head = table.shape[1] // 2
    position = spot[0]
    join_pieces(pieces, branch, rows)
    grad_context[...] = dot_nt(branch[...], weight_out[...]).astype(BF)
    place_rows(mixed, slice(width, 2 * width), keys, position, rows)
    place_rows(mixed, slice(2 * width, 3 * width), values, position, rows)
    grad_keys[...] = jnp.zeros_like(grad_keys)
    grad_values[...] = jnp.zeros_like(grad_values)
    grad_table[...] = jnp.zeros_like(grad_table)
    far[...] = jnp.zeros_like(far)
    lane = lax.broadcasted_iota(jnp.int32, (rows, width), 1)
    padded = lax.broadcasted_iota(jnp.int32, (rows, length + 2 * rows), 1)
    factor = head**-0.5
    slopes[:, :rows] = jnp.zeros((rows, rows), F32)
    slopes[:, rows + length :] = jnp.zeros((rows, rows), F32)
    mirror = (
        lax.broadcasted_iota(jnp.int32, (rows, rows), 0)
        + lax.broadcasted_iota(jnp.int32, (rows, rows), 1)
        == rows - 1
    ).astype(BF)

    def block(index, carry):
        place = pl.multiple_of(index * rows, rows)
        own = pl.ds(pl.multiple_of((position ^ index) * rows, rows), rows)
        query = mixed[own, :width] * jnp.asarray(factor, BF)
        results = []
        for which in range(2):
            mine = lane // head == which
            part = jnp.where(mine, query, jnp.zeros_like(query))
            scores = score_block(part, keys[...], table[...], bias, place, rows, length)
            incoming = grad_context[own, :]
            incoming = jnp.where(mine, incoming, jnp.zeros_like(incoming))
            logs = peaks[own, which * head : which * head + 1]
            probs = jnp.exp(scores - logs)
            grad_probs = dot_nt(incoming, values[...])
            shared = jnp.sum(grad_probs * probs, axis=1, keepdims=True)
            grad_low = (probs * (grad_probs - shared)).astype(BF)
            grad_values[...] += dot_tn(probs.astype(BF), incoming)
            grad_keys[...] += dot_tn(grad_low, part)
            slopes[:, rows : rows + length] = grad_low.astype(F32)
            window = slopes[:, pl.ds(place, 3 * rows)]
            whole = slopes[...]
            early = jnp.sum(jnp.where(padded < place, whole, 0.0), axis=1, keepdims=True)
            late = jnp.sum(
                jnp.where(padded >= place + 3 * rows, whole, 0.0), axis=1, keepdims=True
            )
            window = jnp.concatenate(
                [jnp.zeros((rows, rows), F32), dot_nn(mirror, window.astype(BF))], axis=1
            )
            window = pltpu.roll(
                window, 3 * rows + 1, axis=1, stride=1, stride_axis=0
            ).astype(BF)
            grad_table[...] += dot_tn(window, dot_nn(mirror, part).astype(BF))
            part_wide = part.astype(F32)
            far[0:1, :] += jnp.sum(early * part_wide, axis=0, keepdims=True)
            far[1:2, :] += jnp.sum(late * part_wide, axis=0, keepdims=True)
            close = jnp.dot(
                mirror.astype(F32),
                dot_nn(window, table[...]),
                preferred_element_type=F32,
                precision=lax.Precision.HIGHEST,
            )
            results.append(
                dot_nn(grad_low, keys[...])
                + close
                + early * table[0:1, :].astype(F32)
                + late * table[4 * rows - 1 :, :].astype(F32)
            )
        grad_mixed[own, :width] = (
            jnp.where(lane < head, results[0], results[1]) * factor
        ).astype(BF)
        return carry

    lax.fori_loop(0, SPAN, block, 0)
    for step in range(SPAN):
        source = pl.ds(pl.multiple_of((position ^ step) * rows, rows), rows)
        target = slice(step * rows, (step + 1) * rows)
        grad_mixed[target, width : 2 * width] = grad_keys[source, :].astype(BF)
        grad_mixed[target, 2 * width :] = grad_values[source, :].astype(BF)
    split_rows(dot_nt(grad_mixed[...], weight_in[...]), kept, sent, rows)


def in_steps(blocks):
    near, far = blocks
    return [near[0], far[0], near[2], far[2], near[1], far[1], near[3], far[3]]


def attend(blocks, weight_in, bias_in, weight_out, table, place):
    pieces = in_steps(blocks)
    rows, model = pieces[0].shape
    length, width = SPAN * rows, weight_out.shape[0]
    outs = [
        shape_of(length, model, BF),
        shape_of(length, 3 * width, BF),
        shape_of(length, width, BF),
        shape_of(length, width, F32),
        shape_of(length // 2, model, F32),
        shape_of(length // 2, model, BF),
    ]
    hidden, mixed, context, peaks, kept, sent = kernel_call(
        attend_kernel,
        "attend_forward",
        outs,
        (place.span_spot, *pieces, weight_in, bias_in, weight_out, table),
        scalars=1,
        scratch=[
            pltpu.VMEM((length, width), BF),
            pltpu.VMEM((length, width), BF),
            pltpu.VMEM((rows, length + 2 * rows), F32),
        ],
        flops=12 * length * length * width,
    )
    return group_reduce(kept, sent, place.span_masks), (hidden, mixed, context, peaks)


def attend_back(blocks, saved, weight_in, weight_out, table, place):
    hidden, mixed, context, peaks = saved
    pieces = in_steps(blocks)
    rows, model = pieces[0].shape
    length, width = SPAN * rows, weight_out.shape[0]
    outs = [
        shape_of(length, model, BF),
        shape_of(length, 3 * width, BF),
        shape_of(4 * rows, width, F32),
        shape_of(8, width, F32),
        shape_of(length // 2, model, F32),
        shape_of(length // 2, model, BF),
    ]
    branch, grad_mixed, grad_table, far, kept, sent = kernel_call(
        attend_back_kernel,
        "attend_backward",
        outs,
        (place.span_spot, *pieces, mixed, table, peaks, weight_in, weight_out),
        scalars=1,
        scratch=[
            pltpu.VMEM((length, width), BF),
            pltpu.VMEM((length, width), BF),
            pltpu.VMEM((rows, length + 2 * rows), F32),
            pltpu.VMEM((length, width), BF),
            pltpu.VMEM((length, width), F32),
            pltpu.VMEM((length, width), F32),
            pltpu.VMEM((rows, length + 2 * rows), F32),
        ],
        flops=24 * length * length * width,
    )
    parts = group_reduce(kept, sent, place.span_masks)

    def weights(hidden_rows, mixed_grad, context_rows, branch_rows):
        return (
            dot_tn(hidden_rows, mixed_grad),
            dot_tn(context_rows, branch_rows),
            column_sum(mixed_grad),
        )

    grad_in, grad_out, sums = fused(
        weights,
        "attend_weights",
        [shape_of(model, 3 * width, F32), shape_of(width, model, F32), shape_of(1, 3 * width, F32)],
        hidden,
        grad_mixed,
        context,
        branch,
        flops=8 * length * model * width,
    )
    return parts, grad_in, grad_out, sums, distance_gradient(grad_table, far, rows)


def wide_table(distance, rows):
    index = jnp.clip(jnp.arange(4 * rows) - rows - LEFT, 0, LEFT + RIGHT)
    low = distance[index]
    return jnp.concatenate([low, low], axis=1)


def distance_gradient(grad_table, far, rows):
    first = rows + LEFT
    last = first + LEFT + RIGHT
    head = grad_table.shape[1] // 2
    low = jnp.sum(grad_table[: first + 1], axis=0) + far[0]
    high = jnp.sum(grad_table[last:], axis=0) + far[1]
    total = jnp.concatenate([low[None], grad_table[first + 1 : last], high[None]], axis=0)
    return total[:, :head] + total[:, head:]


def whole_heads(weight_out, head):
    return weight_out.shape[0] % head == 0


def attend_weights(weight_in, weight_out, head, place):
    rows, model = weight_in.shape[0], weight_out.shape[1]
    heads = model // head
    per_device = heads // SPAN
    if not whole_heads(weight_out, head):
        whole = lax.all_gather(weight_in, "shard", axis=0, tiled=True)
        whole = whole.reshape(model, 3, heads, head)
        mine = lax.dynamic_slice_in_dim(whole, place.member * per_device, per_device, 2)
        out = lax.all_gather(weight_out, "shard", axis=0, tiled=True)
        width = per_device * head
        out = lax.dynamic_slice_in_dim(out, place.member * width, width, 0)
        return mine.reshape(model, 3 * width), out
    blocks = weight_in.reshape(rows, 3, per_device, SPAN, head)
    blocks = blocks.transpose(3, 0, 1, 2, 4).reshape(SPAN, rows, 3 * per_device * head)

    def for_member(step):
        return lax.dynamic_index_in_dim(blocks, place.member ^ step, 0, keepdims=False)

    pieces = [for_member(0)] + [flipped(for_member(step), step) for step in range(1, SPAN)]
    group = ordered(pieces, place.span_spot, "order_attend_group")
    steps = range(1, place.shards // SPAN)
    pieces = [group] + [flipped(group, SPAN * step) for step in steps]
    outs = [weight_out] + [flipped(weight_out, SPAN * step) for step in steps]
    return (
        ordered(pieces, place.group_spot, "order_attend_in"),
        ordered(outs, place.group_spot, "order_attend_out"),
    )


def head_row(row, head, place, aligned):
    heads = row.shape[0] // head
    if aligned:
        row = row.reshape(-1, SPAN, head)
        row = lax.dynamic_index_in_dim(row, place.member, 1, keepdims=False)
        return row.reshape(1, -1)
    row = row.reshape(SPAN, -1)
    return lax.dynamic_slice_in_dim(row, place.member, 1, 0)


def head_spread(row, model, head, place, aligned):
    if aligned:
        whole = jnp.zeros((model // head // SPAN, SPAN, head), F32)
        block = row.reshape(-1, 1, head)
        return lax.dynamic_update_slice_in_dim(whole, block, place.member, 1).reshape(1, model)
    whole = jnp.zeros((SPAN, model // SPAN), F32)
    return lax.dynamic_update_slice_in_dim(whole, row, place.member, 0).reshape(1, model)


def attend_weight_grads(grad_in, grad_out, head, place, rows, aligned):
    model = grad_out.shape[1]
    heads = model // head
    per_device = heads // SPAN
    if not aligned:
        whole = jnp.zeros((model, 3, heads, head), F32)
        whole = lax.dynamic_update_slice_in_dim(
            whole, grad_in.reshape(model, 3, per_device, head), place.member * per_device, 2
        )
        whole = lax.psum_scatter(
            whole.reshape(model, 3 * model), "shard", scatter_dimension=0, tiled=True
        )
        out = jnp.zeros((model, model), F32)
        out = lax.dynamic_update_slice_in_dim(out, grad_out, place.member * per_device * head, 0)
        out = lax.psum_scatter(out, "shard", scatter_dimension=0, tiled=True)
        return rep_sum(whole, place), rep_sum(out, place)
    groups = place.shards // SPAN
    extent_in, extent_out = model // groups, grad_out.shape[0] // groups

    def for_group(value, extent, step):
        return lax.dynamic_slice_in_dim(value, (place.group ^ step) * extent, extent, 0)

    sum_in = for_group(grad_in, extent_in, 0)
    sum_out = for_group(grad_out, extent_out, 0)
    for step in range(1, groups):
        arrived = flipped(for_group(grad_in, extent_in, step).astype(BF), SPAN * step)
        sum_in = sum_in + arrived.astype(F32)
        arrived = flipped(for_group(grad_out, extent_out, step).astype(BF), SPAN * step)
        sum_out = sum_out + arrived.astype(F32)
    blocks = sum_in.astype(BF).reshape(SPAN, rows, -1)

    def for_member(step):
        return lax.dynamic_index_in_dim(blocks, place.member ^ step, 0, keepdims=False)

    pieces = [for_member(0)] + [flipped(for_member(step), step) for step in range(1, SPAN)]
    mine = rep_sum(ordered(pieces, place.span_spot, "order_attend_grad"), place)
    mine = mine.reshape(SPAN, rows, 3, per_device, head).transpose(1, 2, 3, 0, 4)
    return mine.reshape(rows, 3 * model), rep_sum(sum_out, place)


def rep_sum(value, place):
    low = value.astype(BF)
    return low.astype(F32) + flipped(low, place.shards).astype(F32)


def tap_rows(padded, depth, rows, offset):
    total = padded[offset : offset + rows, :] * depth[0:1, :]
    for tap in range(1, depth.shape[0]):
        total = total + padded[offset + tap : offset + tap + rows, :] * depth[tap : tap + 1, :]
    return total


def convolve_start(parts, before, out_bias, gain, shift, weight_in):
    rows, model = before.shape

    def body(own, via_first, via_second, base, bias, gain_row, shift_row, w_in):
        current = base + joined((own, via_first, via_second)) + bias
        unit, unused_scale = standard(current)
        hidden = (unit * gain_row + shift_row).astype(BF)
        doubled = dot_nn(hidden, w_in)
        return current, hidden, doubled, doubled[:, :model] * logistic(doubled[:, model:])

    return fused(
        body,
        "convolve_start",
        [
            shape_of(rows, model, F32),
            shape_of(rows, model, BF),
            shape_of(rows, 2 * model, F32),
            shape_of(rows, model, BF),
        ],
        *parts,
        before,
        out_bias,
        gain,
        shift,
        weight_in,
        flops=4 * rows * model * model,
    )


LANES = 128


def convolve_finish(glued, border, depth, norm_two, weight_out, before, norm_next):
    rows, model = before.shape
    edge = border.shape[0]
    taps = depth.shape[0]

    def kernel(
        glued_ref, border_ref, depth_ref, gain, shift, w_out, base, gain_next, shift_next,
        mixed_ref, rest_ref, current_ref, hidden_ref, padded,
    ):
        padded[:edge, :] = border_ref[...].astype(F32)
        padded[edge:, :] = glued_ref[...].astype(F32)
        for column in range(0, model, LANES):
            lanes = slice(column, column + LANES)
            total = jnp.zeros((rows, LANES), F32)
            for tap in range(taps):
                start = edge - taps + 1 + tap
                total += padded[start : start + rows, lanes] * depth_ref[tap : tap + 1, lanes]
            mixed_ref[:, lanes] = total
        unit, unused_scale = standard(mixed_ref[...])
        upper = unit * gain[...] + shift[...]
        rest = (upper * logistic(upper)).astype(BF)
        rest_ref[...] = rest
        current = base[...] + dot_nn(rest, w_out[...])
        current_ref[...] = current
        unit, unused_scale = standard(current)
        hidden_ref[...] = (unit * gain_next[...] + shift_next[...]).astype(BF)

    return kernel_call(
        kernel,
        "convolve_finish",
        [shape_of(rows, model, dtype) for dtype in (F32, BF, F32, BF)],
        (glued, border, depth, *norm_two, weight_out, before, *norm_next),
        scratch=[pltpu.VMEM((edge + rows, model), F32)],
        flops=2 * rows * model * model,
    )


def convolve_back_start(parts, grad, after, gain_next, mixed, depth, norm_two, weight_out, glued,
                        border):
    rows, model = after.shape
    edge = border.shape[0]
    taps = depth.shape[0]

    def kernel(
        own, via_first, via_second, grad_ref, after_ref, gain_next_ref, mixed_ref, depth_ref,
        gain, shift, w_out, glued_ref, border_ref,
        grad_out, branch_ref, main_ref, halo_ref, sums, grad_depth, padded, spread,
    ):
        incoming = own[...] + via_first[...].astype(F32) + via_second[...].astype(F32)
        slope, sum_gain, sum_shift = norm_back(after_ref[...], gain_next_ref[...], incoming)
        current = grad_ref[...] + slope
        grad_out[...] = current
        branch = current.astype(BF)
        branch_ref[...] = branch
        unit, scale = standard(mixed_ref[...])
        upper = unit * gain[...] + shift[...]
        grad_upper = dot_nt(branch, w_out[...]) * silu_slope(upper)
        inner = grad_upper * gain[...]
        first = jnp.mean(inner, axis=-1, keepdims=True)
        second = jnp.mean(inner * unit, axis=-1, keepdims=True)
        padded[:edge, :] = border_ref[...].astype(F32)
        padded[edge:, :] = glued_ref[...].astype(F32)
        spread[:edge, :] = jnp.zeros((edge, model), F32)
        spread[edge : edge + rows, :] = scale * (inner - first - unit * second)
        spread[edge + rows :, :] = jnp.zeros((edge, model), F32)
        sums[0:1, :] = sum_gain
        sums[1:2, :] = sum_shift
        sums[2:3, :] = column_sum(grad_upper * unit)
        sums[3:4, :] = column_sum(grad_upper)
        sums[4:, :] = jnp.zeros((4, model), F32)
        grad_depth[taps:, :] = jnp.zeros((grad_depth.shape[0] - taps, model), F32)
        for column in range(0, model, LANES):
            lanes = slice(column, column + LANES)
            total = jnp.zeros((rows + edge, LANES), F32)
            center = spread[edge : edge + rows, lanes]
            for tap in range(taps):
                start = edge - taps + 1 + tap
                grad_depth[tap : tap + 1, lanes] = jnp.sum(
                    center * padded[start : start + rows, lanes], axis=0, keepdims=True
                )
                begin = taps - 1 - tap
                total += (
                    spread[begin : begin + rows + edge, lanes] * depth_ref[tap : tap + 1, lanes]
                )
            halo_ref[:, lanes] = total[:edge].astype(BF)
            main_ref[:, lanes] = total[edge:]

    return kernel_call(
        kernel,
        "convolve_back_start",
        [
            shape_of(rows, model, F32),
            shape_of(rows, model, BF),
            shape_of(rows, model, F32),
            shape_of(edge, model, BF),
            shape_of(8, model, F32),
            shape_of(-(-taps // 8) * 8 + 8, model, F32),
        ],
        (*parts, grad, after, gain_next, mixed, depth, *norm_two, weight_out, glued, border),
        scratch=[
            pltpu.VMEM((edge + rows, model), F32),
            pltpu.VMEM((rows + 2 * edge, model), F32),
        ],
        flops=2 * rows * model * model,
    )


def convolve_back_finish(main, incoming, doubled, weight_in, before, gain, grad):
    rows, model = before.shape
    edge = incoming.shape[0]

    def body(main_rows, late, both, w_in, base, gain_row, grad_rows):
        glued = jnp.concatenate(
            [main_rows[: rows - edge], main_rows[rows - edge :] + late.astype(F32)], axis=0
        )
        glued = glued.astype(BF).astype(F32)
        gate = logistic(both[:, model:])
        slope = jnp.concatenate(
            [glued * gate, glued * both[:, :model] * gate * (1.0 - gate)], axis=1
        ).astype(BF)
        inner, sum_gain, sum_shift = norm_back(base, gain_row, dot_nt(slope, w_in))
        current = grad_rows + inner
        branch = current.astype(BF)
        sums = jnp.concatenate(
            [sum_gain, sum_shift, column_sum(branch), jnp.zeros((5, model), F32)], axis=0
        )
        return current, branch, slope, sums

    return fused(
        body,
        "convolve_back_finish",
        [
            shape_of(rows, model, F32),
            shape_of(rows, model, BF),
            shape_of(rows, 2 * model, BF),
            shape_of(8, model, F32),
        ],
        main,
        incoming,
        doubled,
        weight_in,
        before,
        gain,
        grad,
        flops=4 * rows * model * model,
    )


def convolve_weight_grads(hidden, slope, rest, branch, place):
    model = hidden.shape[1]

    def body(hidden_rows, slope_rows, rest_rows, branch_rows):
        return dot_tn(hidden_rows, slope_rows), dot_tn(rest_rows, branch_rows)

    grad_in, grad_out = fused(
        body,
        "convolve_weights",
        [shape_of(model, 2 * model, BF), shape_of(model, model, BF)],
        hidden,
        slope,
        rest,
        branch,
        flops=6 * hidden.shape[0] * model * model,
    )
    return tuple(
        rep_sum(lax.psum_scatter(item, "shard", scatter_dimension=0, tiled=True), place)
        for item in (grad_in, grad_out)
    )


def feed_to_attend(parts, before, bias, norm_next):
    rows, model = before.shape

    def body(own, via_first, via_second, base, bias_row, gain, shift):
        current = base.astype(F32) + 0.5 * (joined((own, via_first, via_second)) + bias_row)
        unit, unused_scale = standard(current)
        return current, unit * gain + shift

    outs = [shape_of(rows, model, F32), shape_of(rows, model, BF)]
    return fused(body, "feed_to_attend", outs, *parts, before, bias, *norm_next)


def turn_around(parts, before, bias, norm_last, cotangent):
    rows, model = before.shape

    def body(own, via_first, via_second, base, bias_row, gain, shift, grad):
        current = base + 0.5 * (joined((own, via_first, via_second)) + bias_row)
        unit, unused_scale = standard(current)
        slope, sum_gain, sum_shift = norm_back(current, gain, grad.astype(F32))
        branch = (0.5 * slope).astype(BF)
        sums = jnp.concatenate(
            [sum_gain, sum_shift, column_sum(branch), jnp.zeros((5, model), F32)], axis=0
        )
        return unit * gain + shift, slope, branch, sums

    outs = [
        shape_of(rows, model, BF),
        shape_of(rows, model, F32),
        shape_of(rows, model, BF),
        shape_of(8, model, F32),
    ]
    return fused(body, "turn_around", outs, *parts, before, bias, *norm_last, cotangent)


def attend_to_feed_back(parts, grad, before, gain):
    rows, model = before.shape

    def body(own, via_first, via_second, grad_rows, base, gain_row):
        incoming = joined((own, via_first, via_second))
        slope, sum_gain, sum_shift = norm_back(base, gain_row, incoming)
        current = grad_rows + slope
        branch = (0.5 * current).astype(BF)
        sums = jnp.concatenate(
            [sum_gain, sum_shift, column_sum(branch), jnp.zeros((5, model), F32)], axis=0
        )
        return current, branch, sums

    outs = [shape_of(rows, model, F32), shape_of(rows, model, BF), shape_of(8, model, F32)]
    return fused(body, "attend_to_feed_back", outs, *parts, grad, before, gain)


def last_step(parts, grad, before, gain):
    rows, model = before.shape

    def body(own, via_first, via_second, grad_rows, base, gain_row):
        incoming = joined((own, via_first, via_second))
        slope, sum_gain, sum_shift = norm_back(base.astype(F32), gain_row, incoming)
        sums = jnp.concatenate([sum_gain, sum_shift, jnp.zeros((6, model), F32)], axis=0)
        return grad_rows + slope, sums

    outs = [shape_of(rows, model, F32), shape_of(8, model, F32)]
    return fused(body, "last_step", outs, *parts, grad, before, gain)


def shard_gather(value, place):
    gathered = value[None]
    for bit in range(place.shards.bit_length() - 1):
        arrived = flipped(gathered, 1 << bit)
        low = jnp.bitwise_and(jnp.right_shift(place.shard, bit), 1) == 0
        gathered = jnp.concatenate(
            [jnp.where(low, gathered, arrived), jnp.where(low, arrived, gathered)], axis=0
        )
    return gathered


def shard_reduce(value, place):
    for bit in range(place.shards.bit_length() - 1):
        pairs = value.reshape(value.shape[0] // 2, 2, *value.shape[1:])
        low = jnp.bitwise_and(jnp.right_shift(place.shard, bit), 1) == 0
        staying = jnp.where(low, pairs[:, 0], pairs[:, 1])
        leaving = jnp.where(low, pairs[:, 1], pairs[:, 0])
        value = staying + flipped(leaving, 1 << bit)
    value = value[0]
    return value + flipped(value, place.shards)


def sum_everywhere(value, place):
    for bit in range((2 * place.shards).bit_length() - 1):
        value = value + flipped(value, 1 << bit)
    return value


class Place:
    def __init__(self):
        self.shards = lax.axis_size("shard")
        self.planes = self.shards // QUAD
        self.rep = lax.axis_index("rep")
        self.shard = lax.axis_index("shard")
        self.quad = self.shard % QUAD
        self.plane = self.shard // QUAD
        self.member = self.shard % SPAN
        self.group = self.shard // SPAN
        self.quad_spot = self.quad.reshape(1)
        self.plane_spot = self.plane.reshape(1)
        self.span_spot = self.member.reshape(1)
        self.group_spot = self.group.reshape(1)
        self.feed_masks = (self.shards, 2, 1)
        self.span_masks = (4, 2, 1)


def along(value, by, place):
    count = place.shards
    route = [(i, i + by) for i in range(count) if 0 <= i + by < count]
    return lax.ppermute(value, "shard", route)


def shards(
    inputs,
    ff_in,
    ff_out,
    ff_bias,
    attn_in,
    attn_out,
    conv_in,
    conv_out,
    depthwise,
    distance,
    vectors,
    attn_bias,
    cotangent,
):
    place = Place()
    rows, model = inputs.shape
    head = distance.shape[2]
    taps = depthwise.shape[1]
    edge = -(-(taps - 1) // 16) * 16
    unit = model // place.shards
    half = ff_out.shape[2] // 2
    aligned = whole_heads(attn_out[0], head)
    bias_rows = ff_bias.shape[2] // unit

    blocks = group_gather(inputs, place.feed_masks)
    small = jnp.concatenate(
        [vectors[0], attn_bias, depthwise[0], ff_bias[0].reshape(2 * bias_rows, unit)], axis=0
    )
    small = shard_gather(small, place)
    count = vectors.shape[1]
    wide = small[:, : count + 1 + taps].transpose(1, 0, 2).reshape(-1, model).astype(F32)
    vector = [wide[index : index + 1] for index in range(count)]
    out_bias = wide[count : count + 1]
    depth = wide[count + 1 :]
    feed_bias = small[:, count + 1 + taps :].reshape(place.planes, QUAD, 2, 2, half)
    feed_bias = lax.dynamic_index_in_dim(feed_bias, place.quad, 1, keepdims=False)
    feed_bias = lax.dynamic_index_in_dim(feed_bias, place.rep, 2, keepdims=False)
    feed_bias = feed_bias.transpose(1, 0, 2).reshape(2, 1, -1).astype(F32)
    first_in, first_out = feed_weights(ff_in[0, 0], ff_out[0, 0], place)
    mix_in, mix_out = attend_weights(attn_in[0], attn_out[0], head, place)
    second_in, second_out = feed_weights(ff_in[0, 1], ff_out[0, 1], place)
    glue_in = lax.all_gather(conv_in[0], "shard", axis=0, tiled=True)
    glue_out = lax.all_gather(conv_out[0], "shard", axis=0, tiled=True)
    table = wide_table(distance[0], rows)
    mix_bias = jnp.concatenate(
        [
            head_row(vector[5][0], head, place, aligned),
            jnp.zeros((1, model // SPAN), F32),
            head_row(vector[6][0], head, place, aligned),
        ],
        axis=1,
    )

    parts, saved_first = feed(
        blocks, first_in, feed_bias[0], first_out, (vector[0], vector[1]), place.feed_masks
    )
    after_first, hidden = feed_to_attend(parts, inputs, vector[2], (vector[3], vector[4]))
    parts, saved_attend = attend(
        group_gather(hidden, place.span_masks), mix_in, mix_bias, mix_out, table, place
    )
    after_attend, conv_hidden, doubled, glued = convolve_start(
        parts, after_first, out_bias, vector[7], vector[8], glue_in
    )
    border = along(glued[rows - edge :], 1, place)
    border = jnp.where(place.member == 0, jnp.zeros_like(border), border)
    mixed, rest, after_conv, hidden = convolve_finish(
        glued,
        border,
        depth,
        (vector[9], vector[10]),
        glue_out,
        after_attend,
        (vector[11], vector[12]),
    )
    parts, saved_second = feed(
        group_gather(hidden, place.feed_masks),
        second_in,
        feed_bias[1],
        second_out,
        None,
        place.feed_masks,
    )
    output, grad_last, branch, last_sums = turn_around(
        parts, after_conv, vector[13], (vector[14], vector[15]), cotangent
    )

    parts, second_grad_in, second_grad_out, second_bias = feed_back(
        group_gather(branch, place.feed_masks),
        saved_second,
        second_in,
        second_out,
        place.feed_masks,
        place.plane_spot,
        place.planes,
    )
    grad_conv, conv_branch, main, halo, conv_sums, grad_depth = convolve_back_start(
        parts,
        grad_last,
        after_conv,
        vector[11],
        mixed,
        depth,
        (vector[9], vector[10]),
        glue_out,
        glued,
        border,
    )
    incoming = along(halo, -1, place)
    incoming = jnp.where(place.member == SPAN - 1, jnp.zeros_like(incoming), incoming)
    grad_attend, branch, slope, attend_sums = convolve_back_finish(
        main, incoming, doubled, glue_in, after_attend, vector[7], grad_conv
    )
    conv_grads = convolve_weight_grads(conv_hidden, slope, rest, conv_branch, place)
    parts, mix_grad_in, mix_grad_out, mix_sums, grad_distance = attend_back(
        group_gather(branch, place.span_masks), saved_attend, mix_in, mix_out, table, place
    )
    grad_first, branch, first_sums = attend_to_feed_back(
        parts, grad_attend, after_first, vector[3]
    )
    parts, first_grad_in, first_grad_out, first_bias = feed_back(
        group_gather(branch, place.feed_masks),
        saved_first,
        first_in,
        first_out,
        place.feed_masks,
        place.plane_spot,
        place.planes,
    )
    grad_input, input_sums = last_step(parts, grad_first, inputs, vector[0])

    second_grads = feed_weight_grads(second_grad_in, second_grad_out, place)
    mix_grads = attend_weight_grads(mix_grad_in, mix_grad_out, head, place, unit, aligned)
    first_grads = feed_weight_grads(first_grad_in, first_grad_out, place)
    width = mix_sums.shape[1] // 3
    vector_grads = [
        input_sums[0:2],
        first_sums[2:3],
        first_sums[0:2],
        head_spread(mix_sums[:, :width], model, head, place, aligned),
        head_spread(mix_sums[:, 2 * width :], model, head, place, aligned),
        attend_sums[0:2],
        conv_sums[2:4],
        conv_sums[0:2],
        last_sums[2:3],
        last_sums[0:2],
        attend_sums[2:3],
        grad_depth[:taps],
    ]
    wide_grads = jnp.concatenate(vector_grads, axis=0)
    wide_grads = wide_grads.reshape(-1, place.shards, unit).transpose(1, 0, 2)
    bias_grads = jnp.zeros((place.planes, QUAD, 2, 2, half), F32)
    bias_pair = jnp.stack([first_bias, second_bias]).reshape(2, place.planes, half)
    bias_grads = lax.dynamic_update_slice(
        bias_grads,
        bias_pair.transpose(1, 0, 2)[:, None, :, None, :],
        (0, place.quad, 0, place.rep, 0),
    ).reshape(place.shards, 2 * bias_rows, unit)
    small_grads = shard_reduce(jnp.concatenate([wide_grads, bias_grads], axis=1), place)
    return (
        output,
        grad_input,
        jnp.stack([first_grads[0], second_grads[0]])[None],
        jnp.stack([first_grads[1], second_grads[1]])[None],
        small_grads[count + 1 + taps :].reshape(1, 2, -1),
        mix_grads[0][None],
        mix_grads[1][None],
        conv_grads[0][None],
        conv_grads[1][None],
        small_grads[count + 1 : count + 1 + taps][None],
        sum_everywhere(grad_distance, place)[None],
        small_grads[:count][None],
        small_grads[count : count + 1],
    )


def solution(mesh):
    in_specs = (
        P(("rep", "shard"), None),
        P(None, None, "shard", None),
        P(None, None, "shard", None),
        P(None, None, "shard"),
        P(None, "shard", None),
        P(None, "shard", None),
        P(None, "shard", None),
        P(None, "shard", None),
        P(None, None, "shard"),
        P(),
        P(None, None, "shard"),
        P(None, "shard"),
        P(("rep", "shard"), None),
    )
    out_specs = (
        P(("rep", "shard"), None),
        P(("rep", "shard"), None),
        P(None, None, "shard", None),
        P(None, None, "shard", None),
        P(None, None, "shard"),
        P(None, "shard", None),
        P(None, "shard", None),
        P(None, "shard", None),
        P(None, "shard", None),
        P(None, None, "shard"),
        P(),
        P(None, None, "shard"),
        P(None, "shard"),
    )
    return jax.shard_map(shards, mesh=mesh, in_specs=in_specs, out_specs=out_specs, check_vma=False)
```

```python
import jax
import jax.numpy as jnp
from jax import lax
from jax.experimental import pallas as pl
from jax.experimental.pallas import tpu as pltpu
from jax.sharding import PartitionSpec as P

LEFT = 64
RIGHT = 8
SPAN = 8
QUAD = 4
EPSILON = 1e-05
BF = jnp.bfloat16
F32 = jnp.float32
MIB = 1 << 20


def dot_nn(left, right):
    return jnp.dot(left, right, preferred_element_type=F32)


def dot_nt(left, right):
    return lax.dot_general(left, right, (((1,), (1,)), ((), ())), preferred_element_type=F32)


def dot_tn(left, right):
    return lax.dot_general(left, right, (((0,), (0,)), ((), ())), preferred_element_type=F32)


def column_sum(values):
    return jnp.sum(values.astype(F32), axis=0, keepdims=True)


def standard(values):
    center = values - jnp.mean(values, axis=-1, keepdims=True)
    scale = lax.rsqrt(jnp.mean(center * center, axis=-1, keepdims=True) + EPSILON)
    return center * scale, scale


def norm_back(values, gain, grad):
    unit, scale = standard(values)
    inner = grad * gain
    first = jnp.mean(inner, axis=-1, keepdims=True)
    second = jnp.mean(inner * unit, axis=-1, keepdims=True)
    return scale * (inner - first - unit * second), column_sum(grad * unit), column_sum(grad)


def logistic(values):
    return 1.0 / (1.0 + jnp.exp(-values))


def silu_slope(values):
    gate = logistic(values)
    return gate * (1.0 + values * (1.0 - gate))


def vmem(count):
    return [pl.BlockSpec(memory_space=pltpu.VMEM)] * count


def shape_of(rows, columns, dtype):
    return jax.ShapeDtypeStruct((rows, columns), dtype)


def kernel_call(body, name, outs, operands, scalars=0, scratch=(), flops=0, waits=()):
    moved = sum(item.size * item.dtype.itemsize for item in (*operands[scalars:], *outs))
    count = len(operands)

    def kernel(*refs):
        body(*refs[:count], *refs[count + len(waits) :])

    return pl.pallas_call(
        kernel,
        in_specs=[pl.BlockSpec(memory_space=pltpu.SMEM)] * scalars
        + vmem(count - scalars)
        + [pl.BlockSpec(memory_space=pl.ANY)] * len(waits),
        out_specs=vmem(len(outs)),
        out_shape=list(outs),
        scratch_shapes=list(scratch),
        compiler_params=pltpu.CompilerParams(vmem_limit_bytes=40 * MIB),
        cost_estimate=pl.CostEstimate(flops=flops, bytes_accessed=moved, transcendentals=0),
        name=name,
    )(*operands, *waits)


def fused(body, name, outs, *operands, flops=0, waits=()):
    def kernel(*refs):
        results = body(*[ref[...] for ref in refs[: len(operands)]])
        for ref, value in zip(refs[len(operands) :], results):
            ref[...] = value.astype(ref.dtype)

    return kernel_call(kernel, name, outs, operands, flops=flops, waits=waits)


def flipped(value, mask):
    total = lax.axis_size("rep") * lax.axis_size("shard")
    return lax.ppermute(value, ("rep", "shard"), [(i, i ^ mask) for i in range(total)])


def square_gather(value, masks):
    first, second = masks
    return [
        value,
        flipped(value, first),
        flipped(value, second),
        flipped(value, first | second),
    ]


def square_reduce(parts, masks):
    first, second = masks
    own, via_first, via_second, cross = parts
    return [
        own,
        flipped(cross, first | second),
        flipped(via_first, first),
        flipped(via_second, second),
    ]


def joined(parts):
    return parts[0] + sum(part.astype(F32) for part in parts[1:])


def place_feed(spot, packs, w_in, w_out, unit, half):
    plane, second, core = spot[0], spot[1], spot[2]
    for step, near, ref, start in packs:
        column = (plane ^ step) * 2
        for turn in range(2):
            row = ((column + (second ^ turn)) * 2 + (core ^ near)) * unit
            source = slice(start + turn * unit, start + (turn + 1) * unit)
            w_in[pl.ds(pl.multiple_of(row, unit), unit), :] = ref[source, :]
        row = (column + (core ^ near)) * half
        source = slice(start + 2 * unit, start + 2 * unit + half)
        w_out[pl.ds(pl.multiple_of(row, half), half), :] = ref[source, :]


def pack_views(refs, place):
    planes, size = place.planes, place.pack_rows
    views = []
    if len(refs) == 2:
        for near, ref in enumerate(refs):
            views += [(step, near, ref, step * size) for step in range(planes)]
        return views
    for index, ref in enumerate(refs):
        views.append((index % planes, index // planes, ref, 0))
    return views


def feed(pieces, packs, spot, bias, wide, norm_row, masks, place, waits=()):
    rows, model = pieces[0].shape
    inner = bias.shape[1]
    count, total = len(pieces), len(pieces) * rows
    unit, half = place.unit, place.half

    def kernel(spot_ref, *refs):
        piece_refs, pack_refs = refs[:count], refs[count : count + len(packs)]
        bias_ref, wide_ref, hidden, upper, active = refs[count + len(packs) :][:5]
        outs = refs[count + len(packs) + 5 : -2]
        w_in, w_out = refs[-2:]
        place_feed(spot_ref, pack_views(pack_refs, place), w_in, w_out, unit, half)
        for index, ref in enumerate(piece_refs):
            block = ref[...]
            if norm_row is not None:
                scaled, unused_scale = standard(block.astype(F32))
                gain = wide_ref[norm_row : norm_row + 1, :]
                shift = wide_ref[norm_row + 1 : norm_row + 2, :]
                block = (scaled * gain + shift).astype(BF)
            hidden[index * rows : (index + 1) * rows, :] = block
        before = dot_nn(hidden[...], w_in[...]) + bias_ref[...]
        upper[...] = before
        active[...] = (before * logistic(before)).astype(BF)
        result = dot_nn(active[...], w_out[...])
        for index, ref in enumerate(outs):
            ref[...] = result[index * rows : (index + 1) * rows].astype(ref.dtype)

    outs = [
        shape_of(total, model, BF),
        shape_of(total, inner, F32),
        shape_of(total, inner, BF),
        shape_of(rows, model, F32),
    ] + [shape_of(rows, model, BF)] * (count - 1)
    results = kernel_call(
        kernel,
        "feed_forward",
        outs,
        (spot, *pieces, *packs, bias, wide),
        scalars=1,
        scratch=[pltpu.VMEM((model, inner), BF), pltpu.VMEM((inner, model), BF)],
        flops=4 * total * model * inner,
        waits=waits,
    )
    return square_reduce(results[3:], masks), results[:3]


def feed_back(pieces, packs, spot, saved, masks, place, waits=()):
    hidden, upper, active = saved
    rows, model = pieces[0].shape
    total, inner = upper.shape
    count = len(pieces)
    unit, half = place.unit, place.half

    def kernel(spot_ref, *refs):
        piece_refs, pack_refs = refs[:count], refs[count : count + len(packs)]
        upper_ref, branch, slope, sums = refs[count + len(packs) :][:4]
        outs = refs[count + len(packs) + 4 : -2]
        w_in, w_out = refs[-2:]
        place_feed(spot_ref, pack_views(pack_refs, place), w_in, w_out, unit, half)
        for index, ref in enumerate(piece_refs):
            branch[index * rows : (index + 1) * rows, :] = ref[...]
        grad = dot_nt(branch[...], w_out[...]) * silu_slope(upper_ref[...])
        slope[...] = grad.astype(BF)
        sums[...] = column_sum(slope[...])
        result = dot_nt(slope[...], w_in[...])
        for index, ref in enumerate(outs):
            ref[...] = result[index * rows : (index + 1) * rows].astype(ref.dtype)

    outs = [
        shape_of(total, model, BF),
        shape_of(total, inner, BF),
        shape_of(1, inner, F32),
        shape_of(rows, model, F32),
    ] + [shape_of(rows, model, BF)] * (count - 1)
    results = kernel_call(
        kernel,
        "feed_backward",
        outs,
        (spot, *pieces, *packs, upper),
        scalars=1,
        scratch=[pltpu.VMEM((model, inner), BF), pltpu.VMEM((inner, model), BF)],
        flops=4 * total * model * inner,
        waits=waits,
    )
    branch, slope, sums = results[:3]
    parts = square_reduce(results[3:], masks)
    planes, size = place.planes, place.pack_rows

    def weights(spot_ref, hidden_ref, active_ref, branch_ref, slope_ref, kept, sent, w_in, w_out):
        w_in[...] = dot_tn(hidden_ref[...], slope_ref[...])
        w_out[...] = dot_tn(active_ref[...], branch_ref[...])
        plane, second, core = spot_ref[0], spot_ref[1], spot_ref[2]
        for near, ref in enumerate((kept, sent)):
            for step in range(planes):
                column = (plane ^ step) * 2
                start = step * size
                for turn in range(2):
                    row = ((column + (second ^ turn)) * 2 + (core ^ near)) * unit
                    target = slice(start + turn * unit, start + (turn + 1) * unit)
                    source = pl.ds(pl.multiple_of(row, unit), unit)
                    ref[target, :] = w_in[source, :].astype(BF)
                row = (column + (core ^ near)) * half
                target = slice(start + 2 * unit, start + 2 * unit + half)
                ref[target, :] = w_out[pl.ds(pl.multiple_of(row, half), half), :].astype(BF)

    kept, sent = kernel_call(
        weights,
        "feed_weights",
        [shape_of(planes * size, inner, BF)] * 2,
        (spot, hidden, active, branch, slope),
        scalars=1,
        scratch=[pltpu.VMEM((model, inner), F32), pltpu.VMEM((inner, model), F32)],
        flops=4 * total * model * inner,
    )
    return parts, kept, flipped(sent, 1), sums


def feed_pack(weight_in, weight_out, place):
    rows, hidden = weight_in.shape
    half = weight_out.shape[0] // 2
    columns = weight_in.reshape(rows, place.planes, 2, 2, 2, half)
    columns = lax.dynamic_index_in_dim(columns, place.rep, 4, keepdims=False)
    own = lax.dynamic_index_in_dim(columns, place.second, 2, keepdims=False)
    other = lax.dynamic_index_in_dim(columns, 1 - place.second, 2, keepdims=False)
    own, other = (item.reshape(rows, 2 * place.planes * half) for item in (own, other))
    part_out = lax.dynamic_slice_in_dim(weight_out, place.rep * half, half, 0)
    return own, flipped(other, 2), part_out


def pack_rows(parts, waits=()):
    def body(*values):
        return (jnp.concatenate(values, axis=0),)

    rows = sum(item.shape[0] for item in parts)
    out = shape_of(rows, parts[0].shape[1], BF)
    return fused(body, "pack_rows", [out], *parts, waits=waits)[0]


def plane_bits(place):
    return range(place.planes.bit_length() - 1)


def plane_gather(pack, place):
    pieces = {0: pack}
    for bit in reversed(plane_bits(place)):
        for step in sorted(pieces):
            pieces[step | 1 << bit] = flipped(pieces[step], QUAD << bit)
    near = [pieces[step] for step in range(place.planes)]
    return near + [flipped(item, 1) for item in near]


def plane_reduce(kept, swapped, place):
    size = place.pack_rows
    planes = place.planes

    def total(kept_part, swapped_part):
        both = kept_part.astype(F32) + swapped_part.astype(F32)
        return [both[step * size : (step + 1) * size] for step in range(planes)]

    outs = [shape_of(size, kept.shape[1], F32)]
    outs += [shape_of(size, kept.shape[1], BF)] * (planes - 1)
    pieces = fused(total, "feed_core_sum", outs, kept, swapped)
    pieces = {step: [piece] for step, piece in enumerate(pieces)}
    for bit in plane_bits(place):
        for step in [step for step in sorted(pieces) if step >> bit & 1]:
            values = pieces.pop(step)
            value = values[0] if len(values) == 1 else plane_add(values)
            pieces[step ^ 1 << bit].append(flipped(value, QUAD << bit))
    return plane_add(pieces[0])


def plane_add(values):
    def body(*items):
        return (sum((item.astype(F32) for item in items[1:]), items[0].astype(F32)),)

    return fused(body, "plane_add", [shape_of(*values[0].shape, BF)], *values)[0]


def feed_grads(total, place):
    unit, half = place.unit, place.half
    arrived = flipped(total[unit : 2 * unit], 2)
    own = jnp.concatenate([total[:unit], arrived, total[2 * unit :]], axis=0)
    theirs = flipped(own, place.shards)
    is_first, is_low = place.rep == 0, place.second == 0
    first, last = jnp.where(is_first, own, theirs), jnp.where(is_first, theirs, own)
    grad_out = jnp.concatenate([first[2 * unit :], last[2 * unit :]], axis=0).astype(F32)
    sides = jnp.stack([first[: 2 * unit], last[: 2 * unit]]).reshape(2, 2, unit, -1)
    sides = jnp.where(is_low, sides, sides[:, ::-1])
    sides = sides.reshape(2, 2, unit, place.planes, 2, half).transpose(2, 3, 1, 4, 0, 5)
    return sides.reshape(unit, -1).astype(F32), grad_out


def plane_groups(place):
    return [[quad + QUAD * plane for plane in range(place.planes)] for quad in range(QUAD)]


def score_block(query, keys, table, bias, place, rows, length):
    scores = dot_nt(query, keys)
    spread = dot_nt(query, table)
    band = pltpu.roll(spread, 0, axis=1, stride=1, stride_axis=0)
    column = lax.broadcasted_iota(jnp.int32, (rows, length + 2 * rows), 1)
    bias[...] = jnp.where(column < place, spread[:, :1], spread[:, -1:])
    bias[:, pl.ds(place, 3 * rows)] = band[:, rows:]
    return scores + bias[:, rows : rows + length]


def place_rows(source, columns, target, position, rows):
    for step in range(SPAN):
        spot = pl.ds(pl.multiple_of((position ^ step) * rows, rows), rows)
        target[spot, :] = source[step * rows : (step + 1) * rows, columns]


def split_rows(value, kept, sent, rows):
    for index, step in enumerate((0, 4, 2, 6)):
        target = slice(index * rows, (index + 1) * rows)
        kept[target, :] = value[step * rows : (step + 1) * rows]
        sent[target, :] = value[(step + 1) * rows : (step + 2) * rows].astype(BF)


def join_pieces(refs, target, rows):
    for step, ref in enumerate(refs):
        target[step * rows : (step + 1) * rows, :] = ref[...]


def attend_kernel(*refs):
    spot, pieces, rest = refs[0], refs[1 : 1 + SPAN], refs[1 + SPAN :]
    (weight_in, bias_in, weight_out, table, hidden, mixed, context, peaks, kept, sent) = rest[:10]
    keys, values, bias = rest[10:]
    length, width = context.shape
    rows = length // SPAN
    head = table.shape[1] // 2
    position = spot[0]
    join_pieces(pieces, hidden, rows)
    mixed[...] = (dot_nn(hidden[...], weight_in[...]) + bias_in[...]).astype(BF)
    place_rows(mixed, slice(width, 2 * width), keys, position, rows)
    place_rows(mixed, slice(2 * width, 3 * width), values, position, rows)
    lane = lax.broadcasted_iota(jnp.int32, (rows, width), 1)

    def block(index, carry):
        place = pl.multiple_of(index * rows, rows)
        own = pl.ds(pl.multiple_of((position ^ index) * rows, rows), rows)
        query = mixed[own, :width] * jnp.asarray(head**-0.5, BF)
        results, logs = [], []
        for which in range(2):
            mine = lane // head == which
            part = jnp.where(mine, query, jnp.zeros_like(query))
            scores = score_block(part, keys[...], table[...], bias, place, rows, length)
            top = jnp.max(scores, axis=1, keepdims=True)
            powers = jnp.exp(scores - top)
            total = jnp.sum(powers, axis=1, keepdims=True)
            weights = (powers * (1.0 / total)).astype(BF)
            results.append(dot_nn(weights, values[...]))
            logs.append(top + jnp.log(total))
        context[own, :] = jnp.where(lane < head, results[0], results[1]).astype(BF)
        peaks[own, :] = jnp.where(lane < head, logs[0], logs[1])
        return carry

    lax.fori_loop(0, SPAN, block, 0)
    split_rows(dot_nn(context[...], weight_out[...]), kept, sent, rows)


def attend_back_kernel(*refs):
    spot, pieces, rest = refs[0], refs[1 : 1 + SPAN], refs[1 + SPAN :]
    (mixed, table, peaks, weight_in, weight_out) = rest[:5]
    (branch, grad_mixed, grad_table, far, kept, sent) = rest[5:11]
    keys, values, bias, grad_context, grad_keys, grad_values, slopes = rest[11:]
    length, width = grad_context.shape
    rows = length // SPAN
    head = table.shape[1] // 2
    position = spot[0]
    join_pieces(pieces, branch, rows)
    grad_context[...] = dot_nt(branch[...], weight_out[...]).astype(BF)
    place_rows(mixed, slice(width, 2 * width), keys, position, rows)
    place_rows(mixed, slice(2 * width, 3 * width), values, position, rows)
    grad_keys[...] = jnp.zeros_like(grad_keys)
    grad_values[...] = jnp.zeros_like(grad_values)
    grad_table[...] = jnp.zeros_like(grad_table)
    far[...] = jnp.zeros_like(far)
    lane = lax.broadcasted_iota(jnp.int32, (rows, width), 1)
    padded = lax.broadcasted_iota(jnp.int32, (rows, length + 2 * rows), 1)
    factor = head**-0.5
    slopes[:, :rows] = jnp.zeros((rows, rows), F32)
    slopes[:, rows + length :] = jnp.zeros((rows, rows), F32)
    mirror = (
        lax.broadcasted_iota(jnp.int32, (rows, rows), 0)
        + lax.broadcasted_iota(jnp.int32, (rows, rows), 1)
        == rows - 1
    ).astype(BF)

    def block(index, carry):
        place = pl.multiple_of(index * rows, rows)
        own = pl.ds(pl.multiple_of((position ^ index) * rows, rows), rows)
        query = mixed[own, :width] * jnp.asarray(factor, BF)
        results = []
        for which in range(2):
            mine = lane // head == which
            part = jnp.where(mine, query, jnp.zeros_like(query))
            scores = score_block(part, keys[...], table[...], bias, place, rows, length)
            incoming = grad_context[own, :]
            incoming = jnp.where(mine, incoming, jnp.zeros_like(incoming))
            logs = peaks[own, which * head : which * head + 1]
            probs = jnp.exp(scores - logs)
            grad_probs = dot_nt(incoming, values[...])
            shared = jnp.sum(grad_probs * probs, axis=1, keepdims=True)
            grad_low = (probs * (grad_probs - shared)).astype(BF)
            grad_values[...] += dot_tn(probs.astype(BF), incoming)
            grad_keys[...] += dot_tn(grad_low, part)
            slopes[:, rows : rows + length] = grad_low.astype(F32)
            window = slopes[:, pl.ds(place, 3 * rows)]
            whole = slopes[...]
            early = jnp.sum(jnp.where(padded < place, whole, 0.0), axis=1, keepdims=True)
            late = jnp.sum(
                jnp.where(padded >= place + 3 * rows, whole, 0.0), axis=1, keepdims=True
            )
            window = jnp.concatenate(
                [jnp.zeros((rows, rows), F32), dot_nn(mirror, window.astype(BF))], axis=1
            )
            window = pltpu.roll(
                window, 3 * rows + 1, axis=1, stride=1, stride_axis=0
            ).astype(BF)
            grad_table[...] += dot_tn(window, dot_nn(mirror, part).astype(BF))
            part_wide = part.astype(F32)
            far[0:1, :] += jnp.sum(early * part_wide, axis=0, keepdims=True)
            far[1:2, :] += jnp.sum(late * part_wide, axis=0, keepdims=True)
            close = jnp.dot(
                mirror.astype(F32),
                dot_nn(window, table[...]),
                preferred_element_type=F32,
                precision=lax.Precision.HIGHEST,
            )
            results.append(
                dot_nn(grad_low, keys[...])
                + close
                + early * table[0:1, :].astype(F32)
                + late * table[4 * rows - 1 :, :].astype(F32)
            )
        grad_mixed[own, :width] = (
            jnp.where(lane < head, results[0], results[1]) * factor
        ).astype(BF)
        return carry

    lax.fori_loop(0, SPAN, block, 0)
    for step in range(SPAN):
        source = pl.ds(pl.multiple_of((position ^ step) * rows, rows), rows)
        target = slice(step * rows, (step + 1) * rows)
        grad_mixed[target, width : 2 * width] = grad_keys[source, :].astype(BF)
        grad_mixed[target, 2 * width :] = grad_values[source, :].astype(BF)
    split_rows(dot_nt(grad_mixed[...], weight_in[...]), kept, sent, rows)


def group_gather(value, masks):
    near = square_gather(value, masks)
    return near, [flipped(item, 1) for item in near]


def group_reduce(kept, sent, masks):
    swapped = flipped(sent, 1)
    rows = kept.shape[0] // 4

    def body(kept_part, swapped_part):
        total = kept_part + swapped_part.astype(F32)
        return [total[index * rows : (index + 1) * rows] for index in range(4)]

    outs = [shape_of(rows, kept.shape[1], dtype) for dtype in (F32, BF, BF, BF)]
    return square_reduce(fused(body, "core_sum", outs, kept, swapped), masks)


def in_steps(blocks):
    near, far = blocks
    return [near[0], far[0], near[2], far[2], near[1], far[1], near[3], far[3]]


def attend(blocks, weight_in, bias_in, weight_out, table, place):
    pieces = in_steps(blocks)
    rows, model = pieces[0].shape
    length, width = SPAN * rows, weight_out.shape[0]
    outs = [
        shape_of(length, model, BF),
        shape_of(length, 3 * width, BF),
        shape_of(length, width, BF),
        shape_of(length, width, F32),
        shape_of(length // 2, model, F32),
        shape_of(length // 2, model, BF),
    ]
    hidden, mixed, context, peaks, kept, sent = kernel_call(
        attend_kernel,
        "attend_forward",
        outs,
        (place.span_spot, *pieces, weight_in, bias_in, weight_out, table),
        scalars=1,
        scratch=[
            pltpu.VMEM((length, width), BF),
            pltpu.VMEM((length, width), BF),
            pltpu.VMEM((rows, length + 2 * rows), F32),
        ],
        flops=48 * length * length * width,
    )
    return group_reduce(kept, sent, place.span_masks), (hidden, mixed, context, peaks)


def attend_back(blocks, saved, weight_in, weight_out, table, place, waits):
    hidden, mixed, context, peaks = saved
    pieces = in_steps(blocks)
    rows, model = pieces[0].shape
    length, width = SPAN * rows, weight_out.shape[0]
    outs = [
        shape_of(length, model, BF),
        shape_of(length, 3 * width, BF),
        shape_of(4 * rows, width, F32),
        shape_of(8, width, F32),
        shape_of(length // 2, model, F32),
        shape_of(length // 2, model, BF),
    ]
    branch, grad_mixed, grad_table, far, kept, sent = kernel_call(
        attend_back_kernel,
        "attend_backward",
        outs,
        (place.span_spot, *pieces, mixed, table, peaks, weight_in, weight_out),
        scalars=1,
        scratch=[
            pltpu.VMEM((length, width), BF),
            pltpu.VMEM((length, width), BF),
            pltpu.VMEM((rows, length + 2 * rows), F32),
            pltpu.VMEM((length, width), BF),
            pltpu.VMEM((length, width), F32),
            pltpu.VMEM((length, width), F32),
            pltpu.VMEM((rows, length + 2 * rows), F32),
        ],
        flops=96 * length * length * width,
        waits=waits,
    )
    parts = group_reduce(kept, sent, place.span_masks)

    def weights(hidden_rows, mixed_grad, context_rows, branch_rows):
        return (
            dot_tn(hidden_rows, mixed_grad),
            dot_tn(context_rows, branch_rows),
            column_sum(mixed_grad),
        )

    grad_in, grad_out, sums = fused(
        weights,
        "attend_weights",
        [shape_of(model, 3 * width, BF), shape_of(width, model, BF), shape_of(1, 3 * width, F32)],
        hidden,
        grad_mixed,
        context,
        branch,
        flops=8 * length * model * width,
    )
    return parts, grad_in, grad_out, sums, distance_gradient(grad_table, far, rows)


def wide_table(distance, rows):
    index = jnp.clip(jnp.arange(4 * rows) - rows - LEFT, 0, LEFT + RIGHT)
    low = distance[index]
    return jnp.concatenate([low, low], axis=1)


def distance_gradient(grad_table, far, rows):
    first = rows + LEFT
    last = first + LEFT + RIGHT
    head = grad_table.shape[1] // 2
    low = jnp.sum(grad_table[: first + 1], axis=0) + far[0]
    high = jnp.sum(grad_table[last:], axis=0) + far[1]
    total = jnp.concatenate([low[None], grad_table[first + 1 : last], high[None]], axis=0)
    return total[:, :head] + total[:, head:]


def whole_heads(weight_out, head):
    return weight_out.shape[0] % head == 0


def swap_if(condition, value, axis):
    return jnp.where(condition, jnp.flip(value, axis), value)


def attend_weights(weight_in, weight_out, head, place, waits):
    rows, model = weight_in.shape[0], weight_out.shape[1]
    heads = model // head
    per_device = heads // SPAN
    width = per_device * head
    if not whole_heads(weight_out, head):
        whole = lax.all_gather(weight_in, "shard", axis=0, tiled=True)
        whole = whole.reshape(model, 3, heads, head)
        mine = lax.dynamic_slice_in_dim(whole, place.member * per_device, per_device, 2)
        out = lax.all_gather(weight_out, "shard", axis=0, tiled=True)
        out = lax.dynamic_slice_in_dim(out, place.member * width, width, 0)
        return mine.reshape(model, 3 * width), out
    planes, unit = place.planes, place.unit
    groups, columns = planes // 2, 3 * width
    blocks = weight_in.reshape(rows, 3, groups, 2, 2, 2, -1)
    blocks = blocks.transpose(4, 3, 5, 0, 1, 2, 6).reshape(2, 2, 2 * rows, columns)
    own = lax.dynamic_index_in_dim(blocks, place.second, 0, keepdims=False)
    other = lax.dynamic_index_in_dim(blocks, 1 - place.second, 0, keepdims=False)
    arrived = flipped(other.reshape(4 * rows, columns), 2).reshape(own.shape)

    def arrange(spot, own_ref, arrived_ref, *outs):
        low, core = spot[0] & 1, spot[2]
        for step, out in enumerate(outs):
            for near in range(2):
                source = pl.ds(pl.multiple_of((core ^ near) * unit, unit), unit)
                for turn, ref in enumerate((own_ref, arrived_ref)):
                    start = (2 * near + turn) * unit
                    out[start : start + unit, :] = ref[low ^ step, source, :]

    near, far = kernel_call(
        arrange,
        "attend_columns",
        [shape_of(4 * unit, columns, BF)] * 2,
        (place.spot, own, arrived),
        scalars=1,
        waits=waits,
    )
    pieces = [near] + [
        flipped((near, far)[step & 1], QUAD * step) for step in range(1, planes)
    ]

    def split(*values):
        kept = jnp.concatenate([item[: 2 * unit] for item in values], axis=0)
        sent = jnp.concatenate([item[2 * unit :] for item in values], axis=0)
        return kept, sent

    kept, sent = fused(
        split, "attend_split", [shape_of(2 * planes * unit, columns, BF)] * 2, *pieces
    )
    swapped = flipped(sent, 1)
    outs = [weight_out] + [flipped(weight_out, SPAN * step) for step in range(1, groups)]

    def lay(spot, kept_ref, swapped_ref, *refs):
        plane, second, core = spot[0], spot[1], spot[2]
        w_in, w_out = refs[-2:]
        for near, ref in enumerate((kept_ref, swapped_ref)):
            for step in range(planes):
                for turn in range(2):
                    row = (((plane ^ step) * 2 + (second ^ turn)) * 2 + (core ^ near)) * unit
                    start = (2 * step + turn) * unit
                    w_in[pl.ds(pl.multiple_of(row, unit), unit), :] = ref[start : start + unit, :]
        for step, ref in enumerate(refs[:-2]):
            row = ((plane >> 1) ^ step) * unit
            w_out[pl.ds(pl.multiple_of(row, unit), unit), :] = ref[...]

    return kernel_call(
        lay,
        "attend_lay",
        [shape_of(model, columns, BF), shape_of(width, model, BF)],
        (place.spot, kept, swapped, *outs),
        scalars=1,
    )


def head_row(row, place, aligned):
    if aligned:
        row = row.reshape(-1, SPAN, place.unit)
        row = lax.dynamic_index_in_dim(row, place.member, 1, keepdims=False)
        return row.reshape(1, -1)
    row = row.reshape(SPAN, -1)
    return lax.dynamic_slice_in_dim(row, place.member, 1, 0)


def head_spread(row, model, place, aligned):
    if aligned:
        whole = jnp.zeros((place.planes // 2, SPAN, place.unit), F32)
        block = row.reshape(-1, 1, place.unit)
        return lax.dynamic_update_slice_in_dim(whole, block, place.member, 1).reshape(1, model)
    whole = jnp.zeros((SPAN, model // SPAN), F32)
    return lax.dynamic_update_slice_in_dim(whole, row, place.member, 0).reshape(1, model)


def attend_weight_grads(grad_in, grad_out, head, place, aligned):
    model = grad_out.shape[1]
    heads = model // head
    per_device = heads // SPAN
    if not aligned:
        whole = jnp.zeros((model, 3, heads, head), F32)
        whole = lax.dynamic_update_slice_in_dim(
            whole,
            grad_in.astype(F32).reshape(model, 3, per_device, head),
            place.member * per_device,
            2,
        )
        whole = lax.psum_scatter(
            whole.reshape(model, 3 * model), "shard", scatter_dimension=0, tiled=True
        )
        out = jnp.zeros((model, model), F32)
        out = lax.dynamic_update_slice_in_dim(
            out, grad_out.astype(F32), place.member * per_device * head, 0
        )
        out = lax.psum_scatter(out, "shard", scatter_dimension=0, tiled=True)
        return rep_sum(whole, place), rep_sum(out, place)
    planes, unit = place.planes, place.unit
    groups, columns = planes // 2, grad_in.shape[1]

    def lay(spot, w_in, w_out, kept, sent, *outs):
        plane, second, core = spot[0], spot[1], spot[2]
        for near, ref in enumerate((kept, sent)):
            for step in range(planes):
                for turn in range(2):
                    row = (((plane ^ step) * 2 + (second ^ turn)) * 2 + (core ^ near)) * unit
                    start = (2 * step + turn) * unit
                    ref[start : start + unit, :] = w_in[pl.ds(pl.multiple_of(row, unit), unit), :]
        for step, ref in enumerate(outs):
            row = ((plane >> 1) ^ step) * unit
            ref[...] = w_out[pl.ds(pl.multiple_of(row, unit), unit), :]

    kept, sent, *outs = kernel_call(
        lay,
        "attend_unlay",
        [shape_of(2 * planes * unit, columns, BF)] * 2 + [shape_of(unit, model, BF)] * groups,
        (place.spot, grad_in, grad_out),
        scalars=1,
    )
    swapped = flipped(sent, 1)

    def by_plane(kept_part, swapped_part):
        both = jnp.concatenate([kept_part, swapped_part], axis=1)
        return [both[2 * step * unit : 2 * (step + 1) * unit] for step in range(planes)]

    pieces = fused(
        by_plane,
        "attend_planes",
        [shape_of(2 * unit, 2 * columns, BF)] * planes,
        kept,
        swapped,
    )
    arrived = [pieces[0]] + [flipped(pieces[step], QUAD * step) for step in range(1, planes)]
    outs = [outs[0]] + [flipped(outs[step], SPAN * step) for step in range(1, groups)]

    def total(*values):
        even = sum(item.astype(F32) for item in values[:planes:2])
        odd = sum(item.astype(F32) for item in values[1:planes:2])
        both = jnp.concatenate([even, odd], axis=1)
        out = sum(item.astype(F32) for item in values[planes:])
        return both[:unit], both[unit:], out

    own, other, out = fused(
        total,
        "attend_plane_sum",
        [shape_of(unit, 4 * columns, BF)] * 2 + [shape_of(unit, model, BF)],
        *arrived,
        *outs,
    )
    whole = jnp.stack([own, flipped(other, 2)])
    whole = rep_sum(whole, place).reshape(2, unit, 2, 2, 3, groups, -1)
    whole = swap_if(place.second == 1, whole, 0)
    whole = swap_if(place.plane & 1 == 1, whole, 2)
    whole = swap_if(place.core == 1, whole, 3)
    whole = whole.transpose(1, 4, 5, 2, 0, 3, 6)
    return whole.reshape(unit, 3 * model), rep_sum(out, place)


def rep_sum(value, place):
    low = value.astype(BF)
    return low.astype(F32) + flipped(low, place.shards).astype(F32)


LANES = 128


def row(wide, index):
    return wide[index : index + 1]


def pack_columns(left, right, waits):
    def body(first, second):
        return (jnp.concatenate([first, second], axis=1),)

    out = shape_of(left.shape[0], left.shape[1] + right.shape[1], BF)
    return fused(body, "pack_columns", [out], left, right, waits=waits)[0]


def convolve_start(parts, before, wide, bias_row, weight_in):
    rows, model = before.shape

    def body(*values):
        base, small, w_in = values[4:]
        current = base + joined(values[:4]) + row(small, bias_row)
        unit, unused_scale = standard(current)
        hidden = (unit * row(small, 7) + row(small, 8)).astype(BF)
        doubled = dot_nn(hidden, w_in)
        return current, hidden, doubled, doubled[:, :model] * logistic(doubled[:, model:])

    return fused(
        body,
        "convolve_start",
        [
            shape_of(rows, model, F32),
            shape_of(rows, model, BF),
            shape_of(rows, 2 * model, F32),
            shape_of(rows, model, BF),
        ],
        *parts,
        before,
        wide,
        weight_in,
        flops=4 * rows * model * model,
    )


def convolve_finish(glued, border, wide, taps, weight_out, before):
    rows, model = before.shape
    edge = border.shape[0]

    def kernel(
        glued_ref, border_ref, small, w_out, base,
        mixed_ref, rest_ref, current_ref, hidden_ref, padded,
    ):
        padded[:edge, :] = border_ref[...].astype(F32)
        padded[edge:, :] = glued_ref[...].astype(F32)
        first, count = taps
        for column in range(0, model, LANES):
            lanes = slice(column, column + LANES)
            total = jnp.zeros((rows, LANES), F32)
            for tap in range(count):
                start = edge - count + 1 + tap
                weight = small[first + tap : first + tap + 1, lanes]
                total += padded[start : start + rows, lanes] * weight
            mixed_ref[:, lanes] = total
        unit, unused_scale = standard(mixed_ref[...])
        upper = unit * small[9:10, :] + small[10:11, :]
        rest = (upper * logistic(upper)).astype(BF)
        rest_ref[...] = rest
        current = base[...] + dot_nn(rest, w_out[...])
        current_ref[...] = current
        unit, unused_scale = standard(current)
        hidden_ref[...] = (unit * small[11:12, :] + small[12:13, :]).astype(BF)

    return kernel_call(
        kernel,
        "convolve_finish",
        [shape_of(rows, model, dtype) for dtype in (F32, BF, F32, BF)],
        (glued, border, wide, weight_out, before),
        scratch=[pltpu.VMEM((edge + rows, model), F32)],
        flops=2 * rows * model * model,
    )


def convolve_back_start(parts, grad, after, mixed, wide, taps, weight_out, glued, border, waits):
    rows, model = after.shape
    edge = border.shape[0]
    first, count = taps

    def kernel(
        own, part_one, part_two, part_three, grad_ref, after_ref, mixed_ref, small,
        w_out, glued_ref, border_ref,
        grad_out, branch_ref, main_ref, halo_ref, sums, padded, spread,
    ):
        incoming = joined((own[...], part_one[...], part_two[...], part_three[...]))
        slope, sum_gain, sum_shift = norm_back(after_ref[...], small[11:12, :], incoming)
        current = grad_ref[...] + slope
        grad_out[...] = current
        branch = current.astype(BF)
        branch_ref[...] = branch
        unit, scale = standard(mixed_ref[...])
        upper = unit * small[9:10, :] + small[10:11, :]
        grad_upper = dot_nt(branch, w_out[...]) * silu_slope(upper)
        inner = grad_upper * small[9:10, :]
        mean = jnp.mean(inner, axis=-1, keepdims=True)
        shared = jnp.mean(inner * unit, axis=-1, keepdims=True)
        padded[:edge, :] = border_ref[...].astype(F32)
        padded[edge:, :] = glued_ref[...].astype(F32)
        spread[:edge, :] = jnp.zeros((edge, model), F32)
        spread[edge : edge + rows, :] = scale * (inner - mean - unit * shared)
        spread[edge + rows :, :] = jnp.zeros((edge, model), F32)
        sums[count : count + 1, :] = column_sum(grad_upper * unit)
        sums[count + 1 : count + 2, :] = column_sum(grad_upper)
        sums[count + 2 : count + 3, :] = sum_gain
        sums[count + 3 : count + 4, :] = sum_shift
        for column in range(0, model, LANES):
            lanes = slice(column, column + LANES)
            total = jnp.zeros((rows + edge, LANES), F32)
            center = spread[edge : edge + rows, lanes]
            for tap in range(count):
                start = edge - count + 1 + tap
                sums[tap : tap + 1, lanes] = jnp.sum(
                    center * padded[start : start + rows, lanes], axis=0, keepdims=True
                )
                begin = count - 1 - tap
                weight = small[first + tap : first + tap + 1, lanes]
                total += spread[begin : begin + rows + edge, lanes] * weight
            halo_ref[:, lanes] = total[:edge].astype(BF)
            main_ref[:, lanes] = total[edge:]

    return kernel_call(
        kernel,
        "convolve_back_start",
        [
            shape_of(rows, model, F32),
            shape_of(rows, model, BF),
            shape_of(rows, model, F32),
            shape_of(edge, model, BF),
            shape_of(count + 4, model, F32),
        ],
        (*parts, grad, after, mixed, wide, weight_out, glued, border),
        scratch=[
            pltpu.VMEM((edge + rows, model), F32),
            pltpu.VMEM((rows + 2 * edge, model), F32),
        ],
        flops=2 * rows * model * model,
        waits=waits,
    )


def convolve_back_finish(main, incoming, doubled, weight_in, before, wide, grad):
    rows, model = before.shape
    edge = incoming.shape[0]

    def body(main_rows, late, both, w_in, base, small, grad_rows):
        glued = jnp.concatenate(
            [main_rows[: rows - edge], main_rows[rows - edge :] + late.astype(F32)], axis=0
        )
        glued = glued.astype(BF).astype(F32)
        gate = logistic(both[:, model:])
        slope = jnp.concatenate(
            [glued * gate, glued * both[:, :model] * gate * (1.0 - gate)], axis=1
        ).astype(BF)
        inner, sum_gain, sum_shift = norm_back(base, row(small, 7), dot_nt(slope, w_in))
        current = grad_rows + inner
        branch = current.astype(BF)
        sums = jnp.concatenate([sum_gain, sum_shift, column_sum(branch)], axis=0)
        return current, branch, slope, sums

    return fused(
        body,
        "convolve_back_finish",
        [
            shape_of(rows, model, F32),
            shape_of(rows, model, BF),
            shape_of(rows, 2 * model, BF),
            shape_of(3, model, F32),
        ],
        main,
        incoming,
        doubled,
        weight_in,
        before,
        wide,
        grad,
        flops=4 * rows * model * model,
    )


def convolve_weight_grads(hidden, slope, rest, branch, place):
    model = hidden.shape[1]

    def body(hidden_rows, slope_rows, rest_rows, branch_rows):
        both = dot_tn(hidden_rows, slope_rows), dot_tn(rest_rows, branch_rows)
        return (jnp.concatenate(both, axis=1),)

    total = fused(
        body,
        "convolve_weights",
        [shape_of(model, 3 * model, BF)],
        hidden,
        slope,
        rest,
        branch,
        flops=6 * hidden.shape[0] * model * model,
    )[0]
    total = lax.psum_scatter(total, "shard", scatter_dimension=0, tiled=True)
    total = rep_sum(total, place)
    return total[:, : 2 * model], total[:, 2 * model :]


def feed_to_attend(parts, before, wide, waits):
    rows, model = before.shape

    def body(*values):
        base, small = values[4:]
        current = base.astype(F32) + 0.5 * (joined(values[:4]) + row(small, 2))
        unit, unused_scale = standard(current)
        return current, unit * row(small, 3) + row(small, 4)

    outs = [shape_of(rows, model, F32), shape_of(rows, model, BF)]
    return fused(body, "feed_to_attend", outs, *parts, before, wide, waits=waits)


def turn_around(parts, before, wide, cotangent):
    rows, model = before.shape

    def body(*values):
        base, small, grad = values[4:]
        current = base + 0.5 * (joined(values[:4]) + row(small, 13))
        unit, unused_scale = standard(current)
        slope, sum_gain, sum_shift = norm_back(current, row(small, 14), grad.astype(F32))
        branch = (0.5 * slope).astype(BF)
        sums = jnp.concatenate([column_sum(branch), sum_gain, sum_shift], axis=0)
        return unit * row(small, 14) + row(small, 15), slope, branch, sums

    outs = [
        shape_of(rows, model, BF),
        shape_of(rows, model, F32),
        shape_of(rows, model, BF),
        shape_of(3, model, F32),
    ]
    return fused(body, "turn_around", outs, *parts, before, wide, cotangent)


def attend_to_feed_back(parts, grad, before, wide):
    rows, model = before.shape

    def body(*values):
        grad_rows, base, small = values[4:]
        slope, sum_gain, sum_shift = norm_back(base, row(small, 3), joined(values[:4]))
        current = grad_rows + slope
        branch = (0.5 * current).astype(BF)
        sums = jnp.concatenate([column_sum(branch), sum_gain, sum_shift], axis=0)
        return current, branch, sums

    outs = [shape_of(rows, model, F32), shape_of(rows, model, BF), shape_of(3, model, F32)]
    return fused(body, "attend_to_feed_back", outs, *parts, grad, before, wide)


def last_step(parts, grad, before, wide):
    rows, model = before.shape

    def body(*values):
        grad_rows, base, small = values[4:]
        slope, sum_gain, sum_shift = norm_back(
            base.astype(F32), row(small, 0), joined(values[:4])
        )
        return grad_rows + slope, jnp.concatenate([sum_gain, sum_shift], axis=0)

    outs = [shape_of(rows, model, F32), shape_of(2, model, F32)]
    return fused(body, "last_step", outs, *parts, grad, before, wide)


def shard_gather(value, place):
    gathered = value[None]
    for bit in range(place.shards.bit_length() - 1):
        arrived = flipped(gathered, 1 << bit)
        low = jnp.bitwise_and(jnp.right_shift(place.shard, bit), 1) == 0
        gathered = jnp.concatenate(
            [jnp.where(low, gathered, arrived), jnp.where(low, arrived, gathered)], axis=0
        )
    return gathered


def shard_reduce(value, place):
    both = jnp.concatenate([value, value], axis=0)
    both = lax.all_to_all(both, ("rep", "shard"), 0, 0, tiled=True)
    return jnp.sum(both, axis=0)


def sum_everywhere(value, place, delays):
    arrived = flipped(value, 1)
    for bit in range(1, (2 * place.shards).bit_length() - 1):
        waits = delays[bit - 1 : bit]
        value = fused(
            lambda own, other: (own + other,),
            "table_sum",
            [shape_of(*value.shape, F32)],
            value,
            arrived,
            waits=waits,
        )[0]
        arrived = flipped(value, 1 << bit)
    return value + arrived


class Place:
    def __init__(self, unit, half):
        self.shards = lax.axis_size("shard")
        self.planes = self.shards // QUAD
        self.unit, self.half = unit, half
        self.pack_rows = 2 * unit + half
        self.rep = lax.axis_index("rep")
        self.shard = lax.axis_index("shard")
        self.core = self.shard % 2
        self.second = self.shard // 2 % 2
        self.plane = self.shard // QUAD
        self.member = self.shard % SPAN
        self.spot = jnp.stack([self.plane, self.second, self.core])
        self.flat_spot = jnp.stack([jnp.zeros_like(self.plane), self.second, self.core])
        self.span_spot = self.member.reshape(1)
        self.feed_masks = (self.shards, 2)
        self.span_masks = (4, 2)


def along(value, by, place):
    count = place.shards
    route = [(i, i + by) for i in range(count) if 0 <= i + by < count]
    return lax.ppermute(value, "shard", route)


def shards(
    inputs,
    ff_in,
    ff_out,
    ff_bias,
    attn_in,
    attn_out,
    conv_in,
    conv_out,
    depthwise,
    distance,
    vectors,
    attn_bias,
    cotangent,
):
    rows, model = inputs.shape
    unit, half = ff_in.shape[2], ff_out.shape[2] // 2
    place = Place(unit, half)
    head = distance.shape[2]
    tap_count = depthwise.shape[1]
    edge = -(-(tap_count - 1) // 16) * 16
    aligned = whole_heads(attn_out[0], head)
    bias_rows = ff_bias.shape[2] // unit
    count = vectors.shape[1]
    taps = (count + 1, tap_count)

    small = jnp.concatenate(
        [vectors[0], attn_bias, depthwise[0], ff_bias[0].reshape(2 * bias_rows, unit)], axis=0
    )
    first_pack = pack_rows(feed_pack(ff_in[0, 0], ff_out[0, 0], place))
    first_packs = plane_gather(first_pack, place)
    pieces = square_gather(inputs, place.feed_masks)
    small = shard_gather(small, place)
    wide = small[:, : count + 1 + tap_count].transpose(1, 0, 2).reshape(-1, model).astype(F32)
    feed_bias = small[:, count + 1 + tap_count :].reshape(place.planes, 2, 2, 2, 2, half)
    feed_bias = lax.dynamic_index_in_dim(feed_bias, place.second, 1, keepdims=False)
    feed_bias = lax.dynamic_index_in_dim(feed_bias, place.rep, 3, keepdims=False)
    feed_bias = feed_bias.transpose(2, 0, 1, 3).reshape(2, 1, -1).astype(F32)
    table = wide_table(distance[0], rows)
    mix_bias = jnp.concatenate(
        [
            head_row(wide[5], place, aligned),
            jnp.zeros((1, model // SPAN), F32),
            head_row(wide[6], place, aligned),
        ],
        axis=1,
    )

    arrived = first_packs[: place.planes]
    mix_in, mix_out = attend_weights(attn_in[0], attn_out[0], head, place, arrived)
    glue = pack_columns(conv_in[0], conv_out[0], arrived)
    glue = lax.all_gather(glue, "shard", axis=0, tiled=True)
    second_pack = feed_pack(ff_in[0, 1], ff_out[0, 1], place)

    parts, saved_first = feed(
        pieces, first_packs, place.spot, feed_bias[0], wide, 0, place.feed_masks, place
    )
    second_near = lax.all_gather(
        pack_rows(second_pack, waits=saved_first[:1]),
        "shard",
        axis=0,
        tiled=True,
        axis_index_groups=plane_groups(place),
    )
    second_packs = [second_near, flipped(second_near, 1)]
    after_first, hidden = feed_to_attend(parts, inputs, wide, (mix_in,))
    parts, saved_attend = attend(
        group_gather(hidden, place.span_masks), mix_in, mix_bias, mix_out, table, place
    )
    glue_in, glue_out = glue[:, : 2 * model], glue[:, 2 * model :]
    after_attend, conv_hidden, doubled, glued = convolve_start(
        parts, after_first, wide, count, glue_in
    )
    border = along(glued[rows - edge :], 1, place)
    border = jnp.where(place.member == 0, jnp.zeros_like(border), border)
    mixed, rest, after_conv, hidden = convolve_finish(
        glued, border, wide, taps, glue_out, after_attend
    )
    pieces = square_gather(hidden, place.feed_masks)
    parts, saved_second = feed(
        pieces, second_packs, place.flat_spot, feed_bias[1], wide, None, place.feed_masks, place
    )
    output, grad_last, branch, last_sums = turn_around(parts, after_conv, wide, cotangent)

    pieces = square_gather(branch, place.feed_masks)
    parts, kept, swapped, second_bias = feed_back(
        pieces, second_packs, place.flat_spot, saved_second, place.feed_masks, place
    )
    second_total = fused(
        lambda own, other: (own.astype(F32) + other.astype(F32),),
        "feed_core_total",
        [shape_of(*kept.shape, BF)],
        kept,
        swapped,
    )[0]
    second_sum = lax.psum_scatter(
        second_total,
        "shard",
        scatter_dimension=0,
        tiled=True,
        axis_index_groups=plane_groups(place),
    )
    grad_conv, conv_branch, main, halo, conv_sums = convolve_back_start(
        parts, grad_last, after_conv, mixed, wide, taps, glue_out, glued, border, (second_total,)
    )
    incoming = along(halo, -1, place)
    incoming = jnp.where(place.member == SPAN - 1, jnp.zeros_like(incoming), incoming)
    grad_attend, branch, slope, attend_sums = convolve_back_finish(
        main, incoming, doubled, glue_in, after_attend, wide, grad_conv
    )
    conv_grads = convolve_weight_grads(conv_hidden, slope, rest, conv_branch, place)
    parts, mix_grad_in, mix_grad_out, mix_sums, grad_distance = attend_back(
        group_gather(branch, place.span_masks), saved_attend, mix_in, mix_out, table, place, ()
    )
    grad_first, branch, first_sums = attend_to_feed_back(parts, grad_attend, after_first, wide)
    pieces = square_gather(branch, place.feed_masks)
    parts, kept, swapped, first_bias = feed_back(
        pieces, first_packs, place.spot, saved_first, place.feed_masks, place
    )
    first_sum = plane_reduce(kept, swapped, place)
    grad_input, input_sums = last_step(parts, grad_first, inputs, wide)

    second_grads = feed_grads(second_sum, place)
    mix_grads = attend_weight_grads(mix_grad_in, mix_grad_out, head, place, aligned)
    first_grads = feed_grads(first_sum, place)
    width = mix_sums.shape[1] // 3
    wide_grads = jnp.concatenate(
        [
            input_sums,
            first_sums,
            head_spread(mix_sums[:, :width], model, place, aligned),
            head_spread(mix_sums[:, 2 * width :], model, place, aligned),
            attend_sums[:2],
            conv_sums[tap_count:],
            last_sums,
            attend_sums[2:],
            conv_sums[:tap_count],
        ],
        axis=0,
    )
    wide_grads = wide_grads.reshape(-1, place.shards, unit).transpose(1, 0, 2)
    bias_pair = jnp.stack([first_bias, second_bias]).reshape(2, place.planes, 2, half)
    bias_grads = lax.dynamic_update_slice(
        jnp.zeros((place.planes, 2, 2, 2, 2, half), F32),
        bias_pair.transpose(1, 2, 0, 3)[:, None, :, :, None, :],
        (0, place.second, 0, 0, place.rep, 0),
    ).reshape(place.shards, 2 * bias_rows, unit)
    small_grads = shard_reduce(jnp.concatenate([wide_grads, bias_grads], axis=1), place)
    delays = (grad_first, kept, first_sum)
    grad_distance = sum_everywhere(grad_distance, place, delays)
    return (
        output,
        grad_input,
        jnp.stack([first_grads[0], second_grads[0]])[None],
        jnp.stack([first_grads[1], second_grads[1]])[None],
        small_grads[count + 1 + tap_count :].reshape(1, 2, -1),
        mix_grads[0][None],
        mix_grads[1][None],
        conv_grads[0][None],
        conv_grads[1][None],
        small_grads[count + 1 : count + 1 + tap_count][None],
        grad_distance[None],
        small_grads[:count][None],
        small_grads[count : count + 1],
    )


def solution(mesh):
    in_specs = (
        P(("rep", "shard"), None),
        P(None, None, "shard", None),
        P(None, None, "shard", None),
        P(None, None, "shard"),
        P(None, "shard", None),
        P(None, "shard", None),
        P(None, "shard", None),
        P(None, "shard", None),
        P(None, None, "shard"),
        P(),
        P(None, None, "shard"),
        P(None, "shard"),
        P(("rep", "shard"), None),
    )
    out_specs = (
        P(("rep", "shard"), None),
        P(("rep", "shard"), None),
        P(None, None, "shard", None),
        P(None, None, "shard", None),
        P(None, None, "shard"),
        P(None, "shard", None),
        P(None, "shard", None),
        P(None, "shard", None),
        P(None, "shard", None),
        P(None, None, "shard"),
        P(),
        P(None, None, "shard"),
        P(None, "shard"),
    )
    return jax.shard_map(shards, mesh=mesh, in_specs=in_specs, out_specs=out_specs, check_vma=False)
```

```python
import jax
import jax.numpy as jnp
from jax import lax
from jax.experimental import pallas as pl
from jax.experimental.pallas import tpu as pltpu
from jax.sharding import PartitionSpec as P

LEFT = 64
RIGHT = 8
SPAN = 8
QUAD = 4
EPSILON = 1e-05
BF = jnp.bfloat16
F32 = jnp.float32
MIB = 1 << 20
LANES = 128


def dot_nn(left, right):
    return jnp.dot(left, right, preferred_element_type=F32)


def dot_nt(left, right):
    return lax.dot_general(left, right, (((1,), (1,)), ((), ())), preferred_element_type=F32)


def dot_tn(left, right):
    return lax.dot_general(left, right, (((0,), (0,)), ((), ())), preferred_element_type=F32)


def column_sum(values):
    return jnp.sum(values.astype(F32), axis=0, keepdims=True)


def standard(values):
    center = values - jnp.mean(values, axis=-1, keepdims=True)
    scale = lax.rsqrt(jnp.mean(center * center, axis=-1, keepdims=True) + EPSILON)
    return center * scale, scale


def norm_back(values, gain, grad):
    unit, scale = standard(values)
    inner = grad * gain
    first = jnp.mean(inner, axis=-1, keepdims=True)
    second = jnp.mean(inner * unit, axis=-1, keepdims=True)
    return scale * (inner - first - unit * second), column_sum(grad * unit), column_sum(grad)


def logistic(values):
    return 1.0 / (1.0 + jnp.exp(-values))


def silu_slope(values):
    gate = logistic(values)
    return gate * (1.0 + values * (1.0 - gate))


def vmem(count):
    return [pl.BlockSpec(memory_space=pltpu.VMEM)] * count


def shape_of(rows, columns, dtype):
    return jax.ShapeDtypeStruct((rows, columns), dtype)


def kernel_call(body, name, outs, operands, scalars=0, scratch=(), flops=0, waits=()):
    moved = sum(item.size * item.dtype.itemsize for item in (*operands[scalars:], *outs))
    count = len(operands)

    def kernel(*refs):
        body(*refs[:count], *refs[count + len(waits) :])

    return pl.pallas_call(
        kernel,
        in_specs=[pl.BlockSpec(memory_space=pltpu.SMEM)] * scalars
        + vmem(count - scalars)
        + [pl.BlockSpec(memory_space=pl.ANY)] * len(waits),
        out_specs=vmem(len(outs)),
        out_shape=list(outs),
        scratch_shapes=list(scratch),
        compiler_params=pltpu.CompilerParams(vmem_limit_bytes=24 * MIB),
        cost_estimate=pl.CostEstimate(flops=flops, bytes_accessed=moved, transcendentals=0),
        name=name,
    )(*operands, *waits)


def fused(body, name, outs, *operands, flops=0, waits=()):
    def kernel(*refs):
        results = body(*[ref[...] for ref in refs[: len(operands)]])
        for ref, value in zip(refs[len(operands) :], results):
            ref[...] = value.astype(ref.dtype)

    return kernel_call(kernel, name, outs, operands, flops=flops, waits=waits)


def flipped(value, mask):
    total = lax.axis_size("rep") * lax.axis_size("shard")
    return lax.ppermute(value, ("rep", "shard"), [(i, i ^ mask) for i in range(total)])


def square_groups(place, masks):
    first, second = masks
    total = 2 * place.shards
    groups = []
    for low in range(total):
        if not low & (first | second):
            groups.append([low, low | second, low | first, low | first | second])
    return groups


def square_exchange(blocks, masks, place):
    groups = square_groups(place, masks)
    return lax.all_to_all(blocks, ("rep", "shard"), 0, 0, tiled=True, axis_index_groups=groups)


def square_spread(blocks, masks, place):
    first, second = masks
    rows = blocks.shape[0] // 4

    def kernel(spot, source, *outs):
        member = spot[3] * 2 + spot[1]
        for step, ref in enumerate(outs):
            start = pl.multiple_of((member ^ step) * rows, rows)
            ref[...] = source[pl.ds(start, rows), :]

    parts = kernel_call(
        kernel,
        "square_split",
        [shape_of(rows, blocks.shape[1], BF)] * 4,
        (place.spot, blocks),
        scalars=1,
    )
    masks = (0, second, first, first | second)
    return [parts[0]] + [flipped(part, mask) for part, mask in zip(parts[1:], masks[1:])]


def repeated(value):
    return jnp.concatenate([value] * 4, axis=0)


def joined(parts):
    rows = parts.shape[0] // 4
    return sum(parts[index * rows : (index + 1) * rows].astype(F32) for index in range(4))


def place_feed(spot, packs, w_in, w_out, unit, half):
    plane, second, core = spot[0], spot[1], spot[2]
    for step, near, ref, start in packs:
        column = (plane ^ step) * 2
        for turn in range(2):
            row = ((column + (second ^ turn)) * 2 + (core ^ near)) * unit
            source = slice(start + turn * unit, start + (turn + 1) * unit)
            w_in[pl.ds(pl.multiple_of(row, unit), unit), :] = ref[source, :]
        row = (column + (core ^ near)) * half
        source = slice(start + 2 * unit, start + 2 * unit + half)
        w_out[pl.ds(pl.multiple_of(row, half), half), :] = ref[source, :]


def pack_views(refs, place):
    planes, size = place.planes, place.pack_rows
    views = []
    if len(refs) == 2:
        for near, ref in enumerate(refs):
            views += [(step, near, ref, step * size) for step in range(planes)]
        return views
    for index, ref in enumerate(refs):
        views.append((index % planes, index // planes, ref, 0))
    return views


def feed(blocks, packs, bias, wide, norm_row, masks, place, waits=()):
    total, model = blocks.shape
    inner = bias.shape[1]
    unit, half = place.unit, place.half
    normed = norm_row is not None

    def kernel(spot_ref, *refs):
        blocks_ref, pack_refs = refs[0], refs[1 : 1 + len(packs)]
        bias_ref, wide_ref = refs[1 + len(packs) : 3 + len(packs)]
        outs, (w_in, w_out) = refs[3 + len(packs) : -2], refs[-2:]
        upper, active, result = outs[:3]
        place_feed(spot_ref, pack_views(pack_refs, place), w_in, w_out, unit, half)
        hidden = blocks_ref
        if normed:
            hidden = outs[3]
            scaled, unused_scale = standard(blocks_ref[...].astype(F32))
            gain = wide_ref[norm_row : norm_row + 1, :]
            shift = wide_ref[norm_row + 1 : norm_row + 2, :]
            hidden[...] = (scaled * gain + shift).astype(BF)
        before = dot_nn(hidden[...], w_in[...]) + bias_ref[...]
        upper[...] = before
        active[...] = (before * logistic(before)).astype(BF)
        result[...] = dot_nn(active[...], w_out[...]).astype(BF)

    outs = [
        shape_of(total, inner, F32),
        shape_of(total, inner, BF),
        shape_of(total, model, BF),
    ] + [shape_of(total, model, BF)] * normed
    results = kernel_call(
        kernel,
        "feed_forward",
        outs,
        (place.spot, blocks, *packs, bias, wide),
        scalars=1,
        scratch=[pltpu.VMEM((model, inner), BF), pltpu.VMEM((inner, model), BF)],
        flops=4 * total * model * inner,
        waits=waits,
    )
    upper, active, result = results[:3]
    hidden = results[3] if normed else blocks
    return square_exchange(result, masks, place), (hidden, upper, active)


def feed_back(branch, packs, grad_spot, saved, place, waits=()):
    hidden, upper, active = saved
    total, inner = upper.shape
    model = branch.shape[1]
    unit, half = place.unit, place.half

    def kernel(spot_ref, *refs):
        branch_ref, pack_refs = refs[0], refs[1 : 1 + len(packs)]
        upper_ref, slope, sums, result, w_in, w_out = refs[1 + len(packs) :]
        place_feed(spot_ref, pack_views(pack_refs, place), w_in, w_out, unit, half)
        grad = dot_nt(branch_ref[...], w_out[...]) * silu_slope(upper_ref[...])
        slope[...] = grad.astype(BF)
        sums[...] = column_sum(slope[...])
        result[...] = dot_nt(slope[...], w_in[...]).astype(BF)

    outs = [
        shape_of(total, inner, BF),
        shape_of(1, inner, F32),
        shape_of(total, model, BF),
    ]
    slope, sums, result = kernel_call(
        kernel,
        "feed_backward",
        outs,
        (place.spot, branch, *packs, upper),
        scalars=1,
        scratch=[pltpu.VMEM((model, inner), BF), pltpu.VMEM((inner, model), BF)],
        flops=4 * total * model * inner,
        waits=waits,
    )
    planes, size = place.planes, place.pack_rows

    def weights(spot_ref, hidden_ref, active_ref, branch_ref, slope_ref, kept, sent, w_in, w_out):
        w_in[...] = dot_tn(hidden_ref[...], slope_ref[...])
        w_out[...] = dot_tn(active_ref[...], branch_ref[...])
        plane, second, core = spot_ref[0], spot_ref[1], spot_ref[2]
        for near, ref in enumerate((kept, sent)):
            for step in range(planes):
                column = (plane ^ step) * 2
                start = step * size
                for turn in range(2):
                    row = ((column + (second ^ turn)) * 2 + (core ^ near)) * unit
                    target = slice(start + turn * unit, start + (turn + 1) * unit)
                    source = pl.ds(pl.multiple_of(row, unit), unit)
                    ref[target, :] = w_in[source, :].astype(BF)
                row = (column + (core ^ near)) * half
                target = slice(start + 2 * unit, start + 2 * unit + half)
                ref[target, :] = w_out[pl.ds(pl.multiple_of(row, half), half), :].astype(BF)

    kept, sent = kernel_call(
        weights,
        "feed_weights",
        [shape_of(planes * size, inner, BF)] * 2,
        (grad_spot, hidden, active, branch, slope),
        scalars=1,
        scratch=[pltpu.VMEM((model, inner), F32), pltpu.VMEM((inner, model), F32)],
        flops=4 * total * model * inner,
    )
    return result, kept, flipped(sent, 1), sums


def feed_pack(ff_in, ff_out, module, place):
    rows, hidden = ff_in.shape[2:]
    width, model = ff_out.shape[2:]
    half = width // 2
    count = 2 * place.planes * half
    if half % LANES:
        columns = ff_in[0, module].reshape(rows, place.planes, 2, 2, 2, half)
        columns = lax.dynamic_index_in_dim(columns, place.rep, 4, keepdims=False)
        own = lax.dynamic_index_in_dim(columns, place.second, 2, keepdims=False)
        other = lax.dynamic_index_in_dim(columns, 1 - place.second, 2, keepdims=False)
        own, other = (item.reshape(rows, count) for item in (own, other))
        part_out = lax.dynamic_slice_in_dim(ff_out[0, module], place.rep * half, half, 0)
        return own, flipped(other, 2), part_out

    def kernel(spot, in_ref, out_ref, own, other, part_out):
        second, rep = spot[1], spot[3]
        for turn, ref in enumerate((own, other)):
            for index in range(2 * place.planes):
                plane, core = index // 2, index % 2
                start = (((plane * 2 + (second ^ turn)) * 2 + core) * 2 + rep) * half
                source = pl.ds(pl.multiple_of(start, half), half)
                ref[:, index * half : (index + 1) * half] = in_ref[0, 0, :, source]
        part_out[...] = out_ref[0, 0, pl.ds(pl.multiple_of(rep * half, half), half), :]

    own, other, part_out = pl.pallas_call(
        kernel,
        grid=(1,),
        in_specs=[
            pl.BlockSpec(memory_space=pltpu.SMEM),
            pl.BlockSpec((1, 1, rows, hidden), lambda step: (0, module, 0, 0)),
            pl.BlockSpec((1, 1, width, model), lambda step: (0, module, 0, 0)),
        ],
        out_specs=vmem(3),
        out_shape=[
            shape_of(rows, count, BF),
            shape_of(rows, count, BF),
            shape_of(half, model, BF),
        ],
        compiler_params=pltpu.CompilerParams(vmem_limit_bytes=24 * MIB),
        name="feed_columns",
    )(place.spot, ff_in, ff_out)
    return own, flipped(other, 2), part_out


def pack_rows(parts, waits=()):
    def body(*values):
        return (jnp.concatenate(values, axis=0),)

    rows = sum(item.shape[0] for item in parts)
    out = shape_of(rows, parts[0].shape[1], BF)
    return fused(body, "pack_rows", [out], *parts, waits=waits)[0]


def plane_bits(place):
    return range(place.planes.bit_length() - 1)


def plane_gather(pack, place):
    pieces = {0: pack}
    for bit in reversed(plane_bits(place)):
        for step in sorted(pieces):
            pieces[step | 1 << bit] = flipped(pieces[step], QUAD << bit)
    near = [pieces[step] for step in range(place.planes)]
    return near + [flipped(item, 1) for item in near]


def plane_reduce(kept, swapped, place):
    size = place.pack_rows
    planes = place.planes

    def total(kept_part, swapped_part):
        both = kept_part.astype(F32) + swapped_part.astype(F32)
        return [both[step * size : (step + 1) * size] for step in range(planes)]

    outs = [shape_of(size, kept.shape[1], F32)]
    outs += [shape_of(size, kept.shape[1], BF)] * (planes - 1)
    pieces = fused(total, "feed_core_sum", outs, kept, swapped)
    pieces = {step: [piece] for step, piece in enumerate(pieces)}
    early = pieces[0][0]
    for bit in plane_bits(place):
        for step in [step for step in sorted(pieces) if step >> bit & 1]:
            values = pieces.pop(step)
            value = values[0]
            if len(values) > 1:
                value = early = plane_add(values)
            pieces[step ^ 1 << bit].append(flipped(value, QUAD << bit))
    return plane_add(pieces[0]), early


def plane_add(values):
    def body(*items):
        return (sum((item.astype(F32) for item in items[1:]), items[0].astype(F32)),)

    return fused(body, "plane_add", [shape_of(*values[0].shape, BF)], *values)[0]


def feed_grads(total, place):
    unit, half = place.unit, place.half
    arrived = flipped(total[unit : 2 * unit], 2)
    own = jnp.concatenate([total[:unit], arrived, total[2 * unit :]], axis=0)
    theirs = flipped(own, place.shards)
    is_first, is_low = place.rep == 0, place.second == 0
    first, last = jnp.where(is_first, own, theirs), jnp.where(is_first, theirs, own)
    grad_out = jnp.concatenate([first[2 * unit :], last[2 * unit :]], axis=0).astype(F32)
    sides = jnp.stack([first[: 2 * unit], last[: 2 * unit]]).reshape(2, 2, unit, -1)
    sides = jnp.where(is_low, sides, sides[:, ::-1])
    sides = sides.reshape(2, 2, unit, place.planes, 2, half).transpose(2, 3, 1, 4, 0, 5)
    return sides.reshape(unit, -1).astype(F32), grad_out


def plane_groups(place):
    return [[quad + QUAD * plane for plane in range(place.planes)] for quad in range(QUAD)]


def score_block(query, keys, table, bias, place, rows, length):
    scores = dot_nt(query, keys)
    spread = dot_nt(query, table)
    band = pltpu.roll(spread, 0, axis=1, stride=1, stride_axis=0)
    column = lax.broadcasted_iota(jnp.int32, (rows, length + 2 * rows), 1)
    bias[...] = jnp.where(column < place, spread[:, :1], spread[:, -1:])
    bias[:, pl.ds(place, 3 * rows)] = band[:, rows:]
    return scores + bias[:, rows : rows + length]


def place_rows(source, columns, target, core, rows):
    for step in range(SPAN):
        spot = pl.ds(pl.multiple_of(block_place(step, core) * rows, rows), rows)
        target[spot, :] = source[step * rows : (step + 1) * rows, columns]


def block_place(step, core):
    return step % 4 * 2 + (core ^ step // 4)


def block_step(place, core):
    return place // 2 + 4 * ((place & 1) ^ core)


def attend_kernel(*refs):
    spot, near, other, rest = refs[0], refs[1], refs[2], refs[3:]
    (weight_in, bias_in, weight_out, table, hidden, mixed, context, peaks, kept, sent) = rest[:10]
    keys, values, bias = rest[10:]
    length, width = context.shape
    rows = length // SPAN
    head = table.shape[1] // 2
    core = spot[2]
    hidden[: length // 2, :] = near[...]
    hidden[length // 2 :, :] = other[...]
    mixed[...] = (dot_nn(hidden[...], weight_in[...]) + bias_in[...]).astype(BF)
    place_rows(mixed, slice(width, 2 * width), keys, core, rows)
    place_rows(mixed, slice(2 * width, 3 * width), values, core, rows)
    lane = lax.broadcasted_iota(jnp.int32, (rows, width), 1)

    def block(index, carry):
        place = pl.multiple_of(index * rows, rows)
        own = pl.ds(pl.multiple_of(block_step(index, core) * rows, rows), rows)
        query = mixed[own, :width] * jnp.asarray(head**-0.5, BF)
        results, logs = [], []
        for which in range(2):
            mine = lane // head == which
            part = jnp.where(mine, query, jnp.zeros_like(query))
            scores = score_block(part, keys[...], table[...], bias, place, rows, length)
            top = jnp.max(scores, axis=1, keepdims=True)
            powers = jnp.exp(scores - top)
            total = jnp.sum(powers, axis=1, keepdims=True)
            weights = (powers * (1.0 / total)).astype(BF)
            results.append(dot_nn(weights, values[...]))
            logs.append(top + jnp.log(total))
        context[own, :] = jnp.where(lane < head, results[0], results[1]).astype(BF)
        peaks[own, :] = jnp.where(lane < head, logs[0], logs[1])
        return carry

    lax.fori_loop(0, SPAN, block, 0)
    result = dot_nn(context[...], weight_out[...])
    kept[...] = result[: length // 2]
    sent[...] = result[length // 2 :].astype(BF)


def attend_back_kernel(*refs):
    spot, near, other, rest = refs[0], refs[1], refs[2], refs[3:]
    (mixed, table, peaks, weight_in, weight_out) = rest[:5]
    (branch, grad_mixed, grad_table, far, kept, sent) = rest[5:11]
    keys, values, bias, grad_context, grad_keys, grad_values, slopes = rest[11:]
    length, width = grad_context.shape
    rows = length // SPAN
    head = table.shape[1] // 2
    core = spot[2]
    branch[: length // 2, :] = near[...]
    branch[length // 2 :, :] = other[...]
    grad_context[...] = dot_nt(branch[...], weight_out[...]).astype(BF)
    place_rows(mixed, slice(width, 2 * width), keys, core, rows)
    place_rows(mixed, slice(2 * width, 3 * width), values, core, rows)
    grad_keys[...] = jnp.zeros_like(grad_keys)
    grad_values[...] = jnp.zeros_like(grad_values)
    grad_table[...] = jnp.zeros_like(grad_table)
    far[...] = jnp.zeros_like(far)
    lane = lax.broadcasted_iota(jnp.int32, (rows, width), 1)
    padded = lax.broadcasted_iota(jnp.int32, (rows, length + 2 * rows), 1)
    factor = head**-0.5
    slopes[:, :rows] = jnp.zeros((rows, rows), F32)
    slopes[:, rows + length :] = jnp.zeros((rows, rows), F32)
    mirror = (
        lax.broadcasted_iota(jnp.int32, (rows, rows), 0)
        + lax.broadcasted_iota(jnp.int32, (rows, rows), 1)
        == rows - 1
    ).astype(BF)

    def block(index, carry):
        place = pl.multiple_of(index * rows, rows)
        own = pl.ds(pl.multiple_of(block_step(index, core) * rows, rows), rows)
        query = mixed[own, :width] * jnp.asarray(factor, BF)
        results = []
        for which in range(2):
            mine = lane // head == which
            part = jnp.where(mine, query, jnp.zeros_like(query))
            scores = score_block(part, keys[...], table[...], bias, place, rows, length)
            incoming = grad_context[own, :]
            incoming = jnp.where(mine, incoming, jnp.zeros_like(incoming))
            logs = peaks[own, which * head : which * head + 1]
            probs = jnp.exp(scores - logs)
            grad_probs = dot_nt(incoming, values[...])
            shared = jnp.sum(grad_probs * probs, axis=1, keepdims=True)
            grad_low = (probs * (grad_probs - shared)).astype(BF)
            grad_values[...] += dot_tn(probs.astype(BF), incoming)
            grad_keys[...] += dot_tn(grad_low, part)
            slopes[:, rows : rows + length] = grad_low.astype(F32)
            window = slopes[:, pl.ds(place, 3 * rows)]
            whole = slopes[...]
            early = jnp.sum(jnp.where(padded < place, whole, 0.0), axis=1, keepdims=True)
            late = jnp.sum(
                jnp.where(padded >= place + 3 * rows, whole, 0.0), axis=1, keepdims=True
            )
            window = jnp.concatenate(
                [jnp.zeros((rows, rows), F32), dot_nn(mirror, window.astype(BF))], axis=1
            )
            window = pltpu.roll(
                window, 3 * rows + 1, axis=1, stride=1, stride_axis=0
            ).astype(BF)
            grad_table[...] += dot_tn(window, dot_nn(mirror, part).astype(BF))
            part_wide = part.astype(F32)
            far[0:1, :] += jnp.sum(early * part_wide, axis=0, keepdims=True)
            far[1:2, :] += jnp.sum(late * part_wide, axis=0, keepdims=True)
            close = jnp.dot(
                mirror.astype(F32),
                dot_nn(window, table[...]),
                preferred_element_type=F32,
                precision=lax.Precision.HIGHEST,
            )
            results.append(
                dot_nn(grad_low, keys[...])
                + close
                + early * table[0:1, :].astype(F32)
                + late * table[4 * rows - 1 :, :].astype(F32)
            )
        grad_mixed[own, :width] = (
            jnp.where(lane < head, results[0], results[1]) * factor
        ).astype(BF)
        return carry

    lax.fori_loop(0, SPAN, block, 0)
    for step in range(SPAN):
        source = pl.ds(pl.multiple_of(block_place(step, core) * rows, rows), rows)
        target = slice(step * rows, (step + 1) * rows)
        grad_mixed[target, width : 2 * width] = grad_keys[source, :].astype(BF)
        grad_mixed[target, 2 * width :] = grad_values[source, :].astype(BF)
    result = dot_nt(grad_mixed[...], weight_in[...])
    kept[...] = result[: length // 2]
    sent[...] = result[length // 2 :].astype(BF)


def group_gather(blocks, masks, place):
    near = square_exchange(blocks, masks, place)
    return near, flipped(near, 1)


def group_reduce(kept, sent, masks, place):
    def body(kept_part, swapped_part):
        return (kept_part + swapped_part.astype(F32),)

    total = fused(body, "core_sum", [shape_of(*sent.shape, BF)], kept, flipped(sent, 1))[0]
    return square_exchange(total, masks, place)


def attend(blocks, weight_in, bias_in, weight_out, table, place):
    rows, model = blocks[0].shape[0] // 4, blocks[0].shape[1]
    length, width = SPAN * rows, weight_out.shape[0]
    outs = [
        shape_of(length, model, BF),
        shape_of(length, 3 * width, BF),
        shape_of(length, width, BF),
        shape_of(length, width, F32),
        shape_of(length // 2, model, F32),
        shape_of(length // 2, model, BF),
    ]
    hidden, mixed, context, peaks, kept, sent = kernel_call(
        attend_kernel,
        "attend_forward",
        outs,
        (place.spot, *blocks, weight_in, bias_in, weight_out, table),
        scalars=1,
        scratch=[
            pltpu.VMEM((length, width), BF),
            pltpu.VMEM((length, width), BF),
            pltpu.VMEM((rows, length + 2 * rows), F32),
        ],
        flops=48 * length * length * width,
    )
    return group_reduce(kept, sent, place.span_masks, place), (hidden, mixed, context, peaks)


def attend_back(blocks, saved, weight_in, weight_out, table, place, waits):
    hidden, mixed, context, peaks = saved
    rows, model = blocks[0].shape[0] // 4, blocks[0].shape[1]
    length, width = SPAN * rows, weight_out.shape[0]
    outs = [
        shape_of(length, model, BF),
        shape_of(length, 3 * width, BF),
        shape_of(4 * rows, width, F32),
        shape_of(8, width, F32),
        shape_of(length // 2, model, F32),
        shape_of(length // 2, model, BF),
    ]
    branch, grad_mixed, grad_table, far, kept, sent = kernel_call(
        attend_back_kernel,
        "attend_backward",
        outs,
        (place.spot, *blocks, mixed, table, peaks, weight_in, weight_out),
        scalars=1,
        scratch=[
            pltpu.VMEM((length, width), BF),
            pltpu.VMEM((length, width), BF),
            pltpu.VMEM((rows, length + 2 * rows), F32),
            pltpu.VMEM((length, width), BF),
            pltpu.VMEM((length, width), F32),
            pltpu.VMEM((length, width), F32),
            pltpu.VMEM((rows, length + 2 * rows), F32),
        ],
        flops=96 * length * length * width,
        waits=waits,
    )
    parts = group_reduce(kept, sent, place.span_masks, place)

    def weights(hidden_rows, mixed_grad, context_rows, branch_rows):
        return (
            dot_tn(hidden_rows, mixed_grad),
            dot_tn(context_rows, branch_rows),
            column_sum(mixed_grad),
        )

    grad_in, grad_out, sums = fused(
        weights,
        "attend_weights",
        [shape_of(model, 3 * width, BF), shape_of(width, model, BF), shape_of(1, 3 * width, F32)],
        hidden,
        grad_mixed,
        context,
        branch,
        flops=8 * length * model * width,
    )
    return parts, grad_in, grad_out, sums, distance_gradient(grad_table, far, rows)


def wide_table(distance, rows):
    index = jnp.clip(jnp.arange(4 * rows) - rows - LEFT, 0, LEFT + RIGHT)
    low = distance[index]
    return jnp.concatenate([low, low], axis=1)


def distance_gradient(grad_table, far, rows):
    first = rows + LEFT
    last = first + LEFT + RIGHT
    head = grad_table.shape[1] // 2
    low = jnp.sum(grad_table[: first + 1], axis=0) + far[0]
    high = jnp.sum(grad_table[last:], axis=0) + far[1]
    total = jnp.concatenate([low[None], grad_table[first + 1 : last], high[None]], axis=0)
    return total[:, :head] + total[:, head:]


def whole_heads(weight_out, head):
    return weight_out.shape[0] % head == 0


def swap_if(condition, value, axis):
    return jnp.where(condition, jnp.flip(value, axis), value)


def attend_weights(weight_in, weight_out, head, place, waits):
    rows, model = weight_in.shape[0], weight_out.shape[1]
    heads = model // head
    per_device = heads // SPAN
    width = per_device * head
    if not whole_heads(weight_out, head):
        whole = lax.all_gather(weight_in, "shard", axis=0, tiled=True)
        whole = whole.reshape(model, 3, heads, head)
        mine = lax.dynamic_slice_in_dim(whole, place.member * per_device, per_device, 2)
        out = lax.all_gather(weight_out, "shard", axis=0, tiled=True)
        out = lax.dynamic_slice_in_dim(out, place.member * width, width, 0)
        both = mine.reshape(model, 3 * width), out
        return (), lambda: (both, both)
    planes, unit = place.planes, place.unit
    groups, columns = planes // 2, 3 * width
    blocks = weight_in.reshape(rows, 3, groups, 2, 2, 2, -1)
    blocks = blocks.transpose(4, 3, 5, 0, 1, 2, 6).reshape(2, 2, 2 * rows, columns)
    own = lax.dynamic_index_in_dim(blocks, place.second, 0, keepdims=False)
    other = lax.dynamic_index_in_dim(blocks, 1 - place.second, 0, keepdims=False)
    arrived = flipped(other.reshape(4 * rows, columns), 2).reshape(own.shape)

    def arrange(spot, own_ref, arrived_ref, *outs):
        low, core = spot[0] & 1, spot[2]
        for step, out in enumerate(outs):
            for near in range(2):
                source = pl.ds(pl.multiple_of((core ^ near) * unit, unit), unit)
                for turn, ref in enumerate((own_ref, arrived_ref)):
                    start = (2 * near + turn) * unit
                    out[start : start + unit, :] = ref[low ^ step, source, :]

    near, far = kernel_call(
        arrange,
        "attend_columns",
        [shape_of(4 * unit, columns, BF)] * 2,
        (place.spot, own, arrived),
        scalars=1,
        waits=waits,
    )

    def finish():
        return attend_weights_finish(near, far, weight_out, place)

    return (near, far), finish


def attend_weights_finish(near, far, weight_out, place):
    planes, unit, columns = place.planes, place.unit, near.shape[1]
    groups, width, model = planes // 2, columns // 3, weight_out.shape[1]
    pieces = [near] + [
        flipped((near, far)[step & 1], QUAD * step) for step in range(1, planes)
    ]

    def split(*values):
        kept = jnp.concatenate([item[: 2 * unit] for item in values], axis=0)
        sent = jnp.concatenate([item[2 * unit :] for item in values], axis=0)
        return kept, sent

    kept, sent = fused(
        split, "attend_split", [shape_of(2 * planes * unit, columns, BF)] * 2, *pieces
    )
    swapped = flipped(sent, 1)
    outs = [weight_out] + [flipped(weight_out, SPAN * step) for step in range(1, groups)]

    def lay(spot, kept_ref, swapped_ref, *refs):
        plane, second, core = spot[0], spot[1], spot[2]
        w_in, w_out = refs[-2:]
        for near, ref in enumerate((kept_ref, swapped_ref)):
            for step in range(planes):
                for turn in range(2):
                    row = (((plane ^ step) * 2 + (second ^ turn)) * 2 + (core ^ near)) * unit
                    start = (2 * step + turn) * unit
                    w_in[pl.ds(pl.multiple_of(row, unit), unit), :] = ref[start : start + unit, :]
        for step, ref in enumerate(refs[:-2]):
            row = ((plane >> 1) ^ step) * unit
            w_out[pl.ds(pl.multiple_of(row, unit), unit), :] = ref[...]

    laid = kernel_call(
        lay,
        "attend_lay",
        [shape_of(model, columns, BF), shape_of(width, model, BF)],
        (place.spot, kept, swapped, *outs),
        scalars=1,
    )
    return laid, (kept, sent, *outs)


def head_row(row, place, aligned):
    if aligned:
        row = row.reshape(-1, SPAN, place.unit)
        row = lax.dynamic_index_in_dim(row, place.member, 1, keepdims=False)
        return row.reshape(1, -1)
    row = row.reshape(SPAN, -1)
    return lax.dynamic_slice_in_dim(row, place.member, 1, 0)


def head_spread(row, model, place, aligned):
    if aligned:
        whole = jnp.zeros((place.planes // 2, SPAN, place.unit), F32)
        block = row.reshape(-1, 1, place.unit)
        return lax.dynamic_update_slice_in_dim(whole, block, place.member, 1).reshape(1, model)
    whole = jnp.zeros((SPAN, model // SPAN), F32)
    return lax.dynamic_update_slice_in_dim(whole, row, place.member, 0).reshape(1, model)


def attend_weight_grads(grad_in, grad_out, head, place, aligned):
    model = grad_out.shape[1]
    heads = model // head
    per_device = heads // SPAN
    if not aligned:
        whole = jnp.zeros((model, 3, heads, head), F32)
        whole = lax.dynamic_update_slice_in_dim(
            whole,
            grad_in.astype(F32).reshape(model, 3, per_device, head),
            place.member * per_device,
            2,
        )
        whole = lax.psum_scatter(
            whole.reshape(model, 3 * model), "shard", scatter_dimension=0, tiled=True
        )
        out = jnp.zeros((model, model), F32)
        out = lax.dynamic_update_slice_in_dim(
            out, grad_out.astype(F32), place.member * per_device * head, 0
        )
        out = lax.psum_scatter(out, "shard", scatter_dimension=0, tiled=True)
        return rep_sum(whole, place), rep_sum(out, place)
    planes, unit = place.planes, place.unit
    groups, columns = planes // 2, grad_in.shape[1]

    def lay(spot, w_in, w_out, kept, sent, *outs):
        plane, second, core = spot[0], spot[1], spot[2]
        for near, ref in enumerate((kept, sent)):
            for step in range(planes):
                for turn in range(2):
                    row = (((plane ^ step) * 2 + (second ^ turn)) * 2 + (core ^ near)) * unit
                    start = (2 * step + turn) * unit
                    ref[start : start + unit, :] = w_in[pl.ds(pl.multiple_of(row, unit), unit), :]
        for step, ref in enumerate(outs):
            row = ((plane >> 1) ^ step) * unit
            ref[...] = w_out[pl.ds(pl.multiple_of(row, unit), unit), :]

    kept, sent, *outs = kernel_call(
        lay,
        "attend_unlay",
        [shape_of(2 * planes * unit, columns, BF)] * 2 + [shape_of(unit, model, BF)] * groups,
        (place.spot, grad_in, grad_out),
        scalars=1,
    )
    swapped = flipped(sent, 1)

    def by_plane(kept_part, swapped_part):
        both = jnp.concatenate([kept_part, swapped_part], axis=1)
        return [both[2 * step * unit : 2 * (step + 1) * unit] for step in range(planes)]

    pieces = fused(
        by_plane,
        "attend_planes",
        [shape_of(2 * unit, 2 * columns, BF)] * planes,
        kept,
        swapped,
    )
    arrived = [pieces[0]] + [flipped(pieces[step], QUAD * step) for step in range(1, planes)]
    outs = [outs[0]] + [flipped(outs[step], SPAN * step) for step in range(1, groups)]

    def total(*values):
        even = sum(item.astype(F32) for item in values[:planes:2])
        odd = sum(item.astype(F32) for item in values[1:planes:2])
        both = jnp.concatenate([even, odd], axis=1)
        out = sum(item.astype(F32) for item in values[planes:])
        return both[:unit], both[unit:], out

    own, other, out = fused(
        total,
        "attend_plane_sum",
        [shape_of(unit, 4 * columns, BF)] * 2 + [shape_of(unit, model, BF)],
        *arrived,
        *outs,
    )
    whole = jnp.stack([own, flipped(other, 2)])
    whole = rep_sum(whole, place).reshape(2, unit, 2, 2, 3, groups, -1)
    whole = swap_if(place.second == 1, whole, 0)
    whole = swap_if(place.plane & 1 == 1, whole, 2)
    whole = swap_if(place.core == 1, whole, 3)
    whole = whole.transpose(1, 4, 5, 2, 0, 3, 6)
    return whole.reshape(unit, 3 * model), rep_sum(out, place)


def rep_sum(value, place):
    low = value.astype(BF)
    return low.astype(F32) + flipped(low, place.shards).astype(F32)


def row(wide, index):
    return wide[index : index + 1]


def pack_columns(left, right, waits):
    def body(first, second):
        return (jnp.concatenate([first, second], axis=1),)

    out = shape_of(left.shape[0], left.shape[1] + right.shape[1], BF)
    return fused(body, "pack_columns", [out], left, right, waits=waits)[0]


def convolve_start(parts, before, wide, bias_row, weight_in, waits):
    rows, model = before.shape

    def body(*values):
        base, small, w_in = values[1:]
        current = base + joined(values[0]) + row(small, bias_row)
        unit, unused_scale = standard(current)
        hidden = (unit * row(small, 7) + row(small, 8)).astype(BF)
        doubled = dot_nn(hidden, w_in)
        return current, hidden, doubled, doubled[:, :model] * logistic(doubled[:, model:])

    return fused(
        body,
        "convolve_start",
        [
            shape_of(rows, model, F32),
            shape_of(rows, model, BF),
            shape_of(rows, 2 * model, F32),
            shape_of(rows, model, BF),
        ],
        parts,
        before,
        wide,
        weight_in,
        flops=4 * rows * model * model,
        waits=waits,
    )


def convolve_finish(glued, border, wide, taps, weight_out, before):
    rows, model = before.shape
    edge = border.shape[0]

    def kernel(
        glued_ref, border_ref, small, w_out, base,
        mixed_ref, rest_ref, current_ref, hidden_ref, padded,
    ):
        padded[:edge, :] = border_ref[...].astype(F32)
        padded[edge:, :] = glued_ref[...].astype(F32)
        first, count = taps
        for column in range(0, model, LANES):
            lanes = slice(column, column + LANES)
            total = jnp.zeros((rows, LANES), F32)
            for tap in range(count):
                start = edge - count + 1 + tap
                weight = small[first + tap : first + tap + 1, lanes]
                total += padded[start : start + rows, lanes] * weight
            mixed_ref[:, lanes] = total
        unit, unused_scale = standard(mixed_ref[...])
        upper = unit * small[9:10, :] + small[10:11, :]
        rest = (upper * logistic(upper)).astype(BF)
        rest_ref[...] = rest
        current = base[...] + dot_nn(rest, w_out[...])
        current_ref[...] = current
        unit, unused_scale = standard(current)
        hidden_ref[...] = repeated((unit * small[11:12, :] + small[12:13, :]).astype(BF))

    return kernel_call(
        kernel,
        "convolve_finish",
        [
            shape_of(rows, model, F32),
            shape_of(rows, model, BF),
            shape_of(rows, model, F32),
            shape_of(4 * rows, model, BF),
        ],
        (glued, border, wide, weight_out, before),
        scratch=[pltpu.VMEM((edge + rows, model), F32)],
        flops=2 * rows * model * model,
    )


def convolve_back_start(parts, grad, after, mixed, wide, taps, weight_out, glued, border, waits):
    rows, model = after.shape
    edge = border.shape[0]
    first, count = taps

    def kernel(
        parts_ref, grad_ref, after_ref, mixed_ref, small,
        w_out, glued_ref, border_ref,
        grad_out, branch_ref, main_ref, halo_ref, sums, padded, spread,
    ):
        incoming = joined(parts_ref[...])
        slope, sum_gain, sum_shift = norm_back(after_ref[...], small[11:12, :], incoming)
        current = grad_ref[...] + slope
        grad_out[...] = current
        branch = current.astype(BF)
        branch_ref[...] = branch
        unit, scale = standard(mixed_ref[...])
        upper = unit * small[9:10, :] + small[10:11, :]
        grad_upper = dot_nt(branch, w_out[...]) * silu_slope(upper)
        inner = grad_upper * small[9:10, :]
        mean = jnp.mean(inner, axis=-1, keepdims=True)
        shared = jnp.mean(inner * unit, axis=-1, keepdims=True)
        padded[:edge, :] = border_ref[...].astype(F32)
        padded[edge:, :] = glued_ref[...].astype(F32)
        spread[:edge, :] = jnp.zeros((edge, model), F32)
        spread[edge : edge + rows, :] = scale * (inner - mean - unit * shared)
        spread[edge + rows :, :] = jnp.zeros((edge, model), F32)
        sums[count : count + 1, :] = column_sum(grad_upper * unit)
        sums[count + 1 : count + 2, :] = column_sum(grad_upper)
        sums[count + 2 : count + 3, :] = sum_gain
        sums[count + 3 : count + 4, :] = sum_shift
        for column in range(0, model, LANES):
            lanes = slice(column, column + LANES)
            total = jnp.zeros((rows + edge, LANES), F32)
            center = spread[edge : edge + rows, lanes]
            for tap in range(count):
                start = edge - count + 1 + tap
                sums[tap : tap + 1, lanes] = jnp.sum(
                    center * padded[start : start + rows, lanes], axis=0, keepdims=True
                )
                begin = count - 1 - tap
                weight = small[first + tap : first + tap + 1, lanes]
                total += spread[begin : begin + rows + edge, lanes] * weight
            halo_ref[:, lanes] = total[:edge].astype(BF)
            main_ref[:, lanes] = total[edge:]

    return kernel_call(
        kernel,
        "convolve_back_start",
        [
            shape_of(rows, model, F32),
            shape_of(rows, model, BF),
            shape_of(rows, model, F32),
            shape_of(edge, model, BF),
            shape_of(count + 4, model, F32),
        ],
        (parts, grad, after, mixed, wide, weight_out, glued, border),
        scratch=[
            pltpu.VMEM((edge + rows, model), F32),
            pltpu.VMEM((rows + 2 * edge, model), F32),
        ],
        flops=2 * rows * model * model,
        waits=waits,
    )


def convolve_back_finish(main, incoming, doubled, weight_in, before, wide, grad):
    rows, model = before.shape
    edge = incoming.shape[0]

    def body(main_rows, late, both, w_in, base, small, grad_rows):
        glued = jnp.concatenate(
            [main_rows[: rows - edge], main_rows[rows - edge :] + late.astype(F32)], axis=0
        )
        glued = glued.astype(BF).astype(F32)
        gate = logistic(both[:, model:])
        slope = jnp.concatenate(
            [glued * gate, glued * both[:, :model] * gate * (1.0 - gate)], axis=1
        ).astype(BF)
        inner, sum_gain, sum_shift = norm_back(base, row(small, 7), dot_nt(slope, w_in))
        current = grad_rows + inner
        branch = current.astype(BF)
        sums = jnp.concatenate([sum_gain, sum_shift, column_sum(branch)], axis=0)
        return current, repeated(branch), slope, sums

    return fused(
        body,
        "convolve_back_finish",
        [
            shape_of(rows, model, F32),
            shape_of(4 * rows, model, BF),
            shape_of(rows, 2 * model, BF),
            shape_of(3, model, F32),
        ],
        main,
        incoming,
        doubled,
        weight_in,
        before,
        wide,
        grad,
        flops=4 * rows * model * model,
    )


def convolve_weight_grads(hidden, slope, rest, branch, place):
    model = hidden.shape[1]

    def body(hidden_rows, slope_rows, rest_rows, branch_rows):
        both = dot_tn(hidden_rows, slope_rows), dot_tn(rest_rows, branch_rows)
        return (jnp.concatenate(both, axis=1),)

    total = fused(
        body,
        "convolve_weights",
        [shape_of(model, 3 * model, BF)],
        hidden,
        slope,
        rest,
        branch,
        flops=6 * hidden.shape[0] * model * model,
    )[0]
    total = lax.psum_scatter(total, "shard", scatter_dimension=0, tiled=True)
    total = rep_sum(total, place)
    return total[:, : 2 * model], total[:, 2 * model :]


def feed_to_attend(parts, before, wide, waits):
    rows, model = before.shape

    def body(*values):
        base, small = values[1:]
        current = base.astype(F32) + 0.5 * (joined(values[0]) + row(small, 2))
        unit, unused_scale = standard(current)
        hidden = (unit * row(small, 3) + row(small, 4)).astype(BF)
        return current, repeated(hidden)

    outs = [shape_of(rows, model, F32), shape_of(4 * rows, model, BF)]
    return fused(body, "feed_to_attend", outs, parts, before, wide, waits=waits)


def turn_around(parts, before, wide, cotangent):
    rows, model = before.shape

    def body(*values):
        base, small, grad = values[1:]
        current = base + 0.5 * (joined(values[0]) + row(small, 13))
        unit, unused_scale = standard(current)
        slope, sum_gain, sum_shift = norm_back(current, row(small, 14), grad.astype(F32))
        branch = (0.5 * slope).astype(BF)
        sums = jnp.concatenate([column_sum(branch), sum_gain, sum_shift], axis=0)
        return unit * row(small, 14) + row(small, 15), slope, repeated(branch), sums

    outs = [
        shape_of(rows, model, BF),
        shape_of(rows, model, F32),
        shape_of(4 * rows, model, BF),
        shape_of(3, model, F32),
    ]
    return fused(body, "turn_around", outs, parts, before, wide, cotangent)


def attend_to_feed_back(parts, grad, before, wide):
    rows, model = before.shape

    def body(*values):
        grad_rows, base, small = values[1:]
        slope, sum_gain, sum_shift = norm_back(base, row(small, 3), joined(values[0]))
        current = grad_rows + slope
        branch = (0.5 * current).astype(BF)
        sums = jnp.concatenate([column_sum(branch), sum_gain, sum_shift], axis=0)
        return current, repeated(branch), sums

    outs = [shape_of(rows, model, F32), shape_of(4 * rows, model, BF), shape_of(3, model, F32)]
    return fused(body, "attend_to_feed_back", outs, parts, grad, before, wide)


def last_step(parts, grad, before, wide):
    rows, model = before.shape

    def body(*values):
        grad_rows, base, small = values[4:]
        slope, sum_gain, sum_shift = norm_back(
            base.astype(F32), row(small, 0), sum(part.astype(F32) for part in values[:4])
        )
        return grad_rows + slope, jnp.concatenate([sum_gain, sum_shift], axis=0)

    outs = [shape_of(rows, model, F32), shape_of(2, model, F32)]
    return fused(body, "last_step", outs, *parts, grad, before, wide)


def shard_gather(value, place):
    copies = jnp.broadcast_to(value[None], (place.shards, *value.shape))
    return lax.all_to_all(copies, "shard", 0, 0, tiled=True)


def shard_reduce(value, place):
    both = jnp.concatenate([value, value], axis=0)
    both = lax.all_to_all(both, ("rep", "shard"), 0, 0, tiled=True)
    return jnp.sum(both, axis=0)


def sum_everywhere(value, place, delays):
    arrived = flipped(value, 1)
    for bit in range(1, (2 * place.shards).bit_length() - 1):
        waits = delays[bit - 1 : bit]
        value = fused(
            lambda own, other: (own + other,),
            "table_sum",
            [shape_of(*value.shape, F32)],
            value,
            arrived,
            waits=waits,
        )[0]
        arrived = flipped(value, 1 << bit)
    return value + arrived


class Place:
    def __init__(self, unit, half):
        self.shards = lax.axis_size("shard")
        self.planes = self.shards // QUAD
        self.unit, self.half = unit, half
        self.pack_rows = 2 * unit + half
        self.rep = lax.axis_index("rep")
        self.shard = lax.axis_index("shard")
        self.core = self.shard % 2
        self.second = self.shard // 2 % 2
        self.plane = self.shard // QUAD
        self.member = self.shard % SPAN
        self.spot = jnp.stack([self.plane, self.second, self.core, self.rep])
        self.flat_spot = jnp.stack([jnp.zeros_like(self.plane), self.second, self.core, self.rep])
        self.feed_masks = (self.shards, 2)
        self.span_masks = (4, 2)


def along(value, by, place):
    count = place.shards
    route = [(i, i + by) for i in range(count) if 0 <= i + by < count]
    return lax.ppermute(value, "shard", route)


def shards(
    inputs,
    ff_in,
    ff_out,
    ff_bias,
    attn_in,
    attn_out,
    conv_in,
    conv_out,
    depthwise,
    distance,
    vectors,
    attn_bias,
    cotangent,
):
    rows, model = inputs.shape
    unit, half = ff_in.shape[2], ff_out.shape[2] // 2
    place = Place(unit, half)
    head = distance.shape[2]
    tap_count = depthwise.shape[1]
    edge = -(-(tap_count - 1) // 16) * 16
    aligned = whole_heads(attn_out[0], head)
    bias_rows = ff_bias.shape[2] // unit
    count = vectors.shape[1]
    taps = (count + 1, tap_count)

    small = jnp.concatenate(
        [vectors[0], attn_bias, depthwise[0], ff_bias[0].reshape(2 * bias_rows, unit)], axis=0
    )
    first_pack = pack_rows(feed_pack(ff_in, ff_out, 0, place))
    first_packs = plane_gather(first_pack, place)
    blocks = square_exchange(repeated(inputs), place.feed_masks, place)
    small = shard_gather(small, place)
    wide = small[:, : count + 1 + tap_count].transpose(1, 0, 2).reshape(-1, model).astype(F32)
    feed_bias = small[:, count + 1 + tap_count :].reshape(place.planes, 2, 2, 2, 2, half)
    feed_bias = lax.dynamic_index_in_dim(feed_bias, place.second, 1, keepdims=False)
    feed_bias = lax.dynamic_index_in_dim(feed_bias, place.rep, 3, keepdims=False)
    feed_bias = feed_bias.transpose(2, 0, 1, 3).reshape(2, 1, -1).astype(F32)
    table = wide_table(distance[0], rows)
    mix_bias = jnp.concatenate(
        [
            head_row(wide[5], place, aligned),
            jnp.zeros((1, model // SPAN), F32),
            head_row(wide[6], place, aligned),
        ],
        axis=1,
    )

    arrived = first_packs[: place.planes]
    columns, finish_mix = attend_weights(attn_in[0], attn_out[0], head, place, arrived)
    glue = pack_columns(conv_in[0], conv_out[0], arrived)
    glue = lax.all_gather(glue, "shard", axis=0, tiled=True)
    second_parts = feed_pack(ff_in, ff_out, 1, place)

    parts, saved_first = feed(
        blocks,
        first_packs,
        feed_bias[0],
        wide,
        0,
        place.feed_masks,
        place,
        (*columns, second_parts[1], table, mix_bias),
    )
    (mix_in, mix_out), ready = finish_mix()
    after_first, hidden = feed_to_attend(parts, inputs, wide, ready)
    second_packs = plane_gather(pack_rows(second_parts, waits=(after_first,)), place)
    blocks = group_gather(hidden, place.span_masks, place)
    parts, saved_attend = attend(blocks, mix_in, mix_bias, mix_out, table, place)
    glue_in, glue_out = glue[:, : 2 * model], glue[:, 2 * model :]
    after_attend, conv_hidden, doubled, glued = convolve_start(
        parts, after_first, wide, count, glue_in, second_packs[: place.planes]
    )
    border = along(glued[rows - edge :], 1, place)
    border = jnp.where(place.member == 0, jnp.zeros_like(border), border)
    mixed, rest, after_conv, hidden = convolve_finish(
        glued, border, wide, taps, glue_out, after_attend
    )
    blocks = square_exchange(hidden, place.feed_masks, place)
    parts, saved_second = feed(
        blocks, second_packs, feed_bias[1], wide, None, place.feed_masks, place
    )
    output, grad_last, branch, last_sums = turn_around(parts, after_conv, wide, cotangent)

    branch = square_exchange(branch, place.feed_masks, place)
    result, kept, swapped, second_bias = feed_back(
        branch, second_packs, place.flat_spot, saved_second, place
    )
    parts = square_exchange(result, place.feed_masks, place)
    second_total = fused(
        lambda own, other: (own.astype(F32) + other.astype(F32),),
        "feed_core_total",
        [shape_of(*kept.shape, BF)],
        kept,
        swapped,
    )[0]
    second_sum = lax.psum_scatter(
        second_total,
        "shard",
        scatter_dimension=0,
        tiled=True,
        axis_index_groups=plane_groups(place),
    )
    grad_conv, conv_branch, main, halo, conv_sums = convolve_back_start(
        parts, grad_last, after_conv, mixed, wide, taps, glue_out, glued, border, (second_total,)
    )
    incoming = along(halo, -1, place)
    incoming = jnp.where(place.member == SPAN - 1, jnp.zeros_like(incoming), incoming)
    grad_attend, branch, slope, attend_sums = convolve_back_finish(
        main, incoming, doubled, glue_in, after_attend, wide, grad_conv
    )
    conv_grads = convolve_weight_grads(conv_hidden, slope, rest, conv_branch, place)
    parts, mix_grad_in, mix_grad_out, mix_sums, grad_distance = attend_back(
        group_gather(branch, place.span_masks, place),
        saved_attend,
        mix_in,
        mix_out,
        table,
        place,
        (),
    )
    grad_first, branch, first_sums = attend_to_feed_back(parts, grad_attend, after_first, wide)
    branch = square_exchange(branch, place.feed_masks, place)
    result, kept, swapped, first_bias = feed_back(
        branch, first_packs, place.spot, saved_first, place
    )
    first_sum, first_step = plane_reduce(kept, swapped, place)
    parts = square_spread(result, place.feed_masks, place)
    grad_input, input_sums = last_step(parts, grad_first, inputs, wide)

    second_grads = feed_grads(second_sum, place)
    mix_grads = attend_weight_grads(mix_grad_in, mix_grad_out, head, place, aligned)
    first_grads = feed_grads(first_sum, place)
    width = mix_sums.shape[1] // 3
    wide_grads = jnp.concatenate(
        [
            input_sums,
            first_sums,
            head_spread(mix_sums[:, :width], model, place, aligned),
            head_spread(mix_sums[:, 2 * width :], model, place, aligned),
            attend_sums[:2],
            conv_sums[tap_count:],
            last_sums,
            attend_sums[2:],
            conv_sums[:tap_count],
        ],
        axis=0,
    )
    wide_grads = wide_grads.reshape(-1, place.shards, unit).transpose(1, 0, 2)
    bias_pair = jnp.stack([first_bias, second_bias]).reshape(2, place.planes, 2, half)
    bias_grads = lax.dynamic_update_slice(
        jnp.zeros((place.planes, 2, 2, 2, 2, half), F32),
        bias_pair.transpose(1, 2, 0, 3)[:, None, :, :, None, :],
        (0, place.second, 0, 0, place.rep, 0),
    ).reshape(place.shards, 2 * bias_rows, unit)
    small_grads = shard_reduce(jnp.concatenate([wide_grads, bias_grads], axis=1), place)
    delays = (grad_first, kept, first_step)
    grad_distance = sum_everywhere(grad_distance, place, delays)
    return (
        output,
        grad_input,
        jnp.stack([first_grads[0], second_grads[0]])[None],
        jnp.stack([first_grads[1], second_grads[1]])[None],
        small_grads[count + 1 + tap_count :].reshape(1, 2, -1),
        mix_grads[0][None],
        mix_grads[1][None],
        conv_grads[0][None],
        conv_grads[1][None],
        small_grads[count + 1 : count + 1 + tap_count][None],
        grad_distance[None],
        small_grads[:count][None],
        small_grads[count : count + 1],
    )


def solution(mesh):
    in_specs = (
        P(("rep", "shard"), None),
        P(None, None, "shard", None),
        P(None, None, "shard", None),
        P(None, None, "shard"),
        P(None, "shard", None),
        P(None, "shard", None),
        P(None, "shard", None),
        P(None, "shard", None),
        P(None, None, "shard"),
        P(),
        P(None, None, "shard"),
        P(None, "shard"),
        P(("rep", "shard"), None),
    )
    out_specs = (
        P(("rep", "shard"), None),
        P(("rep", "shard"), None),
        P(None, None, "shard", None),
        P(None, None, "shard", None),
        P(None, None, "shard"),
        P(None, "shard", None),
        P(None, "shard", None),
        P(None, "shard", None),
        P(None, "shard", None),
        P(None, None, "shard"),
        P(),
        P(None, None, "shard"),
        P(None, "shard"),
    )
    return jax.shard_map(shards, mesh=mesh, in_specs=in_specs, out_specs=out_specs, check_vma=False)
```

```python
import jax
import jax.numpy as jnp
from jax import lax
from jax.experimental import pallas as pl
from jax.experimental.pallas import tpu as pltpu
from jax.sharding import PartitionSpec as P

LEFT = 64
RIGHT = 8
SPAN = 8
QUAD = 4
EPSILON = 1e-05
BF = jnp.bfloat16
F32 = jnp.float32
MIB = 1 << 20
LANES = 128


def dot_nn(left, right):
    return jnp.dot(left, right, preferred_element_type=F32)


def dot_nt(left, right):
    return lax.dot_general(left, right, (((1,), (1,)), ((), ())), preferred_element_type=F32)


def dot_tn(left, right):
    return lax.dot_general(left, right, (((0,), (0,)), ((), ())), preferred_element_type=F32)


def column_sum(values):
    return jnp.sum(values.astype(F32), axis=0, keepdims=True)


def standard(values):
    center = values - jnp.mean(values, axis=-1, keepdims=True)
    scale = lax.rsqrt(jnp.mean(center * center, axis=-1, keepdims=True) + EPSILON)
    return center * scale, scale


def norm_back(values, gain, grad):
    unit, scale = standard(values)
    inner = grad * gain
    first = jnp.mean(inner, axis=-1, keepdims=True)
    second = jnp.mean(inner * unit, axis=-1, keepdims=True)
    return scale * (inner - first - unit * second), column_sum(grad * unit), column_sum(grad)


def logistic(values):
    return 1.0 / (1.0 + jnp.exp(-values))


def silu_slope(values):
    gate = logistic(values)
    return gate * (1.0 + values * (1.0 - gate))


def vmem(count):
    return [pl.BlockSpec(memory_space=pltpu.VMEM)] * count


def shape_of(rows, columns, dtype):
    return jax.ShapeDtypeStruct((rows, columns), dtype)


class Part:
    def __init__(self, array, block, index):
        self.array, self.block, self.index = array, block, index
        self.shape, self.dtype = block, array.dtype
        self.size = 1
        for extent in block:
            self.size *= extent


def kernel_call(body, name, outs, operands, scalars=0, scratch=(), flops=0, limit=24):
    moved = sum(item.size * item.dtype.itemsize for item in (*operands[scalars:], *outs))
    specs = [pl.BlockSpec(memory_space=pltpu.SMEM)] * scalars
    arrays = list(operands[:scalars])
    for item in operands[scalars:]:
        if isinstance(item, Part):
            specs.append(pl.BlockSpec(item.block, lambda step, index=item.index: index))
            arrays.append(item.array)
        else:
            specs += vmem(1)
            arrays.append(item)
    return pl.pallas_call(
        body,
        grid=(1,),
        in_specs=specs,
        out_specs=vmem(len(outs)),
        out_shape=list(outs),
        scratch_shapes=list(scratch),
        compiler_params=pltpu.CompilerParams(vmem_limit_bytes=limit * MIB),
        cost_estimate=pl.CostEstimate(flops=flops, bytes_accessed=moved, transcendentals=0),
        name=name,
    )(*arrays)


def fused(body, name, outs, *operands, flops=0):
    def kernel(*refs):
        results = body(*[ref[...] for ref in refs[: len(operands)]])
        for ref, value in zip(refs[len(operands) :], results):
            ref[...] = value.astype(ref.dtype)

    return kernel_call(kernel, name, outs, operands, flops=flops)


def tied(*values):
    return lax.optimization_barrier(values)


def flipped(value, mask):
    total = lax.axis_size("rep") * lax.axis_size("shard")
    return lax.ppermute(value, ("rep", "shard"), [(i, i ^ mask) for i in range(total)])


def square_gather(value, masks):
    first, second = masks
    return [
        value,
        flipped(value, first),
        flipped(value, second),
        flipped(value, first | second),
    ]


def square_reduce(parts, masks):
    first, second = masks
    own, via_first, via_second, cross = parts
    return [
        own,
        flipped(cross, first | second),
        flipped(via_first, first),
        flipped(via_second, second),
    ]


def joined(parts):
    return parts[0] + sum(part.astype(F32) for part in parts[1:])


def place_feed(spot, views, w_in, w_out, unit, half):
    plane, second, core = spot[0], spot[1], spot[2]
    for step, near, in_ref, out_ref, start in views:
        column = (plane ^ step) * 2
        for turn in range(2):
            row = ((column + (second ^ turn)) * 2 + (core ^ near)) * unit
            source = slice(turn * unit, (turn + 1) * unit)
            w_in[pl.ds(pl.multiple_of(row, unit), unit), :] = in_ref[source, :]
        row = (column + (core ^ near)) * half
        w_out[pl.ds(pl.multiple_of(row, half), half), :] = out_ref[start : start + half, :]


def pack_views(refs, place):
    planes, count = place.planes, 2 * place.planes
    if len(refs) == count:
        return [(i % planes, i // planes, ref, ref, 2 * place.unit) for i, ref in enumerate(refs)]
    return [(i % planes, i // planes, refs[i], refs[count + i], 0) for i in range(count)]


def feed(pieces, packs, bias, wide, norm_row, masks, place):
    rows, model = pieces[0].shape
    inner = bias.shape[1]
    count, total = len(pieces), len(pieces) * rows
    unit, half = place.unit, place.half

    def kernel(spot_ref, *refs):
        piece_refs, pack_refs = refs[:count], refs[count : count + len(packs)]
        bias_ref, wide_ref, hidden, upper, active = refs[count + len(packs) :][:5]
        outs = refs[count + len(packs) + 5 : -2]
        w_in, w_out = refs[-2:]
        place_feed(spot_ref, pack_views(pack_refs, place), w_in, w_out, unit, half)
        for index, ref in enumerate(piece_refs):
            block = ref[...]
            if norm_row is not None:
                scaled, unused_scale = standard(block.astype(F32))
                gain = wide_ref[norm_row : norm_row + 1, :]
                shift = wide_ref[norm_row + 1 : norm_row + 2, :]
                block = (scaled * gain + shift).astype(BF)
            hidden[index * rows : (index + 1) * rows, :] = block
        before = dot_nn(hidden[...], w_in[...]) + bias_ref[...]
        upper[...] = before
        active[...] = (before * logistic(before)).astype(BF)
        result = dot_nn(active[...], w_out[...])
        for index, ref in enumerate(outs):
            ref[...] = result[index * rows : (index + 1) * rows].astype(ref.dtype)

    outs = [
        shape_of(total, model, BF),
        shape_of(total, inner, F32),
        shape_of(total, inner, BF),
        shape_of(rows, model, F32),
    ] + [shape_of(rows, model, BF)] * (count - 1)
    results = kernel_call(
        kernel,
        "feed_forward",
        outs,
        (place.spot, *pieces, *packs, bias, wide),
        scalars=1,
        scratch=[pltpu.VMEM((model, inner), BF), pltpu.VMEM((inner, model), BF)],
        flops=4 * total * model * inner,
    )
    return square_reduce(results[3:], masks), results[:3]


def feed_back(pieces, packs, saved, place):
    hidden, upper, active = saved
    rows, model = pieces[0].shape
    total, inner = upper.shape
    count = len(pieces)
    unit, half = place.unit, place.half

    def kernel(spot_ref, *refs):
        piece_refs, pack_refs = refs[:count], refs[count : count + len(packs)]
        upper_ref, branch, slope, sums = refs[count + len(packs) :][:4]
        outs = refs[count + len(packs) + 4 : -2]
        w_in, w_out = refs[-2:]
        place_feed(spot_ref, pack_views(pack_refs, place), w_in, w_out, unit, half)
        for index, ref in enumerate(piece_refs):
            branch[index * rows : (index + 1) * rows, :] = ref[...]
        grad = dot_nt(branch[...], w_out[...]) * silu_slope(upper_ref[...])
        slope[...] = grad.astype(BF)
        sums[...] = column_sum(slope[...])
        result = dot_nt(slope[...], w_in[...])
        for index, ref in enumerate(outs):
            ref[...] = result[index * rows : (index + 1) * rows].astype(ref.dtype)

    outs = [
        shape_of(total, model, BF),
        shape_of(total, inner, BF),
        shape_of(1, inner, F32),
        shape_of(rows, model, F32),
    ] + [shape_of(rows, model, BF)] * (count - 1)
    results = kernel_call(
        kernel,
        "feed_backward",
        outs,
        (place.spot, *pieces, *packs, upper),
        scalars=1,
        scratch=[pltpu.VMEM((model, inner), BF), pltpu.VMEM((inner, model), BF)],
        flops=4 * total * model * inner,
    )
    branch, slope, sums = results[:3]
    return results[3:], branch, slope, sums


def feed_out_grads(active, pieces, place):
    rows, model = pieces[0].shape
    inner = active.shape[1]
    planes, half = place.planes, place.half
    count = len(pieces)

    def kernel(spot, active_ref, *refs):
        total, kept, sent = refs[-1], refs[count], refs[count + 1]
        branch = jnp.concatenate([ref[...] for ref in refs[:count]], axis=0)
        total[...] = dot_tn(active_ref[...], branch)
        for near, ref in enumerate((kept, sent)):
            for step in range(planes):
                row = ((spot[0] ^ step) * 2 + (spot[2] ^ near)) * half
                source = pl.ds(pl.multiple_of(row, half), half)
                ref[step * half : (step + 1) * half, :] = total[source, :].astype(BF)

    return kernel_call(
        kernel,
        "feed_out_grads",
        [shape_of(planes * half, model, BF)] * 2,
        (place.spot, active, *pieces),
        scalars=1,
        scratch=[pltpu.VMEM((inner, model), F32)],
        flops=2 * active.shape[0] * model * inner,
    )


def feed_in_grads(hidden, slope, place):
    model, inner = hidden.shape[1], slope.shape[1]
    planes, unit = place.planes, place.unit

    def kernel(spot, hidden_ref, slope_ref, kept, sent, total):
        total[...] = dot_tn(hidden_ref[...], slope_ref[...])
        for near, ref in enumerate((kept, sent)):
            for step in range(planes):
                for turn in range(2):
                    column = (spot[0] ^ step) * 2 + (spot[1] ^ turn)
                    row = (column * 2 + (spot[2] ^ near)) * unit
                    start = (2 * step + turn) * unit
                    source = pl.ds(pl.multiple_of(row, unit), unit)
                    ref[start : start + unit, :] = total[source, :].astype(BF)

    return kernel_call(
        kernel,
        "feed_in_grads",
        [shape_of(2 * planes * unit, inner, BF)] * 2,
        (place.spot, hidden, slope),
        scalars=1,
        scratch=[pltpu.VMEM((model, inner), F32)],
        flops=2 * hidden.shape[0] * model * inner,
    )


def plane_split(kept, swapped, place):
    planes = place.planes
    size = kept.shape[0] // planes

    def body(kept_part, swapped_part):
        both = kept_part.astype(F32) + swapped_part.astype(F32)
        return [both[step * size : (step + 1) * size] for step in range(planes)]

    outs = [shape_of(size, kept.shape[1], BF)] * planes
    return fused(body, "plane_split", outs, kept, swapped)


def plane_early(pieces, place):
    lists = {step: [piece] for step, piece in enumerate(pieces)}
    top = place.planes.bit_length() - 2
    for bit in range(top):
        for step in [step for step in sorted(lists) if step >> bit & 1]:
            values = lists.pop(step)
            value = values[0] if len(values) == 1 else plane_add(values)
            lists[step ^ 1 << bit].append(flipped(value, QUAD << bit))
    return lists


def plane_last(value, place):
    return flipped(value, QUAD * (place.planes // 2))


def tied_tops(value, all_lists, place):
    top = place.planes // 2
    flat = [item for lists in all_lists for item in lists[top]]
    value, *flat = tied(value, *flat)
    flat = iter(flat)
    return value, [[next(flat) for _ in lists[top]] for lists in all_lists]


def tied_tops_with(value, other, lists, place):
    top = place.planes // 2
    value, other, *flat = tied(value, other, *lists[top])
    return value, other, [flat]


def plane_total(values):
    return values[0] if len(values) == 1 else plane_add(values)


def feed_pack(ff_in, ff_out, module, place):
    rows, hidden = ff_in.shape[2:]
    width, model = ff_out.shape[2:]
    half = width // 2
    count = 2 * place.planes * half
    if half % LANES:
        columns = ff_in[0, module].reshape(rows, place.planes, 2, 2, 2, half)
        columns = lax.dynamic_index_in_dim(columns, place.rep, 4, keepdims=False)
        own = lax.dynamic_index_in_dim(columns, place.second, 2, keepdims=False)
        other = lax.dynamic_index_in_dim(columns, 1 - place.second, 2, keepdims=False)
        own, other = (item.reshape(rows, count) for item in (own, other))
        part_out = lax.dynamic_slice_in_dim(ff_out[0, module], place.rep * half, half, 0)
        return own, flipped(other, 2), part_out

    def kernel(spot, in_ref, out_ref, own, other, part_out):
        second, rep = spot[1], spot[3]
        for turn, ref in enumerate((own, other)):
            for index in range(2 * place.planes):
                plane, core = index // 2, index % 2
                start = (((plane * 2 + (second ^ turn)) * 2 + core) * 2 + rep) * half
                source = pl.ds(pl.multiple_of(start, half), half)
                ref[:, index * half : (index + 1) * half] = in_ref[0, 0, :, source]
        part_out[...] = out_ref[0, 0, pl.ds(pl.multiple_of(rep * half, half), half), :]

    own, other, part_out = pl.pallas_call(
        kernel,
        grid=(1,),
        in_specs=[
            pl.BlockSpec(memory_space=pltpu.SMEM),
            pl.BlockSpec((1, 1, rows, hidden), lambda step: (0, module, 0, 0)),
            pl.BlockSpec((1, 1, width, model), lambda step: (0, module, 0, 0)),
        ],
        out_specs=vmem(3),
        out_shape=[
            shape_of(rows, count, BF),
            shape_of(rows, count, BF),
            shape_of(half, model, BF),
        ],
        compiler_params=pltpu.CompilerParams(vmem_limit_bytes=24 * MIB),
        name="feed_columns",
    )(place.spot, ff_in, ff_out)
    return own, flipped(other, 2), part_out


def pack_rows(parts):
    def body(*values):
        return (jnp.concatenate(values, axis=0),)

    rows = sum(item.shape[0] for item in parts)
    out = shape_of(rows, parts[0].shape[1], BF)
    return fused(body, "pack_rows", [out], *parts)[0]


def plane_bits(place):
    return range(place.planes.bit_length() - 1)


def plane_start(pack, place):
    top = place.planes // 2
    return [flipped(pack, QUAD * top), flipped(pack, QUAD)] if top > 1 else [flipped(pack, QUAD)]


def plane_finish(pack, started, place):
    pieces = {0: pack, place.planes // 2: started[0]}
    if len(started) > 1:
        pieces[1] = started[1]
    for bit in reversed(plane_bits(place)):
        for step in sorted(pieces):
            if step % (2 << bit) == 0 and step | 1 << bit not in pieces:
                pieces[step | 1 << bit] = flipped(pieces[step], QUAD << bit)
    return [pieces[step] for step in range(place.planes)]


def with_core(near):
    return [*near, *(flipped(item, 1) for item in near)]


def plane_add(values):
    def body(*items):
        return (sum((item.astype(F32) for item in items[1:]), items[0].astype(F32)),)

    return fused(body, "plane_add", [shape_of(*values[0].shape, BF)], *values)[0]


def feed_final(modules, place):
    unit, half = place.unit, place.half
    inner = modules[0][0][0].shape[1]
    model = modules[0][2][0].shape[1]
    planes = place.planes
    if half % LANES:
        grads_in, grads_out = [], []
        for in_own, in_other, out in modules:
            sides = jnp.stack([jnp.stack(in_own), jnp.stack(in_other)], axis=1)
            sides = jnp.where(place.second == 0, sides, sides[:, ::-1])
            sides = jnp.where(place.rep == 0, sides, sides[::-1])
            sides = sides.reshape(2, 2, unit, planes, 2, half).transpose(2, 3, 1, 4, 0, 5)
            grads_in.append(sides.reshape(unit, -1).astype(F32))
            both = jnp.stack(out)
            both = jnp.where(place.rep == 0, both, both[::-1])
            grads_out.append(both.reshape(2 * half, model).astype(F32))
        return jnp.stack(grads_in)[None], jnp.stack(grads_out)[None]

    def kernel(spot, *refs):
        grad_in, grad_out = refs[-2:]
        second, rep = spot[1], spot[3]
        for module in range(2):
            own = refs[6 * module : 6 * module + 6]
            for turn in range(2):
                for side in range(2):
                    piece = own[2 * turn + side][...].astype(F32)
                    for index in range(2 * planes):
                        plane, core = index // 2, index % 2
                        start = (((plane * 2 + (second ^ turn)) * 2 + core) * 2 + (rep ^ side)) * half
                        target = pl.ds(pl.multiple_of(start, half), half)
                        grad_in[0, module, :, target] = piece[:, index * half : (index + 1) * half]
            for side in range(2):
                target = pl.ds(pl.multiple_of((rep ^ side) * half, half), half)
                grad_out[0, module, target, :] = own[4 + side][...].astype(F32)

    operands = [item for module in modules for pair in module for item in pair]
    outs = [
        jax.ShapeDtypeStruct((1, 2, unit, 4 * inner), F32),
        jax.ShapeDtypeStruct((1, 2, 2 * half, model), F32),
    ]
    return kernel_call(kernel, "feed_final", outs, (place.spot, *operands), scalars=1)


def feed_arrive(sums, place):
    unit = place.unit
    own = sums[0][:unit]
    other = flipped(sums[0][unit:], 2)
    items = [own, other, *sums[1:]]
    return [(item, flipped(item, place.shards)) for item in items]


def score_block(query, keys, table, bias, place, rows, length):
    scores = dot_nt(query, keys)
    spread = dot_nt(query, table)
    band = pltpu.roll(spread, 0, axis=1, stride=1, stride_axis=0)
    column = lax.broadcasted_iota(jnp.int32, (rows, length + 2 * rows), 1)
    bias[...] = jnp.where(column < place, spread[:, :1], spread[:, -1:])
    bias[:, pl.ds(place, 3 * rows)] = band[:, rows:]
    return scores + bias[:, rows : rows + length]


def place_rows(source, columns, target, position, rows):
    for step in range(SPAN):
        spot = pl.ds(pl.multiple_of((position ^ step) * rows, rows), rows)
        target[spot, :] = source[step * rows : (step + 1) * rows, columns]


def split_rows(value, kept, sent, rows):
    for index, step in enumerate((0, 4, 2, 6)):
        target = slice(index * rows, (index + 1) * rows)
        kept[target, :] = value[step * rows : (step + 1) * rows]
        sent[target, :] = value[(step + 1) * rows : (step + 2) * rows].astype(BF)


def join_pieces(refs, target, rows):
    for step, ref in enumerate(refs):
        target[step * rows : (step + 1) * rows, :] = ref[...]


def attend_kernel(*refs):
    spot, pieces, rest = refs[0], refs[1 : 1 + SPAN], refs[1 + SPAN :]
    (weight_in, bias_in, weight_out, table, hidden, mixed, context, peaks, kept, sent) = rest[:10]
    keys, values, bias = rest[10:]
    length, width = context.shape
    rows = length // SPAN
    head = table.shape[1] // 2
    position = spot[0]
    join_pieces(pieces, hidden, rows)
    mixed[...] = (dot_nn(hidden[...], weight_in[...]) + bias_in[...]).astype(BF)
    place_rows(mixed, slice(width, 2 * width), keys, position, rows)
    place_rows(mixed, slice(2 * width, 3 * width), values, position, rows)
    lane = lax.broadcasted_iota(jnp.int32, (rows, width), 1)

    def block(index, carry):
        place = pl.multiple_of(index * rows, rows)
        own = pl.ds(pl.multiple_of((position ^ index) * rows, rows), rows)
        query = mixed[own, :width] * jnp.asarray(head**-0.5, BF)
        results, logs = [], []
        for which in range(2):
            mine = lane // head == which
            part = jnp.where(mine, query, jnp.zeros_like(query))
            scores = score_block(part, keys[...], table[...], bias, place, rows, length)
            top = jnp.max(scores, axis=1, keepdims=True)
            powers = jnp.exp(scores - top)
            total = jnp.sum(powers, axis=1, keepdims=True)
            weights = (powers * (1.0 / total)).astype(BF)
            results.append(dot_nn(weights, values[...]))
            logs.append(top + jnp.log(total))
        context[own, :] = jnp.where(lane < head, results[0], results[1]).astype(BF)
        peaks[own, :] = jnp.where(lane < head, logs[0], logs[1])
        return carry

    lax.fori_loop(0, SPAN, block, 0)
    split_rows(dot_nn(context[...], weight_out[...]), kept, sent, rows)


def attend_back_kernel(*refs):
    spot, pieces, rest = refs[0], refs[1 : 1 + SPAN], refs[1 + SPAN :]
    (mixed, table, peaks, weight_in, weight_out) = rest[:5]
    (branch, grad_mixed, grad_table, far, kept, sent) = rest[5:11]
    keys, values, bias, grad_context, grad_keys, grad_values, slopes = rest[11:]
    length, width = grad_context.shape
    rows = length // SPAN
    head = table.shape[1] // 2
    position = spot[0]
    join_pieces(pieces, branch, rows)
    grad_context[...] = dot_nt(branch[...], weight_out[...]).astype(BF)
    place_rows(mixed, slice(width, 2 * width), keys, position, rows)
    place_rows(mixed, slice(2 * width, 3 * width), values, position, rows)
    grad_keys[...] = jnp.zeros_like(grad_keys)
    grad_values[...] = jnp.zeros_like(grad_values)
    grad_table[...] = jnp.zeros_like(grad_table)
    far[...] = jnp.zeros_like(far)
    lane = lax.broadcasted_iota(jnp.int32, (rows, width), 1)
    padded = lax.broadcasted_iota(jnp.int32, (rows, length + 2 * rows), 1)
    factor = head**-0.5
    slopes[:, :rows] = jnp.zeros((rows, rows), F32)
    slopes[:, rows + length :] = jnp.zeros((rows, rows), F32)
    mirror = (
        lax.broadcasted_iota(jnp.int32, (rows, rows), 0)
        + lax.broadcasted_iota(jnp.int32, (rows, rows), 1)
        == rows - 1
    ).astype(BF)

    def block(index, carry):
        place = pl.multiple_of(index * rows, rows)
        own = pl.ds(pl.multiple_of((position ^ index) * rows, rows), rows)
        query = mixed[own, :width] * jnp.asarray(factor, BF)
        results = []
        for which in range(2):
            mine = lane // head == which
            part = jnp.where(mine, query, jnp.zeros_like(query))
            scores = score_block(part, keys[...], table[...], bias, place, rows, length)
            incoming = grad_context[own, :]
            incoming = jnp.where(mine, incoming, jnp.zeros_like(incoming))
            logs = peaks[own, which * head : which * head + 1]
            probs = jnp.exp(scores - logs)
            grad_probs = dot_nt(incoming, values[...])
            shared = jnp.sum(grad_probs * probs, axis=1, keepdims=True)
            grad_low = (probs * (grad_probs - shared)).astype(BF)
            grad_values[...] += dot_tn(probs.astype(BF), incoming)
            grad_keys[...] += dot_tn(grad_low, part)
            slopes[:, rows : rows + length] = grad_low.astype(F32)
            window = slopes[:, pl.ds(place, 3 * rows)]
            whole = slopes[...]
            early = jnp.sum(jnp.where(padded < place, whole, 0.0), axis=1, keepdims=True)
            late = jnp.sum(
                jnp.where(padded >= place + 3 * rows, whole, 0.0), axis=1, keepdims=True
            )
            window = jnp.concatenate(
                [jnp.zeros((rows, rows), F32), dot_nn(mirror, window.astype(BF))], axis=1
            )
            window = pltpu.roll(
                window, 3 * rows + 1, axis=1, stride=1, stride_axis=0
            ).astype(BF)
            grad_table[...] += dot_tn(window, dot_nn(mirror, part).astype(BF))
            part_wide = part.astype(F32)
            far[0:1, :] += jnp.sum(early * part_wide, axis=0, keepdims=True)
            far[1:2, :] += jnp.sum(late * part_wide, axis=0, keepdims=True)
            close = jnp.dot(
                mirror.astype(F32),
                dot_nn(window, table[...]),
                preferred_element_type=F32,
                precision=lax.Precision.HIGHEST,
            )
            results.append(
                dot_nn(grad_low, keys[...])
                + close
                + early * table[0:1, :].astype(F32)
                + late * table[4 * rows - 1 :, :].astype(F32)
            )
        grad_mixed[own, :width] = (
            jnp.where(lane < head, results[0], results[1]) * factor
        ).astype(BF)
        return carry

    lax.fori_loop(0, SPAN, block, 0)
    for step in range(SPAN):
        source = pl.ds(pl.multiple_of((position ^ step) * rows, rows), rows)
        target = slice(step * rows, (step + 1) * rows)
        grad_mixed[target, width : 2 * width] = grad_keys[source, :].astype(BF)
        grad_mixed[target, 2 * width :] = grad_values[source, :].astype(BF)
    split_rows(dot_nt(grad_mixed[...], weight_in[...]), kept, sent, rows)


def group_gather(value, masks):
    near = square_gather(value, masks)
    return near, [flipped(item, 1) for item in near]


def group_reduce(kept, sent, masks):
    swapped = flipped(sent, 1)
    rows = kept.shape[0] // 4

    def body(kept_part, swapped_part):
        total = kept_part + swapped_part.astype(F32)
        return [total[index * rows : (index + 1) * rows] for index in range(4)]

    outs = [shape_of(rows, kept.shape[1], dtype) for dtype in (F32, BF, BF, BF)]
    return square_reduce(fused(body, "core_sum", outs, kept, swapped), masks)


def in_steps(blocks):
    near, far = blocks
    return [near[0], far[0], near[2], far[2], near[1], far[1], near[3], far[3]]


def attend(blocks, weight_in, bias_in, weight_out, table, place):
    pieces = in_steps(blocks)
    rows, model = pieces[0].shape
    length, width = SPAN * rows, weight_out.shape[0]
    outs = [
        shape_of(length, model, BF),
        shape_of(length, 3 * width, BF),
        shape_of(length, width, BF),
        shape_of(length, width, F32),
        shape_of(length // 2, model, F32),
        shape_of(length // 2, model, BF),
    ]
    hidden, mixed, context, peaks, kept, sent = kernel_call(
        attend_kernel,
        "attend_forward",
        outs,
        (place.span_spot, *pieces, weight_in, bias_in, weight_out, table),
        scalars=1,
        scratch=[
            pltpu.VMEM((length, width), BF),
            pltpu.VMEM((length, width), BF),
            pltpu.VMEM((rows, length + 2 * rows), F32),
        ],
        flops=48 * length * length * width,
    )
    return (hidden, mixed, context, peaks), kept, sent


def attend_back(blocks, saved, weight_in, weight_out, table, place):
    hidden, mixed, context, peaks = saved
    pieces = in_steps(blocks)
    rows, model = pieces[0].shape
    length, width = SPAN * rows, weight_out.shape[0]
    outs = [
        shape_of(length, model, BF),
        shape_of(length, 3 * width, BF),
        shape_of(4 * rows, width, F32),
        shape_of(8, width, F32),
        shape_of(length // 2, model, F32),
        shape_of(length // 2, model, BF),
    ]
    branch, grad_mixed, grad_table, far, kept, sent = kernel_call(
        attend_back_kernel,
        "attend_backward",
        outs,
        (place.span_spot, *pieces, mixed, table, peaks, weight_in, weight_out),
        scalars=1,
        scratch=[
            pltpu.VMEM((length, width), BF),
            pltpu.VMEM((length, width), BF),
            pltpu.VMEM((rows, length + 2 * rows), F32),
            pltpu.VMEM((length, width), BF),
            pltpu.VMEM((length, width), F32),
            pltpu.VMEM((length, width), F32),
            pltpu.VMEM((rows, length + 2 * rows), F32),
        ],
        flops=96 * length * length * width,
    )
    return grad_mixed, kept, sent, branch, grad_table, far


def attend_grads(saved, grad_mixed, branch, place):
    hidden, unused_mixed, context, unused_peaks = saved
    length, model = hidden.shape
    width = context.shape[1]

    def weights(hidden_rows, mixed_grad, context_rows, branch_rows):
        return (
            dot_tn(hidden_rows, mixed_grad),
            dot_tn(context_rows, branch_rows),
            column_sum(mixed_grad),
        )

    return fused(
        weights,
        "attend_weights",
        [shape_of(model, 3 * width, BF), shape_of(width, model, BF), shape_of(1, 3 * width, F32)],
        hidden,
        grad_mixed,
        context,
        branch,
        flops=8 * length * model * width,
    )


def wide_table(distance, rows):
    index = jnp.clip(jnp.arange(4 * rows) - rows - LEFT, 0, LEFT + RIGHT)
    low = distance[index]
    return jnp.concatenate([low, low], axis=1)


def distance_gradient(grad_table, far, rows):
    first = rows + LEFT
    last = first + LEFT + RIGHT
    head = grad_table.shape[1] // 2
    low = jnp.sum(grad_table[: first + 1], axis=0) + far[0]
    high = jnp.sum(grad_table[last:], axis=0) + far[1]
    total = jnp.concatenate([low[None], grad_table[first + 1 : last], high[None]], axis=0)
    return total[:, :head] + total[:, head:]


def whole_heads(head, place):
    return place.unit == head and 2 * place.unit == LANES and place.planes == 4


def attend_weights_whole(weight_in, weight_out, head, place):
    model = weight_out.shape[1]
    heads = model // head
    per_device = heads // SPAN
    width = per_device * head
    whole = lax.all_gather(weight_in, "shard", axis=0, tiled=True)
    whole = whole.reshape(model, 3, heads, head)
    mine = lax.dynamic_slice_in_dim(whole, place.member * per_device, per_device, 2)
    out = lax.all_gather(weight_out, "shard", axis=0, tiled=True)
    out = lax.dynamic_slice_in_dim(out, place.member * width, width, 0)
    return mine.reshape(model, 3 * width), out


def attend_columns(weight_in, place):
    rows = weight_in.shape[0]
    planes, unit = place.planes, place.unit
    groups, columns = planes // 2, 3 * weight_in.shape[1] // 3 // SPAN
    if 2 * unit == LANES:

        def pick(spot, whole, *outs):
            lane = lax.broadcasted_iota(jnp.int32, (rows, LANES), 1)
            for turn, out in enumerate(outs):
                for low in range(2):
                    for part in range(3):
                        pair = []
                        for group in range(groups):
                            start = ((part * groups + group) * 2 + low) * 2 + (spot[1] ^ turn)
                            source = pl.ds(pl.multiple_of(start * LANES, LANES), LANES)
                            pair.append(whole[:, source].astype(F32))
                        rolled = [pltpu.roll(item, unit, axis=1) for item in pair]
                        cores = (
                            jnp.where(lane < unit, pair[0], rolled[1]),
                            jnp.where(lane < unit, rolled[0], pair[1]),
                        )
                        for core, value in enumerate(cores):
                            out[
                                low,
                                core * rows : (core + 1) * rows,
                                part * LANES : (part + 1) * LANES,
                            ] = value.astype(BF)

        own, other = kernel_call(
            pick,
            "attend_pick",
            [jax.ShapeDtypeStruct((2, 2 * rows, columns), BF)] * 2,
            (place.spot, weight_in),
            scalars=1,
        )
    else:
        blocks = weight_in.reshape(rows, 3, groups, 2, 2, 2, -1)
        blocks = blocks.transpose(4, 3, 5, 0, 1, 2, 6).reshape(2, 2, 2 * rows, columns)
        own = lax.dynamic_index_in_dim(blocks, place.second, 0, keepdims=False)
        other = lax.dynamic_index_in_dim(blocks, 1 - place.second, 0, keepdims=False)
    return own, flipped(other.reshape(4 * rows, columns), 2).reshape(own.shape)


def attend_arrange(own, arrived, place):
    unit, columns = place.unit, own.shape[2]

    def arrange(spot, own_ref, arrived_ref, *outs):
        low, core = spot[0] & 1, spot[2]
        for step, out in enumerate(outs):
            for near in range(2):
                source = pl.ds(pl.multiple_of((core ^ near) * unit, unit), unit)
                for turn, ref in enumerate((own_ref, arrived_ref)):
                    start = (2 * near + turn) * unit
                    out[start : start + unit, :] = ref[low ^ step, source, :]

    near, far = kernel_call(
        arrange,
        "attend_columns",
        [shape_of(4 * unit, columns, BF)] * 2,
        (place.spot, own, arrived),
        scalars=1,
    )
    return near, far


def attend_weights_travel(near, far, weight_out, place):
    size = near.shape[0]
    both = jnp.concatenate([near, far], axis=0)
    pieces = {0: near, 1: flipped(far, QUAD)}
    for step in range(2, place.planes, 2):
        arrived = flipped(both, QUAD * step)
        pieces[step] = arrived[:size]
        pieces[step + 1] = flipped(arrived[size:], QUAD)
    steps = range(1, place.planes // 2)
    outs = [weight_out] + [flipped(weight_out, SPAN * step) for step in steps]
    return [pieces[step] for step in range(place.planes)], outs


def attend_weights_lay(pieces, outs, place):
    planes, unit, columns = place.planes, place.unit, pieces[0].shape[1]
    width, model = columns // 3, outs[0].shape[1]

    def split(*values):
        kept = jnp.concatenate([item[: 2 * unit] for item in values], axis=0)
        sent = jnp.concatenate([item[2 * unit :] for item in values], axis=0)
        return kept, sent

    kept, sent = fused(
        split, "attend_split", [shape_of(2 * planes * unit, columns, BF)] * 2, *pieces
    )
    swapped = flipped(sent, 1)

    def lay(spot, kept_ref, swapped_ref, *refs):
        plane, second, core = spot[0], spot[1], spot[2]
        w_in, w_out = refs[-2:]
        for near, ref in enumerate((kept_ref, swapped_ref)):
            for step in range(planes):
                for turn in range(2):
                    row = (((plane ^ step) * 2 + (second ^ turn)) * 2 + (core ^ near)) * unit
                    start = (2 * step + turn) * unit
                    w_in[pl.ds(pl.multiple_of(row, unit), unit), :] = ref[start : start + unit, :]
        for step, ref in enumerate(refs[:-2]):
            row = ((plane >> 1) ^ step) * unit
            w_out[pl.ds(pl.multiple_of(row, unit), unit), :] = ref[...]

    return kernel_call(
        lay,
        "attend_lay",
        [shape_of(model, columns, BF), shape_of(width, model, BF)],
        (place.spot, kept, swapped, *outs),
        scalars=1,
    )


def attend_grads_whole(grad_in, grad_out, head, place):
    model = grad_out.shape[1]
    heads = model // head
    per_device = heads // SPAN
    whole = jnp.zeros((model, 3, heads, head), F32)
    whole = lax.dynamic_update_slice_in_dim(
        whole,
        grad_in.astype(F32).reshape(model, 3, per_device, head),
        place.member * per_device,
        2,
    )
    whole = lax.psum_scatter(
        whole.reshape(model, 3 * model), "shard", scatter_dimension=0, tiled=True
    )
    out = jnp.zeros((model, model), F32)
    out = lax.dynamic_update_slice_in_dim(
        out, grad_out.astype(F32), place.member * per_device * head, 0
    )
    out = lax.psum_scatter(out, "shard", scatter_dimension=0, tiled=True)
    return rep_sum(whole, place), rep_sum(out, place)


def attend_grads_lay(grad_in, grad_out, place):
    model = grad_out.shape[1]
    planes, unit = place.planes, place.unit
    groups, columns = planes // 2, grad_in.shape[1]

    def lay(spot, w_in, w_out, kept, sent, *outs):
        plane, second, core = spot[0], spot[1], spot[2]
        for near, ref in enumerate((kept, sent)):
            for step in range(planes):
                for turn in range(2):
                    row = (((plane ^ step) * 2 + (second ^ turn)) * 2 + (core ^ near)) * unit
                    start = (2 * step + turn) * unit
                    ref[start : start + unit, :] = w_in[pl.ds(pl.multiple_of(row, unit), unit), :]
        for step, ref in enumerate(outs):
            row = ((plane >> 1) ^ step) * unit
            ref[...] = w_out[pl.ds(pl.multiple_of(row, unit), unit), :]

    return kernel_call(
        lay,
        "attend_unlay",
        [shape_of(2 * planes * unit, columns, BF)] * 2 + [shape_of(unit, model, BF)] * groups,
        (place.spot, grad_in, grad_out),
        scalars=1,
    )


def attend_grads_planes(kept, swapped, place):
    planes, unit, columns = place.planes, place.unit, kept.shape[1]

    def by_plane(kept_part, swapped_part):
        both = jnp.concatenate([kept_part, swapped_part], axis=1)
        pieces = [both[2 * step * unit : 2 * (step + 1) * unit] for step in range(planes)]
        return pieces[0], jnp.concatenate([pieces[1], pieces[3]], axis=0), pieces[2]

    size = 2 * unit
    return fused(
        by_plane,
        "attend_planes",
        [shape_of(count * size, 2 * columns, BF) for count in (1, 2, 1)],
        kept,
        swapped,
    )


def attend_grads_relay(own, odd, even, *outs):
    size = own.shape[0]
    arrived = flipped(jnp.concatenate([even, odd[size:]], axis=0), 2 * QUAD)
    outs = [outs[0]] + [flipped(outs[step], SPAN * step) for step in range(1, len(outs))]
    return [own, odd, arrived, *outs]


def attend_grads_sum(travelled, place):
    unit = place.unit
    size = 2 * unit
    columns, model = travelled[0].shape[1] // 2, travelled[3].shape[1]

    def total(own, near, far, *rest):
        even = own.astype(F32) + far[:size].astype(F32)
        odd = near[:size].astype(F32) + far[size:].astype(F32)
        both = jnp.concatenate([even, odd], axis=1)
        out = sum(item.astype(F32) for item in rest)
        return both[:unit], both[unit:], out

    own, other, out = fused(
        total,
        "attend_plane_sum",
        [shape_of(unit, 4 * columns, BF)] * 2 + [shape_of(unit, model, BF)],
        *travelled,
    )
    return own, other, out


def attend_grads_arrive(sums, place):
    own, other, out = sums
    arrived = flipped(other, 2)
    mine = own, arrived, out
    return mine, tuple(flipped(item, place.shards) for item in mine)


def attend_grads_final(mine, theirs, place):
    unit = place.unit
    model = mine[2].shape[1]
    columns = mine[0].shape[1] // 4
    groups = place.planes // 2

    def kernel(spot, *refs):
        values = [refs[i][...].astype(F32) + refs[3 + i][...].astype(F32) for i in range(3)]
        grad_in, grad_out = refs[6:]
        grad_out[0] = values[2]
        lane = lax.broadcasted_iota(jnp.int32, (unit, LANES), 1)
        low_bit, core = spot[0] & 1, spot[2]
        for turn in range(2):
            for low in range(2):
                for part in range(3):
                    blocks = []
                    for near in range(2):
                        start = (2 * low + near) * columns + part * LANES
                        blocks.append(values[turn][:, start : start + LANES])
                    first = jnp.where(core == 0, blocks[0], blocks[1])
                    last = jnp.where(core == 0, blocks[1], blocks[0])
                    pairs = (
                        jnp.where(lane < unit, first, pltpu.roll(last, unit, axis=1)),
                        jnp.where(lane < unit, pltpu.roll(first, unit, axis=1), last),
                    )
                    for group, value in enumerate(pairs):
                        start = ((part * groups + group) * 2 + (low_bit ^ low)) * 2
                        start = (start + (spot[1] ^ turn)) * LANES
                        grad_in[0, :, pl.ds(pl.multiple_of(start, LANES), LANES)] = value

    outs = [
        jax.ShapeDtypeStruct((1, unit, 3 * model), F32),
        jax.ShapeDtypeStruct((1, unit, model), F32),
    ]
    return kernel_call(kernel, "attend_final", outs, (place.spot, *mine, *theirs), scalars=1)


def rep_sum(value, place):
    low = value.astype(BF)
    return low.astype(F32) + flipped(low, place.shards).astype(F32)


def row(wide, index):
    return wide[index : index + 1]


def conv_pick(weight_in, weight_out, place):
    rows, model = weight_out.shape
    half = rows // 2
    whole = half % 16 != 0
    size = rows if whole else half

    def pick(spot, left, right, out):
        source = pl.ds(pl.multiple_of(spot[3] * half, half), half)
        if whole:
            source = slice(0, rows)
        out[:size, :] = left[source, :model]
        out[size : 2 * size, :] = left[source, model:]
        out[2 * size :, :] = right[source, :]

    outs = [shape_of(3 * size, model, BF)]
    operands = (place.spot, weight_in, weight_out)
    return kernel_call(pick, "conv_pick", outs, operands, scalars=1)[0]


def core_groups(place):
    return [list(range(core, place.shards, 2)) for core in range(2)]


def conv_halved(piece, place):
    return 6 * place.unit == 4 * piece.shape[0]


def conv_planes(piece, place):
    started = plane_start(piece, place)
    return plane_finish(piece, started, place)


def conv_square(own, masks):
    first, second = masks
    half = own.shape[0] // 2
    return own, flipped(own, first), flipped(own, second), half


def conv_relay(own, via_first, via_second, masks):
    first, second = masks
    half = own.shape[0] // 2
    low, high = flipped(via_first[:half], second), flipped(via_second[half:], first)
    near = [own, via_first, via_second, low, high]
    return [*near, *(flipped(item, 1) for item in near)]


def lay_conv(spot, refs, target, unit, first):
    model = target.shape[0]
    plane, second, core, rep = spot[0], spot[1], spot[2], spot[3]
    size = unit if len(refs) == 1 else unit // 2
    columns = (0, 1) if first else (2,)
    for index, ref in enumerate(refs):
        for local in range(ref.shape[0] // (3 * size)):
            start = local * size
            if len(refs) > 1:
                kind, near = index % 5, index // 5
                turn, side = ((0, 0), (0, 1), (1, 0), (1, 1), (1, 1))[kind]
                step = local + (ref.shape[0] // (3 * size) if kind == 4 else 0)
                start = (((plane ^ step) * 2 + (second ^ turn)) * 2 + (core ^ near)) * 2
                start = pl.multiple_of((start + (rep ^ side)) * size, size)
            for place_of, column in enumerate(columns):
                source = (3 * local + column) * size
                target[pl.ds(start, size), place_of * model : (place_of + 1) * model] = ref[
                    source : source + size, :
                ]


def convolve_start(parts, before, wide, bias_row, weights, place):
    rows, model = before.shape
    count = len(weights)

    def kernel(spot, *refs):
        part_refs, (base, small), weight_refs = refs[:4], refs[4:6], refs[6 : 6 + count]
        current_ref, hidden_ref, doubled_ref, glued_ref, w_in = refs[6 + count :]
        lay_conv(spot, weight_refs, w_in, place.unit, True)
        parts_now = [ref[...] for ref in part_refs]
        current = base[...] + joined(parts_now) + small[bias_row : bias_row + 1, :]
        current_ref[...] = current
        unit, unused_scale = standard(current)
        hidden = (unit * small[7:8, :] + small[8:9, :]).astype(BF)
        hidden_ref[...] = hidden
        doubled = dot_nn(hidden, w_in[...])
        doubled_ref[...] = doubled
        glued_ref[...] = (doubled[:, :model] * logistic(doubled[:, model:])).astype(BF)

    return kernel_call(
        kernel,
        "convolve_start",
        [
            shape_of(rows, model, F32),
            shape_of(rows, model, BF),
            shape_of(rows, 2 * model, F32),
            shape_of(rows, model, BF),
        ],
        (place.spot, *parts, before, wide, *weights),
        scalars=1,
        scratch=[pltpu.VMEM((model, 2 * model), BF)],
        limit=56,
        flops=4 * rows * model * model,
    )


def convolve_finish(glued, border, wide, taps, weights, before, place):
    rows, model = before.shape
    edge = border.shape[0]

    def kernel(spot, glued_ref, border_ref, small, base, *refs):
        weight_refs = refs[: len(weights)]
        mixed_ref, rest_ref, current_ref, hidden_ref, padded, w_out = refs[len(weights) :]
        lay_conv(spot, weight_refs, w_out, place.unit, False)
        padded[:edge, :] = border_ref[...].astype(F32)
        padded[edge:, :] = glued_ref[...].astype(F32)
        first, count = taps
        for column in range(0, model, LANES):
            lanes = slice(column, column + LANES)
            total = jnp.zeros((rows, LANES), F32)
            for tap in range(count):
                start = edge - count + 1 + tap
                weight = small[first + tap : first + tap + 1, lanes]
                total += padded[start : start + rows, lanes] * weight
            mixed_ref[:, lanes] = total
        unit, unused_scale = standard(mixed_ref[...])
        upper = unit * small[9:10, :] + small[10:11, :]
        rest = (upper * logistic(upper)).astype(BF)
        rest_ref[...] = rest
        current = base[...] + dot_nn(rest, w_out[...])
        current_ref[...] = current
        unit, unused_scale = standard(current)
        hidden_ref[...] = (unit * small[11:12, :] + small[12:13, :]).astype(BF)

    return kernel_call(
        kernel,
        "convolve_finish",
        [shape_of(rows, model, dtype) for dtype in (F32, BF, F32, BF)],
        (place.spot, glued, border, wide, before, *weights),
        scalars=1,
        scratch=[pltpu.VMEM((edge + rows, model), F32), pltpu.VMEM((model, model), BF)],
        limit=56,
        flops=2 * rows * model * model,
    )


def convolve_back_start(parts, grad, after, mixed, wide, taps, weights, glued, border, place):
    rows, model = after.shape
    edge = border.shape[0]
    first, count = taps

    def kernel(
        spot, own, part_one, part_two, part_three, grad_ref, after_ref, mixed_ref, small,
        glued_ref, border_ref, *refs,
    ):
        weight_refs = refs[: len(weights)]
        grad_out, branch_ref, main_ref, halo_ref, sums = refs[len(weights) : -3]
        padded, spread, w_out = refs[-3:]
        lay_conv(spot, weight_refs, w_out, place.unit, False)
        incoming = joined((own[...], part_one[...], part_two[...], part_three[...]))
        slope, sum_gain, sum_shift = norm_back(after_ref[...], small[11:12, :], incoming)
        current = grad_ref[...] + slope
        grad_out[...] = current
        branch = current.astype(BF)
        branch_ref[...] = branch
        unit, scale = standard(mixed_ref[...])
        upper = unit * small[9:10, :] + small[10:11, :]
        grad_upper = dot_nt(branch, w_out[...]) * silu_slope(upper)
        inner = grad_upper * small[9:10, :]
        mean = jnp.mean(inner, axis=-1, keepdims=True)
        shared = jnp.mean(inner * unit, axis=-1, keepdims=True)
        padded[:edge, :] = border_ref[...].astype(F32)
        padded[edge:, :] = glued_ref[...].astype(F32)
        spread[:edge, :] = jnp.zeros((edge, model), F32)
        spread[edge : edge + rows, :] = scale * (inner - mean - unit * shared)
        spread[edge + rows :, :] = jnp.zeros((edge, model), F32)
        sums[count : count + 1, :] = column_sum(grad_upper * unit)
        sums[count + 1 : count + 2, :] = column_sum(grad_upper)
        sums[count + 2 : count + 3, :] = sum_gain
        sums[count + 3 : count + 4, :] = sum_shift
        for column in range(0, model, LANES):
            lanes = slice(column, column + LANES)
            total = jnp.zeros((rows + edge, LANES), F32)
            center = spread[edge : edge + rows, lanes]
            for tap in range(count):
                start = edge - count + 1 + tap
                sums[tap : tap + 1, lanes] = jnp.sum(
                    center * padded[start : start + rows, lanes], axis=0, keepdims=True
                )
                begin = count - 1 - tap
                weight = small[first + tap : first + tap + 1, lanes]
                total += spread[begin : begin + rows + edge, lanes] * weight
            halo_ref[:, lanes] = total[:edge].astype(BF)
            main_ref[:, lanes] = total[edge:]

    return kernel_call(
        kernel,
        "convolve_back_start",
        [
            shape_of(rows, model, F32),
            shape_of(rows, model, BF),
            shape_of(rows, model, F32),
            shape_of(edge, model, BF),
            shape_of(count + 4, model, F32),
        ],
        (
            place.spot, *parts, grad, after, mixed, wide, glued, border,
            *weights,
        ),
        scalars=1,
        scratch=[
            pltpu.VMEM((edge + rows, model), F32),
            pltpu.VMEM((rows + 2 * edge, model), F32),
            pltpu.VMEM((model, model), BF),
        ],
        limit=56,
        flops=2 * rows * model * model,
    )


def convolve_back_finish(main, incoming, doubled, weights, before, wide, grad, place):
    rows, model = before.shape
    edge = incoming.shape[0]
    count = len(weights)

    def kernel(spot, main_ref, late, both, base, small, grad_rows, *refs):
        current_ref, branch_ref, slope_ref, sums, w_in = refs[count:]
        lay_conv(spot, refs[:count], w_in, place.unit, True)
        last = main_ref[rows - edge :, :] + late[...].astype(F32)
        glued = jnp.concatenate([main_ref[: rows - edge, :], last], axis=0)
        glued = glued.astype(BF).astype(F32)
        gate = logistic(both[:, model:])
        slope_ref[:, :model] = (glued * gate).astype(BF)
        slope_ref[:, model:] = (glued * both[:, :model] * gate * (1.0 - gate)).astype(BF)
        inner, sum_gain, sum_shift = norm_back(
            base[...], small[7:8, :], dot_nt(slope_ref[...], w_in[...])
        )
        current = grad_rows[...] + inner
        current_ref[...] = current
        branch_ref[...] = current.astype(BF)
        sums[0:1, :] = sum_gain
        sums[1:2, :] = sum_shift
        sums[2:3, :] = column_sum(current.astype(BF))

    return kernel_call(
        kernel,
        "convolve_back_finish",
        [
            shape_of(rows, model, F32),
            shape_of(rows, model, BF),
            shape_of(rows, 2 * model, BF),
            shape_of(3, model, F32),
        ],
        (
            place.spot, main, incoming, doubled, before, wide, grad,
            *weights,
        ),
        scalars=1,
        scratch=[pltpu.VMEM((model, 2 * model), BF)],
        limit=56,
        flops=4 * rows * model * model,
    )


def conv_grads_start(hidden, slope, rest, branch, place):
    model = hidden.shape[1]
    unit, planes = place.unit, place.planes
    size = unit // 2
    halved = size % 16 == 0

    def kernel(spot, hidden_ref, slope_ref, rest_ref, branch_ref, kept, sent, total):
        total[:, : 2 * model] = dot_tn(hidden_ref[...], slope_ref[...])
        total[:, 2 * model :] = dot_tn(rest_ref[...], branch_ref[...])
        plane, second, core, rep = spot[0], spot[1], spot[2], spot[3]
        for near, ref in enumerate((kept, sent)):
            if not halved:
                for pair in range(2 * planes):
                    start = pl.multiple_of((pair * 2 + (core ^ near)) * unit, unit)
                    for column in range(3):
                        ref[(3 * pair + column) * unit : (3 * pair + column + 1) * unit, :] = total[
                            pl.ds(start, unit), column * model : (column + 1) * model
                        ].astype(BF)
                continue
            for kind, (turn, side) in enumerate(((0, 0), (0, 1), (1, 0), (1, 1))):
                for step in range(planes):
                    start = (((plane ^ step) * 2 + (second ^ turn)) * 2 + (core ^ near)) * 2
                    start = pl.multiple_of((start + (rep ^ side)) * size, size)
                    for column in range(3):
                        target = ((kind * planes + step) * 3 + column) * size
                        ref[target : target + size, :] = total[
                            pl.ds(start, size), column * model : (column + 1) * model
                        ].astype(BF)

    return kernel_call(
        kernel,
        "conv_grads",
        [shape_of(3 * model // 2, model, BF)] * 2,
        (place.spot, hidden, slope, rest, branch),
        scalars=1,
        scratch=[pltpu.VMEM((model, 3 * model), F32)],
        flops=6 * hidden.shape[0] * model * model,
        limit=36,
    )


def conv_grads_split(kept, swapped, place):
    count = 4 if place.unit // 2 % 16 == 0 else 1
    size = kept.shape[0] // count

    def body(kept_part, swapped_part):
        total = kept_part.astype(F32) + swapped_part.astype(F32)
        return [total[index * size : (index + 1) * size] for index in range(count)]

    outs = [shape_of(size, kept.shape[1], BF)] * count
    return list(fused(body, "conv_grads_split", outs, kept, swapped))


def conv_grads_square(shares, masks):
    first, second = masks
    return [
        shares[0],
        flipped(shares[1], first),
        flipped(shares[2], second),
        flipped(shares[3], first | second),
    ]


def conv_grads_pieces(shares, place):
    size = shares[0].shape[0] // place.planes

    def body(*values):
        total = sum(value.astype(F32) for value in values)
        return [total[step * size : (step + 1) * size] for step in range(place.planes)]

    outs = [shape_of(size, shares[0].shape[1], BF)] * place.planes
    return list(fused(body, "conv_grads_pieces", outs, *shares))


def conv_grads_whole(total, place):
    groups = [list(range(core, place.shards, 2)) for core in range(2)]
    mine = lax.psum_scatter(
        total, "shard", scatter_dimension=0, tiled=True, axis_index_groups=groups
    )
    return rep_sum(mine, place).reshape(3, place.unit, -1)


def conv_grads_final(mine, theirs, place):
    size, model = mine.shape[0] // 3, mine.shape[1]

    def kernel(spot, mine_ref, theirs_ref, grad_in, grad_out):
        for turn, ref in enumerate((mine_ref, theirs_ref)):
            target = pl.ds(pl.multiple_of((spot[3] ^ turn) * size, size), size)
            grad_in[0, target, :model] = ref[:size, :].astype(F32)
            grad_in[0, target, model:] = ref[size : 2 * size, :].astype(F32)
            grad_out[0, target, :] = ref[2 * size :, :].astype(F32)

    outs = [
        jax.ShapeDtypeStruct((1, 2 * size, 2 * model), F32),
        jax.ShapeDtypeStruct((1, 2 * size, model), F32),
    ]
    return kernel_call(kernel, "conv_final", outs, (place.spot, mine, theirs), scalars=1)


def feed_to_attend(parts, before, wide):
    rows, model = before.shape

    def body(*values):
        base, small = values[4:]
        current = base.astype(F32) + 0.5 * (joined(values[:4]) + row(small, 2))
        unit, unused_scale = standard(current)
        return current, unit * row(small, 3) + row(small, 4)

    outs = [shape_of(rows, model, F32), shape_of(rows, model, BF)]
    return fused(body, "feed_to_attend", outs, *parts, before, wide)


def turn_around(parts, before, wide, cotangent):
    rows, model = before.shape

    def body(*values):
        base, small, grad = values[4:]
        current = base + 0.5 * (joined(values[:4]) + row(small, 13))
        unit, unused_scale = standard(current)
        slope, sum_gain, sum_shift = norm_back(current, row(small, 14), grad.astype(F32))
        branch = (0.5 * slope).astype(BF)
        sums = jnp.concatenate([column_sum(branch), sum_gain, sum_shift], axis=0)
        return unit * row(small, 14) + row(small, 15), slope, branch, sums

    outs = [
        shape_of(rows, model, BF),
        shape_of(rows, model, F32),
        shape_of(rows, model, BF),
        shape_of(3, model, F32),
    ]
    return fused(body, "turn_around", outs, *parts, before, wide, cotangent)


def attend_to_feed_back(parts, grad, before, wide):
    rows, model = before.shape

    def body(*values):
        grad_rows, base, small = values[4:]
        slope, sum_gain, sum_shift = norm_back(base, row(small, 3), joined(values[:4]))
        current = grad_rows + slope
        branch = (0.5 * current).astype(BF)
        sums = jnp.concatenate([column_sum(branch), sum_gain, sum_shift], axis=0)
        return current, branch, sums

    outs = [shape_of(rows, model, F32), shape_of(rows, model, BF), shape_of(3, model, F32)]
    return fused(body, "attend_to_feed_back", outs, *parts, grad, before, wide)


def last_step(parts, grad, before, wide):
    rows, model = before.shape

    def body(*values):
        grad_rows, base, small = values[4:]
        slope, sum_gain, sum_shift = norm_back(
            base.astype(F32), row(small, 0), joined(values[:4])
        )
        return grad_rows + slope, jnp.concatenate([sum_gain, sum_shift], axis=0)

    outs = [shape_of(rows, model, F32), shape_of(2, model, F32)]
    return fused(body, "last_step", outs, *parts, grad, before, wide)


def small_unpack(gathered, counts, place):
    rows, modules_rows = counts
    shards, unit, half, planes = place.shards, place.unit, place.half, place.planes
    model = shards * unit
    if not place.aligned:
        wide = gathered[:, :rows].transpose(1, 0, 2).reshape(rows, model).astype(F32)
        bias = gathered[:, rows:].reshape(planes, 2, 2, 2, 2, half)
        bias = lax.dynamic_index_in_dim(bias, place.second, 1, keepdims=False)
        bias = lax.dynamic_index_in_dim(bias, place.rep, 3, keepdims=False)
        bias = bias.transpose(2, 0, 1, 3).reshape(2, -1).astype(F32)
        heads = [
            lax.dynamic_slice_in_dim(wide[index].reshape(SPAN, -1), place.member, 1, 0)
            for index in (5, 6)
        ]
        return wide, bias, jnp.concatenate([heads[0], jnp.zeros_like(heads[0]), heads[1]], axis=1)

    def kernel(spot, ref, wide, bias, mix):
        lane = lax.broadcasted_iota(jnp.int32, (1, LANES), 1)
        second, core, rep = spot[1], spot[2], spot[3]
        member = (spot[0] & 1) * 4 + second * 2 + core

        def doubled(value):
            return jnp.concatenate([value, value], axis=1)

        for pair in range(shards // 2):
            both = [doubled(ref[2 * pair + side].astype(F32)) for side in range(2)]
            value = jnp.where(lane < unit, both[0], both[1])
            wide[:, pair * LANES : (pair + 1) * LANES] = value[:rows]
        for module in range(2):
            for index in range(2 * planes):
                shard = (index // 2 * 2 + second) * 2 + index % 2
                block = doubled(ref[shard].astype(F32))
                start = rows + (module * 2) * 2
                options = [
                    jnp.where(
                        lane < unit,
                        block[start + 2 * side : start + 2 * side + 1],
                        block[start + 2 * side + 1 : start + 2 * side + 2],
                    )
                    for side in range(2)
                ]
                value = jnp.where(rep == 0, options[0], options[1])
                bias[module : module + 1, index * half : (index + 1) * half] = value
        mix[...] = jnp.zeros_like(mix)
        pair = [doubled(ref[member + SPAN * group].astype(F32)) for group in range(2)]
        value = jnp.where(lane < unit, pair[0], pair[1])
        mix[:, :LANES] = value[5:6]
        mix[:, 2 * LANES :] = value[6:7]

    outs = [
        shape_of(rows, model, F32),
        shape_of(2, 2 * planes * half, F32),
        shape_of(1, 3 * LANES, F32),
    ]
    return kernel_call(kernel, "small_unpack", outs, (place.spot, gathered), scalars=1)


def shard_gather(value, place):
    copies = jnp.broadcast_to(value[None], (place.shards, *value.shape))
    return lax.all_to_all(copies, "shard", 0, 0, tiled=True)


def small_reduce(sums, mix_sums, biases, distance, counts, place):
    input_sums, first_sums, attend_sums, conv_sums, last_sums = sums
    rows, taps = counts
    unit, half, planes, shards = place.unit, place.half, place.planes, place.shards
    model = unit * shards
    width = mix_sums.shape[1] // 3
    if not place.aligned:
        heads = []
        for start in (0, 2 * width):
            whole = jnp.zeros((SPAN, model // SPAN), F32)
            block = mix_sums[:, start : start + width]
            whole = lax.dynamic_update_slice_in_dim(whole, block, place.member, 0)
            heads.append(whole.reshape(1, model))
        wide = jnp.concatenate(
            [
                input_sums, first_sums, *heads, attend_sums[:2], conv_sums[taps:], last_sums,
                attend_sums[2:], conv_sums[:taps],
            ],
            axis=0,
        )
        wide = wide.reshape(-1, shards, unit).transpose(1, 0, 2)
        pair = jnp.stack(biases).reshape(2, planes, 2, half)
        bias = lax.dynamic_update_slice(
            jnp.zeros((planes, 2, 2, 2, 2, half), F32),
            pair.transpose(1, 2, 0, 3)[:, None, :, :, None, :],
            (0, place.second, 0, 0, place.rep, 0),
        ).reshape(shards, -1, unit)
        both = jnp.concatenate([wide, bias], axis=1)
        both = lax.all_to_all(
            jnp.concatenate([both, both], axis=0), ("rep", "shard"), 0, 0, tiled=True
        )
        total = jnp.sum(both, axis=0)
        for bit in range((2 * shards).bit_length() - 1):
            distance = distance + flipped(distance, 1 << bit)
        return total[:rows], total[rows:].reshape(2, 2 * half), distance
    extent = -(-(rows + 8) // 8) * 8
    table_rows = distance.shape[0]
    fold = -(-table_rows // 16) * 8

    def pack(spot, in_ref, first, attend_ref, conv, last, mix, bias_one, bias_two, table, out, wide):
        plane, second, core, rep = spot[0], spot[1], spot[2], spot[3]
        wide[...] = jnp.zeros_like(wide)
        wide[0:2, :] = in_ref[...]
        wide[2:5, :] = first[...]
        wide[7:9, :] = attend_ref[0:2, :]
        wide[9:13, :] = conv[taps:, :]
        wide[13:16, :] = last[...]
        wide[16:17, :] = attend_ref[2:3, :]
        wide[17 : 17 + taps, :] = conv[:taps, :]
        lane = lax.broadcasted_iota(jnp.int32, (1, LANES), 1)
        for group in range(2):
            start = ((group * 2 + (plane & 1)) * 2 + second) * LANES
            target = pl.ds(pl.multiple_of(start, LANES), LANES)
            for index, begin in ((5, 0), (6, 2 * width)):
                value = mix[:, begin : begin + LANES]
                moved = pltpu.roll(jnp.broadcast_to(value, (8, LANES)), unit, axis=1)[:1]
                low = value if group == 0 else moved
                high = moved if group == 0 else value
                placed = jnp.where(core == 0, low, high)
                placed = jnp.where(lane // unit == core, placed, 0.0)
                wide[index : index + 1, target] = placed
        for module, ref in enumerate((bias_one, bias_two)):
            for index in range(2 * planes):
                value = ref[:, index * half : (index + 1) * half]
                start = pl.multiple_of((index // 2 * 2 + second) * LANES, LANES)
                for side in range(2):
                    line = rows + ((index % 2) * 2 + module) * 2 + side
                    wide[line : line + 1, pl.ds(start, LANES)] = jnp.where(rep == side, value, 0.0)
        rest = jnp.concatenate(
            [table[fold:, :], jnp.zeros((2 * fold - table_rows, unit), F32)], axis=0
        )
        folded = jnp.concatenate([table[:fold, :], rest], axis=1)
        for target in range(2 * shards):
            pair = target % shards // 2
            out[target, :extent, :] = wide[:, pair * LANES : (pair + 1) * LANES]
            out[target, extent:, :] = folded

    packed = kernel_call(
        pack,
        "small_pack",
        [jax.ShapeDtypeStruct((2 * shards, extent + fold, LANES), F32)],
        (place.spot, *sums, mix_sums, *biases, distance),
        scalars=1,
        scratch=[pltpu.VMEM((extent, model), F32)],
    )[0]
    packed = lax.all_to_all(packed, ("rep", "shard"), 0, 0, tiled=True)

    def unpack(spot, ref, wide, bias, table):
        total = ref[0]
        for index in range(1, 2 * shards):
            total = total + ref[index]
        table[:fold, :] = total[extent:, :unit]
        core = spot[2]
        moved = pltpu.roll(total, unit, axis=1)
        table[fold:, :] = moved[extent : extent + table_rows - fold, :unit]
        wide[...] = jnp.where(core == 0, total, moved)[:rows, :unit]
        for module in range(2):
            for side in range(2):
                lines = [rows + (near * 2 + module) * 2 + side for near in range(2)]
                value = jnp.where(
                    core == 0, total[lines[0] : lines[0] + 1], total[lines[1] : lines[1] + 1]
                )
                bias[module : module + 1, side * half : (side + 1) * half] = value

    return kernel_call(
        unpack,
        "small_sum",
        [shape_of(rows, unit, F32), shape_of(2, 2 * half, F32), shape_of(*distance.shape, F32)],
        (place.spot, packed),
        scalars=1,
    )


class Place:
    def __init__(self, unit, half, head):
        self.shards = lax.axis_size("shard")
        self.planes = self.shards // QUAD
        self.unit, self.half = unit, half
        self.pack_rows = 2 * unit + half
        self.rep = lax.axis_index("rep")
        self.shard = lax.axis_index("shard")
        self.core = self.shard % 2
        self.second = self.shard // 2 % 2
        self.plane = self.shard // QUAD
        self.member = self.shard % SPAN
        self.spot = jnp.stack([self.plane, self.second, self.core, self.rep])
        self.flat_spot = jnp.stack([jnp.zeros_like(self.plane), self.second, self.core, self.rep])
        self.span_spot = self.member.reshape(1)
        self.aligned = whole_heads(head, self)
        self.feed_masks = (self.shards, 2)
        self.span_masks = (4, 2)


def along(value, by, place):
    count = place.shards
    route = [(i, i + by) for i in range(count) if 0 <= i + by < count]
    return lax.ppermute(value, "shard", route)


def shards(
    inputs,
    ff_in,
    ff_out,
    ff_bias,
    attn_in,
    attn_out,
    conv_in,
    conv_out,
    depthwise,
    distance,
    vectors,
    attn_bias,
    cotangent,
):
    rows, model = inputs.shape
    unit, half = ff_in.shape[2], ff_out.shape[2] // 2
    head = distance.shape[2]
    place = Place(unit, half, head)
    tap_count = depthwise.shape[1]
    edge = -(-(tap_count - 1) // 16) * 16
    bias_rows = ff_bias.shape[2] // unit
    count = vectors.shape[1]
    taps = (count + 1, tap_count)
    wide_rows = count + 1 + tap_count

    first_parts = feed_pack(ff_in, ff_out, 0, place)
    small = jnp.concatenate(
        [vectors[0], attn_bias, depthwise[0], ff_bias[0].reshape(2 * bias_rows, unit)], axis=0
    )
    first_pack = pack_rows(first_parts)
    first_pack, current, mix_in, later_in = tied(first_pack, inputs, attn_in[0], ff_in)
    first_far = plane_start(first_pack, place)
    pieces = square_gather(current, place.feed_masks)
    second_parts = feed_pack(later_in, ff_out, 1, place)
    columns = attend_columns(mix_in, place) if place.aligned else (mix_in, mix_in)
    (
        first_far[0], first_far[1], small, second_in, second_other, second_out, *early
    ) = tied(*first_far, small, *second_parts, *columns, *pieces)
    columns, pieces = early[:2], early[2:]
    small = shard_gather(small, place)
    first_near = plane_finish(first_pack, first_far, place)
    first_packs = with_core(first_near)
    wide, feed_bias, mix_bias = small_unpack(small, (wide_rows, 2 * bias_rows), place)
    table = wide_table(distance[0], rows)
    second_in = pack_rows((second_in, second_other))
    if place.aligned:
        columns = attend_arrange(*columns, place)
    glue = conv_pick(conv_in[0], conv_out[0], place)
    last = place.planes - 1
    first_packs[last], glue, second_in, wide, mix_bias, table, *columns = tied(
        first_packs[last], glue, second_in, wide, mix_bias, table, *columns
    )

    parts, saved_first = feed(
        pieces, first_packs, feed_bias[0:1], wide, 0, place.feed_masks, place
    )
    if place.aligned:
        travelled, outs = attend_weights_travel(*columns, attn_out[0], place)
        after_first, hidden = feed_to_attend(parts, inputs, wide)
        hidden, glue, *travelled = tied(hidden, glue, *travelled)
        glue_planes = conv_planes(glue, place)
        mix_in, mix_out = attend_weights_lay(travelled, outs, place)
    else:
        mix_in, mix_out = attend_weights_whole(attn_in[0], attn_out[0], head, place)
        after_first, hidden = feed_to_attend(parts, inputs, wide)
    near, far = group_gather(hidden, place.span_masks)
    if place.aligned:
        far[3], second_in, *glue_planes = tied(far[3], second_in, *glue_planes)
        glue_own = pack_rows(glue_planes)
        glue_own, via_first, via_second, unused_half = conv_square(glue_own, place.feed_masks)
    else:
        glue = [lax.all_gather(glue, "shard", axis=0, tiled=True)]
        far[3], second_in = tied(far[3], second_in)
    second_in_far = plane_start(second_in, place)
    saved_attend, kept, sent = attend((near, far), mix_in, mix_bias, mix_out, table, place)
    if place.aligned:
        sent, *second_in_far, via_first, via_second = tied(
            sent, *second_in_far, via_first, via_second
        )
        glue = conv_relay(glue_own, via_first, via_second, place.feed_masks)
    else:
        sent, *second_in_far = tied(sent, *second_in_far)
    parts = group_reduce(kept, sent, place.span_masks)
    parts[3], second_out, *glue = tied(parts[3], second_out, *glue)
    second_out_far = plane_start(second_out, place)
    after_attend, conv_hidden, doubled, glued = convolve_start(
        parts, after_first, wide, count, glue, place
    )
    border = along(glued[rows - edge :], 1, place)
    border = jnp.where(place.member == 0, jnp.zeros_like(border), border)
    mixed, rest, after_conv, hidden = convolve_finish(
        glued, border, wide, taps, glue, after_attend, place
    )
    hidden, *second_far = tied(hidden, *second_in_far, *second_out_far)
    second_packs = [
        *with_core(plane_finish(second_in, second_far[:2], place)),
        *with_core(plane_finish(second_out, second_far[2:], place)),
    ]
    pieces = square_gather(hidden, place.feed_masks)
    parts, saved_second = feed(
        pieces, second_packs, feed_bias[1:2], wide, None, place.feed_masks, place
    )
    output, grad_last, branch, last_sums = turn_around(parts, after_conv, wide, cotangent)

    pieces = square_gather(branch, place.feed_masks)
    result, branch, slope, second_bias = feed_back(pieces, second_packs, saved_second, place)
    second_grads = [
        *feed_in_grads(saved_second[0], slope, place),
        *feed_out_grads(saved_second[2], pieces, place),
    ]
    *result, second_grads[1], second_grads[3] = tied(*result, second_grads[1], second_grads[3])
    second_grads[1], second_grads[3] = flipped(second_grads[1], 1), flipped(second_grads[3], 1)
    parts = square_reduce(result, place.feed_masks)
    second_split = [plane_split(*pair, place) for pair in (second_grads[:2], second_grads[2:])]
    parts[3], *flat = tied(parts[3], *second_split[0], *second_split[1])
    second_split = [flat[: place.planes], flat[place.planes :]]
    second_lists = [plane_early(pieces, place) for pieces in second_split]
    grad_conv, conv_branch, main, halo, conv_sums = convolve_back_start(
        parts, grad_last, after_conv, mixed, wide, taps, glue, glued, border, place
    )
    incoming = along(halo, -1, place)
    incoming, second_tops = tied_tops(incoming, second_lists, place)
    second_early = [lists[0] for lists in second_lists]
    incoming = jnp.where(place.member == SPAN - 1, jnp.zeros_like(incoming), incoming)
    grad_attend, branch, slope, attend_sums = convolve_back_finish(
        main, incoming, doubled, glue, after_attend, wide, grad_conv, place
    )
    conv_kept, conv_sent = conv_grads_start(conv_hidden, slope, rest, conv_branch, place)
    second_tops = [plane_total(values) for values in second_tops]
    count_early = len(second_early[0])
    branch, conv_kept, conv_sent, *flat = tied(
        branch, conv_kept, conv_sent, *second_tops, *second_early[0], *second_early[1]
    )
    second_tops = flat[:2]
    second_early = [flat[2 : 2 + count_early], flat[2 + count_early :]]
    near, far = group_gather(branch, place.span_masks)
    conv_shares = conv_grads_split(conv_kept, flipped(conv_sent, 1), place)
    far[3], *flat = tied(far[3], *conv_shares, *second_tops)
    conv_shares, second_tops = flat[:-2], flat[-2:]
    if place.aligned:
        conv_shares = conv_grads_square(conv_shares, place.feed_masks)
    second_lasts = [plane_last(top, place) for top in second_tops]
    back = attend_back((near, far), saved_attend, mix_in, mix_out, table, place)
    grad_mixed, kept, sent, branch, grad_table, table_far = back
    sent, *second_lasts = tied(sent, *second_lasts)
    mix_grad_in, mix_grad_out, mix_sums = attend_grads(saved_attend, grad_mixed, branch, place)
    second_sums = [plane_add([*own, last]) for own, last in zip(second_early, second_lasts)]
    if place.aligned:
        mix_kept, mix_swap, *mix_outs = attend_grads_lay(mix_grad_in, mix_grad_out, place)
        kept, mix_swap = tied(kept, mix_swap)
        mix_swap = flipped(mix_swap, 1)
    parts = group_reduce(kept, sent, place.span_masks)
    if place.aligned:
        mix_sent = list(attend_grads_planes(mix_kept, mix_swap, place))
        parts[1], *mix_sent = tied(parts[1], *mix_sent)
        mix_sent[1] = flipped(mix_sent[1], QUAD)
        parts[3], mix_sent[1], *conv_shares = tied(parts[3], mix_sent[1], *conv_shares)
        conv_pieces = conv_grads_pieces(conv_shares, place)
    grad_distance = distance_gradient(grad_table, table_far, rows)
    grad_first, branch, first_sums = attend_to_feed_back(parts, grad_attend, after_first, wide)
    if place.aligned:
        branch, *conv_pieces = tied(branch, *conv_pieces)
        conv_lists = plane_early(conv_pieces, place)
        mix_sent = attend_grads_relay(*mix_sent, *mix_outs)
        pieces = square_gather(branch, place.feed_masks)
        pieces[3], (conv_top,) = tied_tops(pieces[3], [conv_lists], place)
    else:
        pieces = square_gather(branch, place.feed_masks)
        conv_whole = conv_grads_whole(conv_shares[0], place)
        mix_grads = attend_grads_whole(mix_grad_in, mix_grad_out, head, place)
        mix_grads = [item[None] for item in mix_grads]
    kept, sent = feed_out_grads(saved_first[2], pieces, place)
    pieces[0], kept, sent = tied(pieces[0], kept, sent)
    out_swapped = flipped(sent, 1)
    result, branch, slope, first_bias = feed_back(pieces, first_packs, saved_first, place)
    out_split = plane_split(kept, out_swapped, place)
    slope, *out_split = tied(slope, *out_split)
    out_lists = plane_early(out_split, place)
    kept, sent = feed_in_grads(saved_first[0], slope, place)
    kept, *result = tied(kept, *result)
    if place.aligned:
        kept, *mix_sent = tied(kept, *mix_sent)
        mix_own, mix_other, mix_out_sum = attend_grads_sum(mix_sent, place)
        conv_last = plane_last(plane_total(conv_top), place)
    in_swapped = flipped(sent, 1)
    in_swapped, (out_top,) = tied_tops(in_swapped, [out_lists], place)
    out_last = plane_last(plane_total(out_top), place)
    in_lists = plane_early(plane_split(kept, in_swapped, place), place)
    parts = square_reduce(result, place.feed_masks)
    second_other = flipped(second_sums[0][unit:], 2)
    if place.aligned:
        mix_arrived = flipped(mix_other, 2)
        parts[3], mix_arrived, conv_last = tied(parts[3], mix_arrived, conv_last)
        conv_mine = plane_add([*conv_lists[0], conv_last])
    parts[3], second_other, (in_top,) = tied_tops_with(parts[3], second_other, in_lists, place)
    in_last = plane_last(plane_total(in_top), place)
    grad_input, input_sums = last_step(parts, grad_first, inputs, wide)

    second_pack = pack_rows((second_sums[0][:unit], second_other, second_sums[1]))
    second_theirs = flipped(second_pack, place.shards)
    small_grads, bias_grads, grad_distance = small_reduce(
        (input_sums, first_sums, attend_sums, conv_sums, last_sums),
        mix_sums,
        (first_bias, second_bias),
        grad_distance,
        (wide_rows, tap_count),
        place,
    )
    out_sum = plane_add([*out_lists[0], out_last])
    out_theirs = flipped(out_sum, place.shards)
    if place.aligned:
        mix_mine = mix_own, mix_arrived, mix_out_sum
        mix_theirs = [flipped(item, place.shards) for item in mix_mine]
        conv_theirs = flipped(conv_mine, place.shards)
        mix_grads = attend_grads_final(mix_mine, mix_theirs, place)
        conv_grads = conv_grads_final(conv_mine, conv_theirs, place)
    else:
        conv_grads = (
            jnp.concatenate([conv_whole[0], conv_whole[1]], axis=1)[None],
            conv_whole[2][None],
        )
    in_last, small_grads, mix_last, conv_end, second_theirs, out_theirs, *early = tied(
        in_last,
        small_grads,
        mix_grads[0],
        conv_grads[0],
        second_theirs,
        out_theirs,
        *in_lists[0][1:],
    )
    first_mine = feed_arrive([plane_add([in_lists[0][0], *early, in_last])], place)
    first_mine = [*first_mine, (out_sum, out_theirs)]
    cuts = (0, unit, 2 * unit, 2 * unit + half)
    second_mine = [
        (second_pack[cuts[i] : cuts[i + 1]], second_theirs[cuts[i] : cuts[i + 1]])
        for i in range(3)
    ]
    feed_grads = feed_final((first_mine, second_mine), place)
    mix_grads, conv_grads = (mix_last, mix_grads[1]), (conv_end, conv_grads[1])
    return (
        output,
        grad_input,
        *feed_grads,
        bias_grads[None],
        *mix_grads,
        *conv_grads,
        small_grads[count + 1 :][None],
        grad_distance[None],
        small_grads[:count][None],
        small_grads[count : count + 1],
    )


def solution(mesh):
    in_specs = (
        P(("rep", "shard"), None),
        P(None, None, "shard", None),
        P(None, None, "shard", None),
        P(None, None, "shard"),
        P(None, "shard", None),
        P(None, "shard", None),
        P(None, "shard", None),
        P(None, "shard", None),
        P(None, None, "shard"),
        P(),
        P(None, None, "shard"),
        P(None, "shard"),
        P(("rep", "shard"), None),
    )
    out_specs = (
        P(("rep", "shard"), None),
        P(("rep", "shard"), None),
        P(None, None, "shard", None),
        P(None, None, "shard", None),
        P(None, None, "shard"),
        P(None, "shard", None),
        P(None, "shard", None),
        P(None, "shard", None),
        P(None, "shard", None),
        P(None, None, "shard"),
        P(),
        P(None, None, "shard"),
        P(None, "shard"),
    )
    return jax.shard_map(shards, mesh=mesh, in_specs=in_specs, out_specs=out_specs, check_vma=False)
```

```python
import jax
import jax.numpy as jnp
from jax import lax
from jax.experimental import pallas as pl
from jax.experimental.pallas import tpu as pltpu
from jax.sharding import PartitionSpec as P

LEFT = 64
RIGHT = 8
SPAN = 8
QUAD = 4
EPSILON = 1e-05
BF = jnp.bfloat16
F32 = jnp.float32
MIB = 1 << 20
LANES = 128


def dot_nn(left, right):
    return jnp.dot(left, right, preferred_element_type=F32)


def dot_nt(left, right):
    return lax.dot_general(left, right, (((1,), (1,)), ((), ())), preferred_element_type=F32)


def dot_tn(left, right):
    return lax.dot_general(left, right, (((0,), (0,)), ((), ())), preferred_element_type=F32)


def column_sum(values):
    return jnp.sum(values.astype(F32), axis=0, keepdims=True)


def standard(values):
    center = values - jnp.mean(values, axis=-1, keepdims=True)
    scale = lax.rsqrt(jnp.mean(center * center, axis=-1, keepdims=True) + EPSILON)
    return center * scale, scale


def norm_back(values, gain, grad):
    unit, scale = standard(values)
    inner = grad * gain
    first = jnp.mean(inner, axis=-1, keepdims=True)
    second = jnp.mean(inner * unit, axis=-1, keepdims=True)
    return scale * (inner - first - unit * second), column_sum(grad * unit), column_sum(grad)


def logistic(values):
    return 1.0 / (1.0 + jnp.exp(-values))


def silu_slope(values):
    gate = logistic(values)
    return gate * (1.0 + values * (1.0 - gate))


def vmem(count):
    return [pl.BlockSpec(memory_space=pltpu.VMEM)] * count


def shape_of(rows, columns, dtype):
    return jax.ShapeDtypeStruct((rows, columns), dtype)


class Part:
    def __init__(self, array, block, index):
        self.array, self.block, self.index = array, block, index
        self.shape, self.dtype = block, array.dtype
        self.size = 1
        for extent in block:
            self.size *= extent


def kernel_call(body, name, outs, operands, scalars=0, scratch=(), flops=0, limit=24):
    moved = sum(item.size * item.dtype.itemsize for item in (*operands[scalars:], *outs))
    specs = [pl.BlockSpec(memory_space=pltpu.SMEM)] * scalars
    arrays = list(operands[:scalars])
    for item in operands[scalars:]:
        if isinstance(item, Part):
            specs.append(pl.BlockSpec(item.block, lambda step, index=item.index: index))
            arrays.append(item.array)
        else:
            specs += vmem(1)
            arrays.append(item)
    return pl.pallas_call(
        body,
        grid=(1,),
        in_specs=specs,
        out_specs=vmem(len(outs)),
        out_shape=list(outs),
        scratch_shapes=list(scratch),
        compiler_params=pltpu.CompilerParams(vmem_limit_bytes=limit * MIB),
        cost_estimate=pl.CostEstimate(flops=flops, bytes_accessed=moved, transcendentals=0),
        name=name,
    )(*arrays)


def fused(body, name, outs, *operands, flops=0):
    def kernel(*refs):
        results = body(*[ref[...] for ref in refs[: len(operands)]])
        for ref, value in zip(refs[len(operands) :], results):
            ref[...] = value.astype(ref.dtype)

    return kernel_call(kernel, name, outs, operands, flops=flops)


def tied(*values):
    return lax.optimization_barrier(values)


def tied_lists(*lists):
    flat = iter(tied(*[item for values in lists for item in values]))
    return [[next(flat) for _ in values] for values in lists]


def flipped(value, mask):
    total = lax.axis_size("rep") * lax.axis_size("shard")
    return lax.ppermute(value, ("rep", "shard"), [(i, i ^ mask) for i in range(total)])


def square_gather(value, masks):
    first, second = masks
    return [
        value,
        flipped(value, first),
        flipped(value, second),
        flipped(value, first | second),
    ]


def square_reduce(parts, masks):
    first, second = masks
    own, via_first, via_second, cross = parts
    return [
        own,
        flipped(cross, first | second),
        flipped(via_first, first),
        flipped(via_second, second),
    ]


def joined(parts):
    return parts[0] + sum(part.astype(F32) for part in parts[1:])


def place_feed(spot, views, w_in, w_out, unit, half):
    plane, second, core = spot[0], spot[1], spot[2]
    for step, near, in_ref, out_ref, start in views:
        column = (plane ^ step) * 2
        for turn in range(2):
            row = ((column + (second ^ turn)) * 2 + (core ^ near)) * unit
            source = slice(turn * unit, (turn + 1) * unit)
            w_in[pl.ds(pl.multiple_of(row, unit), unit), :] = in_ref[source, :]
        row = (column + (core ^ near)) * half
        w_out[pl.ds(pl.multiple_of(row, half), half), :] = out_ref[start : start + half, :]


def pack_views(refs, place):
    planes, count = place.planes, 2 * place.planes
    if len(refs) == count:
        return [(i % planes, i // planes, ref, ref, 2 * place.unit) for i, ref in enumerate(refs)]
    return [(i % planes, i // planes, refs[i], refs[count + i], 0) for i in range(count)]


def feed(pieces, packs, bias, wide, norm_row, masks, place):
    rows, model = pieces[0].shape
    inner = bias.shape[1]
    count, total = len(pieces), len(pieces) * rows
    unit, half = place.unit, place.half

    def kernel(spot_ref, *refs):
        piece_refs, pack_refs = refs[:count], refs[count : count + len(packs)]
        bias_ref, wide_ref, hidden, upper, active = refs[count + len(packs) :][:5]
        outs = refs[count + len(packs) + 5 : -2]
        w_in, w_out = refs[-2:]
        place_feed(spot_ref, pack_views(pack_refs, place), w_in, w_out, unit, half)
        for index, ref in enumerate(piece_refs):
            block = ref[...]
            if norm_row is not None:
                scaled, unused_scale = standard(block.astype(F32))
                gain = wide_ref[norm_row : norm_row + 1, :]
                shift = wide_ref[norm_row + 1 : norm_row + 2, :]
                block = (scaled * gain + shift).astype(BF)
            hidden[index * rows : (index + 1) * rows, :] = block
        before = dot_nn(hidden[...], w_in[...]) + bias_ref[...]
        upper[...] = before
        active[...] = (before * logistic(before)).astype(BF)
        result = dot_nn(active[...], w_out[...])
        for index, ref in enumerate(outs):
            ref[...] = result[index * rows : (index + 1) * rows].astype(ref.dtype)

    outs = [
        shape_of(total, model, BF),
        shape_of(total, inner, F32),
        shape_of(total, inner, BF),
        shape_of(rows, model, F32),
    ] + [shape_of(rows, model, BF)] * (count - 1)
    results = kernel_call(
        kernel,
        "feed_forward",
        outs,
        (place.spot, *pieces, *packs, bias, wide),
        scalars=1,
        scratch=[pltpu.VMEM((model, inner), BF), pltpu.VMEM((inner, model), BF)],
        flops=4 * total * model * inner,
    )
    return square_reduce(results[3:], masks), results[:3]


def feed_back(pieces, packs, saved, place):
    hidden, upper, active = saved
    rows, model = pieces[0].shape
    total, inner = upper.shape
    count = len(pieces)
    unit, half = place.unit, place.half

    def kernel(spot_ref, *refs):
        piece_refs, pack_refs = refs[:count], refs[count : count + len(packs)]
        upper_ref, branch, slope, sums = refs[count + len(packs) :][:4]
        outs = refs[count + len(packs) + 4 : -2]
        w_in, w_out = refs[-2:]
        place_feed(spot_ref, pack_views(pack_refs, place), w_in, w_out, unit, half)
        for index, ref in enumerate(piece_refs):
            branch[index * rows : (index + 1) * rows, :] = ref[...]
        grad = dot_nt(branch[...], w_out[...]) * silu_slope(upper_ref[...])
        slope[...] = grad.astype(BF)
        sums[...] = column_sum(slope[...])
        result = dot_nt(slope[...], w_in[...])
        for index, ref in enumerate(outs):
            ref[...] = result[index * rows : (index + 1) * rows].astype(ref.dtype)

    outs = [
        shape_of(total, model, BF),
        shape_of(total, inner, BF),
        shape_of(1, inner, F32),
        shape_of(rows, model, F32),
    ] + [shape_of(rows, model, BF)] * (count - 1)
    results = kernel_call(
        kernel,
        "feed_backward",
        outs,
        (place.spot, *pieces, *packs, upper),
        scalars=1,
        scratch=[pltpu.VMEM((model, inner), BF), pltpu.VMEM((inner, model), BF)],
        flops=4 * total * model * inner,
    )
    branch, slope, sums = results[:3]
    return results[3:], branch, slope, sums


def feed_out_grads(active, pieces, place):
    rows, model = pieces[0].shape
    inner = active.shape[1]
    planes, half = place.planes, place.half
    count = len(pieces)

    def kernel(spot, active_ref, *refs):
        total, kept, sent = refs[-1], refs[count], refs[count + 1]
        branch = jnp.concatenate([ref[...] for ref in refs[:count]], axis=0)
        total[...] = dot_tn(active_ref[...], branch)
        for near, ref in enumerate((kept, sent)):
            for step in range(planes):
                row = ((spot[0] ^ step) * 2 + (spot[2] ^ near)) * half
                source = pl.ds(pl.multiple_of(row, half), half)
                ref[step * half : (step + 1) * half, :] = total[source, :].astype(BF)

    return kernel_call(
        kernel,
        "feed_out_grads",
        [shape_of(planes * half, model, BF)] * 2,
        (place.spot, active, *pieces),
        scalars=1,
        scratch=[pltpu.VMEM((inner, model), F32)],
        flops=2 * active.shape[0] * model * inner,
    )


def feed_in_grads(hidden, slope, place):
    model, inner = hidden.shape[1], slope.shape[1]
    planes, unit = place.planes, place.unit

    def kernel(spot, hidden_ref, slope_ref, kept, sent, total):
        total[...] = dot_tn(hidden_ref[...], slope_ref[...])
        for near, ref in enumerate((kept, sent)):
            for step in range(planes):
                for turn in range(2):
                    column = (spot[0] ^ step) * 2 + (spot[1] ^ turn)
                    row = (column * 2 + (spot[2] ^ near)) * unit
                    start = (2 * step + turn) * unit
                    source = pl.ds(pl.multiple_of(row, unit), unit)
                    ref[start : start + unit, :] = total[source, :].astype(BF)

    return kernel_call(
        kernel,
        "feed_in_grads",
        [shape_of(2 * planes * unit, inner, BF)] * 2,
        (place.spot, hidden, slope),
        scalars=1,
        scratch=[pltpu.VMEM((model, inner), F32)],
        flops=2 * hidden.shape[0] * model * inner,
    )


def plane_split(kept, swapped, place):
    planes = place.planes
    size = kept.shape[0] // planes

    def body(kept_part, swapped_part):
        both = kept_part.astype(F32) + swapped_part.astype(F32)
        return [both[step * size : (step + 1) * size] for step in range(planes)]

    outs = [shape_of(size, kept.shape[1], BF)] * planes
    return fused(body, "plane_split", outs, kept, swapped)


def plane_early(pieces, place):
    lists = {step: [piece] for step, piece in enumerate(pieces)}
    top = place.planes.bit_length() - 2
    for bit in range(top):
        for step in [step for step in sorted(lists) if step >> bit & 1]:
            values = lists.pop(step)
            value = values[0] if len(values) == 1 else plane_add(values)
            lists[step ^ 1 << bit].append(flipped(value, QUAD << bit))
    return lists


def plane_last(value, place):
    return flipped(value, QUAD * (place.planes // 2))


def tied_tops(value, all_lists, place):
    top = place.planes // 2
    flat = [item for lists in all_lists for item in lists[top]]
    value, *flat = tied(value, *flat)
    flat = iter(flat)
    return value, [[next(flat) for _ in lists[top]] for lists in all_lists]


def plane_total(values):
    return values[0] if len(values) == 1 else plane_add(values)


def feed_pack(ff_in, ff_out, module, place):
    rows, hidden = ff_in.shape[2:]
    width, model = ff_out.shape[2:]
    half = width // 2
    count = 2 * place.planes * half
    if half % LANES:
        columns = ff_in[0, module].reshape(rows, place.planes, 2, 2, 2, half)
        columns = lax.dynamic_index_in_dim(columns, place.rep, 4, keepdims=False)
        own = lax.dynamic_index_in_dim(columns, place.second, 2, keepdims=False)
        other = lax.dynamic_index_in_dim(columns, 1 - place.second, 2, keepdims=False)
        own, other = (item.reshape(rows, count) for item in (own, other))
        part_out = lax.dynamic_slice_in_dim(ff_out[0, module], place.rep * half, half, 0)
        return own, flipped(other, 2), part_out

    def kernel(spot, in_ref, out_ref, own, other, part_out):
        second, rep = spot[1], spot[3]
        for turn, ref in enumerate((own, other)):
            for index in range(2 * place.planes):
                plane, core = index // 2, index % 2
                start = (((plane * 2 + (second ^ turn)) * 2 + core) * 2 + rep) * half
                source = pl.ds(pl.multiple_of(start, half), half)
                ref[:, index * half : (index + 1) * half] = in_ref[0, 0, :, source]
        part_out[...] = out_ref[0, 0, pl.ds(pl.multiple_of(rep * half, half), half), :]

    own, other, part_out = pl.pallas_call(
        kernel,
        grid=(1,),
        in_specs=[
            pl.BlockSpec(memory_space=pltpu.SMEM),
            pl.BlockSpec((1, 1, rows, hidden), lambda step: (0, module, 0, 0)),
            pl.BlockSpec((1, 1, width, model), lambda step: (0, module, 0, 0)),
        ],
        out_specs=vmem(3),
        out_shape=[
            shape_of(rows, count, BF),
            shape_of(rows, count, BF),
            shape_of(half, model, BF),
        ],
        compiler_params=pltpu.CompilerParams(vmem_limit_bytes=24 * MIB),
        name="feed_columns",
    )(place.spot, ff_in, ff_out)
    return own, flipped(other, 2), part_out


def pack_rows(parts):
    def body(*values):
        return (jnp.concatenate(values, axis=0),)

    rows = sum(item.shape[0] for item in parts)
    out = shape_of(rows, parts[0].shape[1], BF)
    return fused(body, "pack_rows", [out], *parts)[0]


def plane_bits(place):
    return range(place.planes.bit_length() - 1)


def plane_start(pack, place):
    top = place.planes // 2
    return [flipped(pack, QUAD * top), flipped(pack, QUAD)] if top > 1 else [flipped(pack, QUAD)]


def plane_finish(pack, started, place):
    pieces = {0: pack, place.planes // 2: started[0]}
    if len(started) > 1:
        pieces[1] = started[1]
    for bit in reversed(plane_bits(place)):
        for step in sorted(pieces):
            if step % (2 << bit) == 0 and step | 1 << bit not in pieces:
                pieces[step | 1 << bit] = flipped(pieces[step], QUAD << bit)
    return [pieces[step] for step in range(place.planes)]


def with_core(near):
    return [*near, *(flipped(item, 1) for item in near)]


def plane_add(values):
    def body(*items):
        return (sum((item.astype(F32) for item in items[1:]), items[0].astype(F32)),)

    return fused(body, "plane_add", [shape_of(*values[0].shape, BF)], *values)[0]


def feed_final(modules, place):
    unit, half = place.unit, place.half
    inner = modules[0][0][0].shape[1]
    model = modules[0][2][0].shape[1]
    planes = place.planes
    if half % LANES:
        grads_in, grads_out = [], []
        for in_own, in_other, out in modules:
            sides = jnp.stack([jnp.stack(in_own), jnp.stack(in_other)], axis=1)
            sides = jnp.where(place.second == 0, sides, sides[:, ::-1])
            sides = jnp.where(place.rep == 0, sides, sides[::-1])
            sides = sides.reshape(2, 2, unit, planes, 2, half).transpose(2, 3, 1, 4, 0, 5)
            grads_in.append(sides.reshape(unit, -1).astype(F32))
            both = jnp.stack(out)
            both = jnp.where(place.rep == 0, both, both[::-1])
            grads_out.append(both.reshape(2 * half, model).astype(F32))
        return jnp.stack(grads_in)[None], jnp.stack(grads_out)[None]

    def kernel(spot, *refs):
        grad_in, grad_out = refs[-2:]
        second, rep = spot[1], spot[3]
        for module in range(2):
            own = refs[6 * module : 6 * module + 6]
            for turn in range(2):
                for side in range(2):
                    piece = own[2 * turn + side][...].astype(F32)
                    for index in range(2 * planes):
                        plane, core = index // 2, index % 2
                        start = (((plane * 2 + (second ^ turn)) * 2 + core) * 2 + (rep ^ side)) * half
                        target = pl.ds(pl.multiple_of(start, half), half)
                        grad_in[0, module, :, target] = piece[:, index * half : (index + 1) * half]
            for side in range(2):
                target = pl.ds(pl.multiple_of((rep ^ side) * half, half), half)
                grad_out[0, module, target, :] = own[4 + side][...].astype(F32)

    operands = [item for module in modules for pair in module for item in pair]
    outs = [
        jax.ShapeDtypeStruct((1, 2, unit, 4 * inner), F32),
        jax.ShapeDtypeStruct((1, 2, 2 * half, model), F32),
    ]
    return kernel_call(kernel, "feed_final", outs, (place.spot, *operands), scalars=1)


def feed_arrive(sums, place):
    unit = place.unit
    own = sums[0][:unit]
    other = flipped(sums[0][unit:], 2)
    items = [own, other, *sums[1:]]
    return [(item, flipped(item, place.shards)) for item in items]


def score_block(query, keys, table, bias, place, rows, length):
    scores = dot_nt(query, keys)
    spread = dot_nt(query, table)
    band = pltpu.roll(spread, 0, axis=1, stride=1, stride_axis=0)
    column = lax.broadcasted_iota(jnp.int32, (rows, length + 2 * rows), 1)
    bias[...] = jnp.where(column < place, spread[:, :1], spread[:, -1:])
    bias[:, pl.ds(place, 3 * rows)] = band[:, rows:]
    return scores + bias[:, rows : rows + length]


def place_rows(source, columns, target, position, rows):
    for step in range(SPAN):
        spot = pl.ds(pl.multiple_of((position ^ step) * rows, rows), rows)
        target[spot, :] = source[step * rows : (step + 1) * rows, columns]


def split_rows(value, kept, sent, rows):
    for index, step in enumerate((0, 4, 2, 6)):
        target = slice(index * rows, (index + 1) * rows)
        kept[target, :] = value[step * rows : (step + 1) * rows]
        sent[target, :] = value[(step + 1) * rows : (step + 2) * rows].astype(BF)


def join_pieces(refs, target, rows):
    for step, ref in enumerate(refs):
        target[step * rows : (step + 1) * rows, :] = ref[...]


def attend_kernel(*refs):
    spot, pieces, rest = refs[0], refs[1 : 1 + SPAN], refs[1 + SPAN :]
    (weight_in, bias_in, weight_out, table, hidden, mixed, context, peaks, kept, sent) = rest[:10]
    keys, values, bias = rest[10:]
    length, width = context.shape
    rows = length // SPAN
    head = table.shape[1] // 2
    position = spot[0]
    join_pieces(pieces, hidden, rows)
    mixed[...] = (dot_nn(hidden[...], weight_in[...]) + bias_in[...]).astype(BF)
    place_rows(mixed, slice(width, 2 * width), keys, position, rows)
    place_rows(mixed, slice(2 * width, 3 * width), values, position, rows)
    lane = lax.broadcasted_iota(jnp.int32, (rows, width), 1)

    def block(index, carry):
        place = pl.multiple_of(index * rows, rows)
        own = pl.ds(pl.multiple_of((position ^ index) * rows, rows), rows)
        query = mixed[own, :width] * jnp.asarray(head**-0.5, BF)
        results, logs = [], []
        for which in range(2):
            mine = lane // head == which
            part = jnp.where(mine, query, jnp.zeros_like(query))
            scores = score_block(part, keys[...], table[...], bias, place, rows, length)
            top = jnp.max(scores, axis=1, keepdims=True)
            powers = jnp.exp(scores - top)
            total = jnp.sum(powers, axis=1, keepdims=True)
            weights = (powers * (1.0 / total)).astype(BF)
            results.append(dot_nn(weights, values[...]))
            logs.append(top + jnp.log(total))
        context[own, :] = jnp.where(lane < head, results[0], results[1]).astype(BF)
        peaks[own, :] = jnp.where(lane < head, logs[0], logs[1])
        return carry

    lax.fori_loop(0, SPAN, block, 0)
    split_rows(dot_nn(context[...], weight_out[...]), kept, sent, rows)


def attend_back_kernel(*refs):
    spot, pieces, rest = refs[0], refs[1 : 1 + SPAN], refs[1 + SPAN :]
    (mixed, table, peaks, weight_in, weight_out) = rest[:5]
    (branch, grad_mixed, grad_table, far, kept, sent) = rest[5:11]
    keys, values, bias, grad_context, grad_keys, grad_values, slopes = rest[11:]
    length, width = grad_context.shape
    rows = length // SPAN
    head = table.shape[1] // 2
    position = spot[0]
    join_pieces(pieces, branch, rows)
    grad_context[...] = dot_nt(branch[...], weight_out[...]).astype(BF)
    place_rows(mixed, slice(width, 2 * width), keys, position, rows)
    place_rows(mixed, slice(2 * width, 3 * width), values, position, rows)
    grad_keys[...] = jnp.zeros_like(grad_keys)
    grad_values[...] = jnp.zeros_like(grad_values)
    grad_table[...] = jnp.zeros_like(grad_table)
    far[...] = jnp.zeros_like(far)
    lane = lax.broadcasted_iota(jnp.int32, (rows, width), 1)
    padded = lax.broadcasted_iota(jnp.int32, (rows, length + 2 * rows), 1)
    factor = head**-0.5
    slopes[:, :rows] = jnp.zeros((rows, rows), F32)
    slopes[:, rows + length :] = jnp.zeros((rows, rows), F32)
    mirror = (
        lax.broadcasted_iota(jnp.int32, (rows, rows), 0)
        + lax.broadcasted_iota(jnp.int32, (rows, rows), 1)
        == rows - 1
    ).astype(BF)

    def block(index, carry):
        place = pl.multiple_of(index * rows, rows)
        own = pl.ds(pl.multiple_of((position ^ index) * rows, rows), rows)
        query = mixed[own, :width] * jnp.asarray(factor, BF)
        results = []
        for which in range(2):
            mine = lane // head == which
            part = jnp.where(mine, query, jnp.zeros_like(query))
            scores = score_block(part, keys[...], table[...], bias, place, rows, length)
            incoming = grad_context[own, :]
            incoming = jnp.where(mine, incoming, jnp.zeros_like(incoming))
            logs = peaks[own, which * head : which * head + 1]
            probs = jnp.exp(scores - logs)
            grad_probs = dot_nt(incoming, values[...])
            shared = jnp.sum(grad_probs * probs, axis=1, keepdims=True)
            grad_low = (probs * (grad_probs - shared)).astype(BF)
            grad_values[...] += dot_tn(probs.astype(BF), incoming)
            grad_keys[...] += dot_tn(grad_low, part)
            slopes[:, rows : rows + length] = grad_low.astype(F32)
            window = slopes[:, pl.ds(place, 3 * rows)]
            whole = slopes[...]
            early = jnp.sum(jnp.where(padded < place, whole, 0.0), axis=1, keepdims=True)
            late = jnp.sum(
                jnp.where(padded >= place + 3 * rows, whole, 0.0), axis=1, keepdims=True
            )
            window = jnp.concatenate(
                [jnp.zeros((rows, rows), F32), dot_nn(mirror, window.astype(BF))], axis=1
            )
            window = pltpu.roll(
                window, 3 * rows + 1, axis=1, stride=1, stride_axis=0
            ).astype(BF)
            grad_table[...] += dot_tn(window, dot_nn(mirror, part).astype(BF))
            part_wide = part.astype(F32)
            far[0:1, :] += jnp.sum(early * part_wide, axis=0, keepdims=True)
            far[1:2, :] += jnp.sum(late * part_wide, axis=0, keepdims=True)
            close = jnp.dot(
                mirror.astype(F32),
                dot_nn(window, table[...]),
                preferred_element_type=F32,
                precision=lax.Precision.HIGHEST,
            )
            results.append(
                dot_nn(grad_low, keys[...])
                + close
                + early * table[0:1, :].astype(F32)
                + late * table[4 * rows - 1 :, :].astype(F32)
            )
        grad_mixed[own, :width] = (
            jnp.where(lane < head, results[0], results[1]) * factor
        ).astype(BF)
        return carry

    lax.fori_loop(0, SPAN, block, 0)
    for step in range(SPAN):
        source = pl.ds(pl.multiple_of((position ^ step) * rows, rows), rows)
        target = slice(step * rows, (step + 1) * rows)
        grad_mixed[target, width : 2 * width] = grad_keys[source, :].astype(BF)
        grad_mixed[target, 2 * width :] = grad_values[source, :].astype(BF)
    split_rows(dot_nt(grad_mixed[...], weight_in[...]), kept, sent, rows)


def group_gather(value, masks):
    near = square_gather(value, masks)
    return near, [flipped(item, 1) for item in near]


def group_reduce(kept, sent, masks):
    swapped = flipped(sent, 1)
    rows = kept.shape[0] // 4

    def body(kept_part, swapped_part):
        total = kept_part + swapped_part.astype(F32)
        return [total[index * rows : (index + 1) * rows] for index in range(4)]

    outs = [shape_of(rows, kept.shape[1], dtype) for dtype in (F32, BF, BF, BF)]
    return square_reduce(fused(body, "core_sum", outs, kept, swapped), masks)


def in_steps(blocks):
    near, far = blocks
    return [near[0], far[0], near[2], far[2], near[1], far[1], near[3], far[3]]


def attend(blocks, weight_in, bias_in, weight_out, table, place):
    pieces = in_steps(blocks)
    rows, model = pieces[0].shape
    length, width = SPAN * rows, weight_out.shape[0]
    outs = [
        shape_of(length, model, BF),
        shape_of(length, 3 * width, BF),
        shape_of(length, width, BF),
        shape_of(length, width, F32),
        shape_of(length // 2, model, F32),
        shape_of(length // 2, model, BF),
    ]
    hidden, mixed, context, peaks, kept, sent = kernel_call(
        attend_kernel,
        "attend_forward",
        outs,
        (place.span_spot, *pieces, weight_in, bias_in, weight_out, table),
        scalars=1,
        scratch=[
            pltpu.VMEM((length, width), BF),
            pltpu.VMEM((length, width), BF),
            pltpu.VMEM((rows, length + 2 * rows), F32),
        ],
        limit=56,
        flops=48 * length * length * width,
    )
    return (hidden, mixed, context, peaks), kept, sent


def attend_back(blocks, saved, weight_in, weight_out, table, place):
    hidden, mixed, context, peaks = saved
    pieces = in_steps(blocks)
    rows, model = pieces[0].shape
    length, width = SPAN * rows, weight_out.shape[0]
    outs = [
        shape_of(length, model, BF),
        shape_of(length, 3 * width, BF),
        shape_of(4 * rows, width, F32),
        shape_of(8, width, F32),
        shape_of(length // 2, model, F32),
        shape_of(length // 2, model, BF),
    ]
    branch, grad_mixed, grad_table, far, kept, sent = kernel_call(
        attend_back_kernel,
        "attend_backward",
        outs,
        (place.span_spot, *pieces, mixed, table, peaks, weight_in, weight_out),
        scalars=1,
        scratch=[
            pltpu.VMEM((length, width), BF),
            pltpu.VMEM((length, width), BF),
            pltpu.VMEM((rows, length + 2 * rows), F32),
            pltpu.VMEM((length, width), BF),
            pltpu.VMEM((length, width), F32),
            pltpu.VMEM((length, width), F32),
            pltpu.VMEM((rows, length + 2 * rows), F32),
        ],
        flops=96 * length * length * width,
    )
    return grad_mixed, kept, sent, branch, grad_table, far


def attend_grads(saved, grad_mixed, branch, place):
    hidden, unused_mixed, context, unused_peaks = saved
    length, model = hidden.shape
    width = context.shape[1]

    def weights(hidden_rows, mixed_grad, context_rows, branch_rows):
        return (
            dot_tn(hidden_rows, mixed_grad),
            dot_tn(context_rows, branch_rows),
            column_sum(mixed_grad),
        )

    return fused(
        weights,
        "attend_weights",
        [shape_of(model, 3 * width, BF), shape_of(width, model, BF), shape_of(1, 3 * width, F32)],
        hidden,
        grad_mixed,
        context,
        branch,
        flops=8 * length * model * width,
    )


def wide_table(distance, rows):
    index = jnp.clip(jnp.arange(4 * rows) - rows - LEFT, 0, LEFT + RIGHT)
    low = distance[index]
    return jnp.concatenate([low, low], axis=1)


def distance_gradient(grad_table, far, rows):
    first = rows + LEFT
    last = first + LEFT + RIGHT
    head = grad_table.shape[1] // 2
    low = jnp.sum(grad_table[: first + 1], axis=0) + far[0]
    high = jnp.sum(grad_table[last:], axis=0) + far[1]
    total = jnp.concatenate([low[None], grad_table[first + 1 : last], high[None]], axis=0)
    return total[:, :head] + total[:, head:]


def whole_heads(head, place):
    return place.unit == head and 2 * place.unit == LANES and place.planes == 4


def attend_weights_whole(weight_in, weight_out, head, place):
    model = weight_out.shape[1]
    heads = model // head
    per_device = heads // SPAN
    width = per_device * head
    whole = lax.all_gather(weight_in, "shard", axis=0, tiled=True)
    whole = whole.reshape(model, 3, heads, head)
    mine = lax.dynamic_slice_in_dim(whole, place.member * per_device, per_device, 2)
    out = lax.all_gather(weight_out, "shard", axis=0, tiled=True)
    out = lax.dynamic_slice_in_dim(out, place.member * width, width, 0)
    return mine.reshape(model, 3 * width), out


def attend_columns(weight_in, place):
    rows = weight_in.shape[0]
    planes, unit = place.planes, place.unit
    groups, columns = planes // 2, 3 * weight_in.shape[1] // 3 // SPAN
    if 2 * unit == LANES:

        def pick(spot, whole, *outs):
            lane = lax.broadcasted_iota(jnp.int32, (rows, LANES), 1)
            for turn, out in enumerate(outs):
                for low in range(2):
                    for part in range(3):
                        pair = []
                        for group in range(groups):
                            start = ((part * groups + group) * 2 + low) * 2 + (spot[1] ^ turn)
                            source = pl.ds(pl.multiple_of(start * LANES, LANES), LANES)
                            pair.append(whole[:, source].astype(F32))
                        rolled = [pltpu.roll(item, unit, axis=1) for item in pair]
                        cores = (
                            jnp.where(lane < unit, pair[0], rolled[1]),
                            jnp.where(lane < unit, rolled[0], pair[1]),
                        )
                        for core, value in enumerate(cores):
                            out[
                                low,
                                core * rows : (core + 1) * rows,
                                part * LANES : (part + 1) * LANES,
                            ] = value.astype(BF)

        own, other = kernel_call(
            pick,
            "attend_pick",
            [jax.ShapeDtypeStruct((2, 2 * rows, columns), BF)] * 2,
            (place.spot, weight_in),
            scalars=1,
        )
    else:
        blocks = weight_in.reshape(rows, 3, groups, 2, 2, 2, -1)
        blocks = blocks.transpose(4, 3, 5, 0, 1, 2, 6).reshape(2, 2, 2 * rows, columns)
        own = lax.dynamic_index_in_dim(blocks, place.second, 0, keepdims=False)
        other = lax.dynamic_index_in_dim(blocks, 1 - place.second, 0, keepdims=False)
    return own, flipped(other.reshape(4 * rows, columns), 2).reshape(own.shape)


def attend_arrange(own, arrived, glue, place):
    unit, columns = place.unit, own.shape[2]
    size = 4 * unit

    def arrange(spot, own_ref, arrived_ref, glue_ref, near_out, one, two):
        low, core = spot[0] & 1, spot[2]
        for near in range(2):
            source = pl.ds(pl.multiple_of((core ^ near) * unit, unit), unit)
            for turn, ref in enumerate((own_ref, arrived_ref)):
                start = (2 * near + turn) * unit
                mine, other = ref[low, source, :], ref[low ^ 1, source, :]
                near_out[start : start + unit, :] = mine
                two[start : start + unit, :] = mine
                two[size + start : size + start + unit, :] = other
                one[start : start + unit, :] = other
        one[size:, :] = glue_ref[...]
        two[2 * size :, :] = glue_ref[...]

    count = glue.shape[0]
    return kernel_call(
        arrange,
        "attend_columns",
        [
            shape_of(size, columns, BF),
            shape_of(size + count, columns, BF),
            shape_of(2 * size + count, columns, BF),
        ],
        (place.spot, own, arrived, glue),
        scalars=1,
    )


def attend_weights_split(near, glue, travelled, place):
    unit = place.unit
    size = 4 * unit
    columns = near.shape[1]

    def split(near_rows, glue_rows, odd, even, relayed):
        pieces = (near_rows, odd, even, relayed)
        kept = jnp.concatenate([item[: 2 * unit] for item in pieces], axis=0)
        sent = jnp.concatenate([item[2 * unit : size] for item in pieces], axis=0)
        whole = [glue_rows, odd[size:], even[2 * size :], relayed[size:]]
        return kept, sent, jnp.concatenate(whole, axis=0)

    return fused(
        split,
        "attend_split",
        [shape_of(8 * unit, columns, BF)] * 2 + [shape_of(4 * glue.shape[0], columns, BF)],
        near,
        glue,
        *travelled,
    )


def attend_weights_lay(kept, sent, outs, place):
    planes, unit, columns = place.planes, place.unit, kept.shape[1]
    width, model = columns // 3, outs[0].shape[1]
    swapped = flipped(sent, 1)

    def lay(spot, kept_ref, swapped_ref, *refs):
        plane, second, core = spot[0], spot[1], spot[2]
        w_in, w_out = refs[-2:]
        for near, ref in enumerate((kept_ref, swapped_ref)):
            for step in range(planes):
                for turn in range(2):
                    row = (((plane ^ step) * 2 + (second ^ turn)) * 2 + (core ^ near)) * unit
                    start = (2 * step + turn) * unit
                    w_in[pl.ds(pl.multiple_of(row, unit), unit), :] = ref[start : start + unit, :]
        for step, ref in enumerate(refs[:-2]):
            row = ((plane >> 1) ^ step) * unit
            w_out[pl.ds(pl.multiple_of(row, unit), unit), :] = ref[...]

    return kernel_call(
        lay,
        "attend_lay",
        [shape_of(model, columns, BF), shape_of(width, model, BF)],
        (place.spot, kept, swapped, *outs),
        scalars=1,
    )


def attend_grads_whole(grad_in, grad_out, head, place):
    model = grad_out.shape[1]
    heads = model // head
    per_device = heads // SPAN
    whole = jnp.zeros((model, 3, heads, head), F32)
    whole = lax.dynamic_update_slice_in_dim(
        whole,
        grad_in.astype(F32).reshape(model, 3, per_device, head),
        place.member * per_device,
        2,
    )
    whole = lax.psum_scatter(
        whole.reshape(model, 3 * model), "shard", scatter_dimension=0, tiled=True
    )
    out = jnp.zeros((model, model), F32)
    out = lax.dynamic_update_slice_in_dim(
        out, grad_out.astype(F32), place.member * per_device * head, 0
    )
    out = lax.psum_scatter(out, "shard", scatter_dimension=0, tiled=True)
    return rep_sum(whole, place), rep_sum(out, place)


def attend_grads_lay(grad_in, grad_out, place):
    model = grad_out.shape[1]
    planes, unit = place.planes, place.unit
    groups, columns = planes // 2, grad_in.shape[1]

    def lay(spot, w_in, w_out, kept, sent, *outs):
        plane, second, core = spot[0], spot[1], spot[2]
        for near, ref in enumerate((kept, sent)):
            for step in range(planes):
                for turn in range(2):
                    row = (((plane ^ step) * 2 + (second ^ turn)) * 2 + (core ^ near)) * unit
                    start = (2 * step + turn) * unit
                    ref[start : start + unit, :] = w_in[pl.ds(pl.multiple_of(row, unit), unit), :]
        for step, ref in enumerate(outs):
            row = ((plane >> 1) ^ step) * unit
            ref[...] = w_out[pl.ds(pl.multiple_of(row, unit), unit), :]

    return kernel_call(
        lay,
        "attend_unlay",
        [shape_of(2 * planes * unit, columns, BF)] * 2 + [shape_of(unit, model, BF)] * groups,
        (place.spot, grad_in, grad_out),
        scalars=1,
    )


def attend_grads_sum(travelled, place):
    unit = place.unit
    columns, model = travelled[0].shape[1] // 2, travelled[4].shape[1]

    def total(own, one, two, three, *rest):
        even = own.astype(F32) + two.astype(F32)
        odd = one[: three.shape[0]].astype(F32) + three.astype(F32)
        both = jnp.concatenate([even, odd], axis=1)
        out = sum(item.astype(F32) for item in rest)
        return both[:unit], both[unit:], out

    own, other, out = fused(
        total,
        "attend_plane_sum",
        [shape_of(unit, 4 * columns, BF)] * 2 + [shape_of(unit, model, BF)],
        *travelled,
    )
    return own, other, out


def attend_grads_arrive(sums, place):
    own, other, out = sums
    arrived = flipped(other, 2)
    mine = own, arrived, out
    return mine, tuple(flipped(item, place.shards) for item in mine)


def attend_grads_final(mine, theirs, place):
    unit = place.unit
    model = mine[2].shape[1]
    columns = mine[0].shape[1] // 4
    groups = place.planes // 2

    def kernel(spot, *refs):
        values = [refs[i][...].astype(F32) + refs[3 + i][...].astype(F32) for i in range(3)]
        grad_in, grad_out = refs[6:]
        grad_out[0] = values[2]
        lane = lax.broadcasted_iota(jnp.int32, (unit, LANES), 1)
        low_bit, core = spot[0] & 1, spot[2]
        for turn in range(2):
            for low in range(2):
                for part in range(3):
                    blocks = []
                    for near in range(2):
                        start = (2 * low + near) * columns + part * LANES
                        blocks.append(values[turn][:, start : start + LANES])
                    first = jnp.where(core == 0, blocks[0], blocks[1])
                    last = jnp.where(core == 0, blocks[1], blocks[0])
                    pairs = (
                        jnp.where(lane < unit, first, pltpu.roll(last, unit, axis=1)),
                        jnp.where(lane < unit, pltpu.roll(first, unit, axis=1), last),
                    )
                    for group, value in enumerate(pairs):
                        start = ((part * groups + group) * 2 + (low_bit ^ low)) * 2
                        start = (start + (spot[1] ^ turn)) * LANES
                        grad_in[0, :, pl.ds(pl.multiple_of(start, LANES), LANES)] = value

    outs = [
        jax.ShapeDtypeStruct((1, unit, 3 * model), F32),
        jax.ShapeDtypeStruct((1, unit, model), F32),
    ]
    return kernel_call(kernel, "attend_final", outs, (place.spot, *mine, *theirs), scalars=1)


def rep_sum(value, place):
    low = value.astype(BF)
    return low.astype(F32) + flipped(low, place.shards).astype(F32)


def row(wide, index):
    return wide[index : index + 1]


def blocks_of(width, first, model):
    low, high = (0, 2 * model) if first else (2 * model, 3 * model)
    result = []
    for block in range(3 * model // width):
        begin, end = max(block * width, low), min((block + 1) * width, high)
        if begin < end:
            source = slice(begin - block * width, end - block * width)
            result.append((block, source, slice(begin - low, end - low)))
    return result


def conv_pick(weight_in, weight_out, width, place):
    rows, model = weight_out.shape
    half = rows // 2
    whole = half % 16 != 0
    size = rows if whole else half

    def pick(spot, left, right, out):
        source = pl.ds(pl.multiple_of(spot[3] * half, half), half)
        if whole:
            source = slice(0, rows)
        for ref, first in ((left, True), (right, False)):
            for block, own, columns in blocks_of(width, first, model):
                out[block * size : (block + 1) * size, own] = ref[source, columns]

    outs = [shape_of(3 * model // width * size, width, BF)]
    operands = (place.spot, weight_in, weight_out)
    return kernel_call(pick, "conv_pick", outs, operands, scalars=1)[0]


def conv_square(own, masks):
    first, second = masks
    half = own.shape[0] // 2
    return own, flipped(own, first), flipped(own, second), half


def conv_relay(via_first, via_second, masks):
    first, second = masks
    half = via_first.shape[0] // 2
    return flipped(via_first[:half], second), flipped(via_second[half:], first)


def lay_conv(spot, refs, target, unit, first):
    model = target.shape[0]
    plane, second, core, rep = spot[0], spot[1], spot[2], spot[3]
    size = unit if len(refs) == 1 else unit // 2
    width = refs[0].shape[1]
    extent = 3 * model // width * size
    blocks = blocks_of(width, first, model)
    for index, ref in enumerate(refs):
        for local in range(ref.shape[0] // extent):
            start = local * size
            if len(refs) > 1:
                kind, near = index % 5, index // 5
                turn, side = ((0, 0), (0, 1), (1, 0), (1, 1), (1, 1))[kind]
                step = local + (ref.shape[0] // extent if kind == 4 else 0)
                start = (((plane ^ step) * 2 + (second ^ turn)) * 2 + (core ^ near)) * 2
                start = pl.multiple_of((start + (rep ^ side)) * size, size)
            for block, own, columns in blocks:
                source = local * extent + block * size
                target[pl.ds(start, size), columns] = ref[source : source + size, own]


def convolve_start(parts, before, wide, bias_row, weights, place):
    rows, model = before.shape
    count = len(weights)

    def kernel(spot, *refs):
        part_refs, (base, small), weight_refs = refs[:4], refs[4:6], refs[6 : 6 + count]
        current_ref, hidden_ref, doubled_ref, glued_ref, w_in = refs[6 + count :]
        lay_conv(spot, weight_refs, w_in, place.unit, True)
        parts_now = [ref[...] for ref in part_refs]
        current = base[...] + joined(parts_now) + small[bias_row : bias_row + 1, :]
        current_ref[...] = current
        unit, unused_scale = standard(current)
        hidden = (unit * small[7:8, :] + small[8:9, :]).astype(BF)
        hidden_ref[...] = hidden
        doubled = dot_nn(hidden, w_in[...])
        doubled_ref[...] = doubled
        glued_ref[...] = (doubled[:, :model] * logistic(doubled[:, model:])).astype(BF)

    return kernel_call(
        kernel,
        "convolve_start",
        [
            shape_of(rows, model, F32),
            shape_of(rows, model, BF),
            shape_of(rows, 2 * model, F32),
            shape_of(rows, model, BF),
        ],
        (place.spot, *parts, before, wide, *weights),
        scalars=1,
        scratch=[pltpu.VMEM((model, 2 * model), BF)],
        limit=56,
        flops=4 * rows * model * model,
    )


def convolve_finish(glued, border, wide, taps, weights, before, place):
    rows, model = before.shape
    edge = border.shape[0]

    def kernel(spot, glued_ref, border_ref, small, base, *refs):
        weight_refs = refs[: len(weights)]
        mixed_ref, rest_ref, current_ref, hidden_ref, padded, w_out = refs[len(weights) :]
        lay_conv(spot, weight_refs, w_out, place.unit, False)
        padded[:edge, :] = border_ref[...].astype(F32)
        padded[edge:, :] = glued_ref[...].astype(F32)
        first, count = taps
        for column in range(0, model, LANES):
            lanes = slice(column, column + LANES)
            total = jnp.zeros((rows, LANES), F32)
            for tap in range(count):
                start = edge - count + 1 + tap
                weight = small[first + tap : first + tap + 1, lanes]
                total += padded[start : start + rows, lanes] * weight
            mixed_ref[:, lanes] = total
        unit, unused_scale = standard(mixed_ref[...])
        upper = unit * small[9:10, :] + small[10:11, :]
        rest = (upper * logistic(upper)).astype(BF)
        rest_ref[...] = rest
        current = base[...] + dot_nn(rest, w_out[...])
        current_ref[...] = current
        unit, unused_scale = standard(current)
        hidden_ref[...] = (unit * small[11:12, :] + small[12:13, :]).astype(BF)

    return kernel_call(
        kernel,
        "convolve_finish",
        [shape_of(rows, model, dtype) for dtype in (F32, BF, F32, BF)],
        (place.spot, glued, border, wide, before, *weights),
        scalars=1,
        scratch=[pltpu.VMEM((edge + rows, model), F32), pltpu.VMEM((model, model), BF)],
        limit=56,
        flops=2 * rows * model * model,
    )


def convolve_back_start(parts, grad, after, mixed, wide, taps, weights, glued, border, place):
    rows, model = after.shape
    edge = border.shape[0]
    first, count = taps

    def kernel(
        spot, own, part_one, part_two, part_three, grad_ref, after_ref, mixed_ref, small,
        glued_ref, border_ref, *refs,
    ):
        weight_refs = refs[: len(weights)]
        grad_out, branch_ref, main_ref, halo_ref, sums = refs[len(weights) : -3]
        padded, spread, w_out = refs[-3:]
        lay_conv(spot, weight_refs, w_out, place.unit, False)
        incoming = joined((own[...], part_one[...], part_two[...], part_three[...]))
        slope, sum_gain, sum_shift = norm_back(after_ref[...], small[11:12, :], incoming)
        current = grad_ref[...] + slope
        grad_out[...] = current
        branch = current.astype(BF)
        branch_ref[...] = branch
        unit, scale = standard(mixed_ref[...])
        upper = unit * small[9:10, :] + small[10:11, :]
        grad_upper = dot_nt(branch, w_out[...]) * silu_slope(upper)
        inner = grad_upper * small[9:10, :]
        mean = jnp.mean(inner, axis=-1, keepdims=True)
        shared = jnp.mean(inner * unit, axis=-1, keepdims=True)
        padded[:edge, :] = border_ref[...].astype(F32)
        padded[edge:, :] = glued_ref[...].astype(F32)
        spread[:edge, :] = jnp.zeros((edge, model), F32)
        spread[edge : edge + rows, :] = scale * (inner - mean - unit * shared)
        spread[edge + rows :, :] = jnp.zeros((edge, model), F32)
        sums[count : count + 1, :] = column_sum(grad_upper * unit)
        sums[count + 1 : count + 2, :] = column_sum(grad_upper)
        sums[count + 2 : count + 3, :] = sum_gain
        sums[count + 3 : count + 4, :] = sum_shift
        for column in range(0, model, LANES):
            lanes = slice(column, column + LANES)
            total = jnp.zeros((rows + edge, LANES), F32)
            center = spread[edge : edge + rows, lanes]
            for tap in range(count):
                start = edge - count + 1 + tap
                sums[tap : tap + 1, lanes] = jnp.sum(
                    center * padded[start : start + rows, lanes], axis=0, keepdims=True
                )
                begin = count - 1 - tap
                weight = small[first + tap : first + tap + 1, lanes]
                total += spread[begin : begin + rows + edge, lanes] * weight
            halo_ref[:, lanes] = total[:edge].astype(BF)
            main_ref[:, lanes] = total[edge:]

    return kernel_call(
        kernel,
        "convolve_back_start",
        [
            shape_of(rows, model, F32),
            shape_of(rows, model, BF),
            shape_of(rows, model, F32),
            shape_of(edge, model, BF),
            shape_of(count + 4, model, F32),
        ],
        (
            place.spot, *parts, grad, after, mixed, wide, glued, border,
            *weights,
        ),
        scalars=1,
        scratch=[
            pltpu.VMEM((edge + rows, model), F32),
            pltpu.VMEM((rows + 2 * edge, model), F32),
            pltpu.VMEM((model, model), BF),
        ],
        limit=56,
        flops=2 * rows * model * model,
    )


def convolve_back_finish(main, incoming, doubled, weights, before, wide, grad, place):
    rows, model = before.shape
    edge = incoming.shape[0]
    count = len(weights)

    def kernel(spot, main_ref, late, both, base, small, grad_rows, *refs):
        current_ref, branch_ref, slope_ref, sums, w_in = refs[count:]
        lay_conv(spot, refs[:count], w_in, place.unit, True)
        last = main_ref[rows - edge :, :] + late[...].astype(F32)
        glued = jnp.concatenate([main_ref[: rows - edge, :], last], axis=0)
        glued = glued.astype(BF).astype(F32)
        gate = logistic(both[:, model:])
        slope_ref[:, :model] = (glued * gate).astype(BF)
        slope_ref[:, model:] = (glued * both[:, :model] * gate * (1.0 - gate)).astype(BF)
        inner, sum_gain, sum_shift = norm_back(
            base[...], small[7:8, :], dot_nt(slope_ref[...], w_in[...])
        )
        current = grad_rows[...] + inner
        current_ref[...] = current
        branch_ref[...] = current.astype(BF)
        sums[0:1, :] = sum_gain
        sums[1:2, :] = sum_shift
        sums[2:3, :] = column_sum(current.astype(BF))

    return kernel_call(
        kernel,
        "convolve_back_finish",
        [
            shape_of(rows, model, F32),
            shape_of(rows, model, BF),
            shape_of(rows, 2 * model, BF),
            shape_of(3, model, F32),
        ],
        (
            place.spot, main, incoming, doubled, before, wide, grad,
            *weights,
        ),
        scalars=1,
        scratch=[pltpu.VMEM((model, 2 * model), BF)],
        limit=56,
        flops=4 * rows * model * model,
    )


def conv_grads_start(hidden, slope, rest, branch, place):
    model = hidden.shape[1]
    unit, planes = place.unit, place.planes
    size = unit // 2
    halved = place.aligned
    width = 3 * model // 4 if halved else model
    columns = range(0, 3 * model, width)

    def kernel(spot, hidden_ref, slope_ref, rest_ref, branch_ref, kept, sent, total):
        total[:, : 2 * model] = dot_tn(hidden_ref[...], slope_ref[...])
        total[:, 2 * model :] = dot_tn(rest_ref[...], branch_ref[...])
        plane, second, core, rep = spot[0], spot[1], spot[2], spot[3]
        for near, ref in enumerate((kept, sent)):
            if not halved:
                for pair in range(2 * planes):
                    start = pl.multiple_of((pair * 2 + (core ^ near)) * unit, unit)
                    for index, column in enumerate(columns):
                        target = (3 * pair + index) * unit
                        ref[target : target + unit, :] = total[
                            pl.ds(start, unit), column : column + width
                        ].astype(BF)
                continue
            for kind, (turn, side) in enumerate(((0, 0), (0, 1), (1, 0), (1, 1))):
                for step in range(planes):
                    start = (((plane ^ step) * 2 + (second ^ turn)) * 2 + (core ^ near)) * 2
                    start = pl.multiple_of((start + (rep ^ side)) * size, size)
                    for index, column in enumerate(columns):
                        target = ((kind * planes + step) * len(columns) + index) * size
                        ref[target : target + size, :] = total[
                            pl.ds(start, size), column : column + width
                        ].astype(BF)

    return kernel_call(
        kernel,
        "conv_grads",
        [shape_of(len(columns) * model // 2, width, BF)] * 2,
        (place.spot, hidden, slope, rest, branch),
        scalars=1,
        scratch=[pltpu.VMEM((model, 3 * model), F32)],
        flops=6 * hidden.shape[0] * model * model,
        limit=36,
    )


def conv_grads_split(kept, swapped, place):
    count = 4 if place.aligned else 1
    size = kept.shape[0] // count

    def body(kept_part, swapped_part):
        total = kept_part.astype(F32) + swapped_part.astype(F32)
        return [total[index * size : (index + 1) * size] for index in range(count)]

    outs = [shape_of(size, kept.shape[1], BF)] * count
    return list(fused(body, "conv_grads_split", outs, kept, swapped))


def conv_grads_square(shares, masks):
    first, second = masks
    return [
        shares[0],
        flipped(shares[1], first),
        flipped(shares[2], second),
        flipped(shares[3], first | second),
    ]


def plane_pieces(mix_kept, mix_swapped, shares, place):
    planes, unit = place.planes, place.unit
    rows, width = 2 * unit, shares[0].shape[1]
    size = shares[0].shape[0] // planes

    def body(kept, swapped, *values):
        both = jnp.concatenate([kept, swapped], axis=1)
        mix = [both[step * rows : (step + 1) * rows] for step in range(planes)]
        total = sum(value.astype(F32) for value in values).astype(BF)
        conv = [total[step * size : (step + 1) * size] for step in range(planes)]
        joint = jnp.concatenate([mix[1], conv[1], conv[3]], axis=0)
        return mix[0], mix[2], mix[3], conv[0], conv[2], joint

    outs = [shape_of(rows, width, BF)] * 3 + [shape_of(size, width, BF)] * 2
    outs += [shape_of(rows + 2 * size, width, BF)]
    return list(fused(body, "plane_pieces", outs, mix_kept, mix_swapped, *shares))


def conv_grads_top(own, joint):
    size = own.shape[0]

    def body(mine, arrived):
        return (mine.astype(F32) + arrived[arrived.shape[0] - size :].astype(F32),)

    return fused(body, "conv_grads_top", [shape_of(*own.shape, BF)], own, joint)[0]


def conv_grads_sum(own, joint, last):
    size = own.shape[0]

    def body(mine, arrived, late):
        start = arrived.shape[0] - 2 * size
        near = arrived[start : start + size]
        return (mine.astype(F32) + near.astype(F32) + late.astype(F32),)

    return fused(body, "conv_grads_sum", [shape_of(*own.shape, BF)], own, joint, last)[0]


def conv_grads_whole(total, place):
    groups = [list(range(core, place.shards, 2)) for core in range(2)]
    mine = lax.psum_scatter(
        total, "shard", scatter_dimension=0, tiled=True, axis_index_groups=groups
    )
    return rep_sum(mine, place).reshape(3, place.unit, -1)


def conv_grads_final(mine, theirs, place):
    size, width = place.unit // 2, mine.shape[1]
    model = width * mine.shape[0] // size // 3

    def kernel(spot, mine_ref, theirs_ref, grad_in, grad_out):
        for turn, ref in enumerate((mine_ref, theirs_ref)):
            target = pl.ds(pl.multiple_of((spot[3] ^ turn) * size, size), size)
            for out, first in ((grad_in, True), (grad_out, False)):
                for block, own, columns in blocks_of(width, first, model):
                    value = ref[block * size : (block + 1) * size, own]
                    out[0, target, columns] = value.astype(F32)

    outs = [
        jax.ShapeDtypeStruct((1, 2 * size, 2 * model), F32),
        jax.ShapeDtypeStruct((1, 2 * size, model), F32),
    ]
    return kernel_call(kernel, "conv_final", outs, (place.spot, mine, theirs), scalars=1)


def feed_to_attend(parts, before, wide):
    rows, model = before.shape

    def body(*values):
        base, small = values[4:]
        current = base.astype(F32) + 0.5 * (joined(values[:4]) + row(small, 2))
        unit, unused_scale = standard(current)
        return current, unit * row(small, 3) + row(small, 4)

    outs = [shape_of(rows, model, F32), shape_of(rows, model, BF)]
    return fused(body, "feed_to_attend", outs, *parts, before, wide)


def turn_around(parts, before, wide, cotangent):
    rows, model = before.shape

    def body(*values):
        base, small, grad = values[4:]
        current = base + 0.5 * (joined(values[:4]) + row(small, 13))
        unit, unused_scale = standard(current)
        slope, sum_gain, sum_shift = norm_back(current, row(small, 14), grad.astype(F32))
        branch = (0.5 * slope).astype(BF)
        sums = jnp.concatenate([column_sum(branch), sum_gain, sum_shift], axis=0)
        return unit * row(small, 14) + row(small, 15), slope, branch, sums

    outs = [
        shape_of(rows, model, BF),
        shape_of(rows, model, F32),
        shape_of(rows, model, BF),
        shape_of(3, model, F32),
    ]
    return fused(body, "turn_around", outs, *parts, before, wide, cotangent)


def attend_to_feed_back(parts, grad, before, wide):
    rows, model = before.shape

    def body(*values):
        grad_rows, base, small = values[4:]
        slope, sum_gain, sum_shift = norm_back(base, row(small, 3), joined(values[:4]))
        current = grad_rows + slope
        branch = (0.5 * current).astype(BF)
        sums = jnp.concatenate([column_sum(branch), sum_gain, sum_shift], axis=0)
        return current, branch, sums

    outs = [shape_of(rows, model, F32), shape_of(rows, model, BF), shape_of(3, model, F32)]
    return fused(body, "attend_to_feed_back", outs, *parts, grad, before, wide)


def last_step(parts, grad, before, wide):
    rows, model = before.shape

    def body(*values):
        grad_rows, base, small = values[4:]
        slope, sum_gain, sum_shift = norm_back(
            base.astype(F32), row(small, 0), joined(values[:4])
        )
        return grad_rows + slope, jnp.concatenate([sum_gain, sum_shift], axis=0)

    outs = [shape_of(rows, model, F32), shape_of(2, model, F32)]
    return fused(body, "last_step", outs, *parts, grad, before, wide)


def small_unpack(gathered, counts, place):
    rows, modules_rows = counts
    shards, unit, half, planes = place.shards, place.unit, place.half, place.planes
    model = shards * unit
    if not place.aligned:
        wide = gathered[:, :rows].transpose(1, 0, 2).reshape(rows, model).astype(F32)
        bias = gathered[:, rows:].reshape(planes, 2, 2, 2, 2, half)
        bias = lax.dynamic_index_in_dim(bias, place.second, 1, keepdims=False)
        bias = lax.dynamic_index_in_dim(bias, place.rep, 3, keepdims=False)
        bias = bias.transpose(2, 0, 1, 3).reshape(2, -1).astype(F32)
        heads = [
            lax.dynamic_slice_in_dim(wide[index].reshape(SPAN, -1), place.member, 1, 0)
            for index in (5, 6)
        ]
        return wide, bias, jnp.concatenate([heads[0], jnp.zeros_like(heads[0]), heads[1]], axis=1)

    def kernel(spot, ref, wide, bias, mix):
        lane = lax.broadcasted_iota(jnp.int32, (1, LANES), 1)
        second, core, rep = spot[1], spot[2], spot[3]
        member = (spot[0] & 1) * 4 + second * 2 + core

        def doubled(value):
            return jnp.concatenate([value, value], axis=1)

        for pair in range(shards // 2):
            both = [doubled(ref[2 * pair + side].astype(F32)) for side in range(2)]
            value = jnp.where(lane < unit, both[0], both[1])
            wide[:, pair * LANES : (pair + 1) * LANES] = value[:rows]
        for module in range(2):
            for index in range(2 * planes):
                shard = (index // 2 * 2 + second) * 2 + index % 2
                block = doubled(ref[shard].astype(F32))
                start = rows + (module * 2) * 2
                options = [
                    jnp.where(
                        lane < unit,
                        block[start + 2 * side : start + 2 * side + 1],
                        block[start + 2 * side + 1 : start + 2 * side + 2],
                    )
                    for side in range(2)
                ]
                value = jnp.where(rep == 0, options[0], options[1])
                bias[module : module + 1, index * half : (index + 1) * half] = value
        mix[...] = jnp.zeros_like(mix)
        pair = [doubled(ref[member + SPAN * group].astype(F32)) for group in range(2)]
        value = jnp.where(lane < unit, pair[0], pair[1])
        mix[:, :LANES] = value[5:6]
        mix[:, 2 * LANES :] = value[6:7]

    outs = [
        shape_of(rows, model, F32),
        shape_of(2, 2 * planes * half, F32),
        shape_of(1, 3 * LANES, F32),
    ]
    return kernel_call(kernel, "small_unpack", outs, (place.spot, gathered), scalars=1)


def shard_gather(value, place):
    copies = jnp.broadcast_to(value[None], (place.shards, *value.shape))
    return lax.all_to_all(copies, "shard", 0, 0, tiled=True)


def small_reduce(sums, mix_sums, biases, distance, counts, place):
    input_sums, first_sums, attend_sums, conv_sums, last_sums = sums
    rows, taps = counts
    unit, half, planes, shards = place.unit, place.half, place.planes, place.shards
    model = unit * shards
    width = mix_sums.shape[1] // 3
    if not place.aligned:
        heads = []
        for start in (0, 2 * width):
            whole = jnp.zeros((SPAN, model // SPAN), F32)
            block = mix_sums[:, start : start + width]
            whole = lax.dynamic_update_slice_in_dim(whole, block, place.member, 0)
            heads.append(whole.reshape(1, model))
        wide = jnp.concatenate(
            [
                input_sums, first_sums, *heads, attend_sums[:2], conv_sums[taps:], last_sums,
                attend_sums[2:], conv_sums[:taps],
            ],
            axis=0,
        )
        wide = wide.reshape(-1, shards, unit).transpose(1, 0, 2)
        pair = jnp.stack(biases).reshape(2, planes, 2, half)
        bias = lax.dynamic_update_slice(
            jnp.zeros((planes, 2, 2, 2, 2, half), F32),
            pair.transpose(1, 2, 0, 3)[:, None, :, :, None, :],
            (0, place.second, 0, 0, place.rep, 0),
        ).reshape(shards, -1, unit)
        both = jnp.concatenate([wide, bias], axis=1)
        both = lax.all_to_all(
            jnp.concatenate([both, both], axis=0), ("rep", "shard"), 0, 0, tiled=True
        )
        total = jnp.sum(both, axis=0)
        for bit in range((2 * shards).bit_length() - 1):
            distance = distance + flipped(distance, 1 << bit)
        return total[:rows], total[rows:].reshape(2, 2 * half), distance
    extent = -(-(rows + 8) // 32) * 32
    size = extent // 2
    table_rows = distance.shape[0]
    fold = -(-table_rows // 32) * 16

    def pack(spot, in_ref, first, attend_ref, conv, last, mix, bias_one, bias_two, table, out, wide):
        plane, second, core, rep = spot[0], spot[1], spot[2], spot[3]
        wide[...] = jnp.zeros_like(wide)
        wide[0:2, :] = in_ref[...]
        wide[2:5, :] = first[...]
        wide[7:9, :] = attend_ref[0:2, :]
        wide[9:13, :] = conv[taps:, :]
        wide[13:16, :] = last[...]
        wide[16:17, :] = attend_ref[2:3, :]
        wide[17 : 17 + taps, :] = conv[:taps, :]
        lane = lax.broadcasted_iota(jnp.int32, (1, LANES), 1)
        for group in range(2):
            start = ((group * 2 + (plane & 1)) * 2 + second) * LANES
            target = pl.ds(pl.multiple_of(start, LANES), LANES)
            for index, begin in ((5, 0), (6, 2 * width)):
                value = mix[:, begin : begin + LANES]
                moved = pltpu.roll(jnp.broadcast_to(value, (8, LANES)), unit, axis=1)[:1]
                low = value if group == 0 else moved
                high = moved if group == 0 else value
                placed = jnp.where(core == 0, low, high)
                placed = jnp.where(lane // unit == core, placed, 0.0)
                wide[index : index + 1, target] = placed
        for module, ref in enumerate((bias_one, bias_two)):
            for index in range(planes):
                pair = [
                    ref[:, start * half : (start + 1) * half]
                    for start in (2 * index, 2 * index + 1)
                ]
                moved = [
                    pltpu.roll(jnp.broadcast_to(item, (8, LANES)), unit, axis=1)[:1]
                    for item in pair
                ]
                halves = (
                    jnp.where(lane < unit, pair[0], moved[1]),
                    jnp.where(lane < unit, moved[0], pair[1]),
                )
                start = pl.multiple_of((index * 2 + second) * LANES, LANES)
                for side in range(2):
                    for part, value in enumerate(halves):
                        line = rows + (module * 2 + side) * 2 + part
                        wide[line : line + 1, pl.ds(start, LANES)] = jnp.where(
                            rep == side, value, 0.0
                        )
        rest = jnp.concatenate(
            [table[fold:, :], jnp.zeros((2 * fold - table_rows, unit), F32)], axis=0
        )
        folded = jnp.concatenate([table[:fold, :], rest], axis=1)
        folded = folded.astype(BF)
        wide_lane = lax.broadcasted_iota(jnp.int32, (size, LANES), 1)
        for pair in range(shards // 2):
            block = wide[:, pair * LANES : (pair + 1) * LANES]
            upper, lower = block[:size], block[size:]
            both = (
                jnp.where(wide_lane < unit, upper, pltpu.roll(lower, unit, axis=1)),
                jnp.where(wide_lane < unit, pltpu.roll(upper, unit, axis=1), lower),
            )
            for side in range(2):
                for target in (2 * pair + side, 2 * pair + side + shards):
                    out[target, :size, :] = both[side].astype(BF)
                    out[target, size:, :] = folded

    packed = kernel_call(
        pack,
        "small_pack",
        [jax.ShapeDtypeStruct((2 * shards, size + fold, LANES), BF)],
        (place.spot, *sums, mix_sums, *biases, distance),
        scalars=1,
        scratch=[pltpu.VMEM((extent, model), F32)],
    )[0]
    packed = lax.all_to_all(packed, ("rep", "shard"), 0, 0, tiled=True)

    def unpack(spot, ref, wide, bias, table):
        total = ref[0].astype(F32)
        for index in range(1, 2 * shards):
            total = total + ref[index].astype(F32)
        moved = pltpu.roll(total, unit, axis=1)
        table[:fold, :] = total[size:, :unit]
        table[fold:, :] = moved[size : size + table_rows - fold, :unit]
        both = jnp.concatenate([total[:size, :unit], moved[:size, :unit]], axis=0)
        wide[...] = both[:rows]
        for module in range(2):
            for side in range(2):
                line = rows + (module * 2 + side) * 2
                bias[module : module + 1, side * half : (side + 1) * half] = jnp.concatenate(
                    [both[line : line + 1], both[line + 1 : line + 2]], axis=1
                )

    return kernel_call(
        unpack,
        "small_sum",
        [shape_of(rows, unit, F32), shape_of(2, 2 * half, F32), shape_of(*distance.shape, F32)],
        (place.spot, packed),
        scalars=1,
    )


class Place:
    def __init__(self, unit, half, head):
        self.shards = lax.axis_size("shard")
        self.planes = self.shards // QUAD
        self.unit, self.half = unit, half
        self.pack_rows = 2 * unit + half
        self.rep = lax.axis_index("rep")
        self.shard = lax.axis_index("shard")
        self.core = self.shard % 2
        self.second = self.shard // 2 % 2
        self.plane = self.shard // QUAD
        self.member = self.shard % SPAN
        self.spot = jnp.stack([self.plane, self.second, self.core, self.rep])
        self.flat_spot = jnp.stack([jnp.zeros_like(self.plane), self.second, self.core, self.rep])
        self.span_spot = self.member.reshape(1)
        self.aligned = whole_heads(head, self)
        self.feed_masks = (self.shards, 2)
        self.span_masks = (4, 2)


def along(value, by, place):
    count = place.shards
    route = [(i, i + by) for i in range(count) if 0 <= i + by < count]
    return lax.ppermute(value, "shard", route)


def shards(
    inputs,
    ff_in,
    ff_out,
    ff_bias,
    attn_in,
    attn_out,
    conv_in,
    conv_out,
    depthwise,
    distance,
    vectors,
    attn_bias,
    cotangent,
):
    rows, model = inputs.shape
    unit, half = ff_in.shape[2], ff_out.shape[2] // 2
    head = distance.shape[2]
    place = Place(unit, half, head)
    tap_count = depthwise.shape[1]
    edge = -(-(tap_count - 1) // 16) * 16
    bias_rows = ff_bias.shape[2] // unit
    count = vectors.shape[1]
    taps = (count + 1, tap_count)
    wide_rows = count + 1 + tap_count

    first_parts = feed_pack(ff_in, ff_out, 0, place)
    small = jnp.concatenate(
        [vectors[0], attn_bias, depthwise[0], ff_bias[0].reshape(2 * bias_rows, unit)], axis=0
    )
    first_pack = pack_rows(first_parts)
    first_pack, current, mix_in, later_in = tied(first_pack, inputs, attn_in[0], ff_in)
    first_far = plane_start(first_pack, place)
    pieces = square_gather(current, place.feed_masks)
    second_parts = feed_pack(later_in, ff_out, 1, place)
    columns = attend_columns(mix_in, place) if place.aligned else (mix_in, mix_in)
    (
        first_far[0], first_far[1], small, second_in, second_other, second_out, *early
    ) = tied(*first_far, small, *second_parts, *columns, *pieces)
    columns, pieces = early[:2], early[2:]
    small = shard_gather(small, place)
    second_pack = pack_rows((second_in, second_other, second_out))
    glue_width = 3 * model // SPAN if place.aligned else model
    glue = conv_pick(conv_in[0], conv_out[0], glue_width, place)
    if place.aligned:
        columns = attend_arrange(*columns, glue, place)
    first_near = plane_finish(first_pack, first_far, place)
    last = place.planes - 1
    first_near[last], small, glue, second_pack, *columns = tied(
        first_near[last], small, glue, second_pack, *columns
    )
    first_packs = with_core(first_near)
    wide, feed_bias, mix_bias = small_unpack(small, (wide_rows, 2 * bias_rows), place)
    table = wide_table(distance[0], rows)
    wide, mix_bias, table, pieces[0] = tied(wide, mix_bias, table, pieces[0])

    parts, saved_first = feed(
        pieces, first_packs, feed_bias[0:1], wide, 0, place.feed_masks, place
    )
    if place.aligned:
        mix_near, one, two = columns
        odd, even = flipped(one, QUAD), flipped(two, 2 * QUAD)
        parts, (odd, even, mix_out) = tied_lists(parts, (odd, even, attn_out[0]))
        mix_outs = [mix_out, flipped(mix_out, SPAN)]
        relayed = flipped(even[4 * unit :], QUAD)
    after_first, hidden = feed_to_attend(parts, inputs, wide)
    near, far = group_gather(hidden, place.span_masks)
    if place.aligned:
        near, far, (relayed, second_pack, mix_outs[1]) = tied_lists(
            near, far, (relayed, second_pack, mix_outs[1])
        )
        mix_kept, mix_sent, glue = attend_weights_split(
            mix_near, glue, (odd, even, relayed), place
        )
        mix_in, mix_out = attend_weights_lay(mix_kept, mix_sent, mix_outs, place)
        glue, via_first, via_second, unused_half = conv_square(glue, place.feed_masks)
    else:
        mix_in, mix_out = attend_weights_whole(attn_in[0], attn_out[0], head, place)
        glue = [lax.all_gather(glue, "shard", axis=0, tiled=True)]
        near, far, (second_pack,) = tied_lists(near, far, (second_pack,))
    second_far = plane_start(second_pack, place)
    saved_attend, kept, sent = attend((near, far), mix_in, mix_bias, mix_out, table, place)
    if place.aligned:
        sent, via_first, via_second = tied(sent, via_first, via_second)
        low, high = conv_relay(via_first, via_second, place.feed_masks)
    sent, *second_far = tied(sent, *second_far)
    parts = group_reduce(kept, sent, place.span_masks)
    if place.aligned:
        parts, glue, (second_pack, *second_far) = tied_lists(
            parts, (glue, via_first, via_second, low, high), (second_pack, *second_far)
        )
        glue = [*glue, *(flipped(item, 1) for item in glue)]
    else:
        parts, (second_pack, *second_far) = tied_lists(parts, (second_pack, *second_far))
    second_near = plane_finish(second_pack, second_far, place)
    after_attend, conv_hidden, doubled, glued = convolve_start(
        parts, after_first, wide, count, glue, place
    )
    border = along(glued[rows - edge :], 1, place)
    border = jnp.where(place.member == 0, jnp.zeros_like(border), border)
    border, *second_near = tied(border, *second_near)
    second_packs = with_core(second_near)
    mixed, rest, after_conv, hidden = convolve_finish(
        glued, border, wide, taps, glue, after_attend, place
    )
    hidden, *second_packs = tied(hidden, *second_packs)
    pieces = square_gather(hidden, place.feed_masks)
    parts, saved_second = feed(
        pieces, second_packs, feed_bias[1:2], wide, None, place.feed_masks, place
    )
    output, grad_last, branch, last_sums = turn_around(parts, after_conv, wide, cotangent)

    pieces = square_gather(branch, place.feed_masks)
    result, branch, slope, second_bias = feed_back(pieces, second_packs, saved_second, place)
    second_grads = [
        *feed_in_grads(saved_second[0], slope, place),
        *feed_out_grads(saved_second[2], pieces, place),
    ]
    *result, second_grads[1], second_grads[3] = tied(*result, second_grads[1], second_grads[3])
    second_grads[1], second_grads[3] = flipped(second_grads[1], 1), flipped(second_grads[3], 1)
    parts = square_reduce(result, place.feed_masks)
    second_split = [plane_split(*pair, place) for pair in (second_grads[:2], second_grads[2:])]
    parts, *second_split = tied_lists(parts, *second_split)
    second_lists = [plane_early(pieces, place) for pieces in second_split]
    grad_conv, conv_branch, main, halo, conv_sums = convolve_back_start(
        parts, grad_last, after_conv, mixed, wide, taps, glue, glued, border, place
    )
    incoming = along(halo, -1, place)
    incoming, second_tops = tied_tops(incoming, second_lists, place)
    second_early = [lists[0] for lists in second_lists]
    incoming = jnp.where(place.member == SPAN - 1, jnp.zeros_like(incoming), incoming)
    grad_attend, branch, slope, attend_sums = convolve_back_finish(
        main, incoming, doubled, glue, after_attend, wide, grad_conv, place
    )
    conv_kept, conv_sent = conv_grads_start(conv_hidden, slope, rest, conv_branch, place)
    second_tops = [plane_total(values) for values in second_tops]
    count_early = len(second_early[0])
    branch, conv_kept, conv_sent, *flat = tied(
        branch, conv_kept, conv_sent, *second_tops, *second_early[0], *second_early[1]
    )
    second_tops = flat[:2]
    second_early = [flat[2 : 2 + count_early], flat[2 + count_early :]]
    near, far = group_gather(branch, place.span_masks)
    conv_shares = conv_grads_split(conv_kept, flipped(conv_sent, 1), place)
    near, far, conv_shares, second_tops = tied_lists(near, far, conv_shares, second_tops)
    if place.aligned:
        conv_shares = conv_grads_square(conv_shares, place.feed_masks)
    second_lasts = [plane_last(top, place) for top in second_tops]
    back = attend_back((near, far), saved_attend, mix_in, mix_out, table, place)
    grad_mixed, kept, sent, branch, grad_table, table_far = back
    (sent,), second_lasts, conv_shares = tied_lists((sent,), second_lasts, conv_shares)
    mix_grad_in, mix_grad_out, mix_sums = attend_grads(saved_attend, grad_mixed, branch, place)
    second_sums = [plane_add([*own, last]) for own, last in zip(second_early, second_lasts)]
    second_other = flipped(second_sums[0][unit:], 2)
    if place.aligned:
        mix_kept, mix_swap, *mix_outs = attend_grads_lay(mix_grad_in, mix_grad_out, place)
        kept, mix_swap = tied(kept, mix_swap)
        mix_swap = flipped(mix_swap, 1)
        kept, mix_swap = tied(kept, mix_swap)
    kept, second_other = tied(kept, second_other)
    second_pack = pack_rows((second_sums[0][:unit], second_other, second_sums[1]))
    second_theirs = flipped(second_pack, place.shards)
    parts = group_reduce(kept, sent, place.span_masks)
    if place.aligned:
        mix_outs[1] = flipped(mix_outs[1], SPAN)
        planed = plane_pieces(mix_kept, mix_swap, conv_shares, place)
        parts, (second_theirs, mix_outs[1]), planed = tied_lists(
            parts, (second_theirs, mix_outs[1]), planed
        )
    else:
        parts, (second_theirs,) = tied_lists(parts, (second_theirs,))
    grad_distance = distance_gradient(grad_table, table_far, rows)
    grad_first, branch, first_sums = attend_to_feed_back(parts, grad_attend, after_first, wide)
    if place.aligned:
        (branch,), planed = tied_lists((branch,), planed)
        mix_zero, mix_two, mix_three, conv_zero, conv_two, joint = planed
        pieces = square_gather(branch, place.feed_masks)
        joint = flipped(joint, QUAD)
        mix_two = flipped(mix_two, 2 * QUAD)
        pieces, (mix_two, mix_three, joint) = tied_lists(pieces, (mix_two, mix_three, joint))
        mix_three = flipped(mix_three, 3 * QUAD)
        conv_last = plane_last(conv_grads_top(conv_two, joint), place)
    else:
        pieces = square_gather(branch, place.feed_masks)
        conv_whole = conv_grads_whole(conv_shares[0], place)
        mix_grads = attend_grads_whole(mix_grad_in, mix_grad_out, head, place)
        mix_grads = [item[None] for item in mix_grads]
    kept, sent = feed_out_grads(saved_first[2], pieces, place)
    out_split = plane_split(kept, flipped(sent, 1), place)
    pieces, out_split = tied_lists(pieces, out_split)
    out_lists = plane_early(out_split, place)
    result, branch, slope, first_bias = feed_back(pieces, first_packs, saved_first, place)
    slope, (out_top,) = tied_tops(slope, [out_lists], place)
    out_early = out_lists[0]
    if place.aligned:
        slope, conv_last = tied(slope, conv_last)
        conv_mine = conv_grads_sum(conv_zero, joint, conv_last)
    kept, sent = feed_in_grads(saved_first[0], slope, place)
    kept, *result = tied(kept, *result)
    in_swapped = flipped(sent, 1)
    in_lists = plane_early(plane_split(kept, in_swapped, place), place)
    parts = square_reduce(result, place.feed_masks)
    out_last = plane_last(plane_total(out_top), place)
    parts, out_early, *in_lists = tied_lists(parts, out_early, *in_lists.values())
    in_early, in_top = in_lists[0], in_lists[-1]
    in_last = plane_last(plane_total(in_top), place)
    if place.aligned:
        parts[0], mix_three = tied(parts[0], mix_three)
        mix_own, mix_other, mix_out_sum = attend_grads_sum(
            (mix_zero, joint, mix_two, mix_three, *mix_outs), place
        )
        mix_arrived = flipped(mix_other, 2)
        mix_theirs = [flipped(mix_own, place.shards), None, flipped(mix_out_sum, place.shards)]
        conv_theirs = flipped(conv_mine, place.shards)
    grad_input, input_sums = last_step(parts, grad_first, inputs, wide)
    if place.aligned:
        input_sums, out_last, mix_arrived = tied(input_sums, out_last, mix_arrived)
        mix_theirs[1] = flipped(mix_arrived, place.shards)
    out_sum = plane_add([*out_early, out_last])
    out_theirs = flipped(out_sum, place.shards)
    if place.aligned:
        mix_grads = attend_grads_final((mix_own, mix_arrived, mix_out_sum), mix_theirs, place)
        conv_grads = conv_grads_final(conv_mine, conv_theirs, place)
    else:
        conv_grads = (
            jnp.concatenate([conv_whole[0], conv_whole[1]], axis=1)[None],
            conv_whole[2][None],
        )

    (in_last, input_sums, out_theirs), mix_grads, conv_grads = tied_lists(
        (in_last, input_sums, out_theirs), mix_grads, conv_grads
    )
    in_sum = plane_add([*in_early, in_last])
    in_own, in_other = in_sum[:unit], flipped(in_sum[unit:], 2)
    in_theirs = flipped(in_own, place.shards)
    input_sums, in_other, in_theirs = tied(input_sums, in_other, in_theirs)
    first_mine = [(in_own, in_theirs), (in_other, flipped(in_other, place.shards))]
    small_grads, bias_grads, grad_distance = small_reduce(
        (input_sums, first_sums, attend_sums, conv_sums, last_sums),
        mix_sums,
        (first_bias, second_bias),
        grad_distance,
        (wide_rows, tap_count),
        place,
    )
    first_mine = [*first_mine, (out_sum, out_theirs)]
    cuts = (0, unit, 2 * unit, 2 * unit + half)
    second_mine = [
        (second_pack[cuts[i] : cuts[i + 1]], second_theirs[cuts[i] : cuts[i + 1]])
        for i in range(3)
    ]
    feed_grads = feed_final((first_mine, second_mine), place)
    return (
        output,
        grad_input,
        *feed_grads,
        bias_grads[None],
        *mix_grads,
        *conv_grads,
        small_grads[count + 1 :][None],
        grad_distance[None],
        small_grads[:count][None],
        small_grads[count : count + 1],
    )


def solution(mesh):
    in_specs = (
        P(("rep", "shard"), None),
        P(None, None, "shard", None),
        P(None, None, "shard", None),
        P(None, None, "shard"),
        P(None, "shard", None),
        P(None, "shard", None),
        P(None, "shard", None),
        P(None, "shard", None),
        P(None, None, "shard"),
        P(),
        P(None, None, "shard"),
        P(None, "shard"),
        P(("rep", "shard"), None),
    )
    out_specs = (
        P(("rep", "shard"), None),
        P(("rep", "shard"), None),
        P(None, None, "shard", None),
        P(None, None, "shard", None),
        P(None, None, "shard"),
        P(None, "shard", None),
        P(None, "shard", None),
        P(None, "shard", None),
        P(None, "shard", None),
        P(None, None, "shard"),
        P(),
        P(None, None, "shard"),
        P(None, "shard"),
    )
    return jax.shard_map(shards, mesh=mesh, in_specs=in_specs, out_specs=out_specs, check_vma=False)
```

```python
import jax
import jax.numpy as jnp
from jax import lax
from jax.experimental import pallas as pl
from jax.experimental.pallas import tpu as pltpu
from jax.sharding import PartitionSpec as P

LEFT = 64
RIGHT = 8
SPAN = 8
QUAD = 4
EPSILON = 1e-05
BF = jnp.bfloat16
F32 = jnp.float32
MIB = 1 << 20
LANES = 128


def dot_nn(left, right):
    return jnp.dot(left, right, preferred_element_type=F32)


def dot_nt(left, right):
    return lax.dot_general(left, right, (((1,), (1,)), ((), ())), preferred_element_type=F32)


def dot_tn(left, right):
    return lax.dot_general(left, right, (((0,), (0,)), ((), ())), preferred_element_type=F32)


def column_sum(values):
    return jnp.sum(values.astype(F32), axis=0, keepdims=True)


def standard(values):
    center = values - jnp.mean(values, axis=-1, keepdims=True)
    scale = lax.rsqrt(jnp.mean(center * center, axis=-1, keepdims=True) + EPSILON)
    return center * scale, scale


def norm_back(values, gain, grad):
    unit, scale = standard(values)
    inner = grad * gain
    first = jnp.mean(inner, axis=-1, keepdims=True)
    second = jnp.mean(inner * unit, axis=-1, keepdims=True)
    return scale * (inner - first - unit * second), column_sum(grad * unit), column_sum(grad)


def logistic(values):
    return 1.0 / (1.0 + jnp.exp(-values))


def silu_slope(values):
    gate = logistic(values)
    return gate * (1.0 + values * (1.0 - gate))


def vmem(count):
    return [pl.BlockSpec(memory_space=pltpu.VMEM)] * count


def shape_of(rows, columns, dtype):
    return jax.ShapeDtypeStruct((rows, columns), dtype)


class Part:
    def __init__(self, array, block, index):
        self.array, self.block, self.index = array, block, index
        self.shape, self.dtype = block, array.dtype
        self.size = 1
        for extent in block:
            self.size *= extent


def kernel_call(body, name, outs, operands, scalars=0, scratch=(), flops=0, limit=24):
    moved = sum(item.size * item.dtype.itemsize for item in (*operands[scalars:], *outs))
    specs = [pl.BlockSpec(memory_space=pltpu.SMEM)] * scalars
    arrays = list(operands[:scalars])
    for item in operands[scalars:]:
        if isinstance(item, Part):
            specs.append(pl.BlockSpec(item.block, lambda step, index=item.index: index))
            arrays.append(item.array)
        else:
            specs += vmem(1)
            arrays.append(item)
    return pl.pallas_call(
        body,
        grid=(1,),
        in_specs=specs,
        out_specs=vmem(len(outs)),
        out_shape=list(outs),
        scratch_shapes=list(scratch),
        compiler_params=pltpu.CompilerParams(vmem_limit_bytes=limit * MIB),
        cost_estimate=pl.CostEstimate(flops=flops, bytes_accessed=moved, transcendentals=0),
        name=name,
    )(*arrays)


def fused(body, name, outs, *operands, flops=0):
    def kernel(*refs):
        results = body(*[ref[...] for ref in refs[: len(operands)]])
        for ref, value in zip(refs[len(operands) :], results):
            ref[...] = value.astype(ref.dtype)

    return kernel_call(kernel, name, outs, operands, flops=flops)


def tied(*values):
    return lax.optimization_barrier(values)


def tied_lists(*lists):
    flat = iter(tied(*[item for values in lists for item in values]))
    return [[next(flat) for _ in values] for values in lists]


def flipped(value, mask):
    total = lax.axis_size("rep") * lax.axis_size("shard")
    return lax.ppermute(value, ("rep", "shard"), [(i, i ^ mask) for i in range(total)])


def square_gather(value, masks):
    first, second = masks
    return [
        value,
        flipped(value, first),
        flipped(value, second),
        flipped(value, first | second),
    ]


def square_reduce(parts, masks):
    first, second = masks
    own, via_first, via_second, cross = parts
    return [
        own,
        flipped(cross, first | second),
        flipped(via_first, first),
        flipped(via_second, second),
    ]


def joined(parts):
    return parts[0] + sum(part.astype(F32) for part in parts[1:])


def place_feed(spot, views, w_in, w_out, unit, half):
    plane, second, core = spot[0], spot[1], spot[2]
    for step, near, in_ref, out_ref, start in views:
        column = (plane ^ step) * 2
        for turn in range(2):
            row = ((column + (second ^ turn)) * 2 + (core ^ near)) * unit
            source = slice(turn * unit, (turn + 1) * unit)
            w_in[pl.ds(pl.multiple_of(row, unit), unit), :] = in_ref[source, :]
        row = (column + (core ^ near)) * half
        w_out[pl.ds(pl.multiple_of(row, half), half), :] = out_ref[start : start + half, :]


def pack_views(refs, place):
    planes, count = place.planes, 2 * place.planes
    if len(refs) == count:
        return [(i % planes, i // planes, ref, ref, 2 * place.unit) for i, ref in enumerate(refs)]
    return [(i % planes, i // planes, refs[i], refs[count + i], 0) for i in range(count)]


def feed(pieces, packs, bias, wide, norm_row, masks, place):
    rows, model = pieces[0].shape
    inner = bias.shape[1]
    count, total = len(pieces), len(pieces) * rows
    unit, half = place.unit, place.half

    def kernel(spot_ref, *refs):
        piece_refs, pack_refs = refs[:count], refs[count : count + len(packs)]
        bias_ref, wide_ref, hidden, upper, active = refs[count + len(packs) :][:5]
        outs = refs[count + len(packs) + 5 : -2]
        w_in, w_out = refs[-2:]
        place_feed(spot_ref, pack_views(pack_refs, place), w_in, w_out, unit, half)
        for index, ref in enumerate(piece_refs):
            block = ref[...]
            if norm_row is not None:
                scaled, unused_scale = standard(block.astype(F32))
                gain = wide_ref[norm_row : norm_row + 1, :]
                shift = wide_ref[norm_row + 1 : norm_row + 2, :]
                block = (scaled * gain + shift).astype(BF)
            hidden[index * rows : (index + 1) * rows, :] = block
        before = dot_nn(hidden[...], w_in[...]) + bias_ref[...]
        upper[...] = before
        active[...] = (before * logistic(before)).astype(BF)
        result = dot_nn(active[...], w_out[...])
        for index, ref in enumerate(outs):
            ref[...] = result[index * rows : (index + 1) * rows].astype(ref.dtype)

    outs = [
        shape_of(total, model, BF),
        shape_of(total, inner, F32),
        shape_of(total, inner, BF),
        shape_of(rows, model, F32),
    ] + [shape_of(rows, model, BF)] * (count - 1)
    results = kernel_call(
        kernel,
        "feed_forward",
        outs,
        (place.spot, *pieces, *packs, bias, wide),
        scalars=1,
        scratch=[pltpu.VMEM((model, inner), BF), pltpu.VMEM((inner, model), BF)],
        flops=4 * total * model * inner,
    )
    return square_reduce(results[3:], masks), results[:3]


def feed_back(pieces, packs, saved, place):
    hidden, upper, active = saved
    rows, model = pieces[0].shape
    total, inner = upper.shape
    count = len(pieces)
    unit, half = place.unit, place.half

    def kernel(spot_ref, *refs):
        piece_refs, pack_refs = refs[:count], refs[count : count + len(packs)]
        upper_ref, branch, slope, sums = refs[count + len(packs) :][:4]
        outs = refs[count + len(packs) + 4 : -2]
        w_in, w_out = refs[-2:]
        place_feed(spot_ref, pack_views(pack_refs, place), w_in, w_out, unit, half)
        for index, ref in enumerate(piece_refs):
            branch[index * rows : (index + 1) * rows, :] = ref[...]
        grad = dot_nt(branch[...], w_out[...]) * silu_slope(upper_ref[...])
        slope[...] = grad.astype(BF)
        sums[...] = column_sum(slope[...])
        result = dot_nt(slope[...], w_in[...])
        for index, ref in enumerate(outs):
            ref[...] = result[index * rows : (index + 1) * rows].astype(ref.dtype)

    outs = [
        shape_of(total, model, BF),
        shape_of(total, inner, BF),
        shape_of(1, inner, F32),
        shape_of(rows, model, F32),
    ] + [shape_of(rows, model, BF)] * (count - 1)
    results = kernel_call(
        kernel,
        "feed_backward",
        outs,
        (place.spot, *pieces, *packs, upper),
        scalars=1,
        scratch=[pltpu.VMEM((model, inner), BF), pltpu.VMEM((inner, model), BF)],
        flops=4 * total * model * inner,
    )
    branch, slope, sums = results[:3]
    return results[3:], branch, slope, sums


def feed_out_grads(active, pieces, place):
    rows, model = pieces[0].shape
    inner = active.shape[1]
    planes, half = place.planes, place.half
    count = len(pieces)

    def kernel(spot, active_ref, *refs):
        total, kept, sent = refs[-1], refs[count], refs[count + 1]
        branch = jnp.concatenate([ref[...] for ref in refs[:count]], axis=0)
        total[...] = dot_tn(active_ref[...], branch)
        for near, ref in enumerate((kept, sent)):
            for step in range(planes):
                row = ((spot[0] ^ step) * 2 + (spot[2] ^ near)) * half
                source = pl.ds(pl.multiple_of(row, half), half)
                ref[step * half : (step + 1) * half, :] = total[source, :].astype(BF)

    return kernel_call(
        kernel,
        "feed_out_grads",
        [shape_of(planes * half, model, BF)] * 2,
        (place.spot, active, *pieces),
        scalars=1,
        scratch=[pltpu.VMEM((inner, model), F32)],
        flops=2 * active.shape[0] * model * inner,
    )


def feed_in_grads(hidden, slope, place):
    model, inner = hidden.shape[1], slope.shape[1]
    planes, unit = place.planes, place.unit

    def kernel(spot, hidden_ref, slope_ref, kept, sent, total):
        total[...] = dot_tn(hidden_ref[...], slope_ref[...])
        for near, ref in enumerate((kept, sent)):
            for step in range(planes):
                for turn in range(2):
                    column = (spot[0] ^ step) * 2 + (spot[1] ^ turn)
                    row = (column * 2 + (spot[2] ^ near)) * unit
                    start = (2 * step + turn) * unit
                    source = pl.ds(pl.multiple_of(row, unit), unit)
                    ref[start : start + unit, :] = total[source, :].astype(BF)

    return kernel_call(
        kernel,
        "feed_in_grads",
        [shape_of(2 * planes * unit, inner, BF)] * 2,
        (place.spot, hidden, slope),
        scalars=1,
        scratch=[pltpu.VMEM((model, inner), F32)],
        flops=2 * hidden.shape[0] * model * inner,
    )


def plane_split(kept, swapped, place):
    planes = place.planes
    size = kept.shape[0] // planes

    def body(kept_part, swapped_part):
        both = kept_part.astype(F32) + swapped_part.astype(F32)
        return [both[step * size : (step + 1) * size] for step in range(planes)]

    outs = [shape_of(size, kept.shape[1], BF)] * planes
    return fused(body, "plane_split", outs, kept, swapped)


def plane_early(pieces, place):
    lists = {step: [piece] for step, piece in enumerate(pieces)}
    top = place.planes.bit_length() - 2
    for bit in range(top):
        for step in [step for step in sorted(lists) if step >> bit & 1]:
            values = lists.pop(step)
            value = values[0] if len(values) == 1 else plane_add(values)
            lists[step ^ 1 << bit].append(flipped(value, QUAD << bit))
    return lists


def plane_last(value, place):
    return flipped(value, QUAD * (place.planes // 2))


def tied_tops(value, all_lists, place):
    top = place.planes // 2
    flat = [item for lists in all_lists for item in lists[top]]
    value, *flat = tied(value, *flat)
    flat = iter(flat)
    return value, [[next(flat) for _ in lists[top]] for lists in all_lists]


def plane_total(values):
    return values[0] if len(values) == 1 else plane_add(values)


def feed_pack(ff_in, ff_out, module, place):
    rows, hidden = ff_in.shape[2:]
    width, model = ff_out.shape[2:]
    half = width // 2
    count = 2 * place.planes * half
    if half % LANES:
        columns = ff_in[0, module].reshape(rows, place.planes, 2, 2, 2, half)
        columns = lax.dynamic_index_in_dim(columns, place.rep, 4, keepdims=False)
        own = lax.dynamic_index_in_dim(columns, place.second, 2, keepdims=False)
        other = lax.dynamic_index_in_dim(columns, 1 - place.second, 2, keepdims=False)
        own, other = (item.reshape(rows, count) for item in (own, other))
        part_out = lax.dynamic_slice_in_dim(ff_out[0, module], place.rep * half, half, 0)
        return own, flipped(other, 2), part_out

    def kernel(spot, in_ref, out_ref, own, other, part_out):
        second, rep = spot[1], spot[3]
        for turn, ref in enumerate((own, other)):
            for index in range(2 * place.planes):
                plane, core = index // 2, index % 2
                start = (((plane * 2 + (second ^ turn)) * 2 + core) * 2 + rep) * half
                source = pl.ds(pl.multiple_of(start, half), half)
                ref[:, index * half : (index + 1) * half] = in_ref[0, 0, :, source]
        part_out[...] = out_ref[0, 0, pl.ds(pl.multiple_of(rep * half, half), half), :]

    own, other, part_out = pl.pallas_call(
        kernel,
        grid=(1,),
        in_specs=[
            pl.BlockSpec(memory_space=pltpu.SMEM),
            pl.BlockSpec((1, 1, rows, hidden), lambda step: (0, module, 0, 0)),
            pl.BlockSpec((1, 1, width, model), lambda step: (0, module, 0, 0)),
        ],
        out_specs=vmem(3),
        out_shape=[
            shape_of(rows, count, BF),
            shape_of(rows, count, BF),
            shape_of(half, model, BF),
        ],
        compiler_params=pltpu.CompilerParams(vmem_limit_bytes=24 * MIB),
        name="feed_columns",
    )(place.spot, ff_in, ff_out)
    return own, flipped(other, 2), part_out


def pack_rows(parts):
    def body(*values):
        return (jnp.concatenate(values, axis=0),)

    rows = sum(item.shape[0] for item in parts)
    out = shape_of(rows, parts[0].shape[1], BF)
    return fused(body, "pack_rows", [out], *parts)[0]


def plane_bits(place):
    return range(place.planes.bit_length() - 1)


def plane_start(pack, place):
    top = place.planes // 2
    return [flipped(pack, QUAD * top), flipped(pack, QUAD)] if top > 1 else [flipped(pack, QUAD)]


def plane_finish(pack, started, place):
    pieces = {0: pack, place.planes // 2: started[0]}
    if len(started) > 1:
        pieces[1] = started[1]
    for bit in reversed(plane_bits(place)):
        for step in sorted(pieces):
            if step % (2 << bit) == 0 and step | 1 << bit not in pieces:
                pieces[step | 1 << bit] = flipped(pieces[step], QUAD << bit)
    return [pieces[step] for step in range(place.planes)]


def with_core(near):
    return [*near, *(flipped(item, 1) for item in near)]


def plane_add(values):
    def body(*items):
        return (sum((item.astype(F32) for item in items[1:]), items[0].astype(F32)),)

    return fused(body, "plane_add", [shape_of(*values[0].shape, BF)], *values)[0]


def feed_final(modules, place):
    unit, half = place.unit, place.half
    inner = modules[0][0][0].shape[1]
    model = modules[0][2][0].shape[1]
    planes = place.planes
    if half % LANES:
        grads_in, grads_out = [], []
        for in_own, in_other, out in modules:
            sides = jnp.stack([jnp.stack(in_own), jnp.stack(in_other)], axis=1)
            sides = jnp.where(place.second == 0, sides, sides[:, ::-1])
            sides = jnp.where(place.rep == 0, sides, sides[::-1])
            sides = sides.reshape(2, 2, unit, planes, 2, half).transpose(2, 3, 1, 4, 0, 5)
            grads_in.append(sides.reshape(unit, -1).astype(F32))
            both = jnp.stack(out)
            both = jnp.where(place.rep == 0, both, both[::-1])
            grads_out.append(both.reshape(2 * half, model).astype(F32))
        return jnp.stack(grads_in)[None], jnp.stack(grads_out)[None]

    def kernel(spot, *refs):
        grad_in, grad_out = refs[-2:]
        second, rep = spot[1], spot[3]
        for module in range(2):
            own = refs[6 * module : 6 * module + 6]
            for turn in range(2):
                for side in range(2):
                    piece = own[2 * turn + side][...].astype(F32)
                    for index in range(2 * planes):
                        plane, core = index // 2, index % 2
                        start = (((plane * 2 + (second ^ turn)) * 2 + core) * 2 + (rep ^ side)) * half
                        target = pl.ds(pl.multiple_of(start, half), half)
                        grad_in[0, module, :, target] = piece[:, index * half : (index + 1) * half]
            for side in range(2):
                target = pl.ds(pl.multiple_of((rep ^ side) * half, half), half)
                grad_out[0, module, target, :] = own[4 + side][...].astype(F32)

    operands = [item for module in modules for pair in module for item in pair]
    outs = [
        jax.ShapeDtypeStruct((1, 2, unit, 4 * inner), F32),
        jax.ShapeDtypeStruct((1, 2, 2 * half, model), F32),
    ]
    return kernel_call(kernel, "feed_final", outs, (place.spot, *operands), scalars=1)


def feed_arrive(sums, place):
    unit = place.unit
    own = sums[0][:unit]
    other = flipped(sums[0][unit:], 2)
    items = [own, other, *sums[1:]]
    return [(item, flipped(item, place.shards)) for item in items]


def score_block(query, keys, table, bias, place, rows, length):
    scores = dot_nt(query, keys)
    spread = dot_nt(query, table)
    band = pltpu.roll(spread, 0, axis=1, stride=1, stride_axis=0)
    column = lax.broadcasted_iota(jnp.int32, (rows, length + 2 * rows), 1)
    bias[...] = jnp.where(column < place, spread[:, :1], spread[:, -1:])
    bias[:, pl.ds(place, 3 * rows)] = band[:, rows:]
    return scores + bias[:, rows : rows + length]


def place_rows(source, columns, target, position, rows):
    for step in range(SPAN):
        spot = pl.ds(pl.multiple_of((position ^ step) * rows, rows), rows)
        target[spot, :] = source[step * rows : (step + 1) * rows, columns]


def split_rows(value, kept, sent, rows):
    for index, step in enumerate((0, 4, 2, 6)):
        target = slice(index * rows, (index + 1) * rows)
        kept[target, :] = value[step * rows : (step + 1) * rows]
        sent[target, :] = value[(step + 1) * rows : (step + 2) * rows].astype(BF)


def join_pieces(refs, target, rows):
    for step, ref in enumerate(refs):
        target[step * rows : (step + 1) * rows, :] = ref[...]


def attend_kernel(*refs):
    spot, pieces, rest = refs[0], refs[1 : 1 + SPAN], refs[1 + SPAN :]
    (weight_in, bias_in, weight_out, table, hidden, mixed, context, peaks, kept, sent) = rest[:10]
    keys, values, bias = rest[10:]
    length, width = context.shape
    rows = length // SPAN
    head = table.shape[1] // 2
    position = spot[0]
    join_pieces(pieces, hidden, rows)
    mixed[...] = (dot_nn(hidden[...], weight_in[...]) + bias_in[...]).astype(BF)
    place_rows(mixed, slice(width, 2 * width), keys, position, rows)
    place_rows(mixed, slice(2 * width, 3 * width), values, position, rows)
    lane = lax.broadcasted_iota(jnp.int32, (rows, width), 1)

    def block(index, carry):
        place = pl.multiple_of(index * rows, rows)
        own = pl.ds(pl.multiple_of((position ^ index) * rows, rows), rows)
        query = mixed[own, :width] * jnp.asarray(head**-0.5, BF)
        results, logs = [], []
        for which in range(2):
            mine = lane // head == which
            part = jnp.where(mine, query, jnp.zeros_like(query))
            scores = score_block(part, keys[...], table[...], bias, place, rows, length)
            top = jnp.max(scores, axis=1, keepdims=True)
            powers = jnp.exp(scores - top)
            total = jnp.sum(powers, axis=1, keepdims=True)
            weights = (powers * (1.0 / total)).astype(BF)
            results.append(dot_nn(weights, values[...]))
            logs.append(top + jnp.log(total))
        context[own, :] = jnp.where(lane < head, results[0], results[1]).astype(BF)
        peaks[own, :] = jnp.where(lane < head, logs[0], logs[1])
        return carry

    lax.fori_loop(0, SPAN, block, 0)
    split_rows(dot_nn(context[...], weight_out[...]), kept, sent, rows)


def attend_back_kernel(*refs):
    spot, pieces, rest = refs[0], refs[1 : 1 + SPAN], refs[1 + SPAN :]
    (mixed, table, peaks, weight_in, weight_out) = rest[:5]
    (branch, grad_mixed, grad_table, far, kept, sent) = rest[5:11]
    keys, values, bias, grad_context, grad_keys, grad_values, slopes, marked = rest[11:]
    length, width = grad_context.shape
    rows = length // SPAN
    head = table.shape[1] // 2
    position = spot[0]
    join_pieces(pieces, branch, rows)
    grad_context[...] = dot_nt(branch[...], weight_out[...]).astype(BF)
    place_rows(mixed, slice(width, 2 * width), keys, position, rows)
    place_rows(mixed, slice(2 * width, 3 * width), values, position, rows)
    grad_keys[...] = jnp.zeros_like(grad_keys)
    grad_values[...] = jnp.zeros_like(grad_values)
    grad_table[...] = jnp.zeros_like(grad_table)
    far[...] = jnp.zeros_like(far)
    lane = lax.broadcasted_iota(jnp.int32, (rows, width), 1)
    for which in range(2):
        for block_id in range(SPAN):
            own = slice(block_id * rows, (block_id + 1) * rows)
            mark = jnp.where(lane % head == block_id, 1.0, 0.0).astype(BF)
            marked[which, own, :] = jnp.where(lane // head == which, keys[own, :], mark)
    factor = head**-0.5
    slopes[:, :rows] = jnp.zeros((rows, rows), BF)
    slopes[:, rows + length :] = jnp.zeros((rows, rows), BF)
    mirror = (
        lax.broadcasted_iota(jnp.int32, (rows, rows), 0)
        + lax.broadcasted_iota(jnp.int32, (rows, rows), 1)
        == rows - 1
    ).astype(BF)

    def block(index, carry):
        place = pl.multiple_of(index * rows, rows)
        own = pl.ds(pl.multiple_of((position ^ index) * rows, rows), rows)
        query = mixed[own, :width] * jnp.asarray(factor, BF)
        results = []
        for which in range(2):
            mine = lane // head == which
            part = jnp.where(mine, query, jnp.zeros_like(query))
            scores = score_block(part, keys[...], table[...], bias, place, rows, length)
            incoming = grad_context[own, :]
            incoming = jnp.where(mine, incoming, jnp.zeros_like(incoming))
            logs = peaks[own, which * head : which * head + 1]
            probs = jnp.exp(scores - logs)
            grad_probs = dot_nt(incoming, values[...])
            shared = jnp.sum(grad_probs * probs, axis=1, keepdims=True)
            grad_low = (probs * (grad_probs - shared)).astype(BF)
            grad_values[...] += dot_tn(probs.astype(BF), incoming)
            grad_keys[...] += dot_tn(grad_low, part)
            slopes[:, rows : rows + length] = grad_low
            window = slopes[:, pl.ds(place, 3 * rows)]
            direct = dot_nn(grad_low, marked[which])
            block_of = jnp.where(mine, SPAN, lane % head)
            early = jnp.sum(jnp.where(block_of < index - 1, direct, 0.0), axis=1, keepdims=True)
            after = (block_of > index + 1) & (block_of < SPAN)
            late = jnp.sum(jnp.where(after, direct, 0.0), axis=1, keepdims=True)
            window = jnp.concatenate(
                [jnp.zeros((rows, rows), F32), dot_nn(mirror, window)], axis=1
            )
            window = pltpu.roll(
                window, 3 * rows + 1, axis=1, stride=1, stride_axis=0
            ).astype(BF)
            grad_table[...] += dot_tn(window, dot_nn(mirror, part).astype(BF))
            part_wide = part.astype(F32)
            far[0:1, :] += jnp.sum(early * part_wide, axis=0, keepdims=True)
            far[1:2, :] += jnp.sum(late * part_wide, axis=0, keepdims=True)
            close = jnp.dot(
                mirror.astype(F32),
                dot_nn(window, table[...]),
                preferred_element_type=F32,
                precision=lax.Precision.HIGHEST,
            )
            results.append(
                direct
                + close
                + early * table[0:1, :].astype(F32)
                + late * table[4 * rows - 1 :, :].astype(F32)
            )
        grad_mixed[own, :width] = (
            jnp.where(lane < head, results[0], results[1]) * factor
        ).astype(BF)
        return carry

    lax.fori_loop(0, SPAN, block, 0)
    for step in range(SPAN):
        source = pl.ds(pl.multiple_of((position ^ step) * rows, rows), rows)
        target = slice(step * rows, (step + 1) * rows)
        grad_mixed[target, width : 2 * width] = grad_keys[source, :].astype(BF)
        grad_mixed[target, 2 * width :] = grad_values[source, :].astype(BF)
    split_rows(dot_nt(grad_mixed[...], weight_in[...]), kept, sent, rows)


def group_gather(value, masks):
    near = square_gather(value, masks)
    return near, [flipped(item, 1) for item in near]


def group_reduce(kept, sent, masks):
    swapped = flipped(sent, 1)
    rows = kept.shape[0] // 4

    def body(kept_part, swapped_part):
        total = kept_part + swapped_part.astype(F32)
        return [total[index * rows : (index + 1) * rows] for index in range(4)]

    outs = [shape_of(rows, kept.shape[1], dtype) for dtype in (F32, BF, BF, BF)]
    return square_reduce(fused(body, "core_sum", outs, kept, swapped), masks)


def in_steps(blocks):
    near, far = blocks
    return [near[0], far[0], near[2], far[2], near[1], far[1], near[3], far[3]]


def attend(blocks, weight_in, bias_in, weight_out, table, place):
    pieces = in_steps(blocks)
    rows, model = pieces[0].shape
    length, width = SPAN * rows, weight_out.shape[0]
    outs = [
        shape_of(length, model, BF),
        shape_of(length, 3 * width, BF),
        shape_of(length, width, BF),
        shape_of(length, width, F32),
        shape_of(length // 2, model, F32),
        shape_of(length // 2, model, BF),
    ]
    hidden, mixed, context, peaks, kept, sent = kernel_call(
        attend_kernel,
        "attend_forward",
        outs,
        (place.span_spot, *pieces, weight_in, bias_in, weight_out, table),
        scalars=1,
        scratch=[
            pltpu.VMEM((length, width), BF),
            pltpu.VMEM((length, width), BF),
            pltpu.VMEM((rows, length + 2 * rows), F32),
        ],
        limit=56,
        flops=48 * length * length * width,
    )
    return (hidden, mixed, context, peaks), kept, sent


def attend_back(blocks, saved, weight_in, weight_out, table, place):
    hidden, mixed, context, peaks = saved
    pieces = in_steps(blocks)
    rows, model = pieces[0].shape
    length, width = SPAN * rows, weight_out.shape[0]
    outs = [
        shape_of(length, model, BF),
        shape_of(length, 3 * width, BF),
        shape_of(4 * rows, width, F32),
        shape_of(8, width, F32),
        shape_of(length // 2, model, F32),
        shape_of(length // 2, model, BF),
    ]
    branch, grad_mixed, grad_table, far, kept, sent = kernel_call(
        attend_back_kernel,
        "attend_backward",
        outs,
        (place.span_spot, *pieces, mixed, table, peaks, weight_in, weight_out),
        scalars=1,
        scratch=[
            pltpu.VMEM((length, width), BF),
            pltpu.VMEM((length, width), BF),
            pltpu.VMEM((rows, length + 2 * rows), F32),
            pltpu.VMEM((length, width), BF),
            pltpu.VMEM((length, width), F32),
            pltpu.VMEM((length, width), F32),
            pltpu.VMEM((rows, length + 2 * rows), BF),
            pltpu.VMEM((2, length, width), BF),
        ],
        flops=96 * length * length * width,
    )
    return grad_mixed, kept, sent, branch, grad_table, far


def attend_grads(saved, grad_mixed, branch, place):
    hidden, unused_mixed, context, unused_peaks = saved
    length, model = hidden.shape
    width = context.shape[1]

    def weights(hidden_rows, mixed_grad, context_rows, branch_rows):
        return (
            dot_tn(hidden_rows, mixed_grad),
            dot_tn(context_rows, branch_rows),
            column_sum(mixed_grad),
        )

    return fused(
        weights,
        "attend_weights",
        [shape_of(model, 3 * width, BF), shape_of(width, model, BF), shape_of(1, 3 * width, F32)],
        hidden,
        grad_mixed,
        context,
        branch,
        flops=8 * length * model * width,
    )


def wide_table(distance, rows):
    index = jnp.clip(jnp.arange(4 * rows) - rows - LEFT, 0, LEFT + RIGHT)
    low = distance[index]
    return jnp.concatenate([low, low], axis=1)


def distance_gradient(grad_table, far, rows):
    first = rows + LEFT
    last = first + LEFT + RIGHT
    head = grad_table.shape[1] // 2
    low = jnp.sum(grad_table[: first + 1], axis=0) + far[0]
    high = jnp.sum(grad_table[last:], axis=0) + far[1]
    total = jnp.concatenate([low[None], grad_table[first + 1 : last], high[None]], axis=0)
    return total[:, :head] + total[:, head:]


def whole_heads(head, place):
    return place.unit == head and 2 * place.unit == LANES and place.planes == 4


def attend_weights_whole(weight_in, weight_out, head, place):
    model = weight_out.shape[1]
    heads = model // head
    per_device = heads // SPAN
    width = per_device * head
    whole = lax.all_gather(weight_in, "shard", axis=0, tiled=True)
    whole = whole.reshape(model, 3, heads, head)
    mine = lax.dynamic_slice_in_dim(whole, place.member * per_device, per_device, 2)
    out = lax.all_gather(weight_out, "shard", axis=0, tiled=True)
    out = lax.dynamic_slice_in_dim(out, place.member * width, width, 0)
    return mine.reshape(model, 3 * width), out


def attend_columns(weight_in, place):
    rows = weight_in.shape[0]
    planes, unit = place.planes, place.unit
    groups, columns = planes // 2, 3 * weight_in.shape[1] // 3 // SPAN
    if 2 * unit == LANES:

        def pick(spot, whole, *outs):
            lane = lax.broadcasted_iota(jnp.int32, (rows, LANES), 1)
            for turn, out in enumerate(outs):
                for low in range(2):
                    for part in range(3):
                        pair = []
                        for group in range(groups):
                            start = ((part * groups + group) * 2 + low) * 2 + (spot[1] ^ turn)
                            source = pl.ds(pl.multiple_of(start * LANES, LANES), LANES)
                            pair.append(whole[:, source].astype(F32))
                        rolled = [pltpu.roll(item, unit, axis=1) for item in pair]
                        cores = (
                            jnp.where(lane < unit, pair[0], rolled[1]),
                            jnp.where(lane < unit, rolled[0], pair[1]),
                        )
                        for core, value in enumerate(cores):
                            out[
                                low,
                                core * rows : (core + 1) * rows,
                                part * LANES : (part + 1) * LANES,
                            ] = value.astype(BF)

        own, other = kernel_call(
            pick,
            "attend_pick",
            [jax.ShapeDtypeStruct((2, 2 * rows, columns), BF)] * 2,
            (place.spot, weight_in),
            scalars=1,
        )
    else:
        blocks = weight_in.reshape(rows, 3, groups, 2, 2, 2, -1)
        blocks = blocks.transpose(4, 3, 5, 0, 1, 2, 6).reshape(2, 2, 2 * rows, columns)
        own = lax.dynamic_index_in_dim(blocks, place.second, 0, keepdims=False)
        other = lax.dynamic_index_in_dim(blocks, 1 - place.second, 0, keepdims=False)
    return own, flipped(other.reshape(4 * rows, columns), 2).reshape(own.shape)


def attend_arrange(own, arrived, glue, place):
    unit, columns = place.unit, own.shape[2]
    size = 4 * unit

    def arrange(spot, own_ref, arrived_ref, glue_ref, near_out, one, two):
        low, core = spot[0] & 1, spot[2]
        for near in range(2):
            source = pl.ds(pl.multiple_of((core ^ near) * unit, unit), unit)
            for turn, ref in enumerate((own_ref, arrived_ref)):
                start = (2 * near + turn) * unit
                mine, other = ref[low, source, :], ref[low ^ 1, source, :]
                near_out[start : start + unit, :] = mine
                two[start : start + unit, :] = mine
                two[size + start : size + start + unit, :] = other
                one[start : start + unit, :] = other
        one[size:, :] = glue_ref[...]
        two[2 * size :, :] = glue_ref[...]

    count = glue.shape[0]
    return kernel_call(
        arrange,
        "attend_columns",
        [
            shape_of(size, columns, BF),
            shape_of(size + count, columns, BF),
            shape_of(2 * size + count, columns, BF),
        ],
        (place.spot, own, arrived, glue),
        scalars=1,
    )


def attend_weights_split(near, glue, travelled, place):
    unit = place.unit
    size = 4 * unit
    columns = near.shape[1]

    def split(near_rows, glue_rows, odd, even, relayed):
        pieces = (near_rows, odd, even, relayed)
        kept = jnp.concatenate([item[: 2 * unit] for item in pieces], axis=0)
        sent = jnp.concatenate([item[2 * unit : size] for item in pieces], axis=0)
        whole = [glue_rows, odd[size:], even[2 * size :], relayed[size:]]
        return kept, sent, jnp.concatenate(whole, axis=0)

    return fused(
        split,
        "attend_split",
        [shape_of(8 * unit, columns, BF)] * 2 + [shape_of(4 * glue.shape[0], columns, BF)],
        near,
        glue,
        *travelled,
    )


def attend_weights_lay(kept, sent, outs, place):
    planes, unit, columns = place.planes, place.unit, kept.shape[1]
    width, model = columns // 3, outs[0].shape[1]
    swapped = flipped(sent, 1)

    def lay(spot, kept_ref, swapped_ref, *refs):
        plane, second, core = spot[0], spot[1], spot[2]
        w_in, w_out = refs[-2:]
        for near, ref in enumerate((kept_ref, swapped_ref)):
            for step in range(planes):
                for turn in range(2):
                    row = (((plane ^ step) * 2 + (second ^ turn)) * 2 + (core ^ near)) * unit
                    start = (2 * step + turn) * unit
                    w_in[pl.ds(pl.multiple_of(row, unit), unit), :] = ref[start : start + unit, :]
        for step, ref in enumerate(refs[:-2]):
            row = ((plane >> 1) ^ step) * unit
            w_out[pl.ds(pl.multiple_of(row, unit), unit), :] = ref[...]

    return kernel_call(
        lay,
        "attend_lay",
        [shape_of(model, columns, BF), shape_of(width, model, BF)],
        (place.spot, kept, swapped, *outs),
        scalars=1,
    )


def attend_grads_whole(grad_in, grad_out, head, place):
    model = grad_out.shape[1]
    heads = model // head
    per_device = heads // SPAN
    whole = jnp.zeros((model, 3, heads, head), F32)
    whole = lax.dynamic_update_slice_in_dim(
        whole,
        grad_in.astype(F32).reshape(model, 3, per_device, head),
        place.member * per_device,
        2,
    )
    whole = lax.psum_scatter(
        whole.reshape(model, 3 * model), "shard", scatter_dimension=0, tiled=True
    )
    out = jnp.zeros((model, model), F32)
    out = lax.dynamic_update_slice_in_dim(
        out, grad_out.astype(F32), place.member * per_device * head, 0
    )
    out = lax.psum_scatter(out, "shard", scatter_dimension=0, tiled=True)
    return rep_sum(whole, place), rep_sum(out, place)


def attend_grads_lay(grad_in, grad_out, place):
    model = grad_out.shape[1]
    planes, unit = place.planes, place.unit
    groups, columns = planes // 2, grad_in.shape[1]

    def lay(spot, w_in, w_out, kept, sent, *outs):
        plane, second, core = spot[0], spot[1], spot[2]
        for near, ref in enumerate((kept, sent)):
            for step in range(planes):
                for turn in range(2):
                    row = (((plane ^ step) * 2 + (second ^ turn)) * 2 + (core ^ near)) * unit
                    start = (2 * step + turn) * unit
                    ref[start : start + unit, :] = w_in[pl.ds(pl.multiple_of(row, unit), unit), :]
        for step, ref in enumerate(outs):
            row = ((plane >> 1) ^ step) * unit
            ref[...] = w_out[pl.ds(pl.multiple_of(row, unit), unit), :]

    return kernel_call(
        lay,
        "attend_unlay",
        [shape_of(2 * planes * unit, columns, BF)] * 2 + [shape_of(unit, model, BF)] * groups,
        (place.spot, grad_in, grad_out),
        scalars=1,
    )


def attend_grads_sum(travelled, place):
    unit = place.unit
    columns, model = travelled[0].shape[1] // 2, travelled[4].shape[1]

    def total(own, one, two, three, *rest):
        even = own.astype(F32) + two.astype(F32)
        odd = one[: three.shape[0]].astype(F32) + three.astype(F32)
        both = jnp.concatenate([even, odd], axis=1)
        out = sum(item.astype(F32) for item in rest)
        return both[:unit], both[unit:], out

    own, other, out = fused(
        total,
        "attend_plane_sum",
        [shape_of(unit, 4 * columns, BF)] * 2 + [shape_of(unit, model, BF)],
        *travelled,
    )
    return own, other, out


def attend_grads_arrive(sums, place):
    own, other, out = sums
    arrived = flipped(other, 2)
    mine = own, arrived, out
    return mine, tuple(flipped(item, place.shards) for item in mine)


def attend_grads_final(mine, theirs, place):
    unit = place.unit
    model = mine[2].shape[1]
    columns = mine[0].shape[1] // 4
    groups = place.planes // 2

    def kernel(spot, *refs):
        values = [refs[i][...].astype(F32) + refs[3 + i][...].astype(F32) for i in range(3)]
        grad_in, grad_out = refs[6:]
        grad_out[0] = values[2]
        lane = lax.broadcasted_iota(jnp.int32, (unit, LANES), 1)
        low_bit, core = spot[0] & 1, spot[2]
        for turn in range(2):
            for low in range(2):
                for part in range(3):
                    blocks = []
                    for near in range(2):
                        start = (2 * low + near) * columns + part * LANES
                        blocks.append(values[turn][:, start : start + LANES])
                    first = jnp.where(core == 0, blocks[0], blocks[1])
                    last = jnp.where(core == 0, blocks[1], blocks[0])
                    pairs = (
                        jnp.where(lane < unit, first, pltpu.roll(last, unit, axis=1)),
                        jnp.where(lane < unit, pltpu.roll(first, unit, axis=1), last),
                    )
                    for group, value in enumerate(pairs):
                        start = ((part * groups + group) * 2 + (low_bit ^ low)) * 2
                        start = (start + (spot[1] ^ turn)) * LANES
                        grad_in[0, :, pl.ds(pl.multiple_of(start, LANES), LANES)] = value

    outs = [
        jax.ShapeDtypeStruct((1, unit, 3 * model), F32),
        jax.ShapeDtypeStruct((1, unit, model), F32),
    ]
    return kernel_call(kernel, "attend_final", outs, (place.spot, *mine, *theirs), scalars=1)


def rep_sum(value, place):
    low = value.astype(BF)
    return low.astype(F32) + flipped(low, place.shards).astype(F32)


def row(wide, index):
    return wide[index : index + 1]


def blocks_of(width, first, model):
    low, high = (0, 2 * model) if first else (2 * model, 3 * model)
    result = []
    for block in range(3 * model // width):
        begin, end = max(block * width, low), min((block + 1) * width, high)
        if begin < end:
            source = slice(begin - block * width, end - block * width)
            result.append((block, source, slice(begin - low, end - low)))
    return result


def conv_pick(weight_in, weight_out, width, place):
    rows, model = weight_out.shape
    half = rows // 2
    whole = half % 16 != 0
    size = rows if whole else half

    def pick(spot, left, right, out):
        source = pl.ds(pl.multiple_of(spot[3] * half, half), half)
        if whole:
            source = slice(0, rows)
        for ref, first in ((left, True), (right, False)):
            for block, own, columns in blocks_of(width, first, model):
                out[block * size : (block + 1) * size, own] = ref[source, columns]

    outs = [shape_of(3 * model // width * size, width, BF)]
    operands = (place.spot, weight_in, weight_out)
    return kernel_call(pick, "conv_pick", outs, operands, scalars=1)[0]


def conv_square(own, masks):
    first, second = masks
    half = own.shape[0] // 2
    return own, flipped(own, first), flipped(own, second), half


def conv_relay(via_first, via_second, masks):
    first, second = masks
    half = via_first.shape[0] // 2
    low, high = fused(
        lambda one, two: (one[:half], two[half:]),
        "conv_halves",
        [shape_of(half, via_first.shape[1], BF)] * 2,
        via_first,
        via_second,
    )
    return flipped(low, second), flipped(high, first)


def lay_conv(spot, refs, target, unit, first):
    model = target.shape[0]
    plane, second, core, rep = spot[0], spot[1], spot[2], spot[3]
    size = unit if len(refs) == 1 else unit // 2
    width = refs[0].shape[1]
    extent = 3 * model // width * size
    blocks = blocks_of(width, first, model)
    for index, ref in enumerate(refs):
        for local in range(ref.shape[0] // extent):
            start = local * size
            if len(refs) > 1:
                kind, near = index % 5, index // 5
                turn, side = ((0, 0), (0, 1), (1, 0), (1, 1), (1, 1))[kind]
                step = local + (ref.shape[0] // extent if kind == 4 else 0)
                start = (((plane ^ step) * 2 + (second ^ turn)) * 2 + (core ^ near)) * 2
                start = pl.multiple_of((start + (rep ^ side)) * size, size)
            for block, own, columns in blocks:
                source = local * extent + block * size
                target[pl.ds(start, size), columns] = ref[source : source + size, own]


def conv_whole_weights(pieces, model, place):
    def kernel(spot, *refs):
        w_in, w_out = refs[-2:]
        lay_conv(spot, refs[:-2], w_in, place.unit, True)
        lay_conv(spot, refs[:-2], w_out, place.unit, False)

    outs = [shape_of(model, 2 * model, BF), shape_of(model, model, BF)]
    return kernel_call(kernel, "conv_lay", outs, (place.spot, *pieces), scalars=1)


def convolve_start(parts, before, wide, bias_row, weights, place):
    rows, model = before.shape

    def kernel(*refs):
        part_refs, (base, small, w_in) = refs[:4], refs[4:7]
        current_ref, hidden_ref, doubled_ref, glued_ref = refs[7:]
        parts_now = [ref[...] for ref in part_refs]
        current = base[...] + joined(parts_now) + small[bias_row : bias_row + 1, :]
        current_ref[...] = current
        unit, unused_scale = standard(current)
        hidden = (unit * small[7:8, :] + small[8:9, :]).astype(BF)
        hidden_ref[...] = hidden
        doubled = dot_nn(hidden, w_in[...])
        doubled_ref[...] = doubled
        glued_ref[...] = (doubled[:, :model] * logistic(doubled[:, model:])).astype(BF)

    return kernel_call(
        kernel,
        "convolve_start",
        [
            shape_of(rows, model, F32),
            shape_of(rows, model, BF),
            shape_of(rows, 2 * model, F32),
            shape_of(rows, model, BF),
        ],
        (*parts, before, wide, weights[0]),
        flops=4 * rows * model * model,
    )


def convolve_finish(glued, border, wide, taps, weights, before, place):
    rows, model = before.shape
    edge = border.shape[0]

    def kernel(
        glued_ref, border_ref, small, base, w_out, mixed_ref, rest_ref, current_ref, hidden_ref,
        padded,
    ):
        padded[:edge, :] = border_ref[...].astype(F32)
        padded[edge:, :] = glued_ref[...].astype(F32)
        first, count = taps
        for column in range(0, model, LANES):
            lanes = slice(column, column + LANES)
            total = jnp.zeros((rows, LANES), F32)
            for tap in range(count):
                start = edge - count + 1 + tap
                weight = small[first + tap : first + tap + 1, lanes]
                total += padded[start : start + rows, lanes] * weight
            mixed_ref[:, lanes] = total
        unit, unused_scale = standard(mixed_ref[...])
        upper = unit * small[9:10, :] + small[10:11, :]
        rest = (upper * logistic(upper)).astype(BF)
        rest_ref[...] = rest
        current = base[...] + dot_nn(rest, w_out[...])
        current_ref[...] = current
        unit, unused_scale = standard(current)
        hidden_ref[...] = (unit * small[11:12, :] + small[12:13, :]).astype(BF)

    return kernel_call(
        kernel,
        "convolve_finish",
        [shape_of(rows, model, dtype) for dtype in (F32, BF, F32, BF)],
        (glued, border, wide, before, weights[1]),
        scratch=[pltpu.VMEM((edge + rows, model), F32)],
        flops=2 * rows * model * model,
    )


def convolve_back_start(parts, grad, after, mixed, wide, taps, weights, glued, border, place):
    rows, model = after.shape
    edge = border.shape[0]
    first, count = taps

    def kernel(
        own, part_one, part_two, part_three, grad_ref, after_ref, mixed_ref, small,
        glued_ref, border_ref, w_out, grad_out, branch_ref, main_ref, halo_ref, sums,
        padded, spread,
    ):
        incoming = joined((own[...], part_one[...], part_two[...], part_three[...]))
        slope, sum_gain, sum_shift = norm_back(after_ref[...], small[11:12, :], incoming)
        current = grad_ref[...] + slope
        grad_out[...] = current
        branch = current.astype(BF)
        branch_ref[...] = branch
        unit, scale = standard(mixed_ref[...])
        upper = unit * small[9:10, :] + small[10:11, :]
        grad_upper = dot_nt(branch, w_out[...]) * silu_slope(upper)
        inner = grad_upper * small[9:10, :]
        mean = jnp.mean(inner, axis=-1, keepdims=True)
        shared = jnp.mean(inner * unit, axis=-1, keepdims=True)
        padded[:edge, :] = border_ref[...].astype(F32)
        padded[edge:, :] = glued_ref[...].astype(F32)
        spread[:edge, :] = jnp.zeros((edge, model), F32)
        spread[edge : edge + rows, :] = scale * (inner - mean - unit * shared)
        spread[edge + rows :, :] = jnp.zeros((edge, model), F32)
        sums[count : count + 1, :] = column_sum(grad_upper * unit)
        sums[count + 1 : count + 2, :] = column_sum(grad_upper)
        sums[count + 2 : count + 3, :] = sum_gain
        sums[count + 3 : count + 4, :] = sum_shift
        for column in range(0, model, LANES):
            lanes = slice(column, column + LANES)
            total = jnp.zeros((rows + edge, LANES), F32)
            center = spread[edge : edge + rows, lanes]
            for tap in range(count):
                start = edge - count + 1 + tap
                sums[tap : tap + 1, lanes] = jnp.sum(
                    center * padded[start : start + rows, lanes], axis=0, keepdims=True
                )
                begin = count - 1 - tap
                weight = small[first + tap : first + tap + 1, lanes]
                total += spread[begin : begin + rows + edge, lanes] * weight
            halo_ref[:, lanes] = total[:edge].astype(BF)
            main_ref[:, lanes] = total[edge:]

    return kernel_call(
        kernel,
        "convolve_back_start",
        [
            shape_of(rows, model, F32),
            shape_of(rows, model, BF),
            shape_of(rows, model, F32),
            shape_of(edge, model, BF),
            shape_of(count + 4, model, F32),
        ],
        (*parts, grad, after, mixed, wide, glued, border, weights[1]),
        scratch=[
            pltpu.VMEM((edge + rows, model), F32),
            pltpu.VMEM((rows + 2 * edge, model), F32),
        ],
        limit=56,
        flops=2 * rows * model * model,
    )


def convolve_back_finish(main, incoming, doubled, weights, before, wide, grad, place):
    rows, model = before.shape
    edge = incoming.shape[0]

    def kernel(
        main_ref, late, both, base, small, grad_rows, w_in, current_ref, branch_ref, slope_ref,
        sums,
    ):
        last = main_ref[rows - edge :, :] + late[...].astype(F32)
        glued = jnp.concatenate([main_ref[: rows - edge, :], last], axis=0)
        glued = glued.astype(BF).astype(F32)
        gate = logistic(both[:, model:])
        slope_ref[:, :model] = (glued * gate).astype(BF)
        slope_ref[:, model:] = (glued * both[:, :model] * gate * (1.0 - gate)).astype(BF)
        inner, sum_gain, sum_shift = norm_back(
            base[...], small[7:8, :], dot_nt(slope_ref[...], w_in[...])
        )
        current = grad_rows[...] + inner
        current_ref[...] = current
        branch_ref[...] = current.astype(BF)
        sums[0:1, :] = sum_gain
        sums[1:2, :] = sum_shift
        sums[2:3, :] = column_sum(current.astype(BF))

    return kernel_call(
        kernel,
        "convolve_back_finish",
        [
            shape_of(rows, model, F32),
            shape_of(rows, model, BF),
            shape_of(rows, 2 * model, BF),
            shape_of(3, model, F32),
        ],
        (main, incoming, doubled, before, wide, grad, weights[0]),
        flops=4 * rows * model * model,
    )


def conv_grads_start(hidden, slope, rest, branch, place):
    model = hidden.shape[1]
    unit, planes = place.unit, place.planes
    size = unit // 2
    halved = place.aligned
    width = 3 * model // 4 if halved else model
    columns = range(0, 3 * model, width)

    def kernel(spot, hidden_ref, slope_ref, rest_ref, branch_ref, kept, sent, total):
        total[:, : 2 * model] = dot_tn(hidden_ref[...], slope_ref[...])
        total[:, 2 * model :] = dot_tn(rest_ref[...], branch_ref[...])
        plane, second, core, rep = spot[0], spot[1], spot[2], spot[3]
        for near, ref in enumerate((kept, sent)):
            if not halved:
                for pair in range(2 * planes):
                    start = pl.multiple_of((pair * 2 + (core ^ near)) * unit, unit)
                    for index, column in enumerate(columns):
                        target = (3 * pair + index) * unit
                        ref[target : target + unit, :] = total[
                            pl.ds(start, unit), column : column + width
                        ].astype(BF)
                continue
            for kind, (turn, side) in enumerate(((0, 0), (0, 1), (1, 0), (1, 1))):
                for step in range(planes):
                    start = (((plane ^ step) * 2 + (second ^ turn)) * 2 + (core ^ near)) * 2
                    start = pl.multiple_of((start + (rep ^ side)) * size, size)
                    for index, column in enumerate(columns):
                        target = ((kind * planes + step) * len(columns) + index) * size
                        ref[target : target + size, :] = total[
                            pl.ds(start, size), column : column + width
                        ].astype(BF)

    return kernel_call(
        kernel,
        "conv_grads",
        [shape_of(len(columns) * model // 2, width, BF)] * 2,
        (place.spot, hidden, slope, rest, branch),
        scalars=1,
        scratch=[pltpu.VMEM((model, 3 * model), F32)],
        flops=6 * hidden.shape[0] * model * model,
        limit=36,
    )


def conv_grads_split(kept, swapped, place):
    count = 4 if place.aligned else 1
    size = kept.shape[0] // count

    def body(kept_part, swapped_part):
        total = kept_part.astype(F32) + swapped_part.astype(F32)
        return [total[index * size : (index + 1) * size] for index in range(count)]

    outs = [shape_of(size, kept.shape[1], BF)] * count
    return list(fused(body, "conv_grads_split", outs, kept, swapped))


def conv_grads_square(shares, masks):
    first, second = masks
    return [
        shares[0],
        flipped(shares[1], first),
        flipped(shares[2], second),
        flipped(shares[3], first | second),
    ]


def plane_pieces(mix_kept, mix_swapped, shares, place):
    planes, unit = place.planes, place.unit
    rows, width = 2 * unit, shares[0].shape[1]
    size = shares[0].shape[0] // planes

    def body(kept, swapped, *values):
        both = jnp.concatenate([kept, swapped], axis=1)
        mix = [both[step * rows : (step + 1) * rows] for step in range(planes)]
        total = sum(value.astype(F32) for value in values).astype(BF)
        conv = [total[step * size : (step + 1) * size] for step in range(planes)]
        joint = jnp.concatenate([mix[1], conv[1], conv[3]], axis=0)
        return mix[0], mix[2], mix[3], conv[0], conv[2], joint

    outs = [shape_of(rows, width, BF)] * 3 + [shape_of(size, width, BF)] * 2
    outs += [shape_of(rows + 2 * size, width, BF)]
    return list(fused(body, "plane_pieces", outs, mix_kept, mix_swapped, *shares))


def conv_grads_top(own, joint):
    size = own.shape[0]

    def body(mine, arrived):
        return (mine.astype(F32) + arrived[arrived.shape[0] - size :].astype(F32),)

    return fused(body, "conv_grads_top", [shape_of(*own.shape, BF)], own, joint)[0]


def conv_grads_sum(own, joint, last):
    size = own.shape[0]

    def body(mine, arrived, late):
        start = arrived.shape[0] - 2 * size
        near = arrived[start : start + size]
        return (mine.astype(F32) + near.astype(F32) + late.astype(F32),)

    return fused(body, "conv_grads_sum", [shape_of(*own.shape, BF)], own, joint, last)[0]


def conv_grads_whole(total, place):
    groups = [list(range(core, place.shards, 2)) for core in range(2)]
    mine = lax.psum_scatter(
        total, "shard", scatter_dimension=0, tiled=True, axis_index_groups=groups
    )
    return rep_sum(mine, place).reshape(3, place.unit, -1)


def conv_grads_final(mine, theirs, place):
    size, width = place.unit // 2, mine.shape[1]
    model = width * mine.shape[0] // size // 3

    def kernel(spot, mine_ref, theirs_ref, grad_in, grad_out):
        for turn, ref in enumerate((mine_ref, theirs_ref)):
            target = pl.ds(pl.multiple_of((spot[3] ^ turn) * size, size), size)
            for out, first in ((grad_in, True), (grad_out, False)):
                for block, own, columns in blocks_of(width, first, model):
                    value = ref[block * size : (block + 1) * size, own]
                    out[0, target, columns] = value.astype(F32)

    outs = [
        jax.ShapeDtypeStruct((1, 2 * size, 2 * model), F32),
        jax.ShapeDtypeStruct((1, 2 * size, model), F32),
    ]
    return kernel_call(kernel, "conv_final", outs, (place.spot, mine, theirs), scalars=1)


def feed_to_attend(parts, before, wide):
    rows, model = before.shape

    def body(*values):
        base, small = values[4:]
        current = base.astype(F32) + 0.5 * (joined(values[:4]) + row(small, 2))
        unit, unused_scale = standard(current)
        return current, unit * row(small, 3) + row(small, 4)

    outs = [shape_of(rows, model, F32), shape_of(rows, model, BF)]
    return fused(body, "feed_to_attend", outs, *parts, before, wide)


def turn_around(parts, before, wide, cotangent):
    rows, model = before.shape

    def body(*values):
        base, small, grad = values[4:]
        current = base + 0.5 * (joined(values[:4]) + row(small, 13))
        unit, unused_scale = standard(current)
        slope, sum_gain, sum_shift = norm_back(current, row(small, 14), grad.astype(F32))
        branch = (0.5 * slope).astype(BF)
        sums = jnp.concatenate([column_sum(branch), sum_gain, sum_shift], axis=0)
        return unit * row(small, 14) + row(small, 15), slope, branch, sums

    outs = [
        shape_of(rows, model, BF),
        shape_of(rows, model, F32),
        shape_of(rows, model, BF),
        shape_of(3, model, F32),
    ]
    return fused(body, "turn_around", outs, *parts, before, wide, cotangent)


def attend_to_feed_back(parts, grad, before, wide):
    rows, model = before.shape

    def body(*values):
        grad_rows, base, small = values[4:]
        slope, sum_gain, sum_shift = norm_back(base, row(small, 3), joined(values[:4]))
        current = grad_rows + slope
        branch = (0.5 * current).astype(BF)
        sums = jnp.concatenate([column_sum(branch), sum_gain, sum_shift], axis=0)
        return current, branch, sums

    outs = [shape_of(rows, model, F32), shape_of(rows, model, BF), shape_of(3, model, F32)]
    return fused(body, "attend_to_feed_back", outs, *parts, grad, before, wide)


def last_step(parts, grad, before, wide):
    rows, model = before.shape

    def body(*values):
        grad_rows, base, small = values[4:]
        slope, sum_gain, sum_shift = norm_back(
            base.astype(F32), row(small, 0), joined(values[:4])
        )
        return grad_rows + slope, jnp.concatenate([sum_gain, sum_shift], axis=0)

    outs = [shape_of(rows, model, F32), shape_of(2, model, F32)]
    return fused(body, "last_step", outs, *parts, grad, before, wide)


def small_unpack(gathered, counts, place):
    rows, modules_rows = counts
    shards, unit, half, planes = place.shards, place.unit, place.half, place.planes
    model = shards * unit
    if not place.aligned:
        wide = gathered[:, :rows].transpose(1, 0, 2).reshape(rows, model).astype(F32)
        bias = gathered[:, rows:].reshape(planes, 2, 2, 2, 2, half)
        bias = lax.dynamic_index_in_dim(bias, place.second, 1, keepdims=False)
        bias = lax.dynamic_index_in_dim(bias, place.rep, 3, keepdims=False)
        bias = bias.transpose(2, 0, 1, 3).reshape(2, -1).astype(F32)
        heads = [
            lax.dynamic_slice_in_dim(wide[index].reshape(SPAN, -1), place.member, 1, 0)
            for index in (5, 6)
        ]
        return wide, bias, jnp.concatenate([heads[0], jnp.zeros_like(heads[0]), heads[1]], axis=1)

    def kernel(spot, ref, wide, bias, mix):
        lane = lax.broadcasted_iota(jnp.int32, (1, LANES), 1)
        second, core, rep = spot[1], spot[2], spot[3]
        member = (spot[0] & 1) * 4 + second * 2 + core

        def doubled(value):
            return jnp.concatenate([value, value], axis=1)

        for pair in range(shards // 2):
            both = [doubled(ref[2 * pair + side].astype(F32)) for side in range(2)]
            value = jnp.where(lane < unit, both[0], both[1])
            wide[:, pair * LANES : (pair + 1) * LANES] = value[:rows]
        for module in range(2):
            for index in range(2 * planes):
                shard = (index // 2 * 2 + second) * 2 + index % 2
                block = doubled(ref[shard].astype(F32))
                start = rows + (module * 2) * 2
                options = [
                    jnp.where(
                        lane < unit,
                        block[start + 2 * side : start + 2 * side + 1],
                        block[start + 2 * side + 1 : start + 2 * side + 2],
                    )
                    for side in range(2)
                ]
                value = jnp.where(rep == 0, options[0], options[1])
                bias[module : module + 1, index * half : (index + 1) * half] = value
        mix[...] = jnp.zeros_like(mix)
        pair = [doubled(ref[member + SPAN * group].astype(F32)) for group in range(2)]
        value = jnp.where(lane < unit, pair[0], pair[1])
        mix[:, :LANES] = value[5:6]
        mix[:, 2 * LANES :] = value[6:7]

    outs = [
        shape_of(rows, model, F32),
        shape_of(2, 2 * planes * half, F32),
        shape_of(1, 3 * LANES, F32),
    ]
    return kernel_call(kernel, "small_unpack", outs, (place.spot, gathered), scalars=1)


def shard_gather(value, place):
    copies = jnp.broadcast_to(value[None], (place.shards, *value.shape))
    return lax.all_to_all(copies, "shard", 0, 0, tiled=True)


def small_reduce(sums, mix_sums, biases, distance, counts, place):
    input_sums, first_sums, attend_sums, conv_sums, last_sums = sums
    rows, taps = counts
    unit, half, planes, shards = place.unit, place.half, place.planes, place.shards
    model = unit * shards
    width = mix_sums.shape[1] // 3
    if not place.aligned:
        heads = []
        for start in (0, 2 * width):
            whole = jnp.zeros((SPAN, model // SPAN), F32)
            block = mix_sums[:, start : start + width]
            whole = lax.dynamic_update_slice_in_dim(whole, block, place.member, 0)
            heads.append(whole.reshape(1, model))
        wide = jnp.concatenate(
            [
                input_sums, first_sums, *heads, attend_sums[:2], conv_sums[taps:], last_sums,
                attend_sums[2:], conv_sums[:taps],
            ],
            axis=0,
        )
        wide = wide.reshape(-1, shards, unit).transpose(1, 0, 2)
        pair = jnp.stack(biases).reshape(2, planes, 2, half)
        bias = lax.dynamic_update_slice(
            jnp.zeros((planes, 2, 2, 2, 2, half), F32),
            pair.transpose(1, 2, 0, 3)[:, None, :, :, None, :],
            (0, place.second, 0, 0, place.rep, 0),
        ).reshape(shards, -1, unit)
        both = jnp.concatenate([wide, bias], axis=1)
        both = lax.all_to_all(
            jnp.concatenate([both, both], axis=0), ("rep", "shard"), 0, 0, tiled=True
        )
        total = jnp.sum(both, axis=0)
        for bit in range((2 * shards).bit_length() - 1):
            distance = distance + flipped(distance, 1 << bit)
        return total[:rows], total[rows:].reshape(2, 2 * half), distance
    extent = -(-(rows + 8) // 32) * 32
    size = extent // 2
    table_rows = distance.shape[0]
    fold = -(-table_rows // 32) * 16

    def pack(spot, in_ref, first, attend_ref, conv, last, mix, bias_one, bias_two, table, out, wide):
        plane, second, core, rep = spot[0], spot[1], spot[2], spot[3]
        wide[...] = jnp.zeros_like(wide)
        wide[0:2, :] = in_ref[...]
        wide[2:5, :] = first[...]
        wide[7:9, :] = attend_ref[0:2, :]
        wide[9:13, :] = conv[taps:, :]
        wide[13:16, :] = last[...]
        wide[16:17, :] = attend_ref[2:3, :]
        wide[17 : 17 + taps, :] = conv[:taps, :]
        lane = lax.broadcasted_iota(jnp.int32, (1, LANES), 1)
        for group in range(2):
            start = ((group * 2 + (plane & 1)) * 2 + second) * LANES
            target = pl.ds(pl.multiple_of(start, LANES), LANES)
            for index, begin in ((5, 0), (6, 2 * width)):
                value = mix[:, begin : begin + LANES]
                moved = pltpu.roll(jnp.broadcast_to(value, (8, LANES)), unit, axis=1)[:1]
                low = value if group == 0 else moved
                high = moved if group == 0 else value
                placed = jnp.where(core == 0, low, high)
                placed = jnp.where(lane // unit == core, placed, 0.0)
                wide[index : index + 1, target] = placed
        for module, ref in enumerate((bias_one, bias_two)):
            for index in range(planes):
                pair = [
                    ref[:, start * half : (start + 1) * half]
                    for start in (2 * index, 2 * index + 1)
                ]
                moved = [
                    pltpu.roll(jnp.broadcast_to(item, (8, LANES)), unit, axis=1)[:1]
                    for item in pair
                ]
                halves = (
                    jnp.where(lane < unit, pair[0], moved[1]),
                    jnp.where(lane < unit, moved[0], pair[1]),
                )
                start = pl.multiple_of((index * 2 + second) * LANES, LANES)
                for side in range(2):
                    for part, value in enumerate(halves):
                        line = rows + (module * 2 + side) * 2 + part
                        wide[line : line + 1, pl.ds(start, LANES)] = jnp.where(
                            rep == side, value, 0.0
                        )
        rest = jnp.concatenate(
            [table[fold:, :], jnp.zeros((2 * fold - table_rows, unit), F32)], axis=0
        )
        folded = jnp.concatenate([table[:fold, :], rest], axis=1)
        folded = folded.astype(BF)
        wide_lane = lax.broadcasted_iota(jnp.int32, (size, LANES), 1)
        for pair in range(shards // 2):
            block = wide[:, pair * LANES : (pair + 1) * LANES]
            upper, lower = block[:size], block[size:]
            both = (
                jnp.where(wide_lane < unit, upper, pltpu.roll(lower, unit, axis=1)),
                jnp.where(wide_lane < unit, pltpu.roll(upper, unit, axis=1), lower),
            )
            for side in range(2):
                for target in (2 * pair + side, 2 * pair + side + shards):
                    out[target, :size, :] = both[side].astype(BF)
                    out[target, size:, :] = folded

    packed = kernel_call(
        pack,
        "small_pack",
        [jax.ShapeDtypeStruct((2 * shards, size + fold, LANES), BF)],
        (place.spot, *sums, mix_sums, *biases, distance),
        scalars=1,
        scratch=[pltpu.VMEM((extent, model), F32)],
    )[0]
    packed = lax.all_to_all(packed, ("rep", "shard"), 0, 0, tiled=True)

    def unpack(spot, ref, wide, bias, table):
        total = ref[0].astype(F32)
        for index in range(1, 2 * shards):
            total = total + ref[index].astype(F32)
        moved = pltpu.roll(total, unit, axis=1)
        table[:fold, :] = total[size:, :unit]
        table[fold:, :] = moved[size : size + table_rows - fold, :unit]
        both = jnp.concatenate([total[:size, :unit], moved[:size, :unit]], axis=0)
        wide[...] = both[:rows]
        for module in range(2):
            for side in range(2):
                line = rows + (module * 2 + side) * 2
                bias[module : module + 1, side * half : (side + 1) * half] = jnp.concatenate(
                    [both[line : line + 1], both[line + 1 : line + 2]], axis=1
                )

    return kernel_call(
        unpack,
        "small_sum",
        [shape_of(rows, unit, F32), shape_of(2, 2 * half, F32), shape_of(*distance.shape, F32)],
        (place.spot, packed),
        scalars=1,
    )


class Place:
    def __init__(self, unit, half, head):
        self.shards = lax.axis_size("shard")
        self.planes = self.shards // QUAD
        self.unit, self.half = unit, half
        self.pack_rows = 2 * unit + half
        self.rep = lax.axis_index("rep")
        self.shard = lax.axis_index("shard")
        self.core = self.shard % 2
        self.second = self.shard // 2 % 2
        self.plane = self.shard // QUAD
        self.member = self.shard % SPAN
        self.spot = jnp.stack([self.plane, self.second, self.core, self.rep])
        self.flat_spot = jnp.stack([jnp.zeros_like(self.plane), self.second, self.core, self.rep])
        self.span_spot = self.member.reshape(1)
        self.aligned = whole_heads(head, self)
        self.feed_masks = (self.shards, 2)
        self.span_masks = (4, 2)


def along(value, by, place):
    count = place.shards
    route = [(i, i + by) for i in range(count) if 0 <= i + by < count]
    return lax.ppermute(value, "shard", route)


def shards(
    inputs,
    ff_in,
    ff_out,
    ff_bias,
    attn_in,
    attn_out,
    conv_in,
    conv_out,
    depthwise,
    distance,
    vectors,
    attn_bias,
    cotangent,
):
    rows, model = inputs.shape
    unit, half = ff_in.shape[2], ff_out.shape[2] // 2
    head = distance.shape[2]
    place = Place(unit, half, head)
    tap_count = depthwise.shape[1]
    edge = -(-(tap_count - 1) // 16) * 16
    bias_rows = ff_bias.shape[2] // unit
    count = vectors.shape[1]
    taps = (count + 1, tap_count)
    wide_rows = count + 1 + tap_count

    first_parts = feed_pack(ff_in, ff_out, 0, place)
    small = jnp.concatenate(
        [vectors[0], attn_bias, depthwise[0], ff_bias[0].reshape(2 * bias_rows, unit)], axis=0
    )
    first_pack = pack_rows(first_parts)
    first_pack, current, mix_in, later_in = tied(first_pack, inputs, attn_in[0], ff_in)
    first_far = plane_start(first_pack, place)
    pieces = square_gather(current, place.feed_masks)
    second_parts = feed_pack(later_in, ff_out, 1, place)
    columns = attend_columns(mix_in, place) if place.aligned else (mix_in, mix_in)
    (
        first_far[0], first_far[1], small, second_in, second_other, second_out, *early
    ) = tied(*first_far, small, *second_parts, *columns, *pieces)
    columns, pieces = early[:2], early[2:]
    small = shard_gather(small, place)
    second_pack = pack_rows((second_in, second_other, second_out))
    glue_width = 3 * model // SPAN if place.aligned else model
    glue = conv_pick(conv_in[0], conv_out[0], glue_width, place)
    if place.aligned:
        columns = attend_arrange(*columns, glue, place)
    first_near = plane_finish(first_pack, first_far, place)
    last = place.planes - 1
    first_near[last], small, glue, second_pack, *columns = tied(
        first_near[last], small, glue, second_pack, *columns
    )
    first_packs = with_core(first_near)
    wide, feed_bias, mix_bias = small_unpack(small, (wide_rows, 2 * bias_rows), place)
    table = wide_table(distance[0], rows)
    wide, mix_bias, table, pieces[0] = tied(wide, mix_bias, table, pieces[0])

    parts, saved_first = feed(
        pieces, first_packs, feed_bias[0:1], wide, 0, place.feed_masks, place
    )
    if place.aligned:
        mix_near, one, two = columns
        odd, even = flipped(one, QUAD), flipped(two, 2 * QUAD)
        parts, (odd, even, mix_out) = tied_lists(parts, (odd, even, attn_out[0]))
        mix_outs = [mix_out, flipped(mix_out, SPAN)]
        relayed = flipped(even[4 * unit :], QUAD)
    after_first, hidden = feed_to_attend(parts, inputs, wide)
    near, far = group_gather(hidden, place.span_masks)
    if place.aligned:
        near, far, (relayed, second_pack, mix_outs[1]) = tied_lists(
            near, far, (relayed, second_pack, mix_outs[1])
        )
        mix_kept, mix_sent, glue = attend_weights_split(
            mix_near, glue, (odd, even, relayed), place
        )
        mix_in, mix_out = attend_weights_lay(mix_kept, mix_sent, mix_outs, place)
        glue, via_first, via_second, unused_half = conv_square(glue, place.feed_masks)
    else:
        mix_in, mix_out = attend_weights_whole(attn_in[0], attn_out[0], head, place)
        glue = [lax.all_gather(glue, "shard", axis=0, tiled=True)]
        near, far, (second_pack,) = tied_lists(near, far, (second_pack,))
    second_far = plane_start(second_pack, place)
    saved_attend, kept, sent = attend((near, far), mix_in, mix_bias, mix_out, table, place)
    if place.aligned:
        sent, via_first, via_second = tied(sent, via_first, via_second)
        low, high = conv_relay(via_first, via_second, place.feed_masks)
        glue_far = [flipped(item, 1) for item in (glue, via_first, via_second)]
        kept, *glue_far = tied(kept, *glue_far)
    sent, *second_far = tied(sent, *second_far)
    parts = group_reduce(kept, sent, place.span_masks)
    if place.aligned:
        parts, (low, high), (second_pack, *second_far) = tied_lists(
            parts, (low, high), (second_pack, *second_far)
        )
        glue = [glue, via_first, via_second, low, high]
        glue += [*glue_far, flipped(low, 1), flipped(high, 1)]
    else:
        parts, (second_pack, *second_far) = tied_lists(parts, (second_pack, *second_far))
    glue = conv_whole_weights(glue, model, place)
    second_near = plane_finish(second_pack, second_far, place)
    after_attend, conv_hidden, doubled, glued = convolve_start(
        parts, after_first, wide, count, glue, place
    )
    border = along(glued[rows - edge :], 1, place)
    border = jnp.where(place.member == 0, jnp.zeros_like(border), border)
    border, *second_near = tied(border, *second_near)
    second_packs = with_core(second_near)
    mixed, rest, after_conv, hidden = convolve_finish(
        glued, border, wide, taps, glue, after_attend, place
    )
    hidden, *second_packs = tied(hidden, *second_packs)
    pieces = square_gather(hidden, place.feed_masks)
    parts, saved_second = feed(
        pieces, second_packs, feed_bias[1:2], wide, None, place.feed_masks, place
    )
    output, grad_last, branch, last_sums = turn_around(parts, after_conv, wide, cotangent)

    pieces = square_gather(branch, place.feed_masks)
    result, branch, slope, second_bias = feed_back(pieces, second_packs, saved_second, place)
    second_grads = [
        *feed_in_grads(saved_second[0], slope, place),
        *feed_out_grads(saved_second[2], pieces, place),
    ]
    *result, second_grads[1], second_grads[3] = tied(*result, second_grads[1], second_grads[3])
    second_grads[1], second_grads[3] = flipped(second_grads[1], 1), flipped(second_grads[3], 1)
    parts = square_reduce(result, place.feed_masks)
    second_split = [plane_split(*pair, place) for pair in (second_grads[:2], second_grads[2:])]
    parts, *second_split = tied_lists(parts, *second_split)
    second_lists = [plane_early(pieces, place) for pieces in second_split]
    grad_conv, conv_branch, main, halo, conv_sums = convolve_back_start(
        parts, grad_last, after_conv, mixed, wide, taps, glue, glued, border, place
    )
    incoming = along(halo, -1, place)
    incoming, second_tops = tied_tops(incoming, second_lists, place)
    second_early = [lists[0] for lists in second_lists]
    incoming = jnp.where(place.member == SPAN - 1, jnp.zeros_like(incoming), incoming)
    grad_attend, branch, slope, attend_sums = convolve_back_finish(
        main, incoming, doubled, glue, after_attend, wide, grad_conv, place
    )
    conv_kept, conv_sent = conv_grads_start(conv_hidden, slope, rest, conv_branch, place)
    second_tops = [plane_total(values) for values in second_tops]
    count_early = len(second_early[0])
    branch, conv_kept, conv_sent, *flat = tied(
        branch, conv_kept, conv_sent, *second_tops, *second_early[0], *second_early[1]
    )
    second_tops = flat[:2]
    second_early = [flat[2 : 2 + count_early], flat[2 + count_early :]]
    near, far = group_gather(branch, place.span_masks)
    conv_shares = conv_grads_split(conv_kept, flipped(conv_sent, 1), place)
    near, far, conv_shares, second_tops = tied_lists(near, far, conv_shares, second_tops)
    if place.aligned:
        conv_shares = conv_grads_square(conv_shares, place.feed_masks)
    second_lasts = [plane_last(top, place) for top in second_tops]
    back = attend_back((near, far), saved_attend, mix_in, mix_out, table, place)
    grad_mixed, kept, sent, branch, grad_table, table_far = back
    (sent,), second_lasts, conv_shares = tied_lists((sent,), second_lasts, conv_shares)
    mix_grad_in, mix_grad_out, mix_sums = attend_grads(saved_attend, grad_mixed, branch, place)
    second_sums = [plane_add([*own, last]) for own, last in zip(second_early, second_lasts)]
    second_other = flipped(second_sums[0][unit:], 2)
    if place.aligned:
        mix_kept, mix_swap, *mix_outs = attend_grads_lay(mix_grad_in, mix_grad_out, place)
        kept, mix_swap = tied(kept, mix_swap)
        mix_swap = flipped(mix_swap, 1)
        kept, mix_swap = tied(kept, mix_swap)
    parts = group_reduce(kept, sent, place.span_masks)
    if place.aligned:
        mix_outs[1] = flipped(mix_outs[1], SPAN)
        planed = plane_pieces(mix_kept, mix_swap, conv_shares, place)
        parts, (second_other, mix_outs[1]), planed = tied_lists(
            parts, (second_other, mix_outs[1]), planed
        )
    else:
        parts, (second_other,) = tied_lists(parts, (second_other,))
    second_pack = pack_rows((second_sums[0][:unit], second_other, second_sums[1]))
    grad_distance = distance_gradient(grad_table, table_far, rows)
    grad_first, branch, first_sums = attend_to_feed_back(parts, grad_attend, after_first, wide)
    if place.aligned:
        (branch,), planed = tied_lists((branch,), planed)
        mix_zero, mix_two, mix_three, conv_zero, conv_two, joint = planed
        pieces = square_gather(branch, place.feed_masks)
        joint = flipped(joint, QUAD)
        mix_two = flipped(mix_two, 2 * QUAD)
        pieces, (mix_two, mix_three, joint) = tied_lists(pieces, (mix_two, mix_three, joint))
        mix_three = flipped(mix_three, 3 * QUAD)
        conv_last = plane_last(conv_grads_top(conv_two, joint), place)
    else:
        pieces = square_gather(branch, place.feed_masks)
        conv_whole = conv_grads_whole(conv_shares[0], place)
        mix_grads = attend_grads_whole(mix_grad_in, mix_grad_out, head, place)
        mix_grads = [item[None] for item in mix_grads]
    kept, sent = feed_out_grads(saved_first[2], pieces, place)
    out_split = plane_split(kept, flipped(sent, 1), place)
    pieces, out_split, (second_pack,) = tied_lists(pieces, out_split, (second_pack,))
    second_theirs = flipped(second_pack, place.shards)
    out_lists = plane_early(out_split, place)
    result, branch, slope, first_bias = feed_back(pieces, first_packs, saved_first, place)
    slope, (out_top,) = tied_tops(slope, [out_lists], place)
    slope, second_theirs = tied(slope, second_theirs)
    out_early = out_lists[0]
    if place.aligned:
        slope, mix_three = tied(slope, mix_three)
        mix_own, mix_other, mix_out_sum = attend_grads_sum(
            (mix_zero, joint, mix_two, mix_three, *mix_outs), place
        )
        mix_arrived = flipped(mix_other, 2)
        mix_theirs = [flipped(mix_own, place.shards), None, flipped(mix_out_sum, place.shards)]
    kept, sent = feed_in_grads(saved_first[0], slope, place)
    kept, *result = tied(kept, *result)
    in_swapped = flipped(sent, 1)
    in_lists = plane_early(plane_split(kept, in_swapped, place), place)
    parts = square_reduce(result, place.feed_masks)
    out_last = plane_last(plane_total(out_top), place)
    parts, out_early, *in_lists = tied_lists(parts, out_early, *in_lists.values())
    in_early, in_top = in_lists[0], in_lists[-1]
    in_top = plane_total(in_top)
    if place.aligned:
        parts[0], in_top, mix_arrived, mix_theirs[0], mix_theirs[2], conv_last = tied(
            parts[0], in_top, mix_arrived, mix_theirs[0], mix_theirs[2], conv_last
        )
        mix_theirs[1] = flipped(mix_arrived, place.shards)
        conv_mine = conv_grads_sum(conv_zero, joint, conv_last)
        conv_theirs = flipped(conv_mine, place.shards)
    in_last = plane_last(in_top, place)
    grad_input, input_sums = last_step(parts, grad_first, inputs, wide)
    input_sums, out_last = tied(input_sums, out_last)
    out_sum = plane_add([*out_early, out_last])
    out_theirs = flipped(out_sum, place.shards)
    small_grads, bias_grads, grad_distance = small_reduce(
        (input_sums, first_sums, attend_sums, conv_sums, last_sums),
        mix_sums,
        (first_bias, second_bias),
        grad_distance,
        (wide_rows, tap_count),
        place,
    )
    if place.aligned:
        mix_grads = attend_grads_final((mix_own, mix_arrived, mix_out_sum), mix_theirs, place)
        conv_grads = conv_grads_final(conv_mine, conv_theirs, place)
    else:
        conv_grads = (
            jnp.concatenate([conv_whole[0], conv_whole[1]], axis=1)[None],
            conv_whole[2][None],
        )

    (in_last, small_grads, out_theirs), mix_grads, conv_grads = tied_lists(
        (in_last, small_grads, out_theirs), mix_grads, conv_grads
    )
    in_sum = plane_add([*in_early, in_last])
    in_own, in_other = in_sum[:unit], flipped(in_sum[unit:], 2)
    in_theirs = flipped(in_own, place.shards)
    first_mine = [(in_own, in_theirs), (in_other, flipped(in_other, place.shards))]
    first_mine = [*first_mine, (out_sum, out_theirs)]
    cuts = (0, unit, 2 * unit, 2 * unit + half)
    second_mine = [
        (second_pack[cuts[i] : cuts[i + 1]], second_theirs[cuts[i] : cuts[i + 1]])
        for i in range(3)
    ]
    feed_grads = feed_final((first_mine, second_mine), place)
    return (
        output,
        grad_input,
        *feed_grads,
        bias_grads[None],
        *mix_grads,
        *conv_grads,
        small_grads[count + 1 :][None],
        grad_distance[None],
        small_grads[:count][None],
        small_grads[count : count + 1],
    )


def solution(mesh):
    in_specs = (
        P(("rep", "shard"), None),
        P(None, None, "shard", None),
        P(None, None, "shard", None),
        P(None, None, "shard"),
        P(None, "shard", None),
        P(None, "shard", None),
        P(None, "shard", None),
        P(None, "shard", None),
        P(None, None, "shard"),
        P(),
        P(None, None, "shard"),
        P(None, "shard"),
        P(("rep", "shard"), None),
    )
    out_specs = (
        P(("rep", "shard"), None),
        P(("rep", "shard"), None),
        P(None, None, "shard", None),
        P(None, None, "shard", None),
        P(None, None, "shard"),
        P(None, "shard", None),
        P(None, "shard", None),
        P(None, "shard", None),
        P(None, "shard", None),
        P(None, None, "shard"),
        P(),
        P(None, None, "shard"),
        P(None, "shard"),
    )
    return jax.shard_map(shards, mesh=mesh, in_specs=in_specs, out_specs=out_specs, check_vma=False)
```

```python
import jax
import jax.numpy as jnp
from jax import lax
from jax.experimental import pallas as pl
from jax.experimental.pallas import tpu as pltpu
from jax.sharding import PartitionSpec as P

LEFT = 64
RIGHT = 8
SPAN = 8
QUAD = 4
EPSILON = 1e-05
BF = jnp.bfloat16
F32 = jnp.float32
MIB = 1 << 20
LANES = 128


def dot_nn(left, right):
    return jnp.dot(left, right, preferred_element_type=F32)


def dot_nt(left, right):
    return lax.dot_general(left, right, (((1,), (1,)), ((), ())), preferred_element_type=F32)


def dot_tn(left, right):
    return lax.dot_general(left, right, (((0,), (0,)), ((), ())), preferred_element_type=F32)


def column_sum(values):
    return jnp.sum(values.astype(F32), axis=0, keepdims=True)


def standard(values):
    center = values - jnp.mean(values, axis=-1, keepdims=True)
    scale = lax.rsqrt(jnp.mean(center * center, axis=-1, keepdims=True) + EPSILON)
    return center * scale, scale


def norm_back(values, gain, grad):
    unit, scale = standard(values)
    inner = grad * gain
    first = jnp.mean(inner, axis=-1, keepdims=True)
    second = jnp.mean(inner * unit, axis=-1, keepdims=True)
    return scale * (inner - first - unit * second), column_sum(grad * unit), column_sum(grad)


def logistic(values):
    return 1.0 / (1.0 + jnp.exp(-values))


def silu_slope(values):
    gate = logistic(values)
    return gate * (1.0 + values * (1.0 - gate))


def vmem(count):
    return [pl.BlockSpec(memory_space=pltpu.VMEM)] * count


def shape_of(rows, columns, dtype):
    return jax.ShapeDtypeStruct((rows, columns), dtype)


class Part:
    def __init__(self, array, block, index):
        self.array, self.block, self.index = array, block, index
        self.shape, self.dtype = block, array.dtype
        self.size = 1
        for extent in block:
            self.size *= extent


def kernel_call(body, name, outs, operands, scalars=0, scratch=(), flops=0, limit=24):
    moved = sum(item.size * item.dtype.itemsize for item in (*operands[scalars:], *outs))
    specs = [pl.BlockSpec(memory_space=pltpu.SMEM)] * scalars
    arrays = list(operands[:scalars])
    for item in operands[scalars:]:
        if isinstance(item, Part):
            specs.append(pl.BlockSpec(item.block, lambda step, index=item.index: index))
            arrays.append(item.array)
        else:
            specs += vmem(1)
            arrays.append(item)
    return pl.pallas_call(
        body,
        grid=(1,),
        in_specs=specs,
        out_specs=vmem(len(outs)),
        out_shape=list(outs),
        scratch_shapes=list(scratch),
        compiler_params=pltpu.CompilerParams(vmem_limit_bytes=limit * MIB),
        cost_estimate=pl.CostEstimate(flops=flops, bytes_accessed=moved, transcendentals=0),
        name=name,
    )(*arrays)


def fused(body, name, outs, *operands, flops=0):
    def kernel(*refs):
        results = body(*[ref[...] for ref in refs[: len(operands)]])
        for ref, value in zip(refs[len(operands) :], results):
            ref[...] = value.astype(ref.dtype)

    return kernel_call(kernel, name, outs, operands, flops=flops)


def tied(*values):
    return lax.optimization_barrier(values)


def tied_lists(*lists):
    flat = iter(tied(*[item for values in lists for item in values]))
    return [[next(flat) for _ in values] for values in lists]


def flipped(value, mask):
    total = lax.axis_size("rep") * lax.axis_size("shard")
    return lax.ppermute(value, ("rep", "shard"), [(i, i ^ mask) for i in range(total)])


def square_gather(value, masks):
    first, second = masks
    return [
        value,
        flipped(value, first),
        flipped(value, second),
        flipped(value, first | second),
    ]


def square_reduce(parts, masks):
    first, second = masks
    own, via_first, via_second, cross = parts
    return [
        own,
        flipped(cross, first | second),
        flipped(via_first, first),
        flipped(via_second, second),
    ]


def joined(parts):
    return parts[0] + sum(part.astype(F32) for part in parts[1:])


def place_feed(spot, views, w_in, w_out, unit, half):
    plane, second, core = spot[0], spot[1], spot[2]
    for step, near, in_ref, out_ref, start in views:
        column = (plane ^ step) * 2
        for turn in range(2):
            row = ((column + (second ^ turn)) * 2 + (core ^ near)) * unit
            source = slice(turn * unit, (turn + 1) * unit)
            w_in[pl.ds(pl.multiple_of(row, unit), unit), :] = in_ref[source, :]
        row = (column + (core ^ near)) * half
        w_out[pl.ds(pl.multiple_of(row, half), half), :] = out_ref[start : start + half, :]


def pack_views(refs, place):
    planes, count = place.planes, 2 * place.planes
    if len(refs) == count:
        return [(i % planes, i // planes, ref, ref, 2 * place.unit) for i, ref in enumerate(refs)]
    return [(i % planes, i // planes, refs[i], refs[count + i], 0) for i in range(count)]


def feed(pieces, packs, bias, wide, norm_row, masks, place):
    rows, model = pieces[0].shape
    inner = bias.shape[1]
    count, total = len(pieces), len(pieces) * rows
    unit, half = place.unit, place.half

    def kernel(spot_ref, *refs):
        piece_refs, pack_refs = refs[:count], refs[count : count + len(packs)]
        bias_ref, wide_ref, hidden, upper, active = refs[count + len(packs) :][:5]
        outs = refs[count + len(packs) + 5 : -2]
        w_in, w_out = refs[-2:]
        place_feed(spot_ref, pack_views(pack_refs, place), w_in, w_out, unit, half)
        for index, ref in enumerate(piece_refs):
            block = ref[...]
            if norm_row is not None:
                scaled, unused_scale = standard(block.astype(F32))
                gain = wide_ref[norm_row : norm_row + 1, :]
                shift = wide_ref[norm_row + 1 : norm_row + 2, :]
                block = (scaled * gain + shift).astype(BF)
            hidden[index * rows : (index + 1) * rows, :] = block
        before = dot_nn(hidden[...], w_in[...]) + bias_ref[...]
        upper[...] = before
        active[...] = (before * logistic(before)).astype(BF)
        result = dot_nn(active[...], w_out[...])
        for index, ref in enumerate(outs):
            ref[...] = result[index * rows : (index + 1) * rows].astype(ref.dtype)

    outs = [
        shape_of(total, model, BF),
        shape_of(total, inner, F32),
        shape_of(total, inner, BF),
        shape_of(rows, model, F32),
    ] + [shape_of(rows, model, BF)] * (count - 1)
    results = kernel_call(
        kernel,
        "feed_forward",
        outs,
        (place.spot, *pieces, *packs, bias, wide),
        scalars=1,
        scratch=[pltpu.VMEM((model, inner), BF), pltpu.VMEM((inner, model), BF)],
        flops=4 * total * model * inner,
    )
    return square_reduce(results[3:], masks), results[:3]


def feed_back(pieces, packs, saved, place):
    hidden, upper, active = saved
    rows, model = pieces[0].shape
    total, inner = upper.shape
    count = len(pieces)
    unit, half = place.unit, place.half

    def kernel(spot_ref, *refs):
        piece_refs, pack_refs = refs[:count], refs[count : count + len(packs)]
        upper_ref, branch, slope, sums = refs[count + len(packs) :][:4]
        outs = refs[count + len(packs) + 4 : -2]
        w_in, w_out = refs[-2:]
        place_feed(spot_ref, pack_views(pack_refs, place), w_in, w_out, unit, half)
        for index, ref in enumerate(piece_refs):
            branch[index * rows : (index + 1) * rows, :] = ref[...]
        grad = dot_nt(branch[...], w_out[...]) * silu_slope(upper_ref[...])
        slope[...] = grad.astype(BF)
        sums[...] = column_sum(slope[...])
        result = dot_nt(slope[...], w_in[...])
        for index, ref in enumerate(outs):
            ref[...] = result[index * rows : (index + 1) * rows].astype(ref.dtype)

    outs = [
        shape_of(total, model, BF),
        shape_of(total, inner, BF),
        shape_of(1, inner, F32),
        shape_of(rows, model, F32),
    ] + [shape_of(rows, model, BF)] * (count - 1)
    results = kernel_call(
        kernel,
        "feed_backward",
        outs,
        (place.spot, *pieces, *packs, upper),
        scalars=1,
        scratch=[pltpu.VMEM((model, inner), BF), pltpu.VMEM((inner, model), BF)],
        flops=4 * total * model * inner,
    )
    branch, slope, sums = results[:3]
    return results[3:], branch, slope, sums


def feed_out_grads(active, pieces, place):
    rows, model = pieces[0].shape
    inner = active.shape[1]
    planes, half = place.planes, place.half
    count = len(pieces)

    def kernel(spot, active_ref, *refs):
        total, kept, sent = refs[-1], refs[count], refs[count + 1]
        branch = jnp.concatenate([ref[...] for ref in refs[:count]], axis=0)
        total[...] = dot_tn(active_ref[...], branch)
        for near, ref in enumerate((kept, sent)):
            for step in range(planes):
                row = ((spot[0] ^ step) * 2 + (spot[2] ^ near)) * half
                source = pl.ds(pl.multiple_of(row, half), half)
                ref[step * half : (step + 1) * half, :] = total[source, :].astype(BF)

    return kernel_call(
        kernel,
        "feed_out_grads",
        [shape_of(planes * half, model, BF)] * 2,
        (place.spot, active, *pieces),
        scalars=1,
        scratch=[pltpu.VMEM((inner, model), F32)],
        flops=2 * active.shape[0] * model * inner,
    )


def feed_in_grads(hidden, slope, place):
    model, inner = hidden.shape[1], slope.shape[1]
    planes, unit = place.planes, place.unit

    def kernel(spot, hidden_ref, slope_ref, kept, sent, total):
        total[...] = dot_tn(hidden_ref[...], slope_ref[...])
        for near, ref in enumerate((kept, sent)):
            for step in range(planes):
                for turn in range(2):
                    column = (spot[0] ^ step) * 2 + (spot[1] ^ turn)
                    row = (column * 2 + (spot[2] ^ near)) * unit
                    start = (2 * step + turn) * unit
                    source = pl.ds(pl.multiple_of(row, unit), unit)
                    ref[start : start + unit, :] = total[source, :].astype(BF)

    return kernel_call(
        kernel,
        "feed_in_grads",
        [shape_of(2 * planes * unit, inner, BF)] * 2,
        (place.spot, hidden, slope),
        scalars=1,
        scratch=[pltpu.VMEM((model, inner), F32)],
        flops=2 * hidden.shape[0] * model * inner,
    )


def plane_split(kept, swapped, place):
    planes = place.planes
    size = kept.shape[0] // planes

    def body(kept_part, swapped_part):
        both = kept_part.astype(F32) + swapped_part.astype(F32)
        return [both[step * size : (step + 1) * size] for step in range(planes)]

    outs = [shape_of(size, kept.shape[1], BF)] * planes
    return fused(body, "plane_split", outs, kept, swapped)


def plane_early(pieces, place):
    lists = {step: [piece] for step, piece in enumerate(pieces)}
    top = place.planes.bit_length() - 2
    for bit in range(top):
        for step in [step for step in sorted(lists) if step >> bit & 1]:
            values = lists.pop(step)
            value = values[0] if len(values) == 1 else plane_add(values)
            lists[step ^ 1 << bit].append(flipped(value, QUAD << bit))
    return lists


def plane_last(value, place):
    return flipped(value, QUAD * (place.planes // 2))


def tied_tops(value, all_lists, place):
    top = place.planes // 2
    flat = [item for lists in all_lists for item in lists[top]]
    value, *flat = tied(value, *flat)
    flat = iter(flat)
    return value, [[next(flat) for _ in lists[top]] for lists in all_lists]


def plane_total(values):
    return values[0] if len(values) == 1 else plane_add(values)


def feed_pack(ff_in, ff_out, module, place):
    rows, hidden = ff_in.shape[2:]
    width, model = ff_out.shape[2:]
    half = width // 2
    count = 2 * place.planes * half
    if half % LANES:
        columns = ff_in[0, module].reshape(rows, place.planes, 2, 2, 2, half)
        columns = lax.dynamic_index_in_dim(columns, place.rep, 4, keepdims=False)
        own = lax.dynamic_index_in_dim(columns, place.second, 2, keepdims=False)
        other = lax.dynamic_index_in_dim(columns, 1 - place.second, 2, keepdims=False)
        own, other = (item.reshape(rows, count) for item in (own, other))
        part_out = lax.dynamic_slice_in_dim(ff_out[0, module], place.rep * half, half, 0)
        return own, flipped(other, 2), part_out

    def kernel(spot, in_ref, out_ref, own, other, part_out):
        second, rep = spot[1], spot[3]
        for turn, ref in enumerate((own, other)):
            for index in range(2 * place.planes):
                plane, core = index // 2, index % 2
                start = (((plane * 2 + (second ^ turn)) * 2 + core) * 2 + rep) * half
                source = pl.ds(pl.multiple_of(start, half), half)
                ref[:, index * half : (index + 1) * half] = in_ref[0, 0, :, source]
        part_out[...] = out_ref[0, 0, pl.ds(pl.multiple_of(rep * half, half), half), :]

    own, other, part_out = pl.pallas_call(
        kernel,
        grid=(1,),
        in_specs=[
            pl.BlockSpec(memory_space=pltpu.SMEM),
            pl.BlockSpec((1, 1, rows, hidden), lambda step: (0, module, 0, 0)),
            pl.BlockSpec((1, 1, width, model), lambda step: (0, module, 0, 0)),
        ],
        out_specs=vmem(3),
        out_shape=[
            shape_of(rows, count, BF),
            shape_of(rows, count, BF),
            shape_of(half, model, BF),
        ],
        compiler_params=pltpu.CompilerParams(vmem_limit_bytes=24 * MIB),
        name="feed_columns",
    )(place.spot, ff_in, ff_out)
    return own, flipped(other, 2), part_out


def pack_rows(parts):
    def body(*values):
        return (jnp.concatenate(values, axis=0),)

    rows = sum(item.shape[0] for item in parts)
    out = shape_of(rows, parts[0].shape[1], BF)
    return fused(body, "pack_rows", [out], *parts)[0]


def plane_bits(place):
    return range(place.planes.bit_length() - 1)


def plane_start(pack, place):
    top = place.planes // 2
    return [flipped(pack, QUAD * top), flipped(pack, QUAD)] if top > 1 else [flipped(pack, QUAD)]


def plane_finish(pack, started, place):
    pieces = {0: pack, place.planes // 2: started[0]}
    if len(started) > 1:
        pieces[1] = started[1]
    for bit in reversed(plane_bits(place)):
        for step in sorted(pieces):
            if step % (2 << bit) == 0 and step | 1 << bit not in pieces:
                pieces[step | 1 << bit] = flipped(pieces[step], QUAD << bit)
    return [pieces[step] for step in range(place.planes)]


def with_core(near):
    return [*near, *(flipped(item, 1) for item in near)]


def plane_add(values):
    def body(*items):
        return (sum((item.astype(F32) for item in items[1:]), items[0].astype(F32)),)

    return fused(body, "plane_add", [shape_of(*values[0].shape, BF)], *values)[0]


def feed_final(modules, place):
    unit, half = place.unit, place.half
    inner = modules[0][0][0].shape[1]
    model = modules[0][2][0].shape[1]
    planes = place.planes
    if half % LANES:
        grads_in, grads_out = [], []
        for in_own, in_other, out in modules:
            sides = jnp.stack([jnp.stack(in_own), jnp.stack(in_other)], axis=1)
            sides = jnp.where(place.second == 0, sides, sides[:, ::-1])
            sides = jnp.where(place.rep == 0, sides, sides[::-1])
            sides = sides.reshape(2, 2, unit, planes, 2, half).transpose(2, 3, 1, 4, 0, 5)
            grads_in.append(sides.reshape(unit, -1).astype(F32))
            both = jnp.stack(out)
            both = jnp.where(place.rep == 0, both, both[::-1])
            grads_out.append(both.reshape(2 * half, model).astype(F32))
        return jnp.stack(grads_in)[None], jnp.stack(grads_out)[None]

    def kernel(spot, *refs):
        grad_in, grad_out = refs[-2:]
        second, rep = spot[1], spot[3]
        for module in range(2):
            own = refs[6 * module : 6 * module + 6]
            for turn in range(2):
                for side in range(2):
                    piece = own[2 * turn + side][...].astype(F32)
                    for index in range(2 * planes):
                        plane, core = index // 2, index % 2
                        start = (((plane * 2 + (second ^ turn)) * 2 + core) * 2 + (rep ^ side)) * half
                        target = pl.ds(pl.multiple_of(start, half), half)
                        grad_in[0, module, :, target] = piece[:, index * half : (index + 1) * half]
            for side in range(2):
                target = pl.ds(pl.multiple_of((rep ^ side) * half, half), half)
                grad_out[0, module, target, :] = own[4 + side][...].astype(F32)

    operands = [item for module in modules for pair in module for item in pair]
    outs = [
        jax.ShapeDtypeStruct((1, 2, unit, 4 * inner), F32),
        jax.ShapeDtypeStruct((1, 2, 2 * half, model), F32),
    ]
    return kernel_call(kernel, "feed_final", outs, (place.spot, *operands), scalars=1)


def feed_arrive(sums, place):
    unit = place.unit
    own = sums[0][:unit]
    other = flipped(sums[0][unit:], 2)
    items = [own, other, *sums[1:]]
    return [(item, flipped(item, place.shards)) for item in items]


def score_block(query, keys, table, bias, place, rows, length):
    scores = dot_nt(query, keys)
    spread = dot_nt(query, table)
    band = pltpu.roll(spread, 0, axis=1, stride=1, stride_axis=0)
    column = lax.broadcasted_iota(jnp.int32, (rows, length + 2 * rows), 1)
    bias[...] = jnp.where(column < place, spread[:, :1], spread[:, -1:])
    bias[:, pl.ds(place, 3 * rows)] = band[:, rows:]
    return scores + bias[:, rows : rows + length]


def place_rows(source, columns, target, position, rows):
    for step in range(SPAN):
        spot = pl.ds(pl.multiple_of((position ^ step) * rows, rows), rows)
        target[spot, :] = source[step * rows : (step + 1) * rows, columns]


def split_rows(value, kept, sent, rows):
    for index, step in enumerate((0, 4, 2, 6)):
        target = slice(index * rows, (index + 1) * rows)
        kept[target, :] = value[step * rows : (step + 1) * rows]
        sent[target, :] = value[(step + 1) * rows : (step + 2) * rows].astype(BF)


def join_pieces(refs, target, rows):
    for step, ref in enumerate(refs):
        target[step * rows : (step + 1) * rows, :] = ref[...]


def attend_kernel(*refs):
    spot, pieces, rest = refs[0], refs[1 : 1 + SPAN], refs[1 + SPAN :]
    (weight_in, bias_in, weight_out, table, hidden, mixed, context, peaks, kept, sent) = rest[:10]
    keys, values, bias = rest[10:]
    length, width = context.shape
    rows = length // SPAN
    head = table.shape[1] // 2
    position = spot[0]
    join_pieces(pieces, hidden, rows)
    mixed[...] = (dot_nn(hidden[...], weight_in[...]) + bias_in[...]).astype(BF)
    place_rows(mixed, slice(width, 2 * width), keys, position, rows)
    place_rows(mixed, slice(2 * width, 3 * width), values, position, rows)
    lane = lax.broadcasted_iota(jnp.int32, (rows, width), 1)

    def block(index, carry):
        place = pl.multiple_of(index * rows, rows)
        own = pl.ds(pl.multiple_of((position ^ index) * rows, rows), rows)
        query = mixed[own, :width] * jnp.asarray(head**-0.5, BF)
        results, logs = [], []
        for which in range(2):
            mine = lane // head == which
            part = jnp.where(mine, query, jnp.zeros_like(query))
            scores = score_block(part, keys[...], table[...], bias, place, rows, length)
            top = jnp.max(scores, axis=1, keepdims=True)
            powers = jnp.exp(scores - top)
            total = jnp.sum(powers, axis=1, keepdims=True)
            weights = (powers * (1.0 / total)).astype(BF)
            results.append(dot_nn(weights, values[...]))
            logs.append(top + jnp.log(total))
        context[own, :] = jnp.where(lane < head, results[0], results[1]).astype(BF)
        peaks[own, :] = jnp.where(lane < head, logs[0], logs[1])
        return carry

    lax.fori_loop(0, SPAN, block, 0)
    split_rows(dot_nn(context[...], weight_out[...]), kept, sent, rows)


def attend_back_kernel(*refs):
    spot, pieces, rest = refs[0], refs[1 : 1 + SPAN], refs[1 + SPAN :]
    (mixed, table, peaks, weight_in, weight_out) = rest[:5]
    (branch, grad_mixed, grad_table, far, kept, sent) = rest[5:11]
    keys, values, bias, grad_context, grad_keys, grad_values, slopes, marked = rest[11:]
    length, width = grad_context.shape
    rows = length // SPAN
    head = table.shape[1] // 2
    position = spot[0]
    join_pieces(pieces, branch, rows)
    grad_context[...] = dot_nt(branch[...], weight_out[...]).astype(BF)
    place_rows(mixed, slice(width, 2 * width), keys, position, rows)
    place_rows(mixed, slice(2 * width, 3 * width), values, position, rows)
    grad_keys[...] = jnp.zeros_like(grad_keys)
    grad_values[...] = jnp.zeros_like(grad_values)
    grad_table[...] = jnp.zeros_like(grad_table)
    far[...] = jnp.zeros_like(far)
    lane = lax.broadcasted_iota(jnp.int32, (rows, width), 1)
    for which in range(2):
        for block_id in range(SPAN):
            own = slice(block_id * rows, (block_id + 1) * rows)
            mark = jnp.where(lane % head == block_id, 1.0, 0.0).astype(BF)
            marked[which, own, :] = jnp.where(lane // head == which, keys[own, :], mark)
    factor = head**-0.5
    slopes[:, :rows] = jnp.zeros((rows, rows), BF)
    slopes[:, rows + length :] = jnp.zeros((rows, rows), BF)
    mirror = (
        lax.broadcasted_iota(jnp.int32, (rows, rows), 0)
        + lax.broadcasted_iota(jnp.int32, (rows, rows), 1)
        == rows - 1
    ).astype(BF)

    def block(index, carry):
        place = pl.multiple_of(index * rows, rows)
        own = pl.ds(pl.multiple_of((position ^ index) * rows, rows), rows)
        query = mixed[own, :width] * jnp.asarray(factor, BF)
        results = []
        for which in range(2):
            mine = lane // head == which
            part = jnp.where(mine, query, jnp.zeros_like(query))
            scores = score_block(part, keys[...], table[...], bias, place, rows, length)
            incoming = grad_context[own, :]
            incoming = jnp.where(mine, incoming, jnp.zeros_like(incoming))
            logs = peaks[own, which * head : which * head + 1]
            probs = jnp.exp(scores - logs)
            grad_probs = dot_nt(incoming, values[...])
            shared = jnp.sum(grad_probs * probs, axis=1, keepdims=True)
            grad_low = (probs * (grad_probs - shared)).astype(BF)
            grad_values[...] += dot_tn(probs.astype(BF), incoming)
            grad_keys[...] += dot_tn(grad_low, part)
            slopes[:, rows : rows + length] = grad_low
            window = slopes[:, pl.ds(place, 3 * rows)]
            direct = dot_nn(grad_low, marked[which])
            block_of = jnp.where(mine, SPAN, lane % head)
            early = jnp.sum(jnp.where(block_of < index - 1, direct, 0.0), axis=1, keepdims=True)
            after = (block_of > index + 1) & (block_of < SPAN)
            late = jnp.sum(jnp.where(after, direct, 0.0), axis=1, keepdims=True)
            window = jnp.concatenate(
                [jnp.zeros((rows, rows), F32), dot_nn(mirror, window)], axis=1
            )
            window = pltpu.roll(
                window, 3 * rows + 1, axis=1, stride=1, stride_axis=0
            ).astype(BF)
            grad_table[...] += dot_tn(window, dot_nn(mirror, part).astype(BF))
            part_wide = part.astype(F32)
            far[0:1, :] += jnp.sum(early * part_wide, axis=0, keepdims=True)
            far[1:2, :] += jnp.sum(late * part_wide, axis=0, keepdims=True)
            close = jnp.dot(
                mirror.astype(F32),
                dot_nn(window, table[...]),
                preferred_element_type=F32,
                precision=lax.Precision.HIGHEST,
            )
            results.append(
                direct
                + close
                + early * table[0:1, :].astype(F32)
                + late * table[4 * rows - 1 :, :].astype(F32)
            )
        grad_mixed[own, :width] = (
            jnp.where(lane < head, results[0], results[1]) * factor
        ).astype(BF)
        return carry

    lax.fori_loop(0, SPAN, block, 0)
    for step in range(SPAN):
        source = pl.ds(pl.multiple_of((position ^ step) * rows, rows), rows)
        target = slice(step * rows, (step + 1) * rows)
        grad_mixed[target, width : 2 * width] = grad_keys[source, :].astype(BF)
        grad_mixed[target, 2 * width :] = grad_values[source, :].astype(BF)
    split_rows(dot_nt(grad_mixed[...], weight_in[...]), kept, sent, rows)


def group_gather(value, masks):
    near = square_gather(value, masks)
    return near, [flipped(item, 1) for item in near]


def group_reduce(kept, sent, masks):
    swapped = flipped(sent, 1)
    rows = kept.shape[0] // 4

    def body(kept_part, swapped_part):
        total = kept_part + swapped_part.astype(F32)
        return [total[index * rows : (index + 1) * rows] for index in range(4)]

    outs = [shape_of(rows, kept.shape[1], dtype) for dtype in (F32, BF, BF, BF)]
    return square_reduce(fused(body, "core_sum", outs, kept, swapped), masks)


def in_steps(blocks):
    near, far = blocks
    return [near[0], far[0], near[2], far[2], near[1], far[1], near[3], far[3]]


def attend(blocks, weight_in, bias_in, weight_out, table, place):
    pieces = in_steps(blocks)
    rows, model = pieces[0].shape
    length, width = SPAN * rows, weight_out.shape[0]
    outs = [
        shape_of(length, model, BF),
        shape_of(length, 3 * width, BF),
        shape_of(length, width, BF),
        shape_of(length, width, F32),
        shape_of(length // 2, model, F32),
        shape_of(length // 2, model, BF),
    ]
    hidden, mixed, context, peaks, kept, sent = kernel_call(
        attend_kernel,
        "attend_forward",
        outs,
        (place.span_spot, *pieces, weight_in, bias_in, weight_out, table),
        scalars=1,
        scratch=[
            pltpu.VMEM((length, width), BF),
            pltpu.VMEM((length, width), BF),
            pltpu.VMEM((rows, length + 2 * rows), F32),
        ],
        limit=56,
        flops=48 * length * length * width,
    )
    return (hidden, mixed, context, peaks), kept, sent


def attend_back(blocks, saved, weight_in, weight_out, table, place):
    hidden, mixed, context, peaks = saved
    pieces = in_steps(blocks)
    rows, model = pieces[0].shape
    length, width = SPAN * rows, weight_out.shape[0]
    outs = [
        shape_of(length, model, BF),
        shape_of(length, 3 * width, BF),
        shape_of(4 * rows, width, F32),
        shape_of(8, width, F32),
        shape_of(length // 2, model, F32),
        shape_of(length // 2, model, BF),
    ]
    branch, grad_mixed, grad_table, far, kept, sent = kernel_call(
        attend_back_kernel,
        "attend_backward",
        outs,
        (place.span_spot, *pieces, mixed, table, peaks, weight_in, weight_out),
        scalars=1,
        scratch=[
            pltpu.VMEM((length, width), BF),
            pltpu.VMEM((length, width), BF),
            pltpu.VMEM((rows, length + 2 * rows), F32),
            pltpu.VMEM((length, width), BF),
            pltpu.VMEM((length, width), F32),
            pltpu.VMEM((length, width), F32),
            pltpu.VMEM((rows, length + 2 * rows), BF),
            pltpu.VMEM((2, length, width), BF),
        ],
        flops=96 * length * length * width,
    )
    return grad_mixed, kept, sent, branch, grad_table, far


def attend_grads(saved, grad_mixed, branch, place):
    hidden, unused_mixed, context, unused_peaks = saved
    length, model = hidden.shape
    width = context.shape[1]

    def weights(hidden_rows, mixed_grad, context_rows, branch_rows):
        return (
            dot_tn(hidden_rows, mixed_grad),
            dot_tn(context_rows, branch_rows),
            column_sum(mixed_grad),
        )

    return fused(
        weights,
        "attend_weights",
        [shape_of(model, 3 * width, BF), shape_of(width, model, BF), shape_of(1, 3 * width, F32)],
        hidden,
        grad_mixed,
        context,
        branch,
        flops=8 * length * model * width,
    )


def wide_table(distance, rows):
    index = jnp.clip(jnp.arange(4 * rows) - rows - LEFT, 0, LEFT + RIGHT)
    low = distance[index]
    return jnp.concatenate([low, low], axis=1)


def distance_gradient(grad_table, far, rows):
    first = rows + LEFT
    last = first + LEFT + RIGHT
    head = grad_table.shape[1] // 2
    low = jnp.sum(grad_table[: first + 1], axis=0) + far[0]
    high = jnp.sum(grad_table[last:], axis=0) + far[1]
    total = jnp.concatenate([low[None], grad_table[first + 1 : last], high[None]], axis=0)
    return total[:, :head] + total[:, head:]


def whole_heads(head, place):
    return place.unit == head and 2 * place.unit == LANES and place.planes == 4


def attend_weights_whole(weight_in, weight_out, head, place):
    model = weight_out.shape[1]
    heads = model // head
    per_device = heads // SPAN
    width = per_device * head
    whole = lax.all_gather(weight_in, "shard", axis=0, tiled=True)
    whole = whole.reshape(model, 3, heads, head)
    mine = lax.dynamic_slice_in_dim(whole, place.member * per_device, per_device, 2)
    out = lax.all_gather(weight_out, "shard", axis=0, tiled=True)
    out = lax.dynamic_slice_in_dim(out, place.member * width, width, 0)
    return mine.reshape(model, 3 * width), out


def attend_columns(weight_in, place):
    rows = weight_in.shape[0]
    planes, unit = place.planes, place.unit
    groups, columns = planes // 2, 3 * weight_in.shape[1] // 3 // SPAN
    if 2 * unit == LANES:

        def pick(spot, whole, *outs):
            lane = lax.broadcasted_iota(jnp.int32, (rows, LANES), 1)
            for turn, out in enumerate(outs):
                for low in range(2):
                    for part in range(3):
                        pair = []
                        for group in range(groups):
                            start = ((part * groups + group) * 2 + low) * 2 + (spot[1] ^ turn)
                            source = pl.ds(pl.multiple_of(start * LANES, LANES), LANES)
                            pair.append(whole[:, source].astype(F32))
                        rolled = [pltpu.roll(item, unit, axis=1) for item in pair]
                        cores = (
                            jnp.where(lane < unit, pair[0], rolled[1]),
                            jnp.where(lane < unit, rolled[0], pair[1]),
                        )
                        for core, value in enumerate(cores):
                            out[
                                low,
                                core * rows : (core + 1) * rows,
                                part * LANES : (part + 1) * LANES,
                            ] = value.astype(BF)

        own, other = kernel_call(
            pick,
            "attend_pick",
            [jax.ShapeDtypeStruct((2, 2 * rows, columns), BF)] * 2,
            (place.spot, weight_in),
            scalars=1,
        )
    else:
        blocks = weight_in.reshape(rows, 3, groups, 2, 2, 2, -1)
        blocks = blocks.transpose(4, 3, 5, 0, 1, 2, 6).reshape(2, 2, 2 * rows, columns)
        own = lax.dynamic_index_in_dim(blocks, place.second, 0, keepdims=False)
        other = lax.dynamic_index_in_dim(blocks, 1 - place.second, 0, keepdims=False)
    return own, flipped(other.reshape(4 * rows, columns), 2).reshape(own.shape)


def attend_arrange(own, arrived, glue, place):
    unit, columns = place.unit, own.shape[2]
    size = 4 * unit

    def arrange(spot, own_ref, arrived_ref, glue_ref, near_out, one, two):
        low, core = spot[0] & 1, spot[2]
        for near in range(2):
            source = pl.ds(pl.multiple_of((core ^ near) * unit, unit), unit)
            for turn, ref in enumerate((own_ref, arrived_ref)):
                start = (2 * near + turn) * unit
                mine, other = ref[low, source, :], ref[low ^ 1, source, :]
                near_out[start : start + unit, :] = mine
                two[start : start + unit, :] = mine
                two[size + start : size + start + unit, :] = other
                one[start : start + unit, :] = other
        one[size:, :] = glue_ref[...]
        two[2 * size :, :] = glue_ref[...]

    count = glue.shape[0]
    return kernel_call(
        arrange,
        "attend_columns",
        [
            shape_of(size, columns, BF),
            shape_of(size + count, columns, BF),
            shape_of(2 * size + count, columns, BF),
        ],
        (place.spot, own, arrived, glue),
        scalars=1,
    )


def attend_weights_split(near, glue, travelled, place):
    unit = place.unit
    size = 4 * unit
    columns = near.shape[1]

    def split(near_rows, glue_rows, odd, even, relayed):
        pieces = (near_rows, odd, even, relayed)
        kept = jnp.concatenate([item[: 2 * unit] for item in pieces], axis=0)
        sent = jnp.concatenate([item[2 * unit : size] for item in pieces], axis=0)
        whole = [glue_rows, odd[size:], even[2 * size :], relayed[size:]]
        return kept, sent, jnp.concatenate(whole, axis=0)

    return fused(
        split,
        "attend_split",
        [shape_of(8 * unit, columns, BF)] * 2 + [shape_of(4 * glue.shape[0], columns, BF)],
        near,
        glue,
        *travelled,
    )


def attend_weights_lay(kept, sent, outs, place):
    planes, unit, columns = place.planes, place.unit, kept.shape[1]
    width, model = columns // 3, outs[0].shape[1]
    swapped = flipped(sent, 1)

    def lay(spot, kept_ref, swapped_ref, *refs):
        plane, second, core = spot[0], spot[1], spot[2]
        w_in, w_out = refs[-2:]
        for near, ref in enumerate((kept_ref, swapped_ref)):
            for step in range(planes):
                for turn in range(2):
                    row = (((plane ^ step) * 2 + (second ^ turn)) * 2 + (core ^ near)) * unit
                    start = (2 * step + turn) * unit
                    w_in[pl.ds(pl.multiple_of(row, unit), unit), :] = ref[start : start + unit, :]
        for step, ref in enumerate(refs[:-2]):
            row = ((plane >> 1) ^ step) * unit
            w_out[pl.ds(pl.multiple_of(row, unit), unit), :] = ref[...]

    return kernel_call(
        lay,
        "attend_lay",
        [shape_of(model, columns, BF), shape_of(width, model, BF)],
        (place.spot, kept, swapped, *outs),
        scalars=1,
    )


def attend_grads_whole(grad_in, grad_out, head, place):
    model = grad_out.shape[1]
    heads = model // head
    per_device = heads // SPAN
    whole = jnp.zeros((model, 3, heads, head), F32)
    whole = lax.dynamic_update_slice_in_dim(
        whole,
        grad_in.astype(F32).reshape(model, 3, per_device, head),
        place.member * per_device,
        2,
    )
    whole = lax.psum_scatter(
        whole.reshape(model, 3 * model), "shard", scatter_dimension=0, tiled=True
    )
    out = jnp.zeros((model, model), F32)
    out = lax.dynamic_update_slice_in_dim(
        out, grad_out.astype(F32), place.member * per_device * head, 0
    )
    out = lax.psum_scatter(out, "shard", scatter_dimension=0, tiled=True)
    return rep_sum(whole, place), rep_sum(out, place)


def attend_grads_lay(grad_in, grad_out, place):
    model = grad_out.shape[1]
    planes, unit = place.planes, place.unit
    groups, columns = planes // 2, grad_in.shape[1]

    def lay(spot, w_in, w_out, kept, sent, *outs):
        plane, second, core = spot[0], spot[1], spot[2]
        for near, ref in enumerate((kept, sent)):
            for step in range(planes):
                for turn in range(2):
                    row = (((plane ^ step) * 2 + (second ^ turn)) * 2 + (core ^ near)) * unit
                    start = (2 * step + turn) * unit
                    ref[start : start + unit, :] = w_in[pl.ds(pl.multiple_of(row, unit), unit), :]
        for step, ref in enumerate(outs):
            row = ((plane >> 1) ^ step) * unit
            ref[...] = w_out[pl.ds(pl.multiple_of(row, unit), unit), :]

    return kernel_call(
        lay,
        "attend_unlay",
        [shape_of(2 * planes * unit, columns, BF)] * 2 + [shape_of(unit, model, BF)] * groups,
        (place.spot, grad_in, grad_out),
        scalars=1,
    )


def attend_grads_sum(travelled, place):
    unit = place.unit
    columns, model = travelled[0].shape[1] // 2, travelled[4].shape[1]

    def total(own, one, two, three, *rest):
        even = own.astype(F32) + two.astype(F32)
        odd = one[: three.shape[0]].astype(F32) + three.astype(F32)
        both = jnp.concatenate([even, odd], axis=1)
        out = sum(item.astype(F32) for item in rest)
        return both[:unit], both[unit:], out

    own, other, out = fused(
        total,
        "attend_plane_sum",
        [shape_of(unit, 4 * columns, BF)] * 2 + [shape_of(unit, model, BF)],
        *travelled,
    )
    return own, other, out


def attend_grads_arrive(sums, place):
    own, other, out = sums
    arrived = flipped(other, 2)
    mine = own, arrived, out
    return mine, tuple(flipped(item, place.shards) for item in mine)


def attend_grads_final(mine, theirs, place):
    unit = place.unit
    model = mine[2].shape[1]
    columns = mine[0].shape[1] // 4
    groups = place.planes // 2

    def kernel(spot, *refs):
        values = [refs[i][...].astype(F32) + refs[3 + i][...].astype(F32) for i in range(3)]
        grad_in, grad_out = refs[6:]
        grad_out[0] = values[2]
        lane = lax.broadcasted_iota(jnp.int32, (unit, LANES), 1)
        low_bit, core = spot[0] & 1, spot[2]
        for turn in range(2):
            for low in range(2):
                for part in range(3):
                    blocks = []
                    for near in range(2):
                        start = (2 * low + near) * columns + part * LANES
                        blocks.append(values[turn][:, start : start + LANES])
                    first = jnp.where(core == 0, blocks[0], blocks[1])
                    last = jnp.where(core == 0, blocks[1], blocks[0])
                    pairs = (
                        jnp.where(lane < unit, first, pltpu.roll(last, unit, axis=1)),
                        jnp.where(lane < unit, pltpu.roll(first, unit, axis=1), last),
                    )
                    for group, value in enumerate(pairs):
                        start = ((part * groups + group) * 2 + (low_bit ^ low)) * 2
                        start = (start + (spot[1] ^ turn)) * LANES
                        grad_in[0, :, pl.ds(pl.multiple_of(start, LANES), LANES)] = value

    outs = [
        jax.ShapeDtypeStruct((1, unit, 3 * model), F32),
        jax.ShapeDtypeStruct((1, unit, model), F32),
    ]
    return kernel_call(kernel, "attend_final", outs, (place.spot, *mine, *theirs), scalars=1)


def rep_sum(value, place):
    low = value.astype(BF)
    return low.astype(F32) + flipped(low, place.shards).astype(F32)


def row(wide, index):
    return wide[index : index + 1]


def blocks_of(width, first, model):
    low, high = (0, 2 * model) if first else (2 * model, 3 * model)
    result = []
    for block in range(3 * model // width):
        begin, end = max(block * width, low), min((block + 1) * width, high)
        if begin < end:
            source = slice(begin - block * width, end - block * width)
            result.append((block, source, slice(begin - low, end - low)))
    return result


def conv_pick(weight_in, weight_out, width, place):
    rows, model = weight_out.shape
    half = rows // 2
    whole = half % 16 != 0
    size = rows if whole else half

    def pick(spot, left, right, out):
        source = pl.ds(pl.multiple_of(spot[3] * half, half), half)
        if whole:
            source = slice(0, rows)
        for ref, first in ((left, True), (right, False)):
            for block, own, columns in blocks_of(width, first, model):
                out[block * size : (block + 1) * size, own] = ref[source, columns]

    outs = [shape_of(3 * model // width * size, width, BF)]
    operands = (place.spot, weight_in, weight_out)
    return kernel_call(pick, "conv_pick", outs, operands, scalars=1)[0]


def conv_square(own, masks):
    first, second = masks
    half = own.shape[0] // 2
    return own, flipped(own, first), flipped(own, second), half


def conv_relay(via_first, via_second, masks):
    first, second = masks
    half = via_first.shape[0] // 2
    low, high = fused(
        lambda one, two: (one[:half], two[half:]),
        "conv_halves",
        [shape_of(half, via_first.shape[1], BF)] * 2,
        via_first,
        via_second,
    )
    return flipped(low, second), flipped(high, first)


def lay_conv(spot, refs, target, unit, first):
    model = target.shape[0]
    plane, second, core, rep = spot[0], spot[1], spot[2], spot[3]
    size = unit if len(refs) == 1 else unit // 2
    width = refs[0].shape[1]
    extent = 3 * model // width * size
    blocks = blocks_of(width, first, model)
    for index, ref in enumerate(refs):
        for local in range(ref.shape[0] // extent):
            start = local * size
            if len(refs) > 1:
                kind, near = index % 5, index // 5
                turn, side = ((0, 0), (0, 1), (1, 0), (1, 1), (1, 1))[kind]
                step = local + (ref.shape[0] // extent if kind == 4 else 0)
                start = (((plane ^ step) * 2 + (second ^ turn)) * 2 + (core ^ near)) * 2
                start = pl.multiple_of((start + (rep ^ side)) * size, size)
            for block, own, columns in blocks:
                source = local * extent + block * size
                target[pl.ds(start, size), columns] = ref[source : source + size, own]


def conv_whole_weights(pieces, model, place):
    def kernel(spot, *refs):
        w_in, w_out = refs[-2:]
        lay_conv(spot, refs[:-2], w_in, place.unit, True)
        lay_conv(spot, refs[:-2], w_out, place.unit, False)

    outs = [shape_of(model, 2 * model, BF), shape_of(model, model, BF)]
    return kernel_call(kernel, "conv_lay", outs, (place.spot, *pieces), scalars=1)


def convolve_start(parts, before, wide, bias_row, weights, place):
    rows, model = before.shape

    def kernel(*refs):
        part_refs, (base, small, w_in) = refs[:4], refs[4:7]
        current_ref, hidden_ref, doubled_ref, glued_ref = refs[7:]
        parts_now = [ref[...] for ref in part_refs]
        current = base[...] + joined(parts_now) + small[bias_row : bias_row + 1, :]
        current_ref[...] = current
        unit, unused_scale = standard(current)
        hidden = (unit * small[7:8, :] + small[8:9, :]).astype(BF)
        hidden_ref[...] = hidden
        doubled = dot_nn(hidden, w_in[...])
        doubled_ref[...] = doubled
        glued_ref[...] = (doubled[:, :model] * logistic(doubled[:, model:])).astype(BF)

    return kernel_call(
        kernel,
        "convolve_start",
        [
            shape_of(rows, model, F32),
            shape_of(rows, model, BF),
            shape_of(rows, 2 * model, F32),
            shape_of(rows, model, BF),
        ],
        (*parts, before, wide, weights[0]),
        flops=4 * rows * model * model,
    )


def convolve_finish(glued, border, wide, taps, weights, before, place):
    rows, model = before.shape
    edge = border.shape[0]

    def kernel(
        glued_ref, border_ref, small, base, w_out, mixed_ref, rest_ref, current_ref, hidden_ref,
        padded,
    ):
        padded[:edge, :] = border_ref[...].astype(F32)
        padded[edge:, :] = glued_ref[...].astype(F32)
        first, count = taps
        for column in range(0, model, LANES):
            lanes = slice(column, column + LANES)
            total = jnp.zeros((rows, LANES), F32)
            for tap in range(count):
                start = edge - count + 1 + tap
                weight = small[first + tap : first + tap + 1, lanes]
                total += padded[start : start + rows, lanes] * weight
            mixed_ref[:, lanes] = total
        unit, unused_scale = standard(mixed_ref[...])
        upper = unit * small[9:10, :] + small[10:11, :]
        rest = (upper * logistic(upper)).astype(BF)
        rest_ref[...] = rest
        current = base[...] + dot_nn(rest, w_out[...])
        current_ref[...] = current
        unit, unused_scale = standard(current)
        hidden_ref[...] = (unit * small[11:12, :] + small[12:13, :]).astype(BF)

    return kernel_call(
        kernel,
        "convolve_finish",
        [shape_of(rows, model, dtype) for dtype in (F32, BF, F32, BF)],
        (glued, border, wide, before, weights[1]),
        scratch=[pltpu.VMEM((edge + rows, model), F32)],
        flops=2 * rows * model * model,
    )


def convolve_back_start(parts, grad, after, mixed, wide, taps, weights, glued, border, place):
    rows, model = after.shape
    edge = border.shape[0]
    first, count = taps

    def kernel(
        own, part_one, part_two, part_three, grad_ref, after_ref, mixed_ref, small,
        glued_ref, border_ref, w_out, grad_out, branch_ref, main_ref, halo_ref, sums,
        padded, spread,
    ):
        incoming = joined((own[...], part_one[...], part_two[...], part_three[...]))
        slope, sum_gain, sum_shift = norm_back(after_ref[...], small[11:12, :], incoming)
        current = grad_ref[...] + slope
        grad_out[...] = current
        branch = current.astype(BF)
        branch_ref[...] = branch
        unit, scale = standard(mixed_ref[...])
        upper = unit * small[9:10, :] + small[10:11, :]
        grad_upper = dot_nt(branch, w_out[...]) * silu_slope(upper)
        inner = grad_upper * small[9:10, :]
        mean = jnp.mean(inner, axis=-1, keepdims=True)
        shared = jnp.mean(inner * unit, axis=-1, keepdims=True)
        padded[:edge, :] = border_ref[...].astype(F32)
        padded[edge:, :] = glued_ref[...].astype(F32)
        spread[:edge, :] = jnp.zeros((edge, model), F32)
        spread[edge : edge + rows, :] = scale * (inner - mean - unit * shared)
        spread[edge + rows :, :] = jnp.zeros((edge, model), F32)
        sums[count : count + 1, :] = column_sum(grad_upper * unit)
        sums[count + 1 : count + 2, :] = column_sum(grad_upper)
        sums[count + 2 : count + 3, :] = sum_gain
        sums[count + 3 : count + 4, :] = sum_shift
        for column in range(0, model, LANES):
            lanes = slice(column, column + LANES)
            total = jnp.zeros((rows + edge, LANES), F32)
            center = spread[edge : edge + rows, lanes]
            for tap in range(count):
                start = edge - count + 1 + tap
                sums[tap : tap + 1, lanes] = jnp.sum(
                    center * padded[start : start + rows, lanes], axis=0, keepdims=True
                )
                begin = count - 1 - tap
                weight = small[first + tap : first + tap + 1, lanes]
                total += spread[begin : begin + rows + edge, lanes] * weight
            halo_ref[:, lanes] = total[:edge].astype(BF)
            main_ref[:, lanes] = total[edge:]

    return kernel_call(
        kernel,
        "convolve_back_start",
        [
            shape_of(rows, model, F32),
            shape_of(rows, model, BF),
            shape_of(rows, model, F32),
            shape_of(edge, model, BF),
            shape_of(count + 4, model, F32),
        ],
        (*parts, grad, after, mixed, wide, glued, border, weights[1]),
        scratch=[
            pltpu.VMEM((edge + rows, model), F32),
            pltpu.VMEM((rows + 2 * edge, model), F32),
        ],
        limit=56,
        flops=2 * rows * model * model,
    )


def convolve_back_finish(main, incoming, doubled, weights, before, wide, grad, place):
    rows, model = before.shape
    edge = incoming.shape[0]

    def kernel(
        main_ref, late, both, base, small, grad_rows, w_in, current_ref, branch_ref, slope_ref,
        sums,
    ):
        last = main_ref[rows - edge :, :] + late[...].astype(F32)
        glued = jnp.concatenate([main_ref[: rows - edge, :], last], axis=0)
        glued = glued.astype(BF).astype(F32)
        gate = logistic(both[:, model:])
        slope_ref[:, :model] = (glued * gate).astype(BF)
        slope_ref[:, model:] = (glued * both[:, :model] * gate * (1.0 - gate)).astype(BF)
        inner, sum_gain, sum_shift = norm_back(
            base[...], small[7:8, :], dot_nt(slope_ref[...], w_in[...])
        )
        current = grad_rows[...] + inner
        current_ref[...] = current
        branch_ref[...] = current.astype(BF)
        sums[0:1, :] = sum_gain
        sums[1:2, :] = sum_shift
        sums[2:3, :] = column_sum(current.astype(BF))

    return kernel_call(
        kernel,
        "convolve_back_finish",
        [
            shape_of(rows, model, F32),
            shape_of(rows, model, BF),
            shape_of(rows, 2 * model, BF),
            shape_of(3, model, F32),
        ],
        (main, incoming, doubled, before, wide, grad, weights[0]),
        flops=4 * rows * model * model,
    )


def conv_grads_start(hidden, slope, rest, branch, place):
    model = hidden.shape[1]
    unit, planes = place.unit, place.planes
    size = unit // 2
    halved = place.aligned
    width = 3 * model // 4 if halved else model
    columns = range(0, 3 * model, width)

    def kernel(spot, hidden_ref, slope_ref, rest_ref, branch_ref, kept, sent, total):
        total[:, : 2 * model] = dot_tn(hidden_ref[...], slope_ref[...])
        total[:, 2 * model :] = dot_tn(rest_ref[...], branch_ref[...])
        plane, second, core, rep = spot[0], spot[1], spot[2], spot[3]
        for near, ref in enumerate((kept, sent)):
            if not halved:
                for pair in range(2 * planes):
                    start = pl.multiple_of((pair * 2 + (core ^ near)) * unit, unit)
                    for index, column in enumerate(columns):
                        target = (3 * pair + index) * unit
                        ref[target : target + unit, :] = total[
                            pl.ds(start, unit), column : column + width
                        ].astype(BF)
                continue
            for kind, (turn, side) in enumerate(((0, 0), (0, 1), (1, 0), (1, 1))):
                for step in range(planes):
                    start = (((plane ^ step) * 2 + (second ^ turn)) * 2 + (core ^ near)) * 2
                    start = pl.multiple_of((start + (rep ^ side)) * size, size)
                    for index, column in enumerate(columns):
                        target = ((kind * planes + step) * len(columns) + index) * size
                        ref[target : target + size, :] = total[
                            pl.ds(start, size), column : column + width
                        ].astype(BF)

    return kernel_call(
        kernel,
        "conv_grads",
        [shape_of(len(columns) * model // 2, width, BF)] * 2,
        (place.spot, hidden, slope, rest, branch),
        scalars=1,
        scratch=[pltpu.VMEM((model, 3 * model), F32)],
        flops=6 * hidden.shape[0] * model * model,
        limit=36,
    )


def conv_grads_split(kept, swapped, place):
    count = 4 if place.aligned else 1
    size = kept.shape[0] // count

    def body(kept_part, swapped_part):
        total = kept_part.astype(F32) + swapped_part.astype(F32)
        return [total[index * size : (index + 1) * size] for index in range(count)]

    outs = [shape_of(size, kept.shape[1], BF)] * count
    return list(fused(body, "conv_grads_split", outs, kept, swapped))


def conv_grads_square(shares, masks):
    first, second = masks
    return [
        shares[0],
        flipped(shares[1], first),
        flipped(shares[2], second),
        flipped(shares[3], first | second),
    ]


def plane_pieces(mix_kept, mix_swapped, shares, place):
    planes, unit = place.planes, place.unit
    rows, width = 2 * unit, shares[0].shape[1]
    size = shares[0].shape[0] // planes

    def body(kept, swapped, *values):
        both = jnp.concatenate([kept, swapped], axis=1)
        mix = [both[step * rows : (step + 1) * rows] for step in range(planes)]
        total = sum(value.astype(F32) for value in values).astype(BF)
        conv = [total[step * size : (step + 1) * size] for step in range(planes)]
        joint = jnp.concatenate([mix[1], conv[1], conv[3]], axis=0)
        return mix[0], mix[2], mix[3], conv[0], conv[2], joint

    outs = [shape_of(rows, width, BF)] * 3 + [shape_of(size, width, BF)] * 2
    outs += [shape_of(rows + 2 * size, width, BF)]
    return list(fused(body, "plane_pieces", outs, mix_kept, mix_swapped, *shares))


def conv_grads_top(own, joint):
    size = own.shape[0]

    def body(mine, arrived):
        return (mine.astype(F32) + arrived[arrived.shape[0] - size :].astype(F32),)

    return fused(body, "conv_grads_top", [shape_of(*own.shape, BF)], own, joint)[0]


def conv_grads_sum(own, joint, last):
    size = own.shape[0]

    def body(mine, arrived, late):
        start = arrived.shape[0] - 2 * size
        near = arrived[start : start + size]
        return (mine.astype(F32) + near.astype(F32) + late.astype(F32),)

    return fused(body, "conv_grads_sum", [shape_of(*own.shape, BF)], own, joint, last)[0]


def conv_grads_whole(total, place):
    groups = [list(range(core, place.shards, 2)) for core in range(2)]
    mine = lax.psum_scatter(
        total, "shard", scatter_dimension=0, tiled=True, axis_index_groups=groups
    )
    return rep_sum(mine, place).reshape(3, place.unit, -1)


def conv_grads_final(mine, theirs, place):
    size, width = place.unit // 2, mine.shape[1]
    model = width * mine.shape[0] // size // 3

    def kernel(spot, mine_ref, theirs_ref, grad_in, grad_out):
        for turn, ref in enumerate((mine_ref, theirs_ref)):
            target = pl.ds(pl.multiple_of((spot[3] ^ turn) * size, size), size)
            for out, first in ((grad_in, True), (grad_out, False)):
                for block, own, columns in blocks_of(width, first, model):
                    value = ref[block * size : (block + 1) * size, own]
                    out[0, target, columns] = value.astype(F32)

    outs = [
        jax.ShapeDtypeStruct((1, 2 * size, 2 * model), F32),
        jax.ShapeDtypeStruct((1, 2 * size, model), F32),
    ]
    return kernel_call(kernel, "conv_final", outs, (place.spot, mine, theirs), scalars=1)


def feed_to_attend(parts, before, wide):
    rows, model = before.shape

    def body(*values):
        base, small = values[4:]
        current = base.astype(F32) + 0.5 * (joined(values[:4]) + row(small, 2))
        unit, unused_scale = standard(current)
        return current, unit * row(small, 3) + row(small, 4)

    outs = [shape_of(rows, model, F32), shape_of(rows, model, BF)]
    return fused(body, "feed_to_attend", outs, *parts, before, wide)


def turn_around(parts, before, wide, cotangent):
    rows, model = before.shape

    def body(*values):
        base, small, grad = values[4:]
        current = base + 0.5 * (joined(values[:4]) + row(small, 13))
        unit, unused_scale = standard(current)
        slope, sum_gain, sum_shift = norm_back(current, row(small, 14), grad.astype(F32))
        branch = (0.5 * slope).astype(BF)
        sums = jnp.concatenate([column_sum(branch), sum_gain, sum_shift], axis=0)
        return unit * row(small, 14) + row(small, 15), slope, branch, sums

    outs = [
        shape_of(rows, model, BF),
        shape_of(rows, model, F32),
        shape_of(rows, model, BF),
        shape_of(3, model, F32),
    ]
    return fused(body, "turn_around", outs, *parts, before, wide, cotangent)


def attend_to_feed_back(parts, grad, before, wide):
    rows, model = before.shape

    def body(*values):
        grad_rows, base, small = values[4:]
        slope, sum_gain, sum_shift = norm_back(base, row(small, 3), joined(values[:4]))
        current = grad_rows + slope
        branch = (0.5 * current).astype(BF)
        sums = jnp.concatenate([column_sum(branch), sum_gain, sum_shift], axis=0)
        return current, branch, sums

    outs = [shape_of(rows, model, F32), shape_of(rows, model, BF), shape_of(3, model, F32)]
    return fused(body, "attend_to_feed_back", outs, *parts, grad, before, wide)


def last_step(parts, grad, before, wide):
    rows, model = before.shape

    def body(*values):
        grad_rows, base, small = values[4:]
        slope, sum_gain, sum_shift = norm_back(
            base.astype(F32), row(small, 0), joined(values[:4])
        )
        return grad_rows + slope, jnp.concatenate([sum_gain, sum_shift], axis=0)

    outs = [shape_of(rows, model, F32), shape_of(2, model, F32)]
    return fused(body, "last_step", outs, *parts, grad, before, wide)


def small_unpack(gathered, counts, place):
    rows, modules_rows = counts
    shards, unit, half, planes = place.shards, place.unit, place.half, place.planes
    model = shards * unit
    if not place.aligned:
        wide = gathered[:, :rows].transpose(1, 0, 2).reshape(rows, model).astype(F32)
        bias = gathered[:, rows:].reshape(planes, 2, 2, 2, 2, half)
        bias = lax.dynamic_index_in_dim(bias, place.second, 1, keepdims=False)
        bias = lax.dynamic_index_in_dim(bias, place.rep, 3, keepdims=False)
        bias = bias.transpose(2, 0, 1, 3).reshape(2, -1).astype(F32)
        heads = [
            lax.dynamic_slice_in_dim(wide[index].reshape(SPAN, -1), place.member, 1, 0)
            for index in (5, 6)
        ]
        return wide, bias, jnp.concatenate([heads[0], jnp.zeros_like(heads[0]), heads[1]], axis=1)

    def kernel(spot, ref, wide, bias, mix):
        lane = lax.broadcasted_iota(jnp.int32, (1, LANES), 1)
        second, core, rep = spot[1], spot[2], spot[3]
        member = (spot[0] & 1) * 4 + second * 2 + core

        def doubled(value):
            return jnp.concatenate([value, value], axis=1)

        for pair in range(shards // 2):
            both = [doubled(ref[2 * pair + side].astype(F32)) for side in range(2)]
            value = jnp.where(lane < unit, both[0], both[1])
            wide[:, pair * LANES : (pair + 1) * LANES] = value[:rows]
        for module in range(2):
            for index in range(2 * planes):
                shard = (index // 2 * 2 + second) * 2 + index % 2
                block = doubled(ref[shard].astype(F32))
                start = rows + (module * 2) * 2
                options = [
                    jnp.where(
                        lane < unit,
                        block[start + 2 * side : start + 2 * side + 1],
                        block[start + 2 * side + 1 : start + 2 * side + 2],
                    )
                    for side in range(2)
                ]
                value = jnp.where(rep == 0, options[0], options[1])
                bias[module : module + 1, index * half : (index + 1) * half] = value
        mix[...] = jnp.zeros_like(mix)
        pair = [doubled(ref[member + SPAN * group].astype(F32)) for group in range(2)]
        value = jnp.where(lane < unit, pair[0], pair[1])
        mix[:, :LANES] = value[5:6]
        mix[:, 2 * LANES :] = value[6:7]

    outs = [
        shape_of(rows, model, F32),
        shape_of(2, 2 * planes * half, F32),
        shape_of(1, 3 * LANES, F32),
    ]
    return kernel_call(kernel, "small_unpack", outs, (place.spot, gathered), scalars=1)


def shard_gather(value, place):
    copies = jnp.broadcast_to(value[None], (place.shards, *value.shape))
    return lax.all_to_all(copies, "shard", 0, 0, tiled=True)


def small_reduce(sums, mix_sums, biases, distance, counts, place):
    input_sums, first_sums, attend_sums, conv_sums, last_sums = sums
    rows, taps = counts
    unit, half, planes, shards = place.unit, place.half, place.planes, place.shards
    model = unit * shards
    width = mix_sums.shape[1] // 3
    if not place.aligned:
        heads = []
        for start in (0, 2 * width):
            whole = jnp.zeros((SPAN, model // SPAN), F32)
            block = mix_sums[:, start : start + width]
            whole = lax.dynamic_update_slice_in_dim(whole, block, place.member, 0)
            heads.append(whole.reshape(1, model))
        wide = jnp.concatenate(
            [
                input_sums, first_sums, *heads, attend_sums[:2], conv_sums[taps:], last_sums,
                attend_sums[2:], conv_sums[:taps],
            ],
            axis=0,
        )
        wide = wide.reshape(-1, shards, unit).transpose(1, 0, 2)
        pair = jnp.stack(biases).reshape(2, planes, 2, half)
        bias = lax.dynamic_update_slice(
            jnp.zeros((planes, 2, 2, 2, 2, half), F32),
            pair.transpose(1, 2, 0, 3)[:, None, :, :, None, :],
            (0, place.second, 0, 0, place.rep, 0),
        ).reshape(shards, -1, unit)
        both = jnp.concatenate([wide, bias], axis=1)
        both = lax.all_to_all(
            jnp.concatenate([both, both], axis=0), ("rep", "shard"), 0, 0, tiled=True
        )
        total = jnp.sum(both, axis=0)
        for bit in range((2 * shards).bit_length() - 1):
            distance = distance + flipped(distance, 1 << bit)
        return total[:rows], total[rows:].reshape(2, 2 * half), distance
    table_rows = distance.shape[0]
    share = -(-table_rows // shards)
    extent = -(-(rows + 8 + share) // 32) * 32
    size = extent // 2

    def pack(spot, in_ref, first, attend_ref, conv, last, mix, bias_one, bias_two, table, out, wide):
        plane, second, core, rep = spot[0], spot[1], spot[2], spot[3]
        wide[...] = jnp.zeros_like(wide)
        wide[0:2, :] = in_ref[...]
        wide[2:5, :] = first[...]
        wide[7:9, :] = attend_ref[0:2, :]
        wide[9:13, :] = conv[taps:, :]
        wide[13:16, :] = last[...]
        wide[16:17, :] = attend_ref[2:3, :]
        wide[17 : 17 + taps, :] = conv[:taps, :]
        lane = lax.broadcasted_iota(jnp.int32, (1, LANES), 1)
        for group in range(2):
            start = ((group * 2 + (plane & 1)) * 2 + second) * LANES
            target = pl.ds(pl.multiple_of(start, LANES), LANES)
            for index, begin in ((5, 0), (6, 2 * width)):
                value = mix[:, begin : begin + LANES]
                moved = pltpu.roll(jnp.broadcast_to(value, (8, LANES)), unit, axis=1)[:1]
                low = value if group == 0 else moved
                high = moved if group == 0 else value
                placed = jnp.where(core == 0, low, high)
                placed = jnp.where(lane // unit == core, placed, 0.0)
                wide[index : index + 1, target] = placed
        for module, ref in enumerate((bias_one, bias_two)):
            for index in range(planes):
                pair = [
                    ref[:, start * half : (start + 1) * half]
                    for start in (2 * index, 2 * index + 1)
                ]
                moved = [
                    pltpu.roll(jnp.broadcast_to(item, (8, LANES)), unit, axis=1)[:1]
                    for item in pair
                ]
                halves = (
                    jnp.where(lane < unit, pair[0], moved[1]),
                    jnp.where(lane < unit, moved[0], pair[1]),
                )
                start = pl.multiple_of((index * 2 + second) * LANES, LANES)
                for side in range(2):
                    for part, value in enumerate(halves):
                        line = rows + (module * 2 + side) * 2 + part
                        wide[line : line + 1, pl.ds(start, LANES)] = jnp.where(
                            rep == side, value, 0.0
                        )
        whole = jnp.concatenate(
            [table[...], jnp.zeros((share * shards - table_rows, unit), F32)], axis=0
        )
        for pair in range(shards // 2):
            start = 2 * pair * share
            wide[rows + 8 : rows + 8 + share, pair * LANES : (pair + 1) * LANES] = jnp.concatenate(
                [whole[start : start + share], whole[start + share : start + 2 * share]], axis=1
            )
        wide_lane = lax.broadcasted_iota(jnp.int32, (size, LANES), 1)
        for pair in range(shards // 2):
            block = wide[:, pair * LANES : (pair + 1) * LANES]
            upper, lower = block[:size], block[size:]
            both = (
                jnp.where(wide_lane < unit, upper, pltpu.roll(lower, unit, axis=1)),
                jnp.where(wide_lane < unit, pltpu.roll(upper, unit, axis=1), lower),
            )
            for side in range(2):
                for target in (2 * pair + side, 2 * pair + side + shards):
                    out[target] = both[side].astype(BF)

    packed = kernel_call(
        pack,
        "small_pack",
        [jax.ShapeDtypeStruct((2 * shards, size, LANES), BF)],
        (place.spot, *sums, mix_sums, *biases, distance),
        scalars=1,
        scratch=[pltpu.VMEM((extent, model), F32)],
    )[0]
    packed = lax.all_to_all(packed, ("rep", "shard"), 0, 0, tiled=True)

    def unpack(spot, ref, wide, bias, table):
        total = ref[0].astype(F32)
        for index in range(1, 2 * shards):
            total = total + ref[index].astype(F32)
        moved = pltpu.roll(total, unit, axis=1)
        both = jnp.concatenate([total[:size, :unit], moved[:size, :unit]], axis=0)
        wide[...] = both[:rows]
        table[...] = both[rows + 8 : rows + 8 + share]
        for module in range(2):
            for side in range(2):
                line = rows + (module * 2 + side) * 2
                bias[module : module + 1, side * half : (side + 1) * half] = jnp.concatenate(
                    [both[line : line + 1], both[line + 1 : line + 2]], axis=1
                )

    wide, bias, table = kernel_call(
        unpack,
        "small_sum",
        [shape_of(rows, unit, F32), shape_of(2, 2 * half, F32), shape_of(share, unit, F32)],
        (place.spot, packed),
        scalars=1,
    )
    table = jnp.broadcast_to(table[None], (shards, share, unit))
    table = lax.all_to_all(table, "shard", 0, 0, tiled=True)
    return wide, bias, table.reshape(shards * share, unit)[:table_rows]


class Place:
    def __init__(self, unit, half, head):
        self.shards = lax.axis_size("shard")
        self.planes = self.shards // QUAD
        self.unit, self.half = unit, half
        self.pack_rows = 2 * unit + half
        self.rep = lax.axis_index("rep")
        self.shard = lax.axis_index("shard")
        self.core = self.shard % 2
        self.second = self.shard // 2 % 2
        self.plane = self.shard // QUAD
        self.member = self.shard % SPAN
        self.spot = jnp.stack([self.plane, self.second, self.core, self.rep])
        self.flat_spot = jnp.stack([jnp.zeros_like(self.plane), self.second, self.core, self.rep])
        self.span_spot = self.member.reshape(1)
        self.aligned = whole_heads(head, self)
        self.feed_masks = (self.shards, 2)
        self.span_masks = (4, 2)


def along(value, by, place):
    count = place.shards
    route = [(i, i + by) for i in range(count) if 0 <= i + by < count]
    return lax.ppermute(value, "shard", route)


def shards(
    inputs,
    ff_in,
    ff_out,
    ff_bias,
    attn_in,
    attn_out,
    conv_in,
    conv_out,
    depthwise,
    distance,
    vectors,
    attn_bias,
    cotangent,
):
    rows, model = inputs.shape
    unit, half = ff_in.shape[2], ff_out.shape[2] // 2
    head = distance.shape[2]
    place = Place(unit, half, head)
    tap_count = depthwise.shape[1]
    edge = -(-(tap_count - 1) // 16) * 16
    bias_rows = ff_bias.shape[2] // unit
    count = vectors.shape[1]
    taps = (count + 1, tap_count)
    wide_rows = count + 1 + tap_count

    first_parts = feed_pack(ff_in, ff_out, 0, place)
    small = jnp.concatenate(
        [vectors[0], attn_bias, depthwise[0], ff_bias[0].reshape(2 * bias_rows, unit)], axis=0
    )
    first_pack = pack_rows(first_parts)
    first_pack, current, mix_in, later_in = tied(first_pack, inputs, attn_in[0], ff_in)
    first_far = plane_start(first_pack, place)
    pieces = square_gather(current, place.feed_masks)
    second_parts = feed_pack(later_in, ff_out, 1, place)
    columns = attend_columns(mix_in, place) if place.aligned else (mix_in, mix_in)
    (
        first_far[0], first_far[1], small, second_in, second_other, second_out, *early
    ) = tied(*first_far, small, *second_parts, *columns, *pieces)
    columns, pieces = early[:2], early[2:]
    small = shard_gather(small, place)
    second_pack = pack_rows((second_in, second_other, second_out))
    glue_width = 3 * model // SPAN if place.aligned else model
    glue = conv_pick(conv_in[0], conv_out[0], glue_width, place)
    if place.aligned:
        columns = attend_arrange(*columns, glue, place)
    first_near = plane_finish(first_pack, first_far, place)
    last = place.planes - 1
    first_near[last], small, glue, second_pack, *columns = tied(
        first_near[last], small, glue, second_pack, *columns
    )
    first_packs = with_core(first_near)
    wide, feed_bias, mix_bias = small_unpack(small, (wide_rows, 2 * bias_rows), place)
    table = wide_table(distance[0], rows)
    wide, mix_bias, table, pieces[0] = tied(wide, mix_bias, table, pieces[0])

    parts, saved_first = feed(
        pieces, first_packs, feed_bias[0:1], wide, 0, place.feed_masks, place
    )
    if place.aligned:
        mix_near, one, two = columns
        odd, even = flipped(one, QUAD), flipped(two, 2 * QUAD)
        parts, (odd, even, mix_out) = tied_lists(parts, (odd, even, attn_out[0]))
        mix_outs = [mix_out, flipped(mix_out, SPAN)]
        relayed = flipped(even[4 * unit :], QUAD)
    after_first, hidden = feed_to_attend(parts, inputs, wide)
    near, far = group_gather(hidden, place.span_masks)
    if place.aligned:
        near, far, (relayed, second_pack, mix_outs[1]) = tied_lists(
            near, far, (relayed, second_pack, mix_outs[1])
        )
        mix_kept, mix_sent, glue = attend_weights_split(
            mix_near, glue, (odd, even, relayed), place
        )
        mix_in, mix_out = attend_weights_lay(mix_kept, mix_sent, mix_outs, place)
        glue, via_first, via_second, unused_half = conv_square(glue, place.feed_masks)
    else:
        mix_in, mix_out = attend_weights_whole(attn_in[0], attn_out[0], head, place)
        glue = [lax.all_gather(glue, "shard", axis=0, tiled=True)]
        near, far, (second_pack,) = tied_lists(near, far, (second_pack,))
    second_far = plane_start(second_pack, place)
    saved_attend, kept, sent = attend((near, far), mix_in, mix_bias, mix_out, table, place)
    if place.aligned:
        sent, via_first, via_second = tied(sent, via_first, via_second)
        low, high = conv_relay(via_first, via_second, place.feed_masks)
        glue_far = [flipped(item, 1) for item in (glue, via_first, via_second)]
        kept, *glue_far = tied(kept, *glue_far)
    sent, *second_far = tied(sent, *second_far)
    parts = group_reduce(kept, sent, place.span_masks)
    if place.aligned:
        parts, (low, high), (second_pack, *second_far) = tied_lists(
            parts, (low, high), (second_pack, *second_far)
        )
        glue = [glue, via_first, via_second, low, high]
        glue += [*glue_far, flipped(low, 1), flipped(high, 1)]
    else:
        parts, (second_pack, *second_far) = tied_lists(parts, (second_pack, *second_far))
    glue = conv_whole_weights(glue, model, place)
    second_near = plane_finish(second_pack, second_far, place)
    after_attend, conv_hidden, doubled, glued = convolve_start(
        parts, after_first, wide, count, glue, place
    )
    border = along(glued[rows - edge :], 1, place)
    border = jnp.where(place.member == 0, jnp.zeros_like(border), border)
    border, *second_near = tied(border, *second_near)
    second_packs = with_core(second_near)
    mixed, rest, after_conv, hidden = convolve_finish(
        glued, border, wide, taps, glue, after_attend, place
    )
    hidden, *second_packs = tied(hidden, *second_packs)
    pieces = square_gather(hidden, place.feed_masks)
    parts, saved_second = feed(
        pieces, second_packs, feed_bias[1:2], wide, None, place.feed_masks, place
    )
    output, grad_last, branch, last_sums = turn_around(parts, after_conv, wide, cotangent)

    pieces = square_gather(branch, place.feed_masks)
    result, branch, slope, second_bias = feed_back(pieces, second_packs, saved_second, place)
    second_grads = [
        *feed_in_grads(saved_second[0], slope, place),
        *feed_out_grads(saved_second[2], pieces, place),
    ]
    *result, second_grads[1], second_grads[3] = tied(*result, second_grads[1], second_grads[3])
    second_grads[1], second_grads[3] = flipped(second_grads[1], 1), flipped(second_grads[3], 1)
    parts = square_reduce(result, place.feed_masks)
    second_split = [plane_split(*pair, place) for pair in (second_grads[:2], second_grads[2:])]
    parts, *second_split = tied_lists(parts, *second_split)
    second_lists = [plane_early(pieces, place) for pieces in second_split]
    grad_conv, conv_branch, main, halo, conv_sums = convolve_back_start(
        parts, grad_last, after_conv, mixed, wide, taps, glue, glued, border, place
    )
    incoming = along(halo, -1, place)
    incoming, second_tops = tied_tops(incoming, second_lists, place)
    second_early = [lists[0] for lists in second_lists]
    incoming = jnp.where(place.member == SPAN - 1, jnp.zeros_like(incoming), incoming)
    grad_attend, branch, slope, attend_sums = convolve_back_finish(
        main, incoming, doubled, glue, after_attend, wide, grad_conv, place
    )
    conv_kept, conv_sent = conv_grads_start(conv_hidden, slope, rest, conv_branch, place)
    second_tops = [plane_total(values) for values in second_tops]
    count_early = len(second_early[0])
    branch, conv_kept, conv_sent, *flat = tied(
        branch, conv_kept, conv_sent, *second_tops, *second_early[0], *second_early[1]
    )
    second_tops = flat[:2]
    second_early = [flat[2 : 2 + count_early], flat[2 + count_early :]]
    near, far = group_gather(branch, place.span_masks)
    conv_shares = conv_grads_split(conv_kept, flipped(conv_sent, 1), place)
    near, far, conv_shares, second_tops = tied_lists(near, far, conv_shares, second_tops)
    if place.aligned:
        conv_shares = conv_grads_square(conv_shares, place.feed_masks)
    second_lasts = [plane_last(top, place) for top in second_tops]
    back = attend_back((near, far), saved_attend, mix_in, mix_out, table, place)
    grad_mixed, kept, sent, branch, grad_table, table_far = back
    (sent,), second_lasts, conv_shares = tied_lists((sent,), second_lasts, conv_shares)
    mix_grad_in, mix_grad_out, mix_sums = attend_grads(saved_attend, grad_mixed, branch, place)
    second_sums = [plane_add([*own, last]) for own, last in zip(second_early, second_lasts)]
    second_other = flipped(second_sums[0][unit:], 2)
    if place.aligned:
        mix_kept, mix_swap, *mix_outs = attend_grads_lay(mix_grad_in, mix_grad_out, place)
        kept, mix_swap = tied(kept, mix_swap)
        mix_swap = flipped(mix_swap, 1)
        kept, mix_swap = tied(kept, mix_swap)
    parts = group_reduce(kept, sent, place.span_masks)
    if place.aligned:
        mix_outs[1] = flipped(mix_outs[1], SPAN)
        planed = plane_pieces(mix_kept, mix_swap, conv_shares, place)
        parts, (second_other, mix_outs[1]), planed = tied_lists(
            parts, (second_other, mix_outs[1]), planed
        )
    else:
        parts, (second_other,) = tied_lists(parts, (second_other,))
    second_pack = pack_rows((second_sums[0][:unit], second_other, second_sums[1]))
    grad_distance = distance_gradient(grad_table, table_far, rows)
    grad_first, branch, first_sums = attend_to_feed_back(parts, grad_attend, after_first, wide)
    if place.aligned:
        (branch,), planed = tied_lists((branch,), planed)
        mix_zero, mix_two, mix_three, conv_zero, conv_two, joint = planed
        pieces = square_gather(branch, place.feed_masks)
        joint = flipped(joint, QUAD)
        mix_two = flipped(mix_two, 2 * QUAD)
        pieces, (mix_two, mix_three, joint) = tied_lists(pieces, (mix_two, mix_three, joint))
        mix_three = flipped(mix_three, 3 * QUAD)
        conv_last = plane_last(conv_grads_top(conv_two, joint), place)
    else:
        pieces = square_gather(branch, place.feed_masks)
        conv_whole = conv_grads_whole(conv_shares[0], place)
        mix_grads = attend_grads_whole(mix_grad_in, mix_grad_out, head, place)
        mix_grads = [item[None] for item in mix_grads]
    kept, sent = feed_out_grads(saved_first[2], pieces, place)
    out_split = plane_split(kept, flipped(sent, 1), place)
    pieces, out_split, (second_pack,) = tied_lists(pieces, out_split, (second_pack,))
    second_theirs = flipped(second_pack, place.shards)
    out_lists = plane_early(out_split, place)
    result, branch, slope, first_bias = feed_back(pieces, first_packs, saved_first, place)
    slope, (out_top,) = tied_tops(slope, [out_lists], place)
    slope, second_theirs = tied(slope, second_theirs)
    out_early = out_lists[0]
    if place.aligned:
        slope, mix_three = tied(slope, mix_three)
        mix_own, mix_other, mix_out_sum = attend_grads_sum(
            (mix_zero, joint, mix_two, mix_three, *mix_outs), place
        )
        mix_arrived = flipped(mix_other, 2)
        mix_theirs = [flipped(mix_own, place.shards), None, flipped(mix_out_sum, place.shards)]
    kept, sent = feed_in_grads(saved_first[0], slope, place)
    kept, *result = tied(kept, *result)
    in_swapped = flipped(sent, 1)
    in_lists = plane_early(plane_split(kept, in_swapped, place), place)
    parts = square_reduce(result, place.feed_masks)
    out_last = plane_last(plane_total(out_top), place)
    parts, out_early, *in_lists = tied_lists(parts, out_early, *in_lists.values())
    in_early, in_top = in_lists[0], in_lists[-1]
    in_top = plane_total(in_top)
    if place.aligned:
        parts[0], in_top, mix_arrived, mix_theirs[0], mix_theirs[2], conv_last = tied(
            parts[0], in_top, mix_arrived, mix_theirs[0], mix_theirs[2], conv_last
        )
        mix_theirs[1] = flipped(mix_arrived, place.shards)
        conv_mine = conv_grads_sum(conv_zero, joint, conv_last)
        conv_theirs = flipped(conv_mine, place.shards)
    in_last = plane_last(in_top, place)
    grad_input, input_sums = last_step(parts, grad_first, inputs, wide)
    input_sums, out_last = tied(input_sums, out_last)
    out_sum = plane_add([*out_early, out_last])
    out_theirs = flipped(out_sum, place.shards)
    small_grads, bias_grads, grad_distance = small_reduce(
        (input_sums, first_sums, attend_sums, conv_sums, last_sums),
        mix_sums,
        (first_bias, second_bias),
        grad_distance,
        (wide_rows, tap_count),
        place,
    )
    waited = [*mix_theirs, conv_theirs] if place.aligned else []
    (in_last, out_theirs), waited = tied_lists((in_last, out_theirs), waited)
    in_sum = plane_add([*in_early, in_last])
    in_own, in_other = in_sum[:unit], flipped(in_sum[unit:], 2)
    in_theirs = flipped(in_own, place.shards)
    first_mine = [(in_own, in_theirs), (in_other, flipped(in_other, place.shards))]
    if place.aligned:
        mix_grads = attend_grads_final((mix_own, mix_arrived, mix_out_sum), waited[:3], place)
        conv_grads = conv_grads_final(conv_mine, waited[3], place)
    else:
        conv_grads = (
            jnp.concatenate([conv_whole[0], conv_whole[1]], axis=1)[None],
            conv_whole[2][None],
        )
    in_last_theirs = first_mine[1][1]
    small_outs = [
        bias_grads[None],
        small_grads[count + 1 :][None],
        grad_distance[None],
        small_grads[:count][None],
        small_grads[count : count + 1],
    ]
    in_last_theirs, *small_outs = tied(in_last_theirs, *small_outs)
    first_mine = [first_mine[0], (in_other, in_last_theirs), (out_sum, out_theirs)]
    cuts = (0, unit, 2 * unit, 2 * unit + half)
    second_mine = [
        (second_pack[cuts[i] : cuts[i + 1]], second_theirs[cuts[i] : cuts[i + 1]])
        for i in range(3)
    ]
    feed_grads = feed_final((first_mine, second_mine), place)
    return (
        output,
        grad_input,
        *feed_grads,
        small_outs[0],
        *mix_grads,
        *conv_grads,
        *small_outs[1:],
    )


def solution(mesh):
    in_specs = (
        P(("rep", "shard"), None),
        P(None, None, "shard", None),
        P(None, None, "shard", None),
        P(None, None, "shard"),
        P(None, "shard", None),
        P(None, "shard", None),
        P(None, "shard", None),
        P(None, "shard", None),
        P(None, None, "shard"),
        P(),
        P(None, None, "shard"),
        P(None, "shard"),
        P(("rep", "shard"), None),
    )
    out_specs = (
        P(("rep", "shard"), None),
        P(("rep", "shard"), None),
        P(None, None, "shard", None),
        P(None, None, "shard", None),
        P(None, None, "shard"),
        P(None, "shard", None),
        P(None, "shard", None),
        P(None, "shard", None),
        P(None, "shard", None),
        P(None, None, "shard"),
        P(),
        P(None, None, "shard"),
        P(None, "shard"),
    )
    return jax.shard_map(shards, mesh=mesh, in_specs=in_specs, out_specs=out_specs, check_vma=False)
```
